32 devices in a mesh: dp: 8 (over z, core), expert: 4 (over y, x).
Axes of the slice: x: 2, y: 2, z: 4, core: 2. Of those that a mesh axis runs over, the one named last changes fastest.
Arguments:
- tokens: bfloat16 [32, 36, 36, 384], P(('dp', 'expert')), may hold values from -6 to 6
- shifts: int32 [32, 2], P(('dp', 'expert')), may hold values from 1 to 11
- routes: int32 [32, 1296, 1], P(('dp', 'expert')), may hold values from 0 to 3
- cotangent: bfloat16 [32, 36, 36, 384], P(('dp', 'expert')), may hold values from -6 to 6
- in_weight: bfloat16 [384, 1152], replicated, may hold values from -0.3125 to 0.3125
- in_bias: float32 [2, 384], replicated, may hold values from -3 to 3
- logit_scale: float32 [12], replicated, may hold values from 1.8 to 2.8
- bias_net_first_weight: float32 [2, 512], replicated, may hold values from -6 to 6
- bias_net_first_bias: float32 [512], replicated, may hold values from -3 to 3
- bias_net_second_weight: float32 [512, 12], replicated, may hold values from -0.125 to 0.125
- out_weight: bfloat16 [384, 384], replicated, may hold values from -0.3125 to 0.3125
- out_bias: float32 [384], replicated, may hold values from -3 to 3
- up_weight: bfloat16 [384, 1536], replicated, may hold values from -0.3125 to 0.3125
- up_bias: float32 [1536], replicated, may hold values from -3 to 3
- down_weight: bfloat16 [1536, 384], replicated, may hold values from -0.15625 to 0.15625
- down_bias: float32 [384], replicated, may hold values from -3 to 3
- router_weight: float32 [384, 4], replicated, may hold values from -0.15625 to 0.15625
- expert_up: bfloat16 [4, 384, 1536], P('expert'), may hold values from -0.3125 to 0.3125
- expert_up_bias: float32 [4, 1536], P('expert'), may hold values from -3 to 3
- expert_down: bfloat16 [4, 1536, 384], P('expert'), may hold values from -0.15625 to 0.15625
- expert_down_bias: float32 [4, 384], P('expert'), may hold values from -3 to 3
- norm_gain: float32 [3, 384], replicated, may hold values from 0.5 to 1.5
- norm_bias: float32 [3, 384], replicated, may hold values from -3 to 3
Outputs:
- result: bfloat16 [32, 36, 36, 384], P(('dp', 'expert'))
- tokens_grad: float32 [32, 36, 36, 384], P(('dp', 'expert'))
- in_weight_grad: float32 [384, 1152], replicated
- in_bias_grad: float32 [2, 384], replicated
- logit_scale_grad: float32 [12], replicated
- table_first_grad: float32 [2, 512], replicated
- table_first_bias_grad: float32 [512], replicated
- table_second_grad: float32 [512, 12], replicated
- out_weight_grad: float32 [384, 384], replicated
- out_bias_grad: float32 [384], replicated
- up_weight_grad: float32 [384, 1536], replicated
- up_bias_grad: float32 [1536], replicated
- down_weight_grad: float32 [1536, 384], replicated
- down_bias_grad: float32 [384], replicated
- router_weight_grad: float32 [384, 4], replicated
- expert_up_grad: float32 [4, 384, 1536], P('expert')
- expert_up_bias_grad: float32 [4, 1536], P('expert')
- expert_down_grad: float32 [4, 1536, 384], P('expert')
- expert_down_bias_grad: float32 [4, 384], P('expert')
- norm_gain_grad: float32 [3, 384], replicated
- norm_bias_grad: float32 [3, 384], replicated
The draws below stay inside these ranges and needn't reach their ends.
All inputs are finite; a program needn't handle non-finite values.
Results may differ from the reference program's by a relative error of at most 0.025.
Values may be sent and summed in bfloat16 or wider, within the bound.
A program may use at most 320 MiB of HBM per device.

```python
import jax
import jax.numpy as jnp
from jax import lax

D = 384
ATTENTION_HEADS = 12
FF = 1536
BIAS_NET_UNITS = 512
WS = 12
SIDE = 36
IMG_DEV = 1
EXPERTS = 4
TOK_DEV = 1296
IMAGES = 32
CAP = 405


def plant(drawn, key, low, largest):
    longest = drawn.shape.index(max(drawn.shape))
    spots = []
    for shift in (0, 1):
        where = [jax.random.randint(jax.random.fold_in(key, axis), (), 0, length) for axis, length in enumerate(drawn.shape)]
        where[longest] = (where[longest] + shift) % drawn.shape[longest]
        spots.append(tuple(where))
    return drawn.at[spots[0]].set(low).at[spots[1]].set(largest)


def levels(rng, dims, shards, least, high):
    def one(dim, blocks):
        steps = jax.random.uniform(jax.random.fold_in(jax.random.fold_in(rng, 6), dim), (blocks,), jnp.float32, least / len(shards), high / len(shards))
        return jnp.repeat(jnp.exp(steps), dims[dim] // blocks).reshape((-1,) + (1,) * (len(dims) - dim - 1))

    loudness = one(*shards[0])
    for cut in shards[1:]:
        loudness = loudness * one(*cut)
    return loudness


def picks_of(key, rows, count, top, lift):
    sequence = jax.random.permutation(jax.random.fold_in(key, 1), count)
    pull = sequence
    for power in range(3):
        pull = pull * pull // count
    pull = pull * lift // count
    chance = jax.random.randint(jax.random.fold_in(key, 2), (rows, count), 0, 4096) + pull
    sure = jax.random.permutation(jax.random.fold_in(key, 3), rows)[jnp.arange(count) % rows]
    chance = jnp.where(jnp.arange(rows)[:, None] == sure[None, :], 1 << 14, chance)
    score = chance * count + jnp.arange(count)
    return lax.top_k(score.astype(jnp.int32), top)[1].astype(jnp.int32)


def noise(key, shape, scale, bound, cuts=(), kind=jnp.bfloat16):
    gain = levels(key, shape, cuts, -0.22, 0.18) if cuts else 1.0
    result = jax.random.normal(key, shape, jnp.float32) * scale * gain
    return jnp.minimum(jnp.maximum(result, -bound), bound).astype(kind)


def setup_inputs(seed: int = 0) -> dict:
    key_of = jax.random.split(jax.random.key(seed), 24)
    return {
        "tokens": noise(key_of[0], (IMAGES, SIDE, SIDE, D), 1.0, 6.0, ((0, 32),)),
        "shifts": plant(jax.random.randint(key_of[1], (IMAGES, 2), 1, WS), jax.random.fold_in(key_of[1], 1), 1, WS - 1).astype(jnp.int32),
        "routes": picks_of(key_of[2], IMAGES * (SIDE * SIDE), EXPERTS, 1, 2048).reshape((IMAGES, SIDE * SIDE, 1)),
        "cotangent": noise(key_of[3], (IMAGES, SIDE, SIDE, D), 1.0, 6.0, ((0, 32),)),
        "in_weight": noise(key_of[4], (D, 3 * D), D ** -0.5, 0.3125),
        "in_bias": noise(key_of[5], (2, D), 0.5, 3.0, (), jnp.float32),
        "logit_scale": jnp.clip(jax.random.uniform(key_of[6], (ATTENTION_HEADS,), jnp.float32, 1.8, 2.8), 1.8, 2.8),
        "bias_net_first_weight": noise(key_of[7], (2, BIAS_NET_UNITS), 1.0, 6.0, (), jnp.float32),
        "bias_net_first_bias": noise(key_of[8], (BIAS_NET_UNITS,), 0.5, 3.0, (), jnp.float32),
        "bias_net_second_weight": noise(key_of[9], (BIAS_NET_UNITS, ATTENTION_HEADS), 0.02, 0.125, (), jnp.float32),
        "out_weight": noise(key_of[10], (D, D), D ** -0.5, 0.3125),
        "out_bias": noise(key_of[11], (D,), 0.5, 3.0, (), jnp.float32),
        "up_weight": noise(key_of[12], (D, FF), D ** -0.5, 0.3125),
        "up_bias": noise(key_of[13], (FF,), 0.5, 3.0, (), jnp.float32),
        "down_weight": noise(key_of[14], (FF, D), FF ** -0.5, 0.15625),
        "down_bias": noise(key_of[15], (D,), 0.5, 3.0, (), jnp.float32),
        "router_weight": noise(key_of[16], (D, EXPERTS), (4 * D) ** -0.5, 0.15625, (), jnp.float32),
        "expert_up": noise(key_of[17], (EXPERTS, D, FF), D ** -0.5, 0.3125, ((0, 4),)),
        "expert_up_bias": noise(key_of[18], (EXPERTS, FF), 0.5, 3.0, ((0, 4),), jnp.float32),
        "expert_down": noise(key_of[19], (EXPERTS, FF, D), FF ** -0.5, 0.15625, ((0, 4),)),
        "expert_down_bias": noise(key_of[20], (EXPERTS, D), 0.5, 3.0, ((0, 4),), jnp.float32),
        "norm_gain": jnp.clip(1.0 + 0.1 * jax.random.normal(key_of[21], (3, D), jnp.float32), 0.5, 1.5),
        "norm_bias": noise(key_of[22], (3, D), 0.5, 3.0, (), jnp.float32),
    }


@jax.custom_vjp
def low(v):
    return lax.optimization_barrier(v.astype(jnp.bfloat16)).astype(jnp.float32)

@jax.custom_vjp
def low_back(v):
    return v

def low_keep(v):
    return (low(v), None)

def low_pass(kept, grad):
    return (grad,)

def back_keep(v):
    return (v, None)

def back_low(kept, grad):
    return (low(grad),)
low.defvjp(low_keep, low_pass)
low_back.defvjp(back_keep, back_low)

def matmul(operand, matrix):
    return jnp.dot(operand, matrix, precision=lax.Precision.HIGHEST)

def smooth(values):
    return jax.nn.gelu(values, approximate=False)

def layer_norm(values, scales, offset):
    centered = values - lax.optimization_barrier(jnp.mean(values, axis=-1, keepdims=True))
    spread = lax.optimization_barrier(jnp.mean(centered * centered, axis=-1, keepdims=True))
    return centered * lax.rsqrt(spread + 1e-05) * scales + offset

def unit_heads(values):
    shaped = values.reshape(values.shape[:-1] + (ATTENTION_HEADS, D // ATTENTION_HEADS))
    shaped = shaped * lax.rsqrt(1.0 + lax.optimization_barrier(jnp.sum(shaped * shaped, axis=-1, keepdims=True)))
    return shaped.reshape(values.shape)

def to_windows(picture):
    across = SIDE // WS
    shaped = picture.reshape(across, WS, across, WS, picture.shape[-1])
    return shaped.transpose(0, 2, 1, 3, 4).reshape(across * across, WS * WS, picture.shape[-1])

def from_windows(windows):
    across = SIDE // WS
    shaped = windows.reshape(across, across, WS, WS, windows.shape[-1])
    return shaped.transpose(0, 2, 1, 3, 4).reshape(SIDE, SIDE, windows.shape[-1])

def window_mask(offsets):
    places = jnp.arange(SIDE, dtype=jnp.int32)

    def region(amount):
        return jnp.where(places < SIDE - WS, 0, jnp.where(places < SIDE - amount, 1, 2)).astype(jnp.int32)
    labels = region(offsets[0])[:, None] * 3 + region(offsets[1])[None, :]
    window_labels = to_windows(labels[:, :, None])[:, :, 0]
    matching = window_labels[:, :, None] == window_labels[:, None, :]
    return jnp.where(matching, 0.0, -100.0).astype(jnp.float32)

def relative_bias(bias_net_first_weight, bias_net_first_bias, bias_net_second_weight):
    extent = 2 * WS - 1
    steps_along = (jnp.arange(extent, dtype=jnp.int32) - (WS - 1)).astype(jnp.float32) * (8.0 / (WS - 1))
    logged = jnp.sign(steps_along) * jnp.log2(jnp.abs(steps_along) + 1.0) / 3.0
    coords_table = jnp.stack([jnp.repeat(logged, extent), jnp.tile(logged, extent)], axis=1)
    layer_out = smooth(matmul(coords_table, bias_net_first_weight) + bias_net_first_bias)
    values = 16.0 * jax.nn.sigmoid(matmul(layer_out, bias_net_second_weight))
    places = jnp.arange(WS * WS, dtype=jnp.int32)
    rows_at = places // WS
    cols_at = places % WS
    lookup = (rows_at[:, None] - rows_at[None, :] + WS - 1) * extent + (cols_at[:, None] - cols_at[None, :] + WS - 1)
    picked = jnp.take(values, lookup.reshape(-1), axis=0)
    return picked.T.reshape(ATTENTION_HEADS, WS * WS, WS * WS)

def image_layer(picture, offsets, bias_table, dense_set):
    in_weight, in_bias, logit_scale, out_weight, out_bias, up_weight, up_bias, down_weight, down_bias, norm_gain, norm_bias = dense_set
    rolled = jnp.roll(picture, (-offsets[0], -offsets[1]), axis=(0, 1))
    windows = to_windows(rolled)
    number = windows.shape[0]
    head_shape = (number, WS * WS, ATTENTION_HEADS, D // ATTENTION_HEADS)
    complete_bias = jnp.concatenate([in_bias[0], jnp.zeros_like(in_bias[0]), in_bias[1]])
    joint_rows = low_back(matmul(windows.reshape(-1, D), in_weight) + complete_bias)
    queries = low(unit_heads(joint_rows[:, :D])).reshape(head_shape)
    keys_part = low(unit_heads(joint_rows[:, D:2 * D])).reshape(head_shape)
    values = low(joint_rows[:, 2 * D:]).reshape(head_shape)
    raw_scores = low_back(jnp.einsum('nqhd,nkhd->nhqk', queries, keys_part, precision=lax.Precision.HIGHEST))
    scores = raw_scores * jnp.exp(logit_scale)[None, :, None, None] + bias_table[None] + window_mask(offsets)[:, None]
    softmax_result = low(jax.nn.softmax(scores, axis=-1))
    mixture = jnp.einsum('nhqk,nkhd->nqhd', softmax_result, values, precision=lax.Precision.HIGHEST)
    mixture = low(low_back(mixture.reshape(-1, D)))
    branch = low_back(matmul(mixture, out_weight) + out_bias)
    normed = layer_norm(branch, norm_gain[0], norm_bias[0])
    restored = jnp.roll(from_windows(normed.reshape(number, WS * WS, D)), (offsets[0], offsets[1]), axis=(0, 1))
    first_out = (picture + restored).reshape(-1, D)
    hidden = low_back(matmul(low(first_out), up_weight) + up_bias)
    activated = low(smooth(hidden))
    second_branch = low_back(matmul(activated, down_weight) + down_bias)
    return first_out + layer_norm(second_branch, norm_gain[1], norm_bias[1])

def expert_layer(flat_tokens, chosen, router_weight, experts, norm_gain, norm_bias):
    expert_up, expert_up_bias, expert_down, expert_down_bias = experts
    logits = matmul(flat_tokens, router_weight)
    router_probs = jax.nn.softmax(logits, axis=-1)
    onehot = chosen[:, None] == jnp.arange(EXPERTS, dtype=jnp.int32)[None, :]
    gate_value = lax.optimization_barrier(jnp.sum(jnp.where(onehot, router_probs, 0.0), axis=-1))
    running = jnp.cumsum(onehot.astype(jnp.int32), axis=0)
    position = lax.optimization_barrier(jnp.sum(jnp.where(onehot, running, 0), axis=-1)) - 1
    kept_mask = position < CAP
    slot_index = jnp.where(kept_mask, chosen * CAP + position, EXPERTS * CAP).astype(jnp.int32)
    buffer = jnp.zeros((EXPERTS * CAP + 1, D), jnp.float32).at[slot_index].add(low(flat_tokens))
    buffer = low_back(buffer[:-1].reshape(EXPERTS, CAP, D))
    hidden = low_back(jnp.einsum('ecd,edf->ecf', buffer, expert_up, precision=lax.Precision.HIGHEST) + expert_up_bias[:, None, :])
    activated = low(smooth(hidden))
    output = jnp.einsum('ecf,efd->ecd', activated, expert_down, precision=lax.Precision.HIGHEST) + expert_down_bias[:, None, :]
    output = low(low_back(output)).reshape(EXPERTS * CAP, D)
    picked = output[jnp.minimum(slot_index, EXPERTS * CAP - 1)]
    branch = jnp.where(kept_mask[:, None], gate_value[:, None] * picked, 0.0)
    return flat_tokens + layer_norm(branch, norm_gain[2], norm_bias[2])

def reference(tokens, shifts, routes, cotangent, in_weight, in_bias, logit_scale, bias_net_first_weight, bias_net_first_bias, bias_net_second_weight, out_weight, out_bias, up_weight, up_bias, down_weight, down_bias, router_weight, expert_up, expert_up_bias, expert_down, expert_down_bias, norm_gain, norm_bias):
    params = tuple((member.astype(jnp.float32) for member in (in_weight, in_bias, logit_scale, bias_net_first_weight, bias_net_first_bias, bias_net_second_weight, out_weight, out_bias, up_weight, up_bias, down_weight, down_bias, router_weight, expert_up, expert_up_bias, expert_down, expert_down_bias, norm_gain, norm_bias)))

    def forward(image_data, weights_all):
        in_weight, in_bias, logit_scale, bias_net_first_weight, bias_net_first_bias, bias_net_second_weight, out_weight, out_bias, up_weight, up_bias, down_weight, down_bias, router_weight, expert_up, expert_up_bias, expert_down, expert_down_bias, norm_gain, norm_bias = weights_all
        bias_table = relative_bias(bias_net_first_weight, bias_net_first_bias, bias_net_second_weight)
        dense_set = (in_weight, in_bias, logit_scale, out_weight, out_bias, up_weight, up_bias, down_weight, down_bias, norm_gain, norm_bias)
        experts = (expert_up, expert_up_bias, expert_down, expert_down_bias)

        @jax.checkpoint
        def group_step(images, shift_group, route_group):
            layer_one = jax.vmap(lambda single, offsets: image_layer(single, offsets, bias_table, dense_set))(images, shift_group)
            return expert_layer(layer_one.reshape(-1, D), route_group, router_weight, experts, norm_gain, norm_bias)

        def scan_step(carried, pieces):
            return (carried, group_step(pieces[0], pieces[1], pieces[2]))
        groups = (image_data.reshape(-1, IMG_DEV, SIDE, SIDE, D), shifts.reshape(-1, IMG_DEV, 2), routes.reshape(-1, TOK_DEV))
        unused, outputs = lax.scan(scan_step, jnp.zeros((), jnp.float32), groups)
        return outputs.reshape(IMAGES, SIDE, SIDE, D)
    outputs, pullback = jax.vjp(forward, tokens.astype(jnp.float32), params)
    tokens_grad, weight_grads = pullback(cotangent.astype(jnp.float32))
    return (outputs.astype(jnp.bfloat16), tokens_grad, weight_grads[0], weight_grads[1], weight_grads[2], weight_grads[3], weight_grads[4], weight_grads[5], weight_grads[6], weight_grads[7], weight_grads[8], weight_grads[9], weight_grads[10], weight_grads[11], weight_grads[12], weight_grads[13], weight_grads[14], weight_grads[15], weight_grads[16], weight_grads[17], weight_grads[18])
```

```python
import functools

import jax
import jax.numpy as jnp
from jax import lax
from jax.experimental import pallas as pl
from jax.experimental.pallas import tpu as pltpu
from jax.sharding import PartitionSpec as P

D = 384
HEADS = 12
HEAD = D // HEADS
WS = 12
SIDE = 36
AREA = WS * WS
ACROSS = SIDE // WS
WINDOWS = ACROSS * ACROSS
TOKENS = SIDE * SIDE
FF = 1536
EXTENT = 2 * WS - 1
UNITS = 512
TABLE = 640
ROWS = 432
CHUNK = 256
F32 = jnp.float32
BF16 = jnp.bfloat16
I32 = jnp.int32
VMEM_LIMIT = 60 * 1024 * 1024


def dot(left, right, left_dim, right_dim):
    return lax.dot_general(
        left, right, (((left_dim,), (right_dim,)), ((), ())), preferred_element_type=F32
    )


def exact_dot(left, right, left_dim, right_dim):
    return lax.dot_general(
        left,
        right,
        (((left_dim,), (right_dim,)), ((), ())),
        preferred_element_type=F32,
        precision=lax.Precision.HIGHEST,
    )


def split(values):
    high = values.astype(BF16)
    return high, (values - high.astype(F32)).astype(BF16)


def iota(shape, dim):
    return lax.broadcasted_iota(I32, shape, dim)


def gelu_pair(values):
    size = jnp.abs(values)
    t = 1.0 / (1.0 + 0.2316419 * size)
    bell = jnp.exp(-0.5 * values * values) * 0.3989422804014327
    series = t * (
        0.319381530
        + t * (-0.356563782 + t * (1.781477937 + t * (-1.821255978 + t * 1.330274429)))
    )
    tail = series * bell
    phi = jnp.where(values >= 0.0, 1.0 - tail, tail)
    return values * phi, phi + values * bell


def norm_parts(values):
    centered = values - jnp.mean(values, axis=-1, keepdims=True)
    rstd = lax.rsqrt(jnp.mean(centered * centered, axis=-1, keepdims=True) + 1e-05)
    return centered * rstd, rstd


def norm_back(grad_n, n, rstd):
    return rstd * (
        grad_n
        - jnp.mean(grad_n, axis=-1, keepdims=True)
        - n * jnp.mean(grad_n * n, axis=-1, keepdims=True)
    )


def col_sum(values):
    return jnp.sum(values, axis=0, keepdims=True)


def div_ws(values):
    return (values * 171) >> 11


def full(shape, dtype=F32):
    return jax.ShapeDtypeStruct(shape, dtype)


def whole(shape):
    return pl.BlockSpec(shape, lambda *_: (0,) * len(shape))


def smem():
    return pl.BlockSpec(memory_space=pltpu.SMEM)


def params(**more):
    return pltpu.CompilerParams(vmem_limit_bytes=VMEM_LIMIT, **more)


def offsets_row(shape, dim, sign):
    place = iota(shape, dim)
    row = jnp.floor((place.astype(F32) + 0.5) * (1.0 / EXTENT)).astype(I32)
    col = place - row * EXTENT

    def logged(step):
        e = sign * (step - (WS - 1)).astype(F32) * (8.0 / (WS - 1))
        size = jnp.log2(jnp.abs(e) + 1.0) * (1.0 / 3.0)
        return jnp.where(e < 0.0, -size, size)

    return logged(row), logged(col)


def spread_matrix(mirrored):
    token = iota((384, AREA), 1)
    row = div_ws(token)
    lin = row * EXTENT + (token - row * WS)
    if mirrored:
        lin = (WS - 1) * EXTENT + (WS - 1) - lin
    return (iota((384, AREA), 0) == lin).astype(F32)


def prep_kernel(
    capacity, routes, cot, w1, b1, w2, ls, slot_col, slot_row, zbuf, table, scale, flat, u_ref
):
    slots = zbuf.shape[1]
    experts = zbuf.shape[0]
    before = (iota((AREA, AREA), 1) < iota((AREA, AREA), 0)).astype(BF16)
    carry = jnp.zeros((1, 128), F32)
    for block in range(TOKENS // AREA):
        rows = pl.ds(block * AREA, AREA)
        route = routes[rows, :]
        onehot = (route == iota((AREA, 128), 1)).astype(F32)
        ahead = dot(before, onehot.astype(BF16), 1, 0) + carry
        position = jnp.sum(ahead * onehot, axis=1, keepdims=True)
        carry = carry + col_sum(onehot)
        slot = route.astype(F32) * slots + position
        slot_col[rows, :] = jnp.where(position < capacity, slot, -1.0).astype(I32)
    slot_row[...] = jnp.transpose(
        jnp.broadcast_to(slot_col[...].astype(F32), (TOKENS, 128)), (1, 0)
    )[0:1, :].astype(I32)

    for row in range(SIDE):
        flat[row * SIDE : (row + 1) * SIDE, :] = cot[row].astype(F32)
    low = flat[...].astype(BF16)
    for expert in range(experts):
        pick = (iota((slots, TOKENS), 0) + expert * slots == slot_row[...]).astype(BF16)
        zbuf[expert] = dot(pick, low, 1, 0).astype(BF16)

    scale[...] = jnp.exp(ls[...])
    f_row, f_col = offsets_row((UNITS, TABLE), 1, 1.0)
    w1t = jnp.transpose(w1[...], (1, 0))
    b1t = jnp.transpose(b1[...], (1, 0))
    hidden, _ = gelu_pair(w1t[:, 0:1] * f_row + w1t[:, 1:2] * f_col + b1t[:, 0:1])
    values = 16.0 * jax.nn.sigmoid(exact_dot(w2[...], hidden, 0, 0))
    spread = spread_matrix(False).astype(BF16)
    for head in range(HEADS):
        line = jnp.broadcast_to(values[head : head + 1, :], (16, TABLE))
        line = pltpu.roll(line, 0, 1, stride=1, stride_axis=0)
        for key_row in range(WS):
            shift = (EXTENT * key_row - (WS - 1) * EXTENT - (WS - 1)) % TABLE
            rolled = pltpu.roll(line, shift, 1)
            u_ref[key_row * WS : (key_row + 1) * WS, :] = rolled[:WS, :384]
        high, low_part = split(u_ref[...])
        table[head] = dot(high, spread, 1, 0) + dot(low_part, spread, 1, 0)


def prep(routes, cotangent, w1, b1, w2, ls, experts, capacity, slots):
    return pl.pallas_call(
        functools.partial(prep_kernel, capacity),
        out_shape=(
            full((TOKENS, 1), I32),
            full((1, TOKENS), I32),
            full((experts, slots, D), BF16),
            full((HEADS, AREA, AREA)),
            full((1, HEADS)),
        ),
        scratch_shapes=[pltpu.VMEM((TOKENS, D), F32), pltpu.VMEM((AREA, 384), F32)],
        compiler_params=params(),
        name="prep",
    )(routes, cotangent, w1, b1, w2, ls)


def window_labels(window, shift_row, shift_col):
    def labels(shape, dim):
        token = iota(shape, dim)
        row = div_ws(token)
        col = token - row * WS + lax.rem(window, ACROSS) * WS
        row = row + lax.div(window, ACROSS) * WS

        def region(place, shift):
            last = jnp.where(place < SIDE - shift, 1, 2)
            return jnp.where(place < SIDE - WS, 0, last)

        return region(row, shift_row) * 3 + region(col, shift_col)

    return labels((AREA, 1), 0), labels((1, AREA), 1)


def roll_to_windows(read_row, doubled, windows, shift_row, shift_col):
    for row in range(SIDE):
        line = read_row(row)
        doubled[row, :SIDE, :] = line
        doubled[row, SIDE:, :] = line[:WS, :]
    for row in range(SIDE):
        source = row + shift_row
        source = jnp.where(source >= SIDE, source - SIDE, source)
        line = pltpu.roll(doubled[source], SIDE + WS - shift_col, 0)
        for across in range(ACROSS):
            start = ((row // WS) * ACROSS + across) * AREA + (row % WS) * WS
            windows[start : start + WS, :] = line[across * WS : (across + 1) * WS, :]


def roll_to_image(windows, doubled, write_row, shift_row, shift_col):
    for row in range(SIDE):
        for across in range(ACROSS):
            start = ((row // WS) * ACROSS + across) * AREA + (row % WS) * WS
            line = windows[start : start + WS, :]
            doubled[row, across * WS : (across + 1) * WS, :] = line
            if across == ACROSS - 1:
                doubled[row, SIDE:, :] = line
    for row in range(SIDE):
        source = row - shift_row
        source = jnp.where(source < 0, source + SIDE, source)
        write_row(row, pltpu.roll(doubled[source], shift_col, 0)[:SIDE, :])


def attend_kernel(
    shifts, scale, tokens, in_weight, in_bias, table, out_weight, out_bias, gain, offset,
    normed, n_out, rstd_out, joint, probs, mixture, win_t, inverse,
    doubled, windows, in_weight_t, bias_col,
):
    window = pl.program_id(0)
    shift_row, shift_col = shifts[0, 0], shifts[0, 1]

    @pl.when(window == 0)
    def _():
        roll_to_windows(
            lambda row: tokens[row].astype(F32), doubled, windows, shift_row, shift_col
        )
        in_weight_t[...] = jnp.transpose(in_weight[...], (1, 0))
        bias_col[:, 0:2] = jnp.transpose(in_bias[...], (1, 0))

    mine = windows[pl.ds(pl.multiple_of(window * AREA, 16), AREA), :].astype(BF16)
    win_t[0, :D, :] = jnp.transpose(mine, (1, 0))
    win_t[0, D:, :] = (iota((16, AREA), 0) == 0).astype(BF16)
    label_keys, label_queries = window_labels(window, shift_row, shift_col)
    mask = jnp.where(label_keys == label_queries, 0.0, -100.0)
    for head in range(HEADS):
        at = head * HEAD
        query = dot(in_weight_t[at : at + HEAD, :], mine, 1, 1) + bias_col[at : at + HEAD, 0:1]
        key = dot(in_weight_t[D + at : D + at + HEAD, :], mine, 1, 1)
        value = (
            dot(in_weight_t[2 * D + at : 2 * D + at + HEAD, :], mine, 1, 1)
            + bias_col[at : at + HEAD, 1:2]
        ).astype(BF16)
        query_inverse = lax.rsqrt(1.0 + col_sum(query * query))
        key_inverse = lax.rsqrt(1.0 + col_sum(key * key))
        query = (query * query_inverse).astype(BF16)
        key = (key * key_inverse).astype(BF16)
        scores = dot(key, query, 0, 0) * scale[0, head] + (table[head] + mask)
        exponent = jnp.exp(scores - jnp.max(scores, axis=0, keepdims=True))
        low = (exponent * (1.0 / col_sum(exponent))).astype(BF16)
        mixture[0, at : at + HEAD, :] = dot(value, low, 1, 0).astype(BF16)
        probs[0, head] = low
        joint[0, at : at + HEAD, :] = query
        joint[0, D + at : D + at + HEAD, :] = key
        joint[0, 2 * D + at : 2 * D + at + HEAD, :] = value
        inverse[0, head : head + 1, :] = query_inverse
        inverse[0, HEADS + head : HEADS + head + 1, :] = key_inverse
    branch = dot(mixture[0], out_weight[...], 0, 0) + out_bias[...]
    n, rstd = norm_parts(branch)
    normed[...] = n * gain[0:1, :] + offset[0:1, :]
    n_out[...] = n.astype(BF16)
    rstd_out[...] = rstd


def attend(shifts, scale, tokens, in_weight, in_bias, table, out_weight, out_bias, gain, offset):
    per_window = lambda *dims: pl.BlockSpec((1,) + dims, lambda w: (w,) + (0,) * len(dims))
    rows = lambda width: pl.BlockSpec((AREA, width), lambda w: (w, 0))
    return pl.pallas_call(
        attend_kernel,
        grid=(WINDOWS,),
        in_specs=[
            smem(),
            smem(),
            whole((SIDE, SIDE, D)),
            whole((D, 3 * D)),
            whole((2, D)),
            whole((HEADS, AREA, AREA)),
            whole((D, D)),
            whole((1, D)),
            whole((3, D)),
            whole((3, D)),
        ],
        out_specs=(
            rows(D),
            rows(D),
            rows(1),
            per_window(3 * D, AREA),
            per_window(HEADS, AREA, AREA),
            per_window(D, AREA),
            per_window(D + 16, AREA),
            per_window(2 * HEADS, AREA),
        ),
        out_shape=(
            full((TOKENS, D)),
            full((TOKENS, D), BF16),
            full((TOKENS, 1)),
            full((WINDOWS, 3 * D, AREA), BF16),
            full((WINDOWS, HEADS, AREA, AREA), BF16),
            full((WINDOWS, D, AREA), BF16),
            full((WINDOWS, D + 16, AREA), BF16),
            full((WINDOWS, 2 * HEADS, AREA)),
        ),
        scratch_shapes=[
            pltpu.VMEM((SIDE, SIDE + WS, D), F32),
            pltpu.VMEM((TOKENS, D), F32),
            pltpu.VMEM((3 * D, D), BF16),
            pltpu.VMEM((D, 128), F32),
        ],
        compiler_params=params(),
        name="attend",
    )(shifts, scale, tokens, in_weight, in_bias, table, out_weight, out_bias, gain, offset)


def forward_kernel(
    shifts, tokens, normed, up, up_bias, down, down_bias, gain, offset, slot_row,
    first_low, active, slope, n_out, rstd_out, second, buffer,
    doubled, image, second_low,
):
    step = pl.program_id(0)

    @pl.when(step == 0)
    def _():
        def write_row(row, line):
            image[row * SIDE : (row + 1) * SIDE, :] = line + tokens[row].astype(F32)

        roll_to_image(normed, doubled, write_row, shifts[0, 0], shifts[0, 1])

    rows = pl.ds(pl.multiple_of(step * ROWS, 16), ROWS)
    first = image[rows, :]
    low = first.astype(BF16)
    first_low[...] = low
    branch = jnp.broadcast_to(down_bias[...], (ROWS, D))
    for at in range(0, FF, CHUNK):
        hidden = dot(low, up[:, at : at + CHUNK], 1, 0) + up_bias[:, at : at + CHUNK]
        activated, derivative = gelu_pair(hidden)
        activated = activated.astype(BF16)
        active[:, at : at + CHUNK] = activated
        slope[:, at : at + CHUNK] = derivative.astype(BF16)
        branch += dot(activated, down[at : at + CHUNK, :], 1, 0)
    n, rstd = norm_parts(branch)
    n_out[...] = n.astype(BF16)
    rstd_out[...] = rstd
    result = first + n * gain[1:2, :] + offset[1:2, :]
    second[...] = result
    second_low[rows, :] = result.astype(BF16)

    @pl.when(step == TOKENS // ROWS - 1)
    def _():
        slots = buffer.shape[1]
        for expert in range(buffer.shape[0]):
            pick = (iota((slots, TOKENS), 0) + expert * slots == slot_row[...]).astype(BF16)
            buffer[expert] = dot(pick, second_low[...], 1, 0).astype(BF16)


def forward(
    shifts, tokens, normed, up, up_bias, down, down_bias, gain, offset, slot_row, experts, slots
):
    rows = lambda width: pl.BlockSpec((ROWS, width), lambda i: (i, 0))
    return pl.pallas_call(
        forward_kernel,
        grid=(TOKENS // ROWS,),
        in_specs=[
            smem(),
            whole((SIDE, SIDE, D)),
            whole((TOKENS, D)),
            whole((D, FF)),
            whole((1, FF)),
            whole((FF, D)),
            whole((1, D)),
            whole((3, D)),
            whole((3, D)),
            whole((1, TOKENS)),
        ],
        out_specs=(
            rows(D),
            rows(FF),
            rows(FF),
            rows(D),
            rows(1),
            rows(D),
            whole((experts, slots, D)),
        ),
        out_shape=(
            full((TOKENS, D), BF16),
            full((TOKENS, FF), BF16),
            full((TOKENS, FF), BF16),
            full((TOKENS, D), BF16),
            full((TOKENS, 1)),
            full((TOKENS, D)),
            full((experts, slots, D), BF16),
        ),
        scratch_shapes=[
            pltpu.VMEM((SIDE, SIDE + WS, D), F32),
            pltpu.VMEM((TOKENS, D), F32),
            pltpu.VMEM((TOKENS, D), BF16),
        ],
        compiler_params=params(),
        name="forward",
    )(shifts, tokens, normed, up, up_bias, down, down_bias, gain, offset, slot_row)


def expert_kernel(
    arrived, cot, router, up, up_bias, down, down_bias, gain,
    out, grad_in, up_grad, up_bias_grad, down_grad_t, down_bias_grad,
    active, slope, grad_hidden_sum,
):
    source = pl.program_id(0)
    me = lax.axis_index("expert")

    @pl.when(source == 0)
    def _():
        for ref in (up_grad, up_bias_grad, down_grad_t, down_bias_grad):
            ref[...] = jnp.zeros_like(ref)

    features = arrived[0]
    slots = features.shape[0]
    router_high, router_low = split(router[...])
    logits = dot(features, router_high, 1, 0) + dot(features, router_low, 1, 0)
    chances = jnp.exp(logits - jnp.max(logits, axis=1, keepdims=True))
    own = jnp.where(iota(chances.shape, 1) == me, chances, 0.0)
    gate = jnp.sum(own, axis=1, keepdims=True) / jnp.sum(chances, axis=1, keepdims=True)

    output = jnp.broadcast_to(down_bias[...], (slots, D))
    for at in range(0, FF, CHUNK):
        hidden = dot(features, up[:, at : at + CHUNK], 1, 0) + up_bias[:, at : at + CHUNK]
        activated, derivative = gelu_pair(hidden)
        activated = activated.astype(BF16)
        active[:, at : at + CHUNK] = activated
        slope[:, at : at + CHUNK] = derivative
        output += dot(activated, down[at : at + CHUNK, :], 1, 0)
    output = output.astype(BF16)
    out[0] = output
    n, rstd = norm_parts(gate * output.astype(F32))
    grad_output = gate * norm_back(gain[2:3, :] * cot[0].astype(F32), n, rstd)
    grad_low = grad_output.astype(BF16)
    down_bias_grad[...] += col_sum(grad_low.astype(F32))
    grad_low_t = jnp.transpose(grad_low, (1, 0))
    features_t = jnp.transpose(features, (1, 0))
    grad_features = jnp.zeros((slots, D), F32)
    for at in range(0, FF, CHUNK):
        part = slice(at, at + CHUNK)
        grad_hidden = dot(grad_low, down[part, :], 1, 1) * slope[:, part]
        grad_hidden_low = grad_hidden.astype(BF16)
        up_bias_grad[:, part] += col_sum(grad_hidden)
        down_grad_t[:, part] += dot(grad_low_t, active[:, part], 1, 0)
        up_grad[:, part] += dot(features_t, grad_hidden_low, 1, 0)
        grad_features += dot(grad_hidden_low, up[:, part], 1, 1)
    grad_in[0] = grad_features.astype(BF16)


def run_experts(arrived, cot, router, up, up_bias, down, down_bias, gain):
    sources, slots, _ = arrived.shape
    block = pl.BlockSpec((1, slots, D), lambda i: (i, 0, 0))
    return pl.pallas_call(
        expert_kernel,
        grid=(sources,),
        in_specs=[
            block,
            block,
            whole(router.shape),
            whole((D, FF)),
            whole((1, FF)),
            whole((FF, D)),
            whole((1, D)),
            whole((3, D)),
        ],
        out_specs=(
            block,
            block,
            whole((D, FF)),
            whole((1, FF)),
            whole((D, FF)),
            whole((1, D)),
        ),
        out_shape=(
            full((sources, slots, D), BF16),
            full((sources, slots, D), BF16),
            full((D, FF)),
            full((1, FF)),
            full((D, FF)),
            full((1, D)),
        ),
        scratch_shapes=[
            pltpu.VMEM((slots, FF), BF16),
            pltpu.VMEM((slots, FF), F32),
            pltpu.VMEM((8, 128), F32),
        ],
        compiler_params=params(),
        name="experts",
    )(arrived, cot, router, up, up_bias, down, down_bias, gain)


def backward_kernel(
    second, cot, slot_col, routes, outputs, grads, router, first_low, active, slope, n_in, rstd_in,
    up, down, gain, offset,
    result, grad_first, up_grad, up_bias_grad, down_grad_t, down_bias_grad, router_grad,
    gain_grad, offset_grad,
    flat,
):
    step = pl.program_id(0)

    @pl.when(step == 0)
    def _():
        for ref in (
            up_grad, up_bias_grad, down_grad_t, down_bias_grad, router_grad, gain_grad, offset_grad
        ):
            ref[...] = jnp.zeros_like(ref)

    lines = ROWS // SIDE
    for line in range(lines):
        flat[line * SIDE : (line + 1) * SIDE, :] = cot[line].astype(F32)
    z = flat[...]
    x = second[...]
    slots_all = outputs.shape[0]
    pick = (slot_col[...] == iota((ROWS, slots_all), 1)).astype(BF16)
    picked = dot(pick, outputs[...], 1, 0)
    dispatched = dot(pick, grads[...], 1, 0)

    logits = exact_dot(x, router[...], 1, 0)
    chances = jnp.exp(logits - jnp.max(logits, axis=1, keepdims=True))
    chances = chances / jnp.sum(chances, axis=1, keepdims=True)
    onehot = (routes[...] == iota(chances.shape, 1)).astype(F32)
    gate = jnp.sum(chances * onehot, axis=1, keepdims=True)
    n, rstd = norm_parts(gate * picked)
    final = x + n * gain[2:3, :] + offset[2:3, :]
    gain_grad[2:3, :] += col_sum(z * n)
    offset_grad[2:3, :] += col_sum(z)
    grad_moe = norm_back(gain[2:3, :] * z, n, rstd)
    grad_gate = jnp.sum(grad_moe * picked, axis=1, keepdims=True)
    grad_logits = grad_gate * gate * (onehot - chances)
    grad_logits_low = grad_logits.astype(BF16)
    router_grad[...] += dot(x.astype(BF16), grad_logits_low, 0, 0)
    grad_second = z + dispatched + dot(grad_logits_low, router[...].astype(BF16), 1, 1)

    n = n_in[...].astype(F32)
    gain_grad[1:2, :] += col_sum(grad_second * n)
    offset_grad[1:2, :] += col_sum(grad_second)
    grad_branch = norm_back(gain[1:2, :] * grad_second, n, rstd_in[...])
    grad_low = grad_branch.astype(BF16)
    down_bias_grad[...] += col_sum(grad_branch)
    grad_low_t = jnp.transpose(grad_low, (1, 0))
    first_t = jnp.transpose(first_low[...], (1, 0))
    total = jnp.zeros((ROWS, D), F32)
    for at in range(0, FF, CHUNK):
        part = slice(at, at + CHUNK)
        grad_hidden = dot(grad_low, down[part, :], 1, 1) * slope[:, part].astype(F32)
        grad_hidden_low = grad_hidden.astype(BF16)
        up_bias_grad[:, part] += col_sum(grad_hidden)
        down_grad_t[:, part] += dot(grad_low_t, active[:, part], 1, 0)
        up_grad[:, part] += dot(first_t, grad_hidden_low, 1, 0)
        total += dot(grad_hidden_low, up[:, part], 1, 1)
    grad_first[...] = total + grad_second
    flat[...] = final
    for line in range(lines):
        result[line] = flat[line * SIDE : (line + 1) * SIDE, :].astype(BF16)


def backward(
    second, cot, slot_col, routes, outputs, grads, router, first_low, active, slope, n, rstd,
    up, down, gain, offset,
):
    rows = lambda width: pl.BlockSpec((ROWS, width), lambda i: (i, 0))
    lines = pl.BlockSpec((ROWS // SIDE, SIDE, D), lambda i: (i, 0, 0))
    slots_all = outputs.shape[0]
    return pl.pallas_call(
        backward_kernel,
        grid=(TOKENS // ROWS,),
        in_specs=[
            rows(D),
            lines,
            rows(1),
            rows(1),
            whole((slots_all, D)),
            whole((slots_all, D)),
            whole(router.shape),
            rows(D),
            rows(FF),
            rows(FF),
            rows(D),
            rows(1),
            whole((D, FF)),
            whole((FF, D)),
            whole((3, D)),
            whole((3, D)),
        ],
        out_specs=(
            lines,
            rows(D),
            whole((D, FF)),
            whole((1, FF)),
            whole((D, FF)),
            whole((1, D)),
            whole(router.shape),
            whole((3, D)),
            whole((3, D)),
        ),
        out_shape=(
            full((SIDE, SIDE, D), BF16),
            full((TOKENS, D)),
            full((D, FF)),
            full((1, FF)),
            full((D, FF)),
            full((1, D)),
            full(router.shape),
            full((3, D)),
            full((3, D)),
        ),
        scratch_shapes=[pltpu.VMEM((ROWS, D), F32)],
        compiler_params=params(),
        name="backward",
    )(
        second, cot, slot_col, routes, outputs, grads, router, first_low, active, slope, n, rstd,
        up, down, gain, offset,
    )


def attend_back_kernel(
    shifts, scale, grad_first, n_in, rstd_in, joint, probs, mixture, win_t, inverse,
    in_weight, out_weight, gain,
    tokens_grad, in_grad, out_grad, out_bias_grad, gain_grad, offset_grad, scale_grad, table_grad,
    doubled, windows, joint_grad,
):
    window = pl.program_id(0)
    shift_row, shift_col = shifts[0, 0], shifts[0, 1]

    @pl.when(window == 0)
    def _():
        for ref in (
            in_grad, out_grad, out_bias_grad, gain_grad, offset_grad, scale_grad, table_grad
        ):
            ref[...] = jnp.zeros_like(ref)
        roll_to_windows(
            lambda row: grad_first[row * SIDE : (row + 1) * SIDE, :],
            doubled, windows, shift_row, shift_col,
        )

    mine = pl.ds(pl.multiple_of(window * AREA, 16), AREA)
    z = windows[mine, :]
    n = n_in[...].astype(F32)
    gain_grad[...] += col_sum(z * n)
    offset_grad[...] += col_sum(z)
    grad_branch = norm_back(gain[0:1, :] * z, n, rstd_in[...])
    grad_low = grad_branch.astype(BF16)
    out_bias_grad[...] += col_sum(grad_branch)
    out_grad[...] += dot(mixture[0], grad_low, 1, 0)
    for head in range(HEADS):
        at = head * HEAD
        grad_mix = dot(out_weight[at : at + HEAD, :], grad_low, 1, 1)
        grad_mix = grad_mix.astype(BF16)
        low = probs[0, head]
        query = joint[0, at : at + HEAD, :]
        key = joint[0, D + at : D + at + HEAD, :]
        value = joint[0, 2 * D + at : 2 * D + at + HEAD, :]
        weight = low.astype(F32)
        weighted = weight * dot(value, grad_mix, 0, 0)
        grad_scores = weighted - weight * (col_sum(weighted) / col_sum(weight))
        table_grad[head] += grad_scores
        grad_raw = (grad_scores * scale[0, head]).astype(BF16)
        grad_query = dot(key, grad_raw, 1, 0)
        grad_key = dot(query, grad_raw, 1, 1)
        grad_value = dot(grad_mix, low, 1, 1)
        query = query.astype(F32)
        key = key.astype(F32)
        query_inner = col_sum(query * grad_query)
        key_inner = col_sum(key * grad_key)
        scale_grad[head : head + 1, :] += query_inner
        grad_query = inverse[0, head : head + 1, :] * (grad_query - query * query_inner)
        grad_key = inverse[0, HEADS + head : HEADS + head + 1, :] * (grad_key - key * key_inner)
        joint_grad[at : at + HEAD, :] = grad_query.astype(BF16)
        joint_grad[D + at : D + at + HEAD, :] = grad_key.astype(BF16)
        joint_grad[2 * D + at : 2 * D + at + HEAD, :] = grad_value.astype(BF16)
    in_grad[...] += dot(win_t[0], joint_grad[...], 1, 1)
    windows[mine, :] = dot(joint_grad[...], in_weight[...], 0, 1)

    @pl.when(window == WINDOWS - 1)
    def _():
        def write_row(row, line):
            tokens_grad[row] = line + grad_first[row * SIDE : (row + 1) * SIDE, :]

        roll_to_image(windows, doubled, write_row, shift_row, shift_col)


def attend_back(
    shifts, scale, grad_first, n, rstd, joint, probs, mixture, win_t, inverse,
    in_weight, out_weight, gain,
):
    per_window = lambda *dims: pl.BlockSpec((1,) + dims, lambda w: (w,) + (0,) * len(dims))
    rows = lambda width: pl.BlockSpec((AREA, width), lambda w: (w, 0))
    return pl.pallas_call(
        attend_back_kernel,
        grid=(WINDOWS,),
        in_specs=[
            smem(),
            smem(),
            whole((TOKENS, D)),
            rows(D),
            rows(1),
            per_window(3 * D, AREA),
            per_window(HEADS, AREA, AREA),
            per_window(D, AREA),
            per_window(D + 16, AREA),
            per_window(2 * HEADS, AREA),
            whole((D, 3 * D)),
            whole((D, D)),
            whole((3, D)),
        ],
        out_specs=(
            whole((SIDE, SIDE, D)),
            whole((D + 16, 3 * D)),
            whole((D, D)),
            whole((1, D)),
            whole((1, D)),
            whole((1, D)),
            whole((HEADS, AREA)),
            whole((HEADS, AREA, AREA)),
        ),
        out_shape=(
            full((SIDE, SIDE, D)),
            full((D + 16, 3 * D)),
            full((D, D)),
            full((1, D)),
            full((1, D)),
            full((1, D)),
            full((HEADS, AREA)),
            full((HEADS, AREA, AREA)),
        ),
        scratch_shapes=[
            pltpu.VMEM((SIDE, SIDE + WS, D), F32),
            pltpu.VMEM((TOKENS, D), F32),
            pltpu.VMEM((3 * D, AREA), BF16),
        ],
        compiler_params=params(),
        name="attend_back",
    )(
        shifts, scale, grad_first, n, rstd, joint, probs, mixture, win_t, inverse,
        in_weight, out_weight, gain,
    )


def table_back_kernel(table_grad, scale_rows, w1, b1, w2, out1, out2, out3, values_grad):
    spread = spread_matrix(True)
    for head in range(HEADS):
        high, low = split(table_grad[head])
        spread_low = spread.astype(BF16)
        flat = dot(high, spread_low, 1, 1) + dot(low, spread_low, 1, 1)
        flat = jnp.concatenate([flat, jnp.zeros((AREA, TABLE - 384), F32)], axis=1)
        total = jnp.zeros((16, TABLE), F32)
        for key_row in range(WS):
            shift = EXTENT * key_row
            line = flat[key_row * WS : (key_row + 1) * WS, :]
            line = jnp.concatenate([line, jnp.zeros((16 - WS, TABLE), F32)], axis=0)
            total += pltpu.roll(line, shift, 1)
        total = pltpu.roll(total, 0, 1, stride=1, stride_axis=0)
        values_grad[head : head + 1, :] = col_sum(total)
    f_row, f_col = offsets_row((UNITS, TABLE), 1, -1.0)
    w1t = jnp.transpose(w1[...], (1, 0))
    b1t = jnp.transpose(b1[...], (1, 0))
    hidden, slope = gelu_pair(w1t[:, 0:1] * f_row + w1t[:, 1:2] * f_col + b1t[:, 0:1])
    chance = jax.nn.sigmoid(exact_dot(w2[...], hidden, 0, 0))
    grad_pre = values_grad[:HEADS, :] * (16.0 * chance * (1.0 - chance))
    out2[...] = exact_dot(hidden, grad_pre, 1, 1)
    grad_hidden = exact_dot(w2[...], grad_pre, 1, 0) * slope
    f_row, f_col = offsets_row((8, TABLE), 1, -1.0)
    kind = iota((8, TABLE), 0)
    factors = jnp.where(kind == 0, f_row, jnp.where(kind == 1, f_col, 1.0))
    out1[...] = exact_dot(factors, grad_hidden, 1, 1)
    out3[...] = jnp.sum(scale_rows[...], axis=1, keepdims=True)


def table_back(table_grad, scale_rows, w1, b1, w2):
    return pl.pallas_call(
        table_back_kernel,
        out_shape=(full((8, UNITS)), full((UNITS, HEADS)), full((HEADS, 1))),
        scratch_shapes=[pltpu.VMEM((16, TABLE), F32)],
        compiler_params=params(),
        name="table_back",
    )(table_grad, scale_rows, w1, b1, w2)


def per_device(
    tokens, shifts, routes, cotangent, in_weight, in_bias, logit_scale,
    bias_net_first_weight, bias_net_first_bias, bias_net_second_weight,
    out_weight, out_bias, up_weight, up_bias, down_weight, down_bias, router_weight,
    expert_up, expert_up_bias, expert_down, expert_down_bias, norm_gain, norm_bias,
):
    experts = router_weight.shape[1]
    capacity = (5 * TOKENS + 4 * experts - 1) // (4 * experts)
    slots = -(-capacity // 16) * 16
    picture = tokens.reshape(SIDE, SIDE, D)
    cot = cotangent.reshape(SIDE, SIDE, D)
    route_col = routes.reshape(TOKENS, 1)
    first_bias = bias_net_first_bias.reshape(1, UNITS)

    slot_col, slot_row, cot_slots, table, scale = prep(
        route_col, cot, bias_net_first_weight, first_bias, bias_net_second_weight,
        logit_scale.reshape(1, HEADS), experts, capacity, slots,
    )
    exchange = lambda blocks: lax.all_to_all(
        blocks, "expert", split_axis=0, concat_axis=0, tiled=True
    )
    cot_arrived = exchange(cot_slots)
    normed, n_zero, rstd_zero, joint, probs, mixture, win_t, inverse = attend(
        shifts, scale, picture, in_weight, in_bias, table,
        out_weight, out_bias.reshape(1, D), norm_gain, norm_bias,
    )
    first_low, active, slope, n_one, rstd_one, second, buffer = forward(
        shifts, picture, normed, up_weight, up_bias.reshape(1, FF), down_weight,
        down_bias.reshape(1, D), norm_gain, norm_bias, slot_row, experts, slots,
    )
    arrived = exchange(buffer)
    (
        produced, grad_arrived, expert_up_grad, expert_up_bias_grad, expert_down_grad_t,
        expert_down_bias_grad,
    ) = run_experts(
        arrived, cot_arrived, router_weight, expert_up[0], expert_up_bias, expert_down[0],
        expert_down_bias, norm_gain,
    )
    returned = exchange(produced).reshape(-1, D)
    grad_returned = exchange(grad_arrived).reshape(-1, D)
    (
        result, grad_first, up_grad, up_bias_grad, down_grad_t, down_bias_grad, router_grad,
        gain_grad, offset_grad,
    ) = backward(
        second, cot, slot_col, route_col, returned, grad_returned, router_weight, first_low,
        active, slope, n_one, rstd_one, up_weight, down_weight, norm_gain, norm_bias,
    )
    (
        tokens_grad, in_grad, out_grad, out_bias_grad, gain_zero, offset_zero, scale_rows,
        table_grad,
    ) = attend_back(
        shifts, scale, grad_first, n_zero, rstd_zero, joint, probs, mixture, win_t, inverse,
        in_weight, out_weight, norm_gain,
    )
    table_one, table_two, scale_grad = table_back(
        table_grad, scale_rows, bias_net_first_weight, first_bias, bias_net_second_weight
    )

    low_sum = lambda parts, axes: [
        part.astype(F32)
        for part in lax.psum([part.astype(BF16) for part in parts], axes)
    ]
    expert_up_grad, expert_down_grad_t, expert_up_bias_grad, expert_down_bias_grad = low_sum(
        [expert_up_grad, expert_down_grad_t, expert_up_bias_grad, expert_down_bias_grad], "dp"
    )
    both = ("dp", "expert")
    up_grad, down_grad_t = low_sum([up_grad, down_grad_t], both)
    in_weight_grad, out_grad = low_sum([in_grad[:D], out_grad], both)
    smalls = [
        in_grad[D], out_bias_grad, up_bias_grad, down_bias_grad, router_grad,
        gain_zero, gain_grad[1:], offset_zero, offset_grad[1:],
        table_one[:3], table_two, scale_grad,
    ]
    sizes = [small.size for small in smalls]
    packed = lax.psum(jnp.concatenate([small.reshape(-1) for small in smalls]), both)
    pieces = []
    at = 0
    for size in sizes:
        pieces.append(packed[at : at + size])
        at += size
    (
        in_bias_all, out_bias_grad, up_bias_grad, down_bias_grad, router_grad,
        gain_zero, gain_rest, offset_zero, offset_rest, table_one, table_two, scale_grad,
    ) = pieces
    return (
        result.reshape(tokens.shape),
        tokens_grad.reshape(tokens.shape),
        in_weight_grad,
        jnp.stack([in_bias_all[:D], in_bias_all[2 * D :]]),
        scale_grad,
        table_one[: 2 * UNITS].reshape(2, UNITS),
        table_one[2 * UNITS :],
        table_two.reshape(UNITS, HEADS),
        out_grad,
        out_bias_grad,
        up_grad,
        up_bias_grad,
        down_grad_t.T,
        down_bias_grad,
        router_grad.reshape(D, experts),
        expert_up_grad[None],
        expert_up_bias_grad,
        expert_down_grad_t.T[None],
        expert_down_bias_grad,
        jnp.concatenate([gain_zero, gain_rest]).reshape(3, D),
        jnp.concatenate([offset_zero, offset_rest]).reshape(3, D),
    )


def solution(mesh):
    split_all = P(("dp", "expert"))
    placed = (split_all,) * 4 + (P(),) * 13 + (P("expert"),) * 4 + (P(),) * 2
    return jax.shard_map(
        per_device,
        mesh=mesh,
        in_specs=placed,
        out_specs=(split_all,) * 2 + (P(),) * 13 + (P("expert"),) * 4 + (P(),) * 2,
        check_vma=False,
    )
```

```python
import functools

import jax
import jax.numpy as jnp
from jax import lax
from jax.experimental import pallas as pl
from jax.experimental.pallas import tpu as pltpu
from jax.sharding import PartitionSpec as P

D = 384
HEADS = 12
HEAD = D // HEADS
WS = 12
SIDE = 36
AREA = WS * WS
ACROSS = SIDE // WS
WINDOWS = ACROSS * ACROSS
TOKENS = SIDE * SIDE
FF = 1536
EXTENT = 2 * WS - 1
UNITS = 512
TABLE = 640
ROWS = 432
CHUNK = 256
F32 = jnp.float32
BF16 = jnp.bfloat16
I32 = jnp.int32
VMEM_LIMIT = 60 * 1024 * 1024


def dot(left, right, left_dim, right_dim):
    return lax.dot_general(
        left, right, (((left_dim,), (right_dim,)), ((), ())), preferred_element_type=F32
    )


def exact_dot(left, right, left_dim, right_dim):
    return lax.dot_general(
        left,
        right,
        (((left_dim,), (right_dim,)), ((), ())),
        preferred_element_type=F32,
        precision=lax.Precision.HIGHEST,
    )


def split(values):
    high = values.astype(BF16)
    return high, (values - high.astype(F32)).astype(BF16)


def iota(shape, dim):
    return lax.broadcasted_iota(I32, shape, dim)


def gelu_pair(values):
    size = jnp.abs(values)
    t = 1.0 / (1.0 + 0.2316419 * size)
    bell = jnp.exp(-0.5 * values * values) * 0.3989422804014327
    series = t * (
        0.319381530
        + t * (-0.356563782 + t * (1.781477937 + t * (-1.821255978 + t * 1.330274429)))
    )
    tail = series * bell
    phi = jnp.where(values >= 0.0, 1.0 - tail, tail)
    return values * phi, phi + values * bell


def norm_parts(values):
    centered = values - jnp.mean(values, axis=-1, keepdims=True)
    rstd = lax.rsqrt(jnp.mean(centered * centered, axis=-1, keepdims=True) + 1e-05)
    return centered * rstd, rstd


def norm_back(grad_n, n, rstd):
    return rstd * (
        grad_n
        - jnp.mean(grad_n, axis=-1, keepdims=True)
        - n * jnp.mean(grad_n * n, axis=-1, keepdims=True)
    )


def col_sum(values):
    return jnp.sum(values, axis=0, keepdims=True)


def div_ws(values):
    return (values * 171) >> 11


def full(shape, dtype=F32):
    return jax.ShapeDtypeStruct(shape, dtype)


def whole(shape):
    return pl.BlockSpec(shape, lambda *_: (0,) * len(shape))


def smem():
    return pl.BlockSpec(memory_space=pltpu.SMEM)


def params(**more):
    return pltpu.CompilerParams(vmem_limit_bytes=VMEM_LIMIT, **more)


def partner(me, step, count):
    side = 1
    while side * side < count:
        side *= 2
    if side * side != count:
        return lax.rem(me + step, count)
    row = lax.rem(lax.div(me, side) + step // side, side)
    col = lax.rem(lax.rem(me, side) + step % side, side)
    return row * side + col


def opposite(step, count):
    side = 1
    while side * side < count:
        side *= 2
    if side * side != count:
        return (count - step) % count
    return ((side - step // side) % side) * side + (side - step % side) % side


def greet(devices):
    barrier = pltpu.get_barrier_semaphore()
    for device in devices:
        pl.semaphore_signal(barrier, inc=1, device_id=device, device_id_type=pl.DeviceIdType.MESH)
    pl.semaphore_wait(barrier, len(devices))


def levels_of(names):
    dp = lax.axis_index("dp")
    depth = lax.axis_size("dp") // 2
    core = lax.rem(dp, 2)
    place = lax.div(dp, 2)
    levels = [(2, core, lambda j: {"dp": place * 2 + j})]
    if "expert" in names:
        levels.append((lax.axis_size("expert"), lax.axis_index("expert"), lambda j: {"expert": j}))
    if depth > 1:
        levels.append((depth, place, lambda j: {"dp": j * 2 + core}))
    return levels


def level_counts(names, dp, experts):
    counts = [2] + ([experts] if "expert" in names else []) + ([dp // 2] if dp > 2 else [])
    return counts


def padded_rows(rows, counts, tile):
    unit = tile
    for count in counts:
        unit *= count
    return -(-rows // unit) * unit


def land_shapes(rows, width, dtype, counts):
    shapes = []
    for count in counts:
        rows //= count
        shapes.append(pltpu.VMEM((count - 1, rows, width), dtype))
    return shapes


def sum_sems(counts):
    return [pltpu.SemaphoreType.DMA((2 * len(counts), max(counts)))] * 2


class Sum:
    def __init__(self, source, held, result, lands, send, recv, levels):
        self.source, self.held, self.result, self.lands = source, held, result, lands
        self.send, self.recv, self.levels = send, recv, levels
        rows = source.shape[0]
        start = 0
        self.regions = []
        for count, index, _ in levels:
            rows //= count
            self.regions.append((start, rows))
            start = start + index * rows

    def scatter(self, level, begin):
        count, index, device = self.levels[level]
        start, rows = self.regions[level]
        ref = self.held if level else self.source
        into = self.held if level < len(self.levels) - 1 else self.result
        for step in range(1, count):
            to = lax.rem(index + step, count)
            copy = pltpu.make_async_remote_copy(
                src_ref=ref.at[pl.ds(pl.multiple_of(start + to * rows, 8), rows)],
                dst_ref=self.lands[level].at[step - 1],
                send_sem=self.send.at[level, step],
                recv_sem=self.recv.at[level, step],
                device_id=device(to),
                device_id_type=pl.DeviceIdType.MESH,
            )
            copy.start() if begin else copy.wait()
        if begin:
            return
        mine = start + index * rows
        tile = 16 if ref.dtype == BF16 else 8
        chunk = tile
        while rows % (chunk * 2) == 0 and chunk < 128:
            chunk *= 2

        def add(i, carry):
            here = pl.ds(pl.multiple_of(mine + i * chunk, tile), chunk)
            there = pl.ds(pl.multiple_of(i * chunk, tile), chunk)
            total = ref[here, :].astype(F32)
            for step in range(1, count):
                total = total + self.lands[level][step - 1, there, :].astype(F32)
            into[here, :] = total.astype(into.dtype)
            return carry

        lax.fori_loop(0, rows // chunk, add, 0)

    def gather(self, level, begin):
        count, index, device = self.levels[level]
        start, rows = self.regions[level]
        mine = self.result.at[pl.ds(pl.multiple_of(start + index * rows, 8), rows)]
        for step in range(1, count):
            to = lax.rem(index + step, count)
            copy = pltpu.make_async_remote_copy(
                src_ref=mine,
                dst_ref=mine,
                send_sem=self.send.at[len(self.levels) + level, step],
                recv_sem=self.recv.at[len(self.levels) + level, step],
                device_id=device(to),
                device_id_type=pl.DeviceIdType.MESH,
            )
            copy.start() if begin else copy.wait()

    def stages(self):
        last = len(self.levels) - 1
        moves = [(self.scatter, level) for level in range(last + 1)]
        moves += [(self.gather, level) for level in range(last, -1, -1)]

        def stage(k):
            if k:
                moves[k - 1][0](moves[k - 1][1], False)
            if k < len(moves):
                moves[k][0](moves[k][1], True)

        return [functools.partial(stage, k) for k in range(len(moves) + 1)]


def greeted(levels):
    devices = []
    for count, index, device in levels:
        devices += [device(lax.rem(index + step, count)) for step in range(1, count)]
    return devices


def offsets_row(shape, dim, sign):
    place = iota(shape, dim)
    row = jnp.floor((place.astype(F32) + 0.5) * (1.0 / EXTENT)).astype(I32)
    col = place - row * EXTENT

    def logged(step):
        e = sign * (step - (WS - 1)).astype(F32) * (8.0 / (WS - 1))
        size = jnp.log2(jnp.abs(e) + 1.0) * (1.0 / 3.0)
        return jnp.where(e < 0.0, -size, size)

    return logged(row), logged(col)


def spread_matrix(mirrored):
    token = iota((384, AREA), 1)
    row = div_ws(token)
    lin = row * EXTENT + (token - row * WS)
    if mirrored:
        lin = (WS - 1) * EXTENT + (WS - 1) - lin
    return (iota((384, AREA), 0) == lin).astype(F32)


def prep_kernel(
    capacity, routes, cot, w1, b1, w2, ls, slot_col, slot_row, zbuf, table, scale, flat, u_ref
):
    slots = zbuf.shape[1]
    experts = zbuf.shape[0]
    before = (iota((AREA, AREA), 1) < iota((AREA, AREA), 0)).astype(BF16)
    carry = jnp.zeros((1, 128), F32)
    for block in range(TOKENS // AREA):
        rows = pl.ds(block * AREA, AREA)
        route = routes[rows, :]
        onehot = (route == iota((AREA, 128), 1)).astype(F32)
        ahead = dot(before, onehot.astype(BF16), 1, 0) + carry
        position = jnp.sum(ahead * onehot, axis=1, keepdims=True)
        carry = carry + col_sum(onehot)
        slot = route.astype(F32) * slots + position
        slot_col[rows, :] = jnp.where(position < capacity, slot, -1.0).astype(I32)
    slot_row[...] = jnp.transpose(
        jnp.broadcast_to(slot_col[...].astype(F32), (TOKENS, 128)), (1, 0)
    )[0:1, :].astype(I32)

    for row in range(SIDE):
        flat[row * SIDE : (row + 1) * SIDE, :] = cot[row].astype(F32)
    low = flat[...].astype(BF16)
    for expert in range(experts):
        pick = (iota((slots, TOKENS), 0) + expert * slots == slot_row[...]).astype(BF16)
        zbuf[expert] = dot(pick, low, 1, 0).astype(BF16)

    scale[...] = jnp.exp(ls[...])
    f_row, f_col = offsets_row((UNITS, TABLE), 1, 1.0)
    w1t = jnp.transpose(w1[...], (1, 0))
    b1t = jnp.transpose(b1[...], (1, 0))
    hidden, _ = gelu_pair(w1t[:, 0:1] * f_row + w1t[:, 1:2] * f_col + b1t[:, 0:1])
    values = 16.0 * jax.nn.sigmoid(exact_dot(w2[...], hidden, 0, 0))
    spread = spread_matrix(False).astype(BF16)
    for head in range(HEADS):
        line = jnp.broadcast_to(values[head : head + 1, :], (16, TABLE))
        line = pltpu.roll(line, 0, 1, stride=1, stride_axis=0)
        for key_row in range(WS):
            shift = (EXTENT * key_row - (WS - 1) * EXTENT - (WS - 1)) % TABLE
            rolled = pltpu.roll(line, shift, 1)
            u_ref[key_row * WS : (key_row + 1) * WS, :] = rolled[:WS, :384]
        high, low_part = split(u_ref[...])
        table[head] = dot(high, spread, 1, 0) + dot(low_part, spread, 1, 0)


def prep(routes, cotangent, w1, b1, w2, ls, experts, capacity, slots):
    return pl.pallas_call(
        functools.partial(prep_kernel, capacity),
        out_shape=(
            full((TOKENS, 1), I32),
            full((1, TOKENS), I32),
            full((experts, slots, D), BF16),
            full((HEADS, AREA, AREA)),
            full((1, HEADS)),
        ),
        scratch_shapes=[pltpu.VMEM((TOKENS, D), F32), pltpu.VMEM((AREA, 384), F32)],
        compiler_params=params(),
        name="prep",
    )(routes, cotangent, w1, b1, w2, ls)


def window_labels(window, shift_row, shift_col):
    def labels(shape, dim):
        token = iota(shape, dim)
        row = div_ws(token)
        col = token - row * WS + lax.rem(window, ACROSS) * WS
        row = row + lax.div(window, ACROSS) * WS

        def region(place, shift):
            last = jnp.where(place < SIDE - shift, 1, 2)
            return jnp.where(place < SIDE - WS, 0, last)

        return region(row, shift_row) * 3 + region(col, shift_col)

    return labels((AREA, 1), 0), labels((1, AREA), 1)


def roll_to_windows(read_row, doubled, windows, shift_row, shift_col):
    for row in range(SIDE):
        line = read_row(row)
        doubled[row, :SIDE, :] = line
        doubled[row, SIDE:, :] = line[:WS, :]
    for row in range(SIDE):
        source = row + shift_row
        source = jnp.where(source >= SIDE, source - SIDE, source)
        line = pltpu.roll(doubled[source], SIDE + WS - shift_col, 0)
        for across in range(ACROSS):
            start = ((row // WS) * ACROSS + across) * AREA + (row % WS) * WS
            windows[start : start + WS, :] = line[across * WS : (across + 1) * WS, :]


def roll_to_image(windows, doubled, write_row, shift_row, shift_col):
    for row in range(SIDE):
        for across in range(ACROSS):
            start = ((row // WS) * ACROSS + across) * AREA + (row % WS) * WS
            line = windows[start : start + WS, :]
            doubled[row, across * WS : (across + 1) * WS, :] = line
            if across == ACROSS - 1:
                doubled[row, SIDE:, :] = line
    for row in range(SIDE):
        source = row - shift_row
        source = jnp.where(source < 0, source + SIDE, source)
        write_row(row, pltpu.roll(doubled[source], shift_col, 0)[:SIDE, :])


def attend_kernel(
    cot_slots, shifts, scale, tokens, in_weight, in_bias, table, out_weight, out_bias, gain, offset,
    cot_arrived, normed, n_out, rstd_out, joint, probs, mixture, win_t, inverse,
    doubled, windows, in_weight_t, bias_col, send, recv, local,
):
    window = pl.program_id(0)
    shift_row, shift_col = shifts[0, 0], shifts[0, 1]
    me = lax.axis_index("expert")
    count = cot_slots.shape[0]

    def move(step):
        to = partner(me, step, count)
        return pltpu.make_async_remote_copy(
            src_ref=cot_slots.at[to],
            dst_ref=cot_arrived.at[me],
            send_sem=send.at[step],
            recv_sem=recv.at[step],
            device_id={"expert": to},
            device_id_type=pl.DeviceIdType.MESH,
        )

    keep = pltpu.make_async_copy(cot_slots.at[me], cot_arrived.at[me], local)

    @pl.when(window == 0)
    def _():
        greet([{"expert": partner(me, step, count)} for step in range(1, count)])
        for step in range(1, count):
            move(step).start()
        keep.start()
        roll_to_windows(
            lambda row: tokens[row].astype(F32), doubled, windows, shift_row, shift_col
        )
        in_weight_t[...] = jnp.transpose(in_weight[...], (1, 0))
        bias_col[:, 0:2] = jnp.transpose(in_bias[...], (1, 0))

    mine = windows[pl.ds(pl.multiple_of(window * AREA, 16), AREA), :].astype(BF16)
    win_t[0, :D, :] = jnp.transpose(mine, (1, 0))
    win_t[0, D:, :] = (iota((16, AREA), 0) == 0).astype(BF16)
    label_keys, label_queries = window_labels(window, shift_row, shift_col)
    mask = jnp.where(label_keys == label_queries, 0.0, -100.0)
    for head in range(HEADS):
        at = head * HEAD
        query = dot(in_weight_t[at : at + HEAD, :], mine, 1, 1) + bias_col[at : at + HEAD, 0:1]
        key = dot(in_weight_t[D + at : D + at + HEAD, :], mine, 1, 1)
        value = (
            dot(in_weight_t[2 * D + at : 2 * D + at + HEAD, :], mine, 1, 1)
            + bias_col[at : at + HEAD, 1:2]
        ).astype(BF16)
        query_inverse = lax.rsqrt(1.0 + col_sum(query * query))
        key_inverse = lax.rsqrt(1.0 + col_sum(key * key))
        query = (query * query_inverse).astype(BF16)
        key = (key * key_inverse).astype(BF16)
        scores = dot(key, query, 0, 0) * scale[0, head] + (table[head] + mask)
        exponent = jnp.exp(scores - jnp.max(scores, axis=0, keepdims=True))
        low = (exponent * (1.0 / col_sum(exponent))).astype(BF16)
        mixture[0, at : at + HEAD, :] = dot(value, low, 1, 0).astype(BF16)
        probs[0, head] = low
        joint[0, at : at + HEAD, :] = query
        joint[0, D + at : D + at + HEAD, :] = key
        joint[0, 2 * D + at : 2 * D + at + HEAD, :] = value
        inverse[0, head : head + 1, :] = query_inverse
        inverse[0, HEADS + head : HEADS + head + 1, :] = key_inverse
    branch = dot(mixture[0], out_weight[...], 0, 0) + out_bias[...]
    n, rstd = norm_parts(branch)
    normed[...] = n * gain[0:1, :] + offset[0:1, :]
    n_out[...] = n.astype(BF16)
    rstd_out[...] = rstd

    @pl.when(window == WINDOWS - 1)
    def _():
        for step in range(1, count):
            move(step).wait()
        keep.wait()


def attend(
    cot_slots, shifts, scale, tokens, in_weight, in_bias, table, out_weight, out_bias, gain, offset
):
    per_window = lambda *dims: pl.BlockSpec((1,) + dims, lambda w: (w,) + (0,) * len(dims))
    rows = lambda width: pl.BlockSpec((AREA, width), lambda w: (w, 0))
    return pl.pallas_call(
        attend_kernel,
        grid=(WINDOWS,),
        in_specs=[
            pl.BlockSpec(memory_space=pl.ANY),
            smem(),
            smem(),
            whole((SIDE, SIDE, D)),
            whole((D, 3 * D)),
            whole((2, D)),
            whole((HEADS, AREA, AREA)),
            whole((D, D)),
            whole((1, D)),
            whole((3, D)),
            whole((3, D)),
        ],
        out_specs=(
            pl.BlockSpec(memory_space=pl.ANY),
            rows(D),
            rows(D),
            rows(1),
            per_window(3 * D, AREA),
            per_window(HEADS, AREA, AREA),
            per_window(D, AREA),
            per_window(D + 16, AREA),
            per_window(2 * HEADS, AREA),
        ),
        out_shape=(
            full(cot_slots.shape, BF16),
            full((TOKENS, D)),
            full((TOKENS, D), BF16),
            full((TOKENS, 1)),
            full((WINDOWS, 3 * D, AREA), BF16),
            full((WINDOWS, HEADS, AREA, AREA), BF16),
            full((WINDOWS, D, AREA), BF16),
            full((WINDOWS, D + 16, AREA), BF16),
            full((WINDOWS, 2 * HEADS, AREA)),
        ),
        scratch_shapes=[
            pltpu.VMEM((SIDE, SIDE + WS, D), F32),
            pltpu.VMEM((TOKENS, D), F32),
            pltpu.VMEM((3 * D, D), BF16),
            pltpu.VMEM((D, 128), F32),
            pltpu.SemaphoreType.DMA((cot_slots.shape[0],)),
            pltpu.SemaphoreType.DMA((cot_slots.shape[0],)),
            pltpu.SemaphoreType.DMA(()),
        ],
        compiler_params=params(collective_id=0, has_side_effects=True),
        name="attend",
    )(cot_slots, shifts, scale, tokens, in_weight, in_bias, table, out_weight, out_bias, gain, offset)


def forward_kernel(
    shifts, tokens, normed, up, up_bias, down, down_bias, gain, offset, slot_row,
    first_low, active, slope, n_out, rstd_out, second, buffer,
    doubled, image, second_low,
):
    step = pl.program_id(0)

    @pl.when(step == 0)
    def _():
        def write_row(row, line):
            image[row * SIDE : (row + 1) * SIDE, :] = line + tokens[row].astype(F32)

        roll_to_image(normed, doubled, write_row, shifts[0, 0], shifts[0, 1])

    rows = pl.ds(pl.multiple_of(step * ROWS, 16), ROWS)
    first = image[rows, :]
    low = first.astype(BF16)
    first_low[...] = low
    branch = jnp.broadcast_to(down_bias[...], (ROWS, D))
    for at in range(0, FF, CHUNK):
        hidden = dot(low, up[:, at : at + CHUNK], 1, 0) + up_bias[:, at : at + CHUNK]
        activated, derivative = gelu_pair(hidden)
        activated = activated.astype(BF16)
        active[:, at : at + CHUNK] = activated
        slope[:, at : at + CHUNK] = derivative.astype(BF16)
        branch += dot(activated, down[at : at + CHUNK, :], 1, 0)
    n, rstd = norm_parts(branch)
    n_out[...] = n.astype(BF16)
    rstd_out[...] = rstd
    result = first + n * gain[1:2, :] + offset[1:2, :]
    second[...] = result
    second_low[rows, :] = result.astype(BF16)

    @pl.when(step == TOKENS // ROWS - 1)
    def _():
        slots = buffer.shape[1]
        for expert in range(buffer.shape[0]):
            pick = (iota((slots, TOKENS), 0) + expert * slots == slot_row[...]).astype(BF16)
            buffer[expert] = dot(pick, second_low[...], 1, 0).astype(BF16)


def forward(
    shifts, tokens, normed, up, up_bias, down, down_bias, gain, offset, slot_row, experts, slots
):
    rows = lambda width: pl.BlockSpec((ROWS, width), lambda i: (i, 0))
    return pl.pallas_call(
        forward_kernel,
        grid=(TOKENS // ROWS,),
        in_specs=[
            smem(),
            whole((SIDE, SIDE, D)),
            whole((TOKENS, D)),
            whole((D, FF)),
            whole((1, FF)),
            whole((FF, D)),
            whole((1, D)),
            whole((3, D)),
            whole((3, D)),
            whole((1, TOKENS)),
        ],
        out_specs=(
            rows(D),
            rows(FF),
            rows(FF),
            rows(D),
            rows(1),
            rows(D),
            whole((experts, slots, D)),
        ),
        out_shape=(
            full((TOKENS, D), BF16),
            full((TOKENS, FF), BF16),
            full((TOKENS, FF), BF16),
            full((TOKENS, D), BF16),
            full((TOKENS, 1)),
            full((TOKENS, D)),
            full((experts, slots, D), BF16),
        ),
        scratch_shapes=[
            pltpu.VMEM((SIDE, SIDE + WS, D), F32),
            pltpu.VMEM((TOKENS, D), F32),
            pltpu.VMEM((TOKENS, D), BF16),
        ],
        compiler_params=params(),
        name="forward",
    )(shifts, tokens, normed, up, up_bias, down, down_bias, gain, offset, slot_row)


def expert_kernel(
    buffer, cot, router, up, up_bias, down, down_bias, gain,
    out, grad_in, packed,
    arrived, outs, grads, active, slope, up_grad, down_grad_t, up_bias_grad, down_bias_grad,
    send, recv,
):
    me = lax.axis_index("expert")
    count, slots, _ = buffer.shape
    others = range(1, count)

    def move(kind, step, source, target, to):
        return pltpu.make_async_remote_copy(
            src_ref=source,
            dst_ref=target,
            send_sem=send.at[kind, step],
            recv_sem=recv.at[kind, step],
            device_id={"expert": to},
            device_id_type=pl.DeviceIdType.MESH,
        )

    greet([{"expert": partner(me, step, count)} for step in others])
    for step in others:
        to = partner(me, step, count)
        move(0, step, buffer.at[to], arrived.at[step], to).start()
    arrived[0] = buffer[me]
    for ref in (up_grad, up_bias_grad, down_grad_t, down_bias_grad):
        ref[...] = jnp.zeros_like(ref)
    router_high, router_low = split(router[...])

    def work(step, carry):
        if count == 4:
            owner = lax.rem(lax.div(me, 2) + lax.div(step, 2), 2) * 2
            owner = owner + lax.rem(lax.rem(me, 2) + lax.rem(step, 2), 2)
        else:
            side = 1
            while side * side < count:
                side *= 2
            if side * side == count:
                owner = lax.rem(lax.div(me, side) + side - lax.div(step, side), side) * side
                owner = owner + lax.rem(lax.rem(me, side) + side - lax.rem(step, side), side)
            else:
                owner = lax.rem(me + count - step, count)

        @pl.when(step > 0)
        def _():
            move(0, step, buffer.at[owner], arrived.at[step], owner).wait_recv()

        features = arrived[step]
        logits = dot(features, router_high, 1, 0) + dot(features, router_low, 1, 0)
        chances = jnp.exp(logits - jnp.max(logits, axis=1, keepdims=True))
        own = jnp.where(iota(chances.shape, 1) == me, chances, 0.0)
        gate = jnp.sum(own, axis=1, keepdims=True) / jnp.sum(chances, axis=1, keepdims=True)

        output = jnp.zeros((slots, D), F32)
        for at in range(0, FF, CHUNK):
            hidden = dot(features, up[:, at : at + CHUNK], 1, 0) + up_bias[:, at : at + CHUNK]
            activated, derivative = gelu_pair(hidden)
            activated = activated.astype(BF16)
            active[:, at : at + CHUNK] = activated
            slope[:, at : at + CHUNK] = derivative
            output += dot(activated, down[at : at + CHUNK, :], 1, 0)
        output = (output + down_bias[...]).astype(BF16)
        outs[step] = output

        @pl.when(step > 0)
        def _():
            move(1, step, outs.at[step], out.at[me], owner).start()

        n, rstd = norm_parts(gate * output.astype(F32))
        grad_output = gate * norm_back(gain[2:3, :] * cot[owner].astype(F32), n, rstd)
        grad_low = grad_output.astype(BF16)
        down_bias_grad[...] += col_sum(grad_low.astype(F32))
        grad_low_t = jnp.transpose(grad_low, (1, 0))
        features_t = jnp.transpose(features, (1, 0))
        grad_features = jnp.zeros((slots, D), F32)
        for at in range(0, FF, CHUNK):
            part = slice(at, at + CHUNK)
            grad_hidden = dot(grad_low, down[part, :], 1, 1) * slope[:, part]
            grad_hidden_low = grad_hidden.astype(BF16)
            up_bias_grad[:, part] += col_sum(grad_hidden)
            down_grad_t[:, part] += dot(grad_low_t, active[:, part], 1, 0)
            up_grad[:, part] += dot(features_t, grad_hidden_low, 1, 0)
            grad_features += dot(grad_hidden_low, up[:, part], 1, 1)
        grads[step] = grad_features.astype(BF16)

        @pl.when(step > 0)
        def _():
            move(2, step, grads.at[step], grad_in.at[me], owner).start()

        return carry

    lax.fori_loop(0, count, work, 0)
    out[me] = outs[0]
    grad_in[me] = grads[0]
    pack_pair(packed, up_grad, down_grad_t)
    packed[2 * FF :, :] = jnp.zeros_like(packed[2 * FF :, :])
    tail = jnp.concatenate(
        [up_bias_grad[:, at : at + D] for at in range(0, FF, D)]
        + [down_bias_grad[...], jnp.zeros((11, D), F32)],
        axis=0,
    )
    packed[2 * FF : 2 * FF + 16, :] = tail.astype(BF16)
    for step in others:
        to = partner(me, step, count)
        move(0, step, buffer.at[to], arrived.at[step], to).wait_send()
        for kind, source, target in ((1, outs, out), (2, grads, grad_in)):
            move(kind, step, source.at[step], target.at[me], to).wait()


def pack_pair(packed, up_grad, down_grad_t):
    for block in range(FF // D):
        part = slice(block * D, (block + 1) * D)
        packed[part, :] = up_grad[:, part].astype(BF16)
        packed[FF + block * D : FF + (block + 1) * D, :] = jnp.transpose(
            down_grad_t[:, part].astype(BF16), (1, 0)
        )


def run_experts(buffer, cot, router, up, up_bias, down, down_bias, gain, packed_rows):
    count, slots, _ = buffer.shape
    blocks = (count, slots, D)
    return pl.pallas_call(
        expert_kernel,
        out_shape=(full(blocks, BF16), full(blocks, BF16), full((packed_rows, D), BF16)),
        scratch_shapes=[
            pltpu.VMEM(blocks, BF16),
            pltpu.VMEM(blocks, BF16),
            pltpu.VMEM(blocks, BF16),
            pltpu.VMEM((slots, FF), BF16),
            pltpu.VMEM((slots, FF), F32),
            pltpu.VMEM((D, FF), F32),
            pltpu.VMEM((D, FF), F32),
            pltpu.VMEM((1, FF), F32),
            pltpu.VMEM((1, D), F32),
            pltpu.SemaphoreType.DMA((3, count)),
            pltpu.SemaphoreType.DMA((3, count)),
        ],
        compiler_params=params(collective_id=1, has_side_effects=True),
        name="experts",
    )(buffer, cot, router, up, up_bias, down, down_bias, gain)


def backward_kernel(
    second, cot, slot_col, routes, outputs, grads, router, first_low, active, slope, n_in, rstd_in,
    up, down, gain, offset,
    result, grad_first, packed, up_bias_grad, down_bias_grad, router_grad,
    gain_grad, offset_grad,
    flat, up_grad, down_grad_t,
):
    step = pl.program_id(0)

    @pl.when(step == 0)
    def _():
        for ref in (
            up_grad, up_bias_grad, down_grad_t, down_bias_grad, router_grad, gain_grad, offset_grad
        ):
            ref[...] = jnp.zeros_like(ref)

    lines = ROWS // SIDE
    for line in range(lines):
        flat[line * SIDE : (line + 1) * SIDE, :] = cot[line].astype(F32)
    z = flat[...]
    x = second[...]
    slots_all = outputs.shape[0]
    pick = (slot_col[...] == iota((ROWS, slots_all), 1)).astype(BF16)
    picked = dot(pick, outputs[...], 1, 0)
    dispatched = dot(pick, grads[...], 1, 0)

    logits = exact_dot(x, router[...], 1, 0)
    chances = jnp.exp(logits - jnp.max(logits, axis=1, keepdims=True))
    chances = chances / jnp.sum(chances, axis=1, keepdims=True)
    onehot = (routes[...] == iota(chances.shape, 1)).astype(F32)
    gate = jnp.sum(chances * onehot, axis=1, keepdims=True)
    n, rstd = norm_parts(gate * picked)
    final = x + n * gain[2:3, :] + offset[2:3, :]
    gain_grad[2:3, :] += col_sum(z * n)
    offset_grad[2:3, :] += col_sum(z)
    grad_moe = norm_back(gain[2:3, :] * z, n, rstd)
    grad_gate = jnp.sum(grad_moe * picked, axis=1, keepdims=True)
    grad_logits = grad_gate * gate * (onehot - chances)
    grad_logits_low = grad_logits.astype(BF16)
    router_grad[...] += dot(grad_logits_low, x.astype(BF16), 0, 0)
    grad_second = z + dispatched + dot(grad_logits_low, router[...].astype(BF16), 1, 1)

    n = n_in[...].astype(F32)
    gain_grad[1:2, :] += col_sum(grad_second * n)
    offset_grad[1:2, :] += col_sum(grad_second)
    grad_branch = norm_back(gain[1:2, :] * grad_second, n, rstd_in[...])
    grad_low = grad_branch.astype(BF16)
    down_bias_grad[...] += col_sum(grad_branch)
    grad_low_t = jnp.transpose(grad_low, (1, 0))
    first_t = jnp.transpose(first_low[...], (1, 0))
    total = jnp.zeros((ROWS, D), F32)
    for at in range(0, FF, CHUNK):
        part = slice(at, at + CHUNK)
        grad_hidden = dot(grad_low, down[part, :], 1, 1) * slope[:, part].astype(F32)
        grad_hidden_low = grad_hidden.astype(BF16)
        up_bias_grad[:, part] += col_sum(grad_hidden)
        down_grad_t[:, part] += dot(grad_low_t, active[:, part], 1, 0)
        up_grad[:, part] += dot(first_t, grad_hidden_low, 1, 0)
        total += dot(grad_hidden_low, up[:, part], 1, 1)
    grad_first[...] = total + grad_second
    flat[...] = final
    for line in range(lines):
        result[line] = flat[line * SIDE : (line + 1) * SIDE, :].astype(BF16)

    @pl.when(step == TOKENS // ROWS - 1)
    def _():
        pack_pair(packed, up_grad, down_grad_t)
        if packed.shape[0] > 2 * FF:
            packed[2 * FF :, :] = jnp.zeros_like(packed[2 * FF :, :])


def backward(
    second, cot, slot_col, routes, outputs, grads, router, first_low, active, slope, n, rstd,
    up, down, gain, offset, packed_rows,
):
    rows = lambda width: pl.BlockSpec((ROWS, width), lambda i: (i, 0))
    lines = pl.BlockSpec((ROWS // SIDE, SIDE, D), lambda i: (i, 0, 0))
    slots_all = outputs.shape[0]
    return pl.pallas_call(
        backward_kernel,
        grid=(TOKENS // ROWS,),
        in_specs=[
            rows(D),
            lines,
            rows(1),
            rows(1),
            whole((slots_all, D)),
            whole((slots_all, D)),
            whole(router.shape),
            rows(D),
            rows(FF),
            rows(FF),
            rows(D),
            rows(1),
            whole((D, FF)),
            whole((FF, D)),
            whole((3, D)),
            whole((3, D)),
        ],
        out_specs=(
            lines,
            rows(D),
            whole((packed_rows, D)),
            whole((1, FF)),
            whole((1, D)),
            whole((router.shape[1], D)),
            whole((3, D)),
            whole((3, D)),
        ),
        out_shape=(
            full((SIDE, SIDE, D), BF16),
            full((TOKENS, D)),
            full((packed_rows, D), BF16),
            full((1, FF)),
            full((1, D)),
            full((router.shape[1], D)),
            full((3, D)),
            full((3, D)),
        ),
        scratch_shapes=[
            pltpu.VMEM((ROWS, D), F32),
            pltpu.VMEM((D, FF), F32),
            pltpu.VMEM((D, FF), F32),
        ],
        compiler_params=params(),
        name="backward",
    )(
        second, cot, slot_col, routes, outputs, grads, router, first_low, active, slope, n, rstd,
        up, down, gain, offset,
    )


def attend_back_kernel(
    shifts, scale, grad_first, n_in, rstd_in, joint, probs, mixture, win_t, inverse,
    in_weight, out_weight, gain,
    tokens_grad, packed, in_bias_grad, out_bias_grad, gain_grad, offset_grad, scale_grad, table_grad,
    doubled, windows, joint_grad, in_grad, out_grad,
):
    window = pl.program_id(0)
    shift_row, shift_col = shifts[0, 0], shifts[0, 1]

    @pl.when(window == 0)
    def _():
        for ref in (
            in_grad, out_grad, out_bias_grad, gain_grad, offset_grad, scale_grad, table_grad
        ):
            ref[...] = jnp.zeros_like(ref)
        roll_to_windows(
            lambda row: grad_first[row * SIDE : (row + 1) * SIDE, :],
            doubled, windows, shift_row, shift_col,
        )

    mine = pl.ds(pl.multiple_of(window * AREA, 16), AREA)
    z = windows[mine, :]
    n = n_in[...].astype(F32)
    gain_grad[...] += col_sum(z * n)
    offset_grad[...] += col_sum(z)
    grad_branch = norm_back(gain[0:1, :] * z, n, rstd_in[...])
    grad_low = grad_branch.astype(BF16)
    out_bias_grad[...] += col_sum(grad_branch)
    out_grad[...] += dot(mixture[0], grad_low, 1, 0)
    for head in range(HEADS):
        at = head * HEAD
        grad_mix = dot(out_weight[at : at + HEAD, :], grad_low, 1, 1)
        grad_mix = grad_mix.astype(BF16)
        low = probs[0, head]
        query = joint[0, at : at + HEAD, :]
        key = joint[0, D + at : D + at + HEAD, :]
        value = joint[0, 2 * D + at : 2 * D + at + HEAD, :]
        weight = low.astype(F32)
        weighted = weight * dot(value, grad_mix, 0, 0)
        grad_scores = weighted - weight * (col_sum(weighted) / col_sum(weight))
        table_grad[head] += grad_scores
        grad_raw = (grad_scores * scale[0, head]).astype(BF16)
        grad_query = dot(key, grad_raw, 1, 0)
        grad_key = dot(query, grad_raw, 1, 1)
        grad_value = dot(grad_mix, low, 1, 1)
        query = query.astype(F32)
        key = key.astype(F32)
        query_inner = col_sum(query * grad_query)
        key_inner = col_sum(key * grad_key)
        scale_grad[head : head + 1, :] += query_inner
        grad_query = inverse[0, head : head + 1, :] * (grad_query - query * query_inner)
        grad_key = inverse[0, HEADS + head : HEADS + head + 1, :] * (grad_key - key * key_inner)
        joint_grad[at : at + HEAD, :] = grad_query.astype(BF16)
        joint_grad[D + at : D + at + HEAD, :] = grad_key.astype(BF16)
        joint_grad[2 * D + at : 2 * D + at + HEAD, :] = grad_value.astype(BF16)
    in_grad[...] += dot(win_t[0], joint_grad[...], 1, 1)
    windows[mine, :] = dot(joint_grad[...], in_weight[...], 0, 1)

    @pl.when(window == WINDOWS - 1)
    def _():
        def write_row(row, line):
            tokens_grad[row] = line + grad_first[row * SIDE : (row + 1) * SIDE, :]

        roll_to_image(windows, doubled, write_row, shift_row, shift_col)
        for block in range(3):
            packed[block * D : (block + 1) * D, :] = in_grad[
                :D, block * D : (block + 1) * D
            ].astype(BF16)
        packed[3 * D : 4 * D, :] = out_grad[...].astype(BF16)
        if packed.shape[0] > 4 * D:
            packed[4 * D :, :] = jnp.zeros_like(packed[4 * D :, :])
        in_bias_grad[...] = in_grad[D : D + 1, :]


def attend_back(
    shifts, scale, grad_first, n, rstd, joint, probs, mixture, win_t, inverse,
    in_weight, out_weight, gain, packed_rows,
):
    per_window = lambda *dims: pl.BlockSpec((1,) + dims, lambda w: (w,) + (0,) * len(dims))
    rows = lambda width: pl.BlockSpec((AREA, width), lambda w: (w, 0))
    return pl.pallas_call(
        attend_back_kernel,
        grid=(WINDOWS,),
        in_specs=[
            smem(),
            smem(),
            whole((TOKENS, D)),
            rows(D),
            rows(1),
            per_window(3 * D, AREA),
            per_window(HEADS, AREA, AREA),
            per_window(D, AREA),
            per_window(D + 16, AREA),
            per_window(2 * HEADS, AREA),
            whole((D, 3 * D)),
            whole((D, D)),
            whole((3, D)),
        ],
        out_specs=(
            whole((SIDE, SIDE, D)),
            whole((packed_rows, D)),
            whole((1, 3 * D)),
            whole((1, D)),
            whole((1, D)),
            whole((1, D)),
            whole((HEADS, AREA)),
            whole((HEADS, AREA, AREA)),
        ),
        out_shape=(
            full((SIDE, SIDE, D)),
            full((packed_rows, D), BF16),
            full((1, 3 * D)),
            full((1, D)),
            full((1, D)),
            full((1, D)),
            full((HEADS, AREA)),
            full((HEADS, AREA, AREA)),
        ),
        scratch_shapes=[
            pltpu.VMEM((SIDE, SIDE + WS, D), F32),
            pltpu.VMEM((TOKENS, D), F32),
            pltpu.VMEM((3 * D, AREA), BF16),
            pltpu.VMEM((D + 16, 3 * D), F32),
            pltpu.VMEM((D, D), F32),
        ],
        compiler_params=params(),
        name="attend_back",
    )(
        shifts, scale, grad_first, n, rstd, joint, probs, mixture, win_t, inverse,
        in_weight, out_weight, gain,
    )


SMALL = (
    ("in_bias", 1, 3 * D),
    ("out_bias", 1, D),
    ("up_bias", 1, FF),
    ("down_bias", 1, D),
    ("gain_first", 1, D),
    ("gain_rest", 2, D),
    ("offset_first", 1, D),
    ("offset_rest", 2, D),
    ("table_one", 3, UNITS),
    ("table_two", HEADS, UNITS),
    ("scale", HEADS, 128),
    ("router", 0, D),
)


def small_places(experts):
    places, at = {}, 0
    for name, rows, width in SMALL:
        rows = rows or experts
        places[name] = (at, rows, width)
        at += rows * (width // 128)
    return places, at


def put_small(ref, places, name, value):
    at, rows, width = places[name]
    for lane in range(0, width, 128):
        ref[at : at + rows, :] = value[:, lane : lane + 128]
        at += rows


def get_small(ref, places, name):
    at, rows, width = places[name]
    return jnp.concatenate(
        [ref[at + i * rows : at + (i + 1) * rows, :] for i in range(width // 128)], axis=1
    )


def table_back_kernel(
    places, table_grad, scale_rows, w1, b1, w2, in_bias, out_bias, up_bias, down_bias,
    gain_first, gain_rest, offset_first, offset_rest, router, small, values_grad,
):
    spread = spread_matrix(True)
    for head in range(HEADS):
        high, low = split(table_grad[head])
        spread_low = spread.astype(BF16)
        flat = dot(high, spread_low, 1, 1) + dot(low, spread_low, 1, 1)
        flat = jnp.concatenate([flat, jnp.zeros((AREA, TABLE - 384), F32)], axis=1)
        total = jnp.zeros((16, TABLE), F32)
        for key_row in range(WS):
            shift = EXTENT * key_row
            line = flat[key_row * WS : (key_row + 1) * WS, :]
            line = jnp.concatenate([line, jnp.zeros((16 - WS, TABLE), F32)], axis=0)
            total += pltpu.roll(line, shift, 1)
        total = pltpu.roll(total, 0, 1, stride=1, stride_axis=0)
        values_grad[head : head + 1, :] = col_sum(total)
    f_row, f_col = offsets_row((UNITS, TABLE), 1, -1.0)
    w1t = jnp.transpose(w1[...], (1, 0))
    b1t = jnp.transpose(b1[...], (1, 0))
    hidden, slope = gelu_pair(w1t[:, 0:1] * f_row + w1t[:, 1:2] * f_col + b1t[:, 0:1])
    chance = jax.nn.sigmoid(exact_dot(w2[...], hidden, 0, 0))
    grad_pre = values_grad[:HEADS, :] * (16.0 * chance * (1.0 - chance))
    small[...] = jnp.zeros_like(small)
    put_small(small, places, "table_two", exact_dot(grad_pre, hidden, 1, 1))
    grad_hidden = exact_dot(w2[...], grad_pre, 1, 0) * slope
    f_row, f_col = offsets_row((8, TABLE), 1, -1.0)
    kind = iota((8, TABLE), 0)
    factors = jnp.where(kind == 0, f_row, jnp.where(kind == 1, f_col, 1.0))
    put_small(small, places, "table_one", exact_dot(factors, grad_hidden, 1, 1)[:3, :])
    scales = jnp.sum(scale_rows[...], axis=1, keepdims=True)
    put_small(small, places, "scale", jnp.broadcast_to(scales, (HEADS, 128)))
    put_small(small, places, "in_bias", in_bias[...])
    put_small(small, places, "out_bias", out_bias[...])
    put_small(small, places, "up_bias", up_bias[...])
    put_small(small, places, "down_bias", down_bias[...])
    put_small(small, places, "gain_first", gain_first[...])
    put_small(small, places, "gain_rest", gain_rest[1:, :])
    put_small(small, places, "offset_first", offset_first[...])
    put_small(small, places, "offset_rest", offset_rest[1:, :])
    put_small(small, places, "router", router[...])


def table_back(small_rows, experts, *args):
    places, _ = small_places(experts)
    return pl.pallas_call(
        functools.partial(table_back_kernel, places),
        out_shape=full((small_rows, 128)),
        scratch_shapes=[pltpu.VMEM((16, TABLE), F32)],
        compiler_params=params(),
        name="table_back",
    )(*args)


def reduce_kernel(names, *refs):
    count = len(names)
    sources, outs, refs = refs[:count], refs[count : 2 * count], refs[2 * count :]
    sums = []
    for name, source, out in zip(names, sources, outs):
        levels = levels_of(name)
        depth = len(levels)
        held, lands, (send, recv) = refs[0], refs[1 : 1 + depth], refs[1 + depth : 3 + depth]
        refs = refs[3 + depth :]
        sums.append(Sum(source, held, out, lands, send, recv, levels).stages())
    greet(greeted(levels_of(("dp", "expert"))))
    for k in range(max(len(stages) for stages in sums)):
        for stages in sums:
            if k < len(stages):
                stages[k]()


def reduce_all(names, arrays, dp, experts):
    scratch = []
    for name, array in zip(names, arrays):
        counts = level_counts(name, dp, experts)
        scratch.append(pltpu.VMEM(array.shape, array.dtype))
        scratch += land_shapes(array.shape[0], array.shape[1], array.dtype, counts)
        scratch += sum_sems(counts)
    return pl.pallas_call(
        functools.partial(reduce_kernel, names),
        out_shape=tuple(full(array.shape, array.dtype) for array in arrays),
        scratch_shapes=scratch,
        compiler_params=params(collective_id=2, has_side_effects=True),
        name="reduce",
    )(*arrays)


def unpack_kernel(
    places, own, dense, last, small,
    in_grad, in_bias, scale, table_first, table_first_bias, table_second, out_grad, out_bias,
    up_grad, up_bias, down_grad, down_bias, router, own_up, own_up_bias, own_down, own_down_bias,
    gain, offset,
):
    for block in range(3):
        part = slice(block * D, (block + 1) * D)
        in_grad[:, part] = last[part, :].astype(F32)
    out_grad[...] = last[3 * D : 4 * D, :].astype(F32)
    for source, up, down in ((dense, up_grad, down_grad), (own, own_up, own_down)):
        for block in range(FF // D):
            part = slice(block * D, (block + 1) * D)
            up[:, part] = source[part, :].astype(F32)
            down[part, :] = source[FF + block * D : FF + (block + 1) * D, :].astype(F32)
    tail = own[2 * FF : 2 * FF + 16, :].astype(F32)
    for block in range(FF // D):
        own_up_bias[:, block * D : (block + 1) * D] = tail[block : block + 1, :]
    own_down_bias[...] = tail[FF // D : FF // D + 1, :]
    get = functools.partial(get_small, small, places)
    row = get("in_bias")
    in_bias[0:1, :] = row[:, :D]
    in_bias[1:2, :] = row[:, 2 * D :]
    scale[...] = get("scale")[:, 0:1]
    one = get("table_one")
    table_first[...] = one[0:2, :]
    table_first_bias[...] = one[2:3, :]
    table_second[...] = jnp.transpose(get("table_two"), (1, 0))
    out_bias[...] = get("out_bias")
    up_bias[...] = get("up_bias")
    down_bias[...] = get("down_bias")
    router[...] = jnp.transpose(get("router"), (1, 0))
    gain[0:1, :] = get("gain_first")
    gain[1:3, :] = get("gain_rest")
    offset[0:1, :] = get("offset_first")
    offset[1:3, :] = get("offset_rest")


def unpack(own, dense, last, small, experts):
    places, _ = small_places(experts)
    return pl.pallas_call(
        functools.partial(unpack_kernel, places),
        out_shape=(
            full((D, 3 * D)),
            full((2, D)),
            full((HEADS, 1)),
            full((2, UNITS)),
            full((1, UNITS)),
            full((UNITS, HEADS)),
            full((D, D)),
            full((1, D)),
            full((D, FF)),
            full((1, FF)),
            full((FF, D)),
            full((1, D)),
            full((D, experts)),
            full((D, FF)),
            full((1, FF)),
            full((FF, D)),
            full((1, D)),
            full((3, D)),
            full((3, D)),
        ),
        compiler_params=params(),
        name="unpack",
    )(own, dense, last, small)


def per_device(
    tokens, shifts, routes, cotangent, in_weight, in_bias, logit_scale,
    bias_net_first_weight, bias_net_first_bias, bias_net_second_weight,
    out_weight, out_bias, up_weight, up_bias, down_weight, down_bias, router_weight,
    expert_up, expert_up_bias, expert_down, expert_down_bias, norm_gain, norm_bias,
):
    experts = router_weight.shape[1]
    dp = lax.axis_size("dp")
    group = lax.axis_size("expert")
    capacity = (5 * TOKENS + 4 * experts - 1) // (4 * experts)
    slots = -(-capacity // 16) * 16
    own, both = ("dp",), ("dp", "expert")
    own_counts, both_counts = level_counts(own, dp, group), level_counts(both, dp, group)
    own_rows = padded_rows(2 * FF + 16, own_counts, 16)
    dense_rows = padded_rows(2 * FF, both_counts, 16)
    last_rows = padded_rows(4 * D, both_counts, 16)
    small_rows = padded_rows(small_places(experts)[1], both_counts, 8)

    picture = tokens.reshape(SIDE, SIDE, D)
    cot = cotangent.reshape(SIDE, SIDE, D)
    route_col = routes.reshape(TOKENS, 1)
    first_bias = bias_net_first_bias.reshape(1, UNITS)

    slot_col, slot_row, cot_slots, table, scale = prep(
        route_col, cot, bias_net_first_weight, first_bias, bias_net_second_weight,
        logit_scale.reshape(1, HEADS), experts, capacity, slots,
    )
    cot_arrived, normed, n_zero, rstd_zero, joint, probs, mixture, win_t, inverse = attend(
        cot_slots, shifts, scale, picture, in_weight, in_bias, table,
        out_weight, out_bias.reshape(1, D), norm_gain, norm_bias,
    )
    first_low, active, slope, n_one, rstd_one, second, buffer = forward(
        shifts, picture, normed, up_weight, up_bias.reshape(1, FF), down_weight,
        down_bias.reshape(1, D), norm_gain, norm_bias, slot_row, experts, slots,
    )
    returned, grad_returned, own_packed = run_experts(
        buffer, cot_arrived, router_weight, expert_up[0], expert_up_bias, expert_down[0],
        expert_down_bias, norm_gain, own_rows,
    )
    (
        result, grad_first, dense_packed, up_bias_grad, down_bias_grad, router_grad,
        gain_grad, offset_grad,
    ) = backward(
        second, cot, slot_col, route_col, returned.reshape(-1, D), grad_returned.reshape(-1, D),
        router_weight, first_low, active, slope, n_one, rstd_one, up_weight, down_weight,
        norm_gain, norm_bias, dense_rows,
    )
    (
        tokens_grad, last_packed, in_bias_grad, out_bias_grad, gain_zero, offset_zero, scale_rows,
        table_grad,
    ) = attend_back(
        shifts, scale, grad_first, n_zero, rstd_zero, joint, probs, mixture, win_t, inverse,
        in_weight, out_weight, norm_gain, last_rows,
    )
    small = table_back(
        small_rows, experts, table_grad, scale_rows, bias_net_first_weight, first_bias,
        bias_net_second_weight, in_bias_grad, out_bias_grad, up_bias_grad, down_bias_grad,
        gain_zero, gain_grad, offset_zero, offset_grad, router_grad,
    )
    sums = reduce_all(
        (own, both, both, both), (own_packed, dense_packed, last_packed, small), dp, group
    )
    (
        in_weight_grad, in_bias_grad, scale_grad, table_one, table_bias, table_two, out_grad,
        out_bias_grad, up_grad, up_bias_grad, down_grad, down_bias_grad, router_grad,
        own_up, own_up_bias, own_down, own_down_bias, gain_grad, offset_grad,
    ) = unpack(*sums, experts)
    return (
        result.reshape(tokens.shape),
        tokens_grad.reshape(tokens.shape),
        in_weight_grad,
        in_bias_grad,
        scale_grad.reshape(HEADS),
        table_one,
        table_bias.reshape(UNITS),
        table_two,
        out_grad,
        out_bias_grad.reshape(D),
        up_grad,
        up_bias_grad.reshape(FF),
        down_grad,
        down_bias_grad.reshape(D),
        router_grad,
        own_up[None],
        own_up_bias,
        own_down[None],
        own_down_bias,
        gain_grad,
        offset_grad,
    )


def solution(mesh):
    split_all = P(("dp", "expert"))
    placed = (split_all,) * 4 + (P(),) * 13 + (P("expert"),) * 4 + (P(),) * 2
    return jax.shard_map(
        per_device,
        mesh=mesh,
        in_specs=placed,
        out_specs=(split_all,) * 2 + (P(),) * 13 + (P("expert"),) * 4 + (P(),) * 2,
        check_vma=False,
    )
```

```python
import functools

import jax
import jax.numpy as jnp
from jax import lax
from jax.experimental import pallas as pl
from jax.experimental.pallas import tpu as pltpu
from jax.sharding import PartitionSpec as P

D = 384
HEADS = 12
HEAD = D // HEADS
WS = 12
SIDE = 36
AREA = WS * WS
ACROSS = SIDE // WS
WINDOWS = ACROSS * ACROSS
TOKENS = SIDE * SIDE
FF = 1536
EXTENT = 2 * WS - 1
UNITS = 512
TABLE = 640
ROWS = 432
CHUNK = 256
F32 = jnp.float32
BF16 = jnp.bfloat16
I32 = jnp.int32
VMEM_LIMIT = 60 * 1024 * 1024


def dot(left, right, left_dim, right_dim):
    return lax.dot_general(
        left, right, (((left_dim,), (right_dim,)), ((), ())), preferred_element_type=F32
    )


def exact_dot(left, right, left_dim, right_dim):
    return lax.dot_general(
        left,
        right,
        (((left_dim,), (right_dim,)), ((), ())),
        preferred_element_type=F32,
        precision=lax.Precision.HIGHEST,
    )


def split(values):
    high = values.astype(BF16)
    return high, (values - high.astype(F32)).astype(BF16)


def iota(shape, dim):
    return lax.broadcasted_iota(I32, shape, dim)


def gelu_pair(values):
    size = jnp.abs(values)
    t = 1.0 / (1.0 + 0.2316419 * size)
    bell = jnp.exp(-0.5 * values * values) * 0.3989422804014327
    series = t * (
        0.319381530
        + t * (-0.356563782 + t * (1.781477937 + t * (-1.821255978 + t * 1.330274429)))
    )
    tail = series * bell
    phi = jnp.where(values >= 0.0, 1.0 - tail, tail)
    return values * phi, phi + values * bell


def norm_parts(values):
    centered = values - jnp.mean(values, axis=-1, keepdims=True)
    rstd = lax.rsqrt(jnp.mean(centered * centered, axis=-1, keepdims=True) + 1e-05)
    return centered * rstd, rstd


def norm_back(grad_n, n, rstd):
    return rstd * (
        grad_n
        - jnp.mean(grad_n, axis=-1, keepdims=True)
        - n * jnp.mean(grad_n * n, axis=-1, keepdims=True)
    )


def row_of(ref):
    return ref[...].reshape(1, ref.shape[0])


def col_sum(values):
    return jnp.sum(values, axis=0, keepdims=True)


def div_ws(values):
    return (values * 171) >> 11


def full(shape, dtype=F32):
    return jax.ShapeDtypeStruct(shape, dtype)


def whole(shape):
    return pl.BlockSpec(shape, lambda *_: (0,) * len(shape))


def smem():
    return pl.BlockSpec(memory_space=pltpu.SMEM)


def params(**more):
    return pltpu.CompilerParams(vmem_limit_bytes=VMEM_LIMIT, **more)


def partner(me, step, count):
    side = 1
    while side * side < count:
        side *= 2
    if side * side != count:
        return lax.rem(me + step, count)
    row = lax.rem(lax.div(me, side) + step // side, side)
    col = lax.rem(lax.rem(me, side) + step % side, side)
    return row * side + col


def opposite(step, count):
    side = 1
    while side * side < count:
        side *= 2
    if side * side != count:
        return (count - step) % count
    return ((side - step // side) % side) * side + (side - step % side) % side


def greet(devices):
    barrier = pltpu.get_barrier_semaphore()
    for device in devices:
        pl.semaphore_signal(barrier, inc=1, device_id=device, device_id_type=pl.DeviceIdType.MESH)
    pl.semaphore_wait(barrier, len(devices))


def levels_of(names):
    dp = lax.axis_index("dp")
    depth = lax.axis_size("dp") // 2
    core = lax.rem(dp, 2)
    place = lax.div(dp, 2)
    levels = [(2, core, lambda j: {"dp": place * 2 + j})]
    if "expert" in names:
        levels.append((lax.axis_size("expert"), lax.axis_index("expert"), lambda j: {"expert": j}))
    if depth > 1:
        levels.append((depth, place, lambda j: {"dp": j * 2 + core}))
    return levels


def level_counts(names, dp, experts):
    counts = [2] + ([experts] if "expert" in names else []) + ([dp // 2] if dp > 2 else [])
    return counts


def padded_rows(rows, counts, tile):
    unit = tile
    for count in counts:
        unit *= count
    return -(-rows // unit) * unit


def land_shapes(rows, width, dtype, counts):
    shapes = []
    for count in counts:
        rows //= count
        shapes.append(pltpu.VMEM((count - 1, rows, width), dtype))
    return shapes


def sum_sems(counts):
    return [pltpu.SemaphoreType.DMA((2 * len(counts), max(counts)))] * 2


class Sum:
    def __init__(self, source, held, result, lands, send, recv, levels):
        self.source, self.held, self.result, self.lands = source, held, result, lands
        self.send, self.recv, self.levels = send, recv, levels
        rows = source.shape[0]
        start = 0
        self.regions = []
        for count, index, _ in levels:
            rows //= count
            self.regions.append((start, rows))
            start = start + index * rows

    def scatter(self, level, begin):
        count, index, device = self.levels[level]
        start, rows = self.regions[level]
        ref = self.held if level else self.source
        into = self.held if level < len(self.levels) - 1 else self.result
        for step in range(1, count):
            to = lax.rem(index + step, count)
            copy = pltpu.make_async_remote_copy(
                src_ref=ref.at[pl.ds(pl.multiple_of(start + to * rows, 8), rows)],
                dst_ref=self.lands[level].at[step - 1],
                send_sem=self.send.at[level, step],
                recv_sem=self.recv.at[level, step],
                device_id=device(to),
                device_id_type=pl.DeviceIdType.MESH,
            )
            copy.start() if begin else copy.wait()
        if begin:
            return
        mine = start + index * rows
        tile = 16 if ref.dtype == BF16 else 8
        chunk = tile
        while rows % (chunk * 2) == 0 and chunk < 128:
            chunk *= 2

        def add(i, carry):
            here = pl.ds(pl.multiple_of(mine + i * chunk, tile), chunk)
            there = pl.ds(pl.multiple_of(i * chunk, tile), chunk)
            total = ref[here, :].astype(F32)
            for step in range(1, count):
                total = total + self.lands[level][step - 1, there, :].astype(F32)
            into[here, :] = total.astype(into.dtype)
            return carry

        lax.fori_loop(0, rows // chunk, add, 0)

    def gather(self, level, begin):
        count, index, device = self.levels[level]
        start, rows = self.regions[level]
        mine = self.result.at[pl.ds(pl.multiple_of(start + index * rows, 8), rows)]
        for step in range(1, count):
            to = lax.rem(index + step, count)
            copy = pltpu.make_async_remote_copy(
                src_ref=mine,
                dst_ref=mine,
                send_sem=self.send.at[len(self.levels) + level, step],
                recv_sem=self.recv.at[len(self.levels) + level, step],
                device_id=device(to),
                device_id_type=pl.DeviceIdType.MESH,
            )
            copy.start() if begin else copy.wait()

    def stages(self):
        last = len(self.levels) - 1
        moves = [(self.scatter, level) for level in range(last + 1)]
        moves += [(self.gather, level) for level in range(last, -1, -1)]

        def stage(k):
            if k:
                moves[k - 1][0](moves[k - 1][1], False)
            if k < len(moves):
                moves[k][0](moves[k][1], True)

        return [functools.partial(stage, k) for k in range(len(moves) + 1)]


def greeted(levels):
    devices = []
    for count, index, device in levels:
        devices += [device(lax.rem(index + step, count)) for step in range(1, count)]
    return devices


def offsets_row(shape, dim, sign):
    place = iota(shape, dim)
    row = jnp.floor((place.astype(F32) + 0.5) * (1.0 / EXTENT)).astype(I32)
    col = place - row * EXTENT

    def logged(step):
        e = sign * (step - (WS - 1)).astype(F32) * (8.0 / (WS - 1))
        size = jnp.log2(jnp.abs(e) + 1.0) * (1.0 / 3.0)
        return jnp.where(e < 0.0, -size, size)

    return logged(row), logged(col)


def spread_matrix(mirrored):
    token = iota((384, AREA), 1)
    row = div_ws(token)
    lin = row * EXTENT + (token - row * WS)
    if mirrored:
        lin = (WS - 1) * EXTENT + (WS - 1) - lin
    return (iota((384, AREA), 0) == lin).astype(F32)


def prep_kernel(
    capacity, routes, cot, w1, b1, w2, ls, slot_col, slot_row, zbuf, table, scale, flat, u_ref, route_col
):
    slots = zbuf.shape[1]
    experts = zbuf.shape[0]
    route_col[...] = jnp.transpose(
        jnp.broadcast_to(routes[...].astype(F32), (128, TOKENS)), (1, 0)
    )
    before = (iota((AREA, AREA), 1) < iota((AREA, AREA), 0)).astype(BF16)
    carry = jnp.zeros((1, 128), F32)
    for block in range(TOKENS // AREA):
        rows = pl.ds(block * AREA, AREA)
        route = route_col[rows, 0:1]
        onehot = (route == iota((AREA, 128), 1).astype(F32)).astype(F32)
        ahead = dot(before, onehot.astype(BF16), 1, 0) + carry
        position = jnp.sum(ahead * onehot, axis=1, keepdims=True)
        carry = carry + col_sum(onehot)
        slot = route * slots + position
        slot_col[rows, :] = jnp.where(position < capacity, slot, -1.0).astype(I32)
    slot_row[...] = jnp.transpose(
        jnp.broadcast_to(slot_col[...].astype(F32), (TOKENS, 128)), (1, 0)
    )[0:1, :].astype(I32)

    for row in range(SIDE):
        flat[row * SIDE : (row + 1) * SIDE, :] = cot[row].astype(F32)
    low = flat[...].astype(BF16)
    for expert in range(experts):
        pick = (iota((slots, TOKENS), 0) + expert * slots == slot_row[...]).astype(BF16)
        zbuf[expert] = dot(pick, low, 1, 0).astype(BF16)

    scale[...] = jnp.exp(row_of(ls))
    f_row, f_col = offsets_row((UNITS, TABLE), 1, 1.0)
    w1t = jnp.transpose(w1[...], (1, 0))
    b1t = jnp.transpose(row_of(b1), (1, 0))
    hidden, _ = gelu_pair(w1t[:, 0:1] * f_row + w1t[:, 1:2] * f_col + b1t[:, 0:1])
    values = 16.0 * jax.nn.sigmoid(exact_dot(w2[...], hidden, 1, 0))
    spread = spread_matrix(False).astype(BF16)
    for head in range(HEADS):
        line = jnp.broadcast_to(values[head : head + 1, :], (16, TABLE))
        line = pltpu.roll(line, 0, 1, stride=1, stride_axis=0)
        for key_row in range(WS):
            shift = (EXTENT * key_row - (WS - 1) * EXTENT - (WS - 1)) % TABLE
            rolled = pltpu.roll(line, shift, 1)
            u_ref[key_row * WS : (key_row + 1) * WS, :] = rolled[:WS, :384]
        high, low_part = split(u_ref[...])
        table[head] = dot(high, spread, 1, 0) + dot(low_part, spread, 1, 0)


def prep(routes, cotangent, w1, b1, w2, ls, experts, capacity, slots):
    return pl.pallas_call(
        functools.partial(prep_kernel, capacity),
        out_shape=(
            full((TOKENS, 1), I32),
            full((1, TOKENS), I32),
            full((experts, slots, D), BF16),
            full((HEADS, AREA, AREA)),
            full((1, HEADS)),
        ),
        scratch_shapes=[
            pltpu.VMEM((TOKENS, D), F32),
            pltpu.VMEM((AREA, 384), F32),
            pltpu.VMEM((TOKENS, 128), F32),
        ],
        compiler_params=params(),
        name="prep",
    )(routes, cotangent, w1, b1, w2, ls)


def window_labels(window, shift_row, shift_col):
    def labels(shape, dim):
        token = iota(shape, dim)
        row = div_ws(token)
        col = token - row * WS + lax.rem(window, ACROSS) * WS
        row = row + lax.div(window, ACROSS) * WS

        def region(place, shift):
            last = jnp.where(place < SIDE - shift, 1, 2)
            return jnp.where(place < SIDE - WS, 0, last)

        return region(row, shift_row) * 3 + region(col, shift_col)

    return labels((AREA, 1), 0), labels((1, AREA), 1)


def roll_to_windows(read_row, doubled, windows, shift_row, shift_col):
    for row in range(SIDE):
        line = read_row(row)
        doubled[row, :SIDE, :] = line
        doubled[row, SIDE:, :] = line[:WS, :]
    for row in range(SIDE):
        source = row + shift_row
        source = jnp.where(source >= SIDE, source - SIDE, source)
        line = pltpu.roll(doubled[source], SIDE + WS - shift_col, 0)
        for across in range(ACROSS):
            start = ((row // WS) * ACROSS + across) * AREA + (row % WS) * WS
            windows[start : start + WS, :] = line[across * WS : (across + 1) * WS, :]


def roll_to_image(windows, doubled, write_row, shift_row, shift_col):
    for row in range(SIDE):
        for across in range(ACROSS):
            start = ((row // WS) * ACROSS + across) * AREA + (row % WS) * WS
            line = windows[start : start + WS, :]
            doubled[row, across * WS : (across + 1) * WS, :] = line
            if across == ACROSS - 1:
                doubled[row, SIDE:, :] = line
    for row in range(SIDE):
        source = row - shift_row
        source = jnp.where(source < 0, source + SIDE, source)
        write_row(row, pltpu.roll(doubled[source], shift_col, 0)[:SIDE, :])


def attend_kernel(
    cot_slots, shifts, scale, tokens, in_weight, in_bias, table, out_weight, out_bias, gain, offset,
    cot_arrived, normed, n_out, rstd_out, joint, probs, mixture, win_t, inverse,
    doubled, windows, in_weight_t, bias_col, joined, send, recv, local,
):
    window = pl.program_id(0)
    shift_row, shift_col = shifts[0, 0], shifts[0, 1]
    me = lax.axis_index("expert")
    count = cot_slots.shape[0]

    def move(step):
        to = partner(me, step, count)
        return pltpu.make_async_remote_copy(
            src_ref=cot_slots.at[to],
            dst_ref=cot_arrived.at[me],
            send_sem=send.at[step],
            recv_sem=recv.at[step],
            device_id={"expert": to},
            device_id_type=pl.DeviceIdType.MESH,
        )

    keep = pltpu.make_async_copy(cot_slots.at[me], cot_arrived.at[me], local)

    @pl.when(window == 0)
    def _():
        greet([{"expert": partner(me, step, count)} for step in range(1, count)])
        for step in range(1, count):
            move(step).start()
        keep.start()
        roll_to_windows(
            lambda row: tokens[row].astype(F32), doubled, windows, shift_row, shift_col
        )
        in_weight_t[...] = jnp.transpose(in_weight[...], (1, 0))
        bias_col[:, 0:2] = jnp.transpose(in_bias[...], (1, 0))

    mine = windows[pl.ds(pl.multiple_of(window * AREA, 16), AREA), :].astype(BF16)
    win_t[0, :D, :] = jnp.transpose(mine, (1, 0))
    win_t[0, D:, :] = (iota((16, AREA), 0) == 0).astype(BF16)
    label_keys, label_queries = window_labels(window, shift_row, shift_col)
    mask = jnp.where(label_keys == label_queries, 0.0, -100.0)
    joined[...] = dot(in_weight_t[...], mine, 1, 1)

    def unit(rows, bias, place):
        shaped = (joined[rows, :] + bias).reshape(HEADS, HEAD, AREA)
        inner = lax.rsqrt(1.0 + jnp.sum(shaped * shaped, axis=1, keepdims=True))
        for head in range(HEADS):
            inverse[0, place + head : place + head + 1, :] = inner[head]
        return (shaped * inner).reshape(D, AREA).astype(BF16)

    queries = unit(slice(0, D), bias_col[:, 0:1], 0)
    keys = unit(slice(D, 2 * D), 0.0, HEADS)
    values = (joined[2 * D :, :] + bias_col[:, 1:2]).astype(BF16)
    joint[0, :D, :] = queries
    joint[0, D : 2 * D, :] = keys
    joint[0, 2 * D :, :] = values
    key_rows = jnp.transpose(keys, (1, 0))
    blank = jnp.zeros((HEAD, AREA), BF16)

    def scores_of(group):
        lanes = key_rows[:, group * 128 : (group + 1) * 128]
        found = []
        for head in range(4):
            at = group * 128 + head * HEAD
            parts = [blank] * 4
            parts[head] = queries[at : at + HEAD, :]
            found.append(dot(lanes, jnp.concatenate(parts, axis=0), 1, 0))
        return found

    ahead = scores_of(0)
    for group in range(HEADS // 4):
        current = ahead
        if group + 1 < HEADS // 4:
            ahead = scores_of(group + 1)
        lows = []
        for i in range(4):
            head = group * 4 + i
            scores = current[i] * scale[0, head] + (table[head] + mask)
            exponent = jnp.exp(scores - jnp.max(scores, axis=0, keepdims=True))
            low = (exponent * (1.0 / col_sum(exponent))).astype(BF16)
            probs[0, head] = low
            lows.append(low)
        for i in range(4):
            at = (group * 4 + i) * HEAD
            mixture[0, at : at + HEAD, :] = dot(values[at : at + HEAD, :], lows[i], 1, 0).astype(BF16)
    branch = dot(mixture[0], out_weight[...], 0, 0) + row_of(out_bias)
    n, rstd = norm_parts(branch)
    normed[...] = n * gain[0:1, :] + offset[0:1, :]
    n_out[...] = n.astype(BF16)
    rstd_out[...] = rstd

    @pl.when(window == WINDOWS - 1)
    def _():
        for step in range(1, count):
            move(step).wait()
        keep.wait()


def attend(
    cot_slots, shifts, scale, tokens, in_weight, in_bias, table, out_weight, out_bias, gain, offset
):
    per_window = lambda *dims: pl.BlockSpec((1,) + dims, lambda w: (w,) + (0,) * len(dims))
    rows = lambda width: pl.BlockSpec((AREA, width), lambda w: (w, 0))
    return pl.pallas_call(
        attend_kernel,
        grid=(WINDOWS,),
        in_specs=[
            pl.BlockSpec(memory_space=pl.ANY),
            smem(),
            smem(),
            whole((SIDE, SIDE, D)),
            whole((D, 3 * D)),
            whole((2, D)),
            whole((HEADS, AREA, AREA)),
            whole((D, D)),
            whole((D,)),
            whole((3, D)),
            whole((3, D)),
        ],
        out_specs=(
            pl.BlockSpec(memory_space=pl.ANY),
            rows(D),
            rows(D),
            rows(1),
            per_window(3 * D, AREA),
            per_window(HEADS, AREA, AREA),
            per_window(D, AREA),
            per_window(D + 16, AREA),
            per_window(2 * HEADS, AREA),
        ),
        out_shape=(
            full(cot_slots.shape, BF16),
            full((TOKENS, D)),
            full((TOKENS, D), BF16),
            full((TOKENS, 1)),
            full((WINDOWS, 3 * D, AREA), BF16),
            full((WINDOWS, HEADS, AREA, AREA), BF16),
            full((WINDOWS, D, AREA), BF16),
            full((WINDOWS, D + 16, AREA), BF16),
            full((WINDOWS, 2 * HEADS, AREA)),
        ),
        scratch_shapes=[
            pltpu.VMEM((SIDE, SIDE + WS, D), F32),
            pltpu.VMEM((TOKENS, D), F32),
            pltpu.VMEM((3 * D, D), BF16),
            pltpu.VMEM((D, 128), F32),
            pltpu.VMEM((3 * D, AREA), F32),
            pltpu.SemaphoreType.DMA((cot_slots.shape[0],)),
            pltpu.SemaphoreType.DMA((cot_slots.shape[0],)),
            pltpu.SemaphoreType.DMA(()),
        ],
        compiler_params=params(collective_id=0, has_side_effects=True),
        name="attend",
    )(cot_slots, shifts, scale, tokens, in_weight, in_bias, table, out_weight, out_bias, gain, offset)


def forward_kernel(
    shifts, tokens, normed, up, up_bias, down, down_bias, gain, offset, slot_row,
    first_low, active, slope, n_out, rstd_out, second, buffer,
    doubled, image, second_low,
):
    step = pl.program_id(0)

    @pl.when(step == 0)
    def _():
        def write_row(row, line):
            image[row * SIDE : (row + 1) * SIDE, :] = line + tokens[row].astype(F32)

        roll_to_image(normed, doubled, write_row, shifts[0, 0], shifts[0, 1])

    rows = pl.ds(pl.multiple_of(step * ROWS, 16), ROWS)
    first = image[rows, :]
    low = first.astype(BF16)
    first_low[...] = low
    up_row = row_of(up_bias)
    branch = jnp.broadcast_to(row_of(down_bias), (ROWS, D))
    for at in range(0, FF, CHUNK):
        hidden = dot(low, up[:, at : at + CHUNK], 1, 0) + up_row[:, at : at + CHUNK]
        activated, derivative = gelu_pair(hidden)
        activated = activated.astype(BF16)
        active[:, at : at + CHUNK] = activated
        slope[:, at : at + CHUNK] = derivative.astype(BF16)
        branch += dot(activated, down[at : at + CHUNK, :], 1, 0)
    n, rstd = norm_parts(branch)
    n_out[...] = n.astype(BF16)
    rstd_out[...] = rstd
    result = first + n * gain[1:2, :] + offset[1:2, :]
    second[...] = result
    second_low[rows, :] = result.astype(BF16)

    @pl.when(step == TOKENS // ROWS - 1)
    def _():
        slots = buffer.shape[1]
        for expert in range(buffer.shape[0]):
            pick = (iota((slots, TOKENS), 0) + expert * slots == slot_row[...]).astype(BF16)
            buffer[expert] = dot(pick, second_low[...], 1, 0).astype(BF16)


def forward(
    shifts, tokens, normed, up, up_bias, down, down_bias, gain, offset, slot_row, experts, slots
):
    rows = lambda width: pl.BlockSpec((ROWS, width), lambda i: (i, 0))
    return pl.pallas_call(
        forward_kernel,
        grid=(TOKENS // ROWS,),
        in_specs=[
            smem(),
            whole((SIDE, SIDE, D)),
            whole((TOKENS, D)),
            whole((D, FF)),
            whole((FF,)),
            whole((FF, D)),
            whole((D,)),
            whole((3, D)),
            whole((3, D)),
            whole((1, TOKENS)),
        ],
        out_specs=(
            rows(D),
            rows(FF),
            rows(FF),
            rows(D),
            rows(1),
            rows(D),
            whole((experts, slots, D)),
        ),
        out_shape=(
            full((TOKENS, D), BF16),
            full((TOKENS, FF), BF16),
            full((TOKENS, FF), BF16),
            full((TOKENS, D), BF16),
            full((TOKENS, 1)),
            full((TOKENS, D)),
            full((experts, slots, D), BF16),
        ),
        scratch_shapes=[
            pltpu.VMEM((SIDE, SIDE + WS, D), F32),
            pltpu.VMEM((TOKENS, D), F32),
            pltpu.VMEM((TOKENS, D), BF16),
        ],
        compiler_params=params(),
        name="forward",
    )(shifts, tokens, normed, up, up_bias, down, down_bias, gain, offset, slot_row)


def expert_kernel(
    buffer, cot, router, up, up_bias, down, down_bias, gain,
    out, grad_in, packed,
    arrived, outs, grads, active, slope, up_grad, down_grad_t, up_bias_grad, down_bias_grad,
    send, recv,
):
    me = lax.axis_index("expert")
    count, slots, _ = buffer.shape
    others = range(1, count)

    def move(kind, step, source, target, to):
        return pltpu.make_async_remote_copy(
            src_ref=source,
            dst_ref=target,
            send_sem=send.at[kind, step],
            recv_sem=recv.at[kind, step],
            device_id={"expert": to},
            device_id_type=pl.DeviceIdType.MESH,
        )

    greet([{"expert": partner(me, step, count)} for step in others])
    for step in others:
        to = partner(me, step, count)
        move(0, step, buffer.at[to], arrived.at[step], to).start()
    arrived[0] = buffer[me]
    for ref in (up_grad, up_bias_grad, down_grad_t, down_bias_grad):
        ref[...] = jnp.zeros_like(ref)
    router_high, router_low = split(router[...])

    def work(step, carry):
        if count == 4:
            owner = lax.rem(lax.div(me, 2) + lax.div(step, 2), 2) * 2
            owner = owner + lax.rem(lax.rem(me, 2) + lax.rem(step, 2), 2)
        else:
            side = 1
            while side * side < count:
                side *= 2
            if side * side == count:
                owner = lax.rem(lax.div(me, side) + side - lax.div(step, side), side) * side
                owner = owner + lax.rem(lax.rem(me, side) + side - lax.rem(step, side), side)
            else:
                owner = lax.rem(me + count - step, count)

        @pl.when(step > 0)
        def _():
            move(0, step, buffer.at[owner], arrived.at[step], owner).wait_recv()

        features = arrived[step]
        logits = dot(features, router_high, 1, 1) + dot(features, router_low, 1, 1)
        chances = jnp.exp(logits - jnp.max(logits, axis=1, keepdims=True))
        own = jnp.where(iota(chances.shape, 1) == me, chances, 0.0)
        gate = jnp.sum(own, axis=1, keepdims=True) / jnp.sum(chances, axis=1, keepdims=True)

        output = jnp.zeros((slots, D), F32)
        for at in range(0, FF, CHUNK):
            hidden = dot(features, up[:, at : at + CHUNK], 1, 0) + up_bias[:, at : at + CHUNK]
            activated, derivative = gelu_pair(hidden)
            activated = activated.astype(BF16)
            active[:, at : at + CHUNK] = activated
            slope[:, at : at + CHUNK] = derivative
            output += dot(activated, down[at : at + CHUNK, :], 1, 0)
        output = (output + down_bias[...]).astype(BF16)
        outs[step] = output

        @pl.when(step > 0)
        def _():
            move(1, step, outs.at[step], out.at[me], owner).start()

        n, rstd = norm_parts(gate * output.astype(F32))
        grad_output = gate * norm_back(gain[2:3, :] * cot[owner].astype(F32), n, rstd)
        grad_low = grad_output.astype(BF16)
        down_bias_grad[...] += col_sum(grad_low.astype(F32))
        grad_low_t = jnp.transpose(grad_low, (1, 0))
        features_t = jnp.transpose(features, (1, 0))
        grad_features = jnp.zeros((slots, D), F32)
        for at in range(0, FF, CHUNK):
            part = slice(at, at + CHUNK)
            grad_hidden = dot(grad_low, down[part, :], 1, 1) * slope[:, part]
            grad_hidden_low = grad_hidden.astype(BF16)
            up_bias_grad[:, part] += col_sum(grad_hidden)
            down_grad_t[:, part] += dot(grad_low_t, active[:, part], 1, 0)
            up_grad[:, part] += dot(features_t, grad_hidden_low, 1, 0)
            grad_features += dot(grad_hidden_low, up[:, part], 1, 1)
        grads[step] = grad_features.astype(BF16)

        @pl.when(step > 0)
        def _():
            move(2, step, grads.at[step], grad_in.at[me], owner).start()

        return carry

    lax.fori_loop(0, count, work, 0)
    out[me] = outs[0]
    grad_in[me] = grads[0]
    pack_pair(packed, up_grad, down_grad_t)
    packed[2 * FF :, :] = jnp.zeros_like(packed[2 * FF :, :])
    tail = jnp.concatenate(
        [up_bias_grad[:, at : at + D] for at in range(0, FF, D)]
        + [down_bias_grad[...], jnp.zeros((11, D), F32)],
        axis=0,
    )
    packed[2 * FF : 2 * FF + 16, :] = tail.astype(BF16)
    for step in others:
        to = partner(me, step, count)
        move(0, step, buffer.at[to], arrived.at[step], to).wait_send()
        for kind, source, target in ((1, outs, out), (2, grads, grad_in)):
            move(kind, step, source.at[step], target.at[me], to).wait()


def pack_pair(packed, up_grad, down_grad_t):
    for block in range(FF // D):
        part = slice(block * D, (block + 1) * D)
        packed[part, :] = up_grad[:, part].astype(BF16)
        packed[FF + block * D : FF + (block + 1) * D, :] = jnp.transpose(
            down_grad_t[:, part].astype(BF16), (1, 0)
        )


def run_experts(buffer, cot, router, up, up_bias, down, down_bias, gain, packed_rows):
    count, slots, _ = buffer.shape
    blocks = (count, slots, D)
    return pl.pallas_call(
        expert_kernel,
        out_shape=(full(blocks, BF16), full(blocks, BF16), full((packed_rows, D), BF16)),
        scratch_shapes=[
            pltpu.VMEM(blocks, BF16),
            pltpu.VMEM(blocks, BF16),
            pltpu.VMEM(blocks, BF16),
            pltpu.VMEM((slots, FF), BF16),
            pltpu.VMEM((slots, FF), F32),
            pltpu.VMEM((D, FF), F32),
            pltpu.VMEM((D, FF), F32),
            pltpu.VMEM((1, FF), F32),
            pltpu.VMEM((1, D), F32),
            pltpu.SemaphoreType.DMA((3, count)),
            pltpu.SemaphoreType.DMA((3, count)),
        ],
        compiler_params=params(collective_id=1, has_side_effects=True),
        name="experts",
    )(buffer, cot, router, up, up_bias, down, down_bias, gain)


def backward_kernel(
    second, cot, slot_col, outputs, grads, router, first_low, active, slope, n_in, rstd_in,
    up, down, gain, offset,
    result, grad_first, packed, up_bias_grad, down_bias_grad, router_grad,
    gain_grad, offset_grad,
    flat, up_grad, down_grad_t,
):
    step = pl.program_id(0)

    @pl.when(step == 0)
    def _():
        for ref in (
            up_grad, up_bias_grad, down_grad_t, down_bias_grad, router_grad, gain_grad, offset_grad
        ):
            ref[...] = jnp.zeros_like(ref)

    lines = ROWS // SIDE
    for line in range(lines):
        flat[line * SIDE : (line + 1) * SIDE, :] = cot[line].astype(F32)
    z = flat[...]
    x = second[...]
    slots_all = outputs.shape[0]
    pick = (slot_col[...] == iota((ROWS, slots_all), 1)).astype(BF16)
    picked = dot(pick, outputs[...], 1, 0)
    dispatched = dot(pick, grads[...], 1, 0)

    logits = exact_dot(x, router[...], 1, 1)
    chances = jnp.exp(logits - jnp.max(logits, axis=1, keepdims=True))
    chances = chances / jnp.sum(chances, axis=1, keepdims=True)
    slots = slots_all // chances.shape[1]
    within = slot_col[...] - iota(chances.shape, 1) * slots
    onehot = ((within >= 0) & (within < slots)).astype(F32)
    gate = jnp.sum(chances * onehot, axis=1, keepdims=True)
    n, rstd = norm_parts(gate * picked)
    final = x + n * gain[2:3, :] + offset[2:3, :]
    gain_grad[2:3, :] += col_sum(z * n)
    offset_grad[2:3, :] += col_sum(z)
    grad_moe = norm_back(gain[2:3, :] * z, n, rstd)
    grad_gate = jnp.sum(grad_moe * picked, axis=1, keepdims=True)
    grad_logits = grad_gate * gate * (onehot - chances)
    grad_logits_low = grad_logits.astype(BF16)
    router_grad[...] += dot(grad_logits_low, x.astype(BF16), 0, 0)
    grad_second = z + dispatched + dot(grad_logits_low, router[...].astype(BF16), 1, 0)

    n = n_in[...].astype(F32)
    gain_grad[1:2, :] += col_sum(grad_second * n)
    offset_grad[1:2, :] += col_sum(grad_second)
    grad_branch = norm_back(gain[1:2, :] * grad_second, n, rstd_in[...])
    grad_low = grad_branch.astype(BF16)
    down_bias_grad[...] += col_sum(grad_branch)
    grad_low_t = jnp.transpose(grad_low, (1, 0))
    first_t = jnp.transpose(first_low[...], (1, 0))
    total = jnp.zeros((ROWS, D), F32)
    for at in range(0, FF, CHUNK):
        part = slice(at, at + CHUNK)
        grad_hidden = dot(grad_low, down[part, :], 1, 1) * slope[:, part].astype(F32)
        grad_hidden_low = grad_hidden.astype(BF16)
        up_bias_grad[:, part] += col_sum(grad_hidden)
        down_grad_t[:, part] += dot(grad_low_t, active[:, part], 1, 0)
        up_grad[:, part] += dot(first_t, grad_hidden_low, 1, 0)
        total += dot(grad_hidden_low, up[:, part], 1, 1)
    grad_first[...] = total + grad_second
    flat[...] = final
    for line in range(lines):
        result[line] = flat[line * SIDE : (line + 1) * SIDE, :].astype(BF16)

    @pl.when(step == TOKENS // ROWS - 1)
    def _():
        pack_pair(packed, up_grad, down_grad_t)
        if packed.shape[0] > 2 * FF:
            packed[2 * FF :, :] = jnp.zeros_like(packed[2 * FF :, :])


def backward(
    second, cot, slot_col, outputs, grads, router, first_low, active, slope, n, rstd,
    up, down, gain, offset, packed_rows,
):
    rows = lambda width: pl.BlockSpec((ROWS, width), lambda i: (i, 0))
    lines = pl.BlockSpec((ROWS // SIDE, SIDE, D), lambda i: (i, 0, 0))
    slots_all = outputs.shape[0]
    return pl.pallas_call(
        backward_kernel,
        grid=(TOKENS // ROWS,),
        in_specs=[
            rows(D),
            lines,
            rows(1),
            whole((slots_all, D)),
            whole((slots_all, D)),
            whole(router.shape),
            rows(D),
            rows(FF),
            rows(FF),
            rows(D),
            rows(1),
            whole((D, FF)),
            whole((FF, D)),
            whole((3, D)),
            whole((3, D)),
        ],
        out_specs=(
            lines,
            rows(D),
            whole((packed_rows, D)),
            whole((1, FF)),
            whole((1, D)),
            whole(router.shape),
            whole((3, D)),
            whole((3, D)),
        ),
        out_shape=(
            full((SIDE, SIDE, D), BF16),
            full((TOKENS, D)),
            full((packed_rows, D), BF16),
            full((1, FF)),
            full((1, D)),
            full(router.shape),
            full((3, D)),
            full((3, D)),
        ),
        scratch_shapes=[
            pltpu.VMEM((ROWS, D), F32),
            pltpu.VMEM((D, FF), F32),
            pltpu.VMEM((D, FF), F32),
        ],
        compiler_params=params(),
        name="backward",
    )(
        second, cot, slot_col, outputs, grads, router, first_low, active, slope, n, rstd,
        up, down, gain, offset,
    )


def attend_back_kernel(
    shifts, scale, grad_first, n_in, rstd_in, joint, probs, mixture, win_t, inverse,
    in_weight, out_weight, gain,
    tokens_grad, packed, in_bias_grad, out_bias_grad, gain_grad, offset_grad, scale_grad, table_grad,
    doubled, windows, joint_grad, grads_f32, in_grad, out_grad,
):
    window = pl.program_id(0)
    shift_row, shift_col = shifts[0, 0], shifts[0, 1]

    @pl.when(window == 0)
    def _():
        for ref in (
            in_grad, out_grad, out_bias_grad, gain_grad, offset_grad, scale_grad, table_grad
        ):
            ref[...] = jnp.zeros_like(ref)
        roll_to_windows(
            lambda row: grad_first[row * SIDE : (row + 1) * SIDE, :],
            doubled, windows, shift_row, shift_col,
        )

    mine = pl.ds(pl.multiple_of(window * AREA, 16), AREA)
    z = windows[mine, :]
    n = n_in[...].astype(F32)
    gain_grad[...] += col_sum(z * n)
    offset_grad[...] += col_sum(z)
    grad_branch = norm_back(gain[0:1, :] * z, n, rstd_in[...])
    grad_low = grad_branch.astype(BF16)
    out_bias_grad[...] += col_sum(grad_branch)
    out_grad[...] += dot(mixture[0], grad_low, 1, 0)
    grad_mixture = dot(out_weight[...], grad_low, 1, 1).astype(BF16)
    value_rows = jnp.transpose(joint[0, 2 * D :, :], (1, 0))
    blank = jnp.zeros((HEAD, AREA), BF16)

    def probs_grads(group):
        lanes = value_rows[:, group * 128 : (group + 1) * 128]
        found = []
        for head in range(4):
            at = group * 128 + head * HEAD
            parts = [blank] * 4
            parts[head] = grad_mixture[at : at + HEAD, :]
            found.append(dot(lanes, jnp.concatenate(parts, axis=0), 1, 0))
        return found

    ahead = probs_grads(0)
    for group in range(HEADS // 4):
        current = ahead
        if group + 1 < HEADS // 4:
            ahead = probs_grads(group + 1)
        raws = []
        for i in range(4):
            head = group * 4 + i
            weight = probs[0, head].astype(F32)
            weighted = weight * current[i]
            grad_scores = weighted - weight * (col_sum(weighted) / col_sum(weight))
            table_grad[head] += grad_scores
            raws.append((grad_scores * scale[0, head]).astype(BF16))
        for i in range(4):
            at = (group * 4 + i) * HEAD
            grads_f32[at : at + HEAD, :] = dot(joint[0, D + at : D + at + HEAD, :], raws[i], 1, 0)
            grads_f32[D + at : D + at + HEAD, :] = dot(joint[0, at : at + HEAD, :], raws[i], 1, 1)
            joint_grad[2 * D + at : 2 * D + at + HEAD, :] = dot(
                grad_mixture[at : at + HEAD, :], probs[0, group * 4 + i], 1, 1
            ).astype(BF16)

    def unit_back(rows, place):
        shaped = grads_f32[rows, :].reshape(HEADS, HEAD, AREA)
        unit = joint[0, rows, :].astype(F32).reshape(HEADS, HEAD, AREA)
        inner = jnp.sum(unit * shaped, axis=1, keepdims=True)
        shaped = shaped - unit * inner
        for head in range(HEADS):
            at = rows.start + head * HEAD
            joint_grad[at : at + HEAD, :] = (
                shaped[head] * inverse[0, place + head : place + head + 1, :]
            ).astype(BF16)
        return inner

    inner = unit_back(slice(0, D), 0)
    for head in range(HEADS):
        scale_grad[head : head + 1, :] += inner[head]
    unit_back(slice(D, 2 * D), HEADS)
    in_grad[...] += dot(win_t[0], joint_grad[...], 1, 1)
    windows[mine, :] = dot(joint_grad[...], in_weight[...], 0, 1)

    @pl.when(window == WINDOWS - 1)
    def _():
        def write_row(row, line):
            tokens_grad[row] = line + grad_first[row * SIDE : (row + 1) * SIDE, :]

        roll_to_image(windows, doubled, write_row, shift_row, shift_col)
        for block in range(3):
            packed[block * D : (block + 1) * D, :] = in_grad[
                :D, block * D : (block + 1) * D
            ].astype(BF16)
        packed[3 * D : 4 * D, :] = out_grad[...].astype(BF16)
        if packed.shape[0] > 4 * D:
            packed[4 * D :, :] = jnp.zeros_like(packed[4 * D :, :])
        in_bias_grad[...] = in_grad[D : D + 1, :]


def attend_back(
    shifts, scale, grad_first, n, rstd, joint, probs, mixture, win_t, inverse,
    in_weight, out_weight, gain, packed_rows,
):
    per_window = lambda *dims: pl.BlockSpec((1,) + dims, lambda w: (w,) + (0,) * len(dims))
    rows = lambda width: pl.BlockSpec((AREA, width), lambda w: (w, 0))
    return pl.pallas_call(
        attend_back_kernel,
        grid=(WINDOWS,),
        in_specs=[
            smem(),
            smem(),
            whole((TOKENS, D)),
            rows(D),
            rows(1),
            per_window(3 * D, AREA),
            per_window(HEADS, AREA, AREA),
            per_window(D, AREA),
            per_window(D + 16, AREA),
            per_window(2 * HEADS, AREA),
            whole((D, 3 * D)),
            whole((D, D)),
            whole((3, D)),
        ],
        out_specs=(
            whole((SIDE, SIDE, D)),
            whole((packed_rows, D)),
            whole((1, 3 * D)),
            whole((1, D)),
            whole((1, D)),
            whole((1, D)),
            whole((HEADS, AREA)),
            whole((HEADS, AREA, AREA)),
        ),
        out_shape=(
            full((SIDE, SIDE, D)),
            full((packed_rows, D), BF16),
            full((1, 3 * D)),
            full((1, D)),
            full((1, D)),
            full((1, D)),
            full((HEADS, AREA)),
            full((HEADS, AREA, AREA)),
        ),
        scratch_shapes=[
            pltpu.VMEM((SIDE, SIDE + WS, D), F32),
            pltpu.VMEM((TOKENS, D), F32),
            pltpu.VMEM((3 * D, AREA), BF16),
            pltpu.VMEM((2 * D, AREA), F32),
            pltpu.VMEM((D + 16, 3 * D), F32),
            pltpu.VMEM((D, D), F32),
        ],
        compiler_params=params(),
        name="attend_back",
    )(
        shifts, scale, grad_first, n, rstd, joint, probs, mixture, win_t, inverse,
        in_weight, out_weight, gain,
    )


SMALL = (
    ("in_bias", 1, 3 * D),
    ("out_bias", 1, D),
    ("up_bias", 1, FF),
    ("down_bias", 1, D),
    ("gain_first", 1, D),
    ("gain_rest", 2, D),
    ("offset_first", 1, D),
    ("offset_rest", 2, D),
    ("table_one", 3, UNITS),
    ("table_two", HEADS, UNITS),
    ("scale", HEADS, 128),
    ("router", 0, D),
)


def small_places(experts):
    places, at = {}, 0
    for name, rows, width in SMALL:
        rows = rows or experts
        places[name] = (at, rows, width)
        at += rows * (width // 128)
    return places, at


def put_small(ref, places, name, value):
    at, rows, width = places[name]
    for lane in range(0, width, 128):
        ref[at : at + rows, :] = value[:, lane : lane + 128]
        at += rows


def get_small(ref, places, name):
    at, rows, width = places[name]
    return jnp.concatenate(
        [ref[at + i * rows : at + (i + 1) * rows, :] for i in range(width // 128)], axis=1
    )


def table_back_kernel(
    places, table_grad, scale_rows, w1, b1, w2, in_bias, out_bias, up_bias, down_bias,
    gain_first, gain_rest, offset_first, offset_rest, router, small, values_grad,
):
    spread = spread_matrix(True)
    for head in range(HEADS):
        high, low = split(table_grad[head])
        spread_low = spread.astype(BF16)
        flat = dot(high, spread_low, 1, 1) + dot(low, spread_low, 1, 1)
        flat = jnp.concatenate([flat, jnp.zeros((AREA, TABLE - 384), F32)], axis=1)
        total = jnp.zeros((16, TABLE), F32)
        for key_row in range(WS):
            shift = EXTENT * key_row
            line = flat[key_row * WS : (key_row + 1) * WS, :]
            line = jnp.concatenate([line, jnp.zeros((16 - WS, TABLE), F32)], axis=0)
            total += pltpu.roll(line, shift, 1)
        total = pltpu.roll(total, 0, 1, stride=1, stride_axis=0)
        values_grad[head : head + 1, :] = col_sum(total)
    f_row, f_col = offsets_row((UNITS, TABLE), 1, -1.0)
    w1t = jnp.transpose(w1[...], (1, 0))
    b1t = jnp.transpose(row_of(b1), (1, 0))
    hidden, slope = gelu_pair(w1t[:, 0:1] * f_row + w1t[:, 1:2] * f_col + b1t[:, 0:1])
    chance = jax.nn.sigmoid(exact_dot(w2[...], hidden, 1, 0))
    grad_pre = values_grad[:HEADS, :] * (16.0 * chance * (1.0 - chance))
    small[...] = jnp.zeros_like(small)
    put_small(small, places, "table_two", exact_dot(grad_pre, hidden, 1, 1))
    grad_hidden = exact_dot(w2[...], grad_pre, 0, 0) * slope
    f_row, f_col = offsets_row((8, TABLE), 1, -1.0)
    kind = iota((8, TABLE), 0)
    factors = jnp.where(kind == 0, f_row, jnp.where(kind == 1, f_col, 1.0))
    put_small(small, places, "table_one", exact_dot(factors, grad_hidden, 1, 1)[:3, :])
    scales = jnp.sum(scale_rows[...], axis=1, keepdims=True)
    put_small(small, places, "scale", jnp.broadcast_to(scales, (HEADS, 128)))
    put_small(small, places, "in_bias", in_bias[...])
    put_small(small, places, "out_bias", out_bias[...])
    put_small(small, places, "up_bias", up_bias[...])
    put_small(small, places, "down_bias", down_bias[...])
    put_small(small, places, "gain_first", gain_first[...])
    put_small(small, places, "gain_rest", gain_rest[1:, :])
    put_small(small, places, "offset_first", offset_first[...])
    put_small(small, places, "offset_rest", offset_rest[1:, :])
    put_small(small, places, "router", router[...])


def table_back(small_rows, experts, *args):
    places, _ = small_places(experts)
    return pl.pallas_call(
        functools.partial(table_back_kernel, places),
        out_shape=full((small_rows, 128)),
        scratch_shapes=[pltpu.VMEM((16, TABLE), F32)],
        compiler_params=params(),
        name="table_back",
    )(*args)


def reduce_kernel(names, *refs):
    count = len(names)
    sources, outs, refs = refs[:count], refs[count : 2 * count], refs[2 * count :]
    sums = []
    for name, source, out in zip(names, sources, outs):
        levels = levels_of(name)
        depth = len(levels)
        held, lands, (send, recv) = refs[0], refs[1 : 1 + depth], refs[1 + depth : 3 + depth]
        refs = refs[3 + depth :]
        sums.append(Sum(source, held, out, lands, send, recv, levels).stages())
    greet(greeted(levels_of(("dp", "expert"))))
    for k in range(max(len(stages) for stages in sums)):
        for stages in sums:
            if k < len(stages):
                stages[k]()


def reduce_all(names, arrays, dp, experts):
    scratch = []
    for name, array in zip(names, arrays):
        counts = level_counts(name, dp, experts)
        scratch.append(pltpu.VMEM(array.shape, array.dtype))
        scratch += land_shapes(array.shape[0], array.shape[1], array.dtype, counts)
        scratch += sum_sems(counts)
    return pl.pallas_call(
        functools.partial(reduce_kernel, names),
        out_shape=tuple(full(array.shape, array.dtype) for array in arrays),
        scratch_shapes=scratch,
        compiler_params=params(collective_id=2, has_side_effects=True),
        name="reduce",
    )(*arrays)


def unpack_kernel(
    places, own, dense, last, small,
    in_grad, in_bias, scale, table_first, table_first_bias, table_second, out_grad, out_bias,
    up_grad, up_bias, down_grad, down_bias, router, own_up, own_up_bias, own_down, own_down_bias,
    gain, offset,
):
    for block in range(3):
        part = slice(block * D, (block + 1) * D)
        in_grad[:, part] = last[part, :].astype(F32)
    out_grad[...] = last[3 * D : 4 * D, :].astype(F32)
    for source, up, down in ((dense, up_grad, down_grad), (own, own_up, own_down)):
        for block in range(FF // D):
            part = slice(block * D, (block + 1) * D)
            up[:, part] = source[part, :].astype(F32)
            down[part, :] = source[FF + block * D : FF + (block + 1) * D, :].astype(F32)
    tail = own[2 * FF : 2 * FF + 16, :].astype(F32)
    for block in range(FF // D):
        own_up_bias[:, block * D : (block + 1) * D] = tail[block : block + 1, :]
    own_down_bias[...] = tail[FF // D : FF // D + 1, :]
    get = functools.partial(get_small, small, places)
    row = get("in_bias")
    in_bias[0:1, :] = row[:, :D]
    in_bias[1:2, :] = row[:, 2 * D :]
    scale[...] = get("scale")[:, 0:1]
    one = get("table_one")
    table_first[...] = one[0:2, :]
    table_first_bias[...] = one[2:3, :].reshape(UNITS)
    table_second[...] = get("table_two")
    out_bias[...] = get("out_bias").reshape(D)
    up_bias[...] = get("up_bias").reshape(FF)
    down_bias[...] = get("down_bias").reshape(D)
    router[...] = get("router")
    gain[0:1, :] = get("gain_first")
    gain[1:3, :] = get("gain_rest")
    offset[0:1, :] = get("offset_first")
    offset[1:3, :] = get("offset_rest")


def unpack(own, dense, last, small, experts):
    places, _ = small_places(experts)
    return pl.pallas_call(
        functools.partial(unpack_kernel, places),
        out_shape=(
            full((D, 3 * D)),
            full((2, D)),
            full((HEADS, 1)),
            full((2, UNITS)),
            full((UNITS,)),
            full((HEADS, UNITS)),
            full((D, D)),
            full((D,)),
            full((D, FF)),
            full((FF,)),
            full((FF, D)),
            full((D,)),
            full((experts, D)),
            full((D, FF)),
            full((1, FF)),
            full((FF, D)),
            full((1, D)),
            full((3, D)),
            full((3, D)),
        ),
        compiler_params=params(),
        name="unpack",
    )(own, dense, last, small)


def per_device(
    tokens, shifts, routes, cotangent, in_weight, in_bias, logit_scale,
    bias_net_first_weight, bias_net_first_bias, bias_net_second_weight,
    out_weight, out_bias, up_weight, up_bias, down_weight, down_bias, router_weight,
    expert_up, expert_up_bias, expert_down, expert_down_bias, norm_gain, norm_bias,
):
    experts = router_weight.shape[1]
    dp = lax.axis_size("dp")
    group = lax.axis_size("expert")
    capacity = (5 * TOKENS + 4 * experts - 1) // (4 * experts)
    slots = -(-capacity // 16) * 16
    own, both = ("dp",), ("dp", "expert")
    own_counts, both_counts = level_counts(own, dp, group), level_counts(both, dp, group)
    own_rows = padded_rows(2 * FF + 16, own_counts, 16)
    dense_rows = padded_rows(2 * FF, both_counts, 16)
    last_rows = padded_rows(4 * D, both_counts, 16)
    small_rows = padded_rows(small_places(experts)[1], both_counts, 8)

    picture = tokens.reshape(SIDE, SIDE, D)
    cot = cotangent.reshape(SIDE, SIDE, D)
    router_t = router_weight.T
    second_t = bias_net_second_weight.T

    slot_col, slot_row, cot_slots, table, scale = prep(
        routes.reshape(1, TOKENS), cot, bias_net_first_weight, bias_net_first_bias, second_t,
        logit_scale, experts, capacity, slots,
    )
    cot_arrived, normed, n_zero, rstd_zero, joint, probs, mixture, win_t, inverse = attend(
        cot_slots, shifts, scale, picture, in_weight, in_bias, table,
        out_weight, out_bias, norm_gain, norm_bias,
    )
    first_low, active, slope, n_one, rstd_one, second, buffer = forward(
        shifts, picture, normed, up_weight, up_bias, down_weight,
        down_bias, norm_gain, norm_bias, slot_row, experts, slots,
    )
    returned, grad_returned, own_packed = run_experts(
        buffer, cot_arrived, router_t, expert_up[0], expert_up_bias, expert_down[0],
        expert_down_bias, norm_gain, own_rows,
    )
    (
        result, grad_first, dense_packed, up_bias_grad, down_bias_grad, router_grad,
        gain_grad, offset_grad,
    ) = backward(
        second, cot, slot_col, returned.reshape(-1, D), grad_returned.reshape(-1, D),
        router_t, first_low, active, slope, n_one, rstd_one, up_weight, down_weight,
        norm_gain, norm_bias, dense_rows,
    )
    (
        tokens_grad, last_packed, in_bias_grad, out_bias_grad, gain_zero, offset_zero, scale_rows,
        table_grad,
    ) = attend_back(
        shifts, scale, grad_first, n_zero, rstd_zero, joint, probs, mixture, win_t, inverse,
        in_weight, out_weight, norm_gain, last_rows,
    )
    small = table_back(
        small_rows, experts, table_grad, scale_rows, bias_net_first_weight, bias_net_first_bias,
        second_t, in_bias_grad, out_bias_grad, up_bias_grad, down_bias_grad,
        gain_zero, gain_grad, offset_zero, offset_grad, router_grad,
    )
    sums = reduce_all(
        (own, both, both, both), (own_packed, dense_packed, last_packed, small), dp, group
    )
    (
        in_weight_grad, in_bias_grad, scale_grad, table_one, table_bias, table_two, out_grad,
        out_bias_grad, up_grad, up_bias_grad, down_grad, down_bias_grad, router_grad,
        own_up, own_up_bias, own_down, own_down_bias, gain_grad, offset_grad,
    ) = unpack(*sums, experts)
    return (
        result.reshape(tokens.shape),
        tokens_grad.reshape(tokens.shape),
        in_weight_grad,
        in_bias_grad,
        scale_grad.reshape(HEADS),
        table_one,
        table_bias,
        table_two.T,
        out_grad,
        out_bias_grad,
        up_grad,
        up_bias_grad,
        down_grad,
        down_bias_grad,
        router_grad.T,
        own_up[None],
        own_up_bias,
        own_down[None],
        own_down_bias,
        gain_grad,
        offset_grad,
    )


def solution(mesh):
    split_all = P(("dp", "expert"))
    placed = (split_all,) * 4 + (P(),) * 13 + (P("expert"),) * 4 + (P(),) * 2
    return jax.shard_map(
        per_device,
        mesh=mesh,
        in_specs=placed,
        out_specs=(split_all,) * 2 + (P(),) * 13 + (P("expert"),) * 4 + (P(),) * 2,
        check_vma=False,
    )
```

```python
import functools

import jax
import jax.numpy as jnp
from jax import lax
from jax.experimental import pallas as pl
from jax.experimental.pallas import tpu as pltpu
from jax.sharding import PartitionSpec as P

D = 384
HEADS = 12
HEAD = D // HEADS
WS = 12
SIDE = 36
AREA = WS * WS
ACROSS = SIDE // WS
WINDOWS = ACROSS * ACROSS
TOKENS = SIDE * SIDE
FF = 1536
EXTENT = 2 * WS - 1
UNITS = 512
TABLE = 640
ROWS = 432
CHUNK = 256
F32 = jnp.float32
BF16 = jnp.bfloat16
I32 = jnp.int32
VMEM_LIMIT = 60 * 1024 * 1024


def dot(left, right, left_dim, right_dim):
    return lax.dot_general(
        left, right, (((left_dim,), (right_dim,)), ((), ())), preferred_element_type=F32
    )


def exact_dot(left, right, left_dim, right_dim):
    return lax.dot_general(
        left,
        right,
        (((left_dim,), (right_dim,)), ((), ())),
        preferred_element_type=F32,
        precision=lax.Precision.HIGHEST,
    )


def split(values):
    high = values.astype(BF16)
    return high, (values - high.astype(F32)).astype(BF16)


def iota(shape, dim):
    return lax.broadcasted_iota(I32, shape, dim)


def gelu_pair(values):
    size = jnp.abs(values)
    t = 1.0 / (1.0 + 0.2316419 * size)
    bell = jnp.exp(-0.5 * values * values) * 0.3989422804014327
    series = t * (
        0.319381530
        + t * (-0.356563782 + t * (1.781477937 + t * (-1.821255978 + t * 1.330274429)))
    )
    tail = series * bell
    phi = jnp.where(values >= 0.0, 1.0 - tail, tail)
    return values * phi, phi + values * bell


def norm_parts(values):
    centered = values - jnp.mean(values, axis=-1, keepdims=True)
    rstd = lax.rsqrt(jnp.mean(centered * centered, axis=-1, keepdims=True) + 1e-05)
    return centered * rstd, rstd


def norm_back(grad_n, n, rstd):
    return rstd * (
        grad_n
        - jnp.mean(grad_n, axis=-1, keepdims=True)
        - n * jnp.mean(grad_n * n, axis=-1, keepdims=True)
    )


def row_of(ref):
    return ref[...].reshape(1, ref.shape[0])


def col_sum(values):
    return jnp.sum(values, axis=0, keepdims=True)


def div_ws(values):
    return (values * 171) >> 11


def full(shape, dtype=F32):
    return jax.ShapeDtypeStruct(shape, dtype)


def whole(shape):
    return pl.BlockSpec(shape, lambda *_: (0,) * len(shape))


def smem():
    return pl.BlockSpec(memory_space=pltpu.SMEM)


def params(**more):
    return pltpu.CompilerParams(vmem_limit_bytes=VMEM_LIMIT, **more)


def partner(me, step, count):
    side = 1
    while side * side < count:
        side *= 2
    if side * side != count:
        return lax.rem(me + step, count)
    row = lax.rem(lax.div(me, side) + step // side, side)
    col = lax.rem(lax.rem(me, side) + step % side, side)
    return row * side + col


def opposite(step, count):
    side = 1
    while side * side < count:
        side *= 2
    if side * side != count:
        return (count - step) % count
    return ((side - step // side) % side) * side + (side - step % side) % side


def greet(devices):
    barrier = pltpu.get_barrier_semaphore()
    for device in devices:
        pl.semaphore_signal(barrier, inc=1, device_id=device, device_id_type=pl.DeviceIdType.MESH)
    pl.semaphore_wait(barrier, len(devices))


class Level:
    def __init__(self, count, index, device):
        self.count, self.index, self.device = count, index, device

    def others(self):
        return [lax.rem(self.index + step, self.count) for step in range(1, self.count)]

    def devices(self):
        return [self.device(to) for to in self.others()]


def core_level():
    place = lax.div(lax.axis_index("dp"), 2)
    return Level(2, lax.rem(lax.axis_index("dp"), 2), lambda j: {"dp": place * 2 + j})


def plane_level():
    return Level(lax.axis_size("expert"), lax.axis_index("expert"), lambda j: {"expert": j})


def depth_level():
    core = lax.rem(lax.axis_index("dp"), 2)
    place = lax.div(lax.axis_index("dp"), 2)
    return Level(lax.axis_size("dp") // 2, place, lambda j: {"dp": j * 2 + core})


def padded_rows(rows, counts, tile):
    unit = tile
    for count in counts:
        unit *= count
    return -(-rows // unit) * unit


def pair_of_sems(count):
    return [pltpu.SemaphoreType.DMA((count,)), pltpu.SemaphoreType.DMA((count,))]


def scatter(level, source, land, out, sems, begin):
    rows = source.shape[0] // level.count
    tile = 16 if source.dtype == BF16 else 8
    for step, to in enumerate(level.others(), 1):
        copy = pltpu.make_async_remote_copy(
            src_ref=source.at[pl.ds(pl.multiple_of(to * rows, tile), rows)],
            dst_ref=land.at[step - 1],
            send_sem=sems[0].at[step],
            recv_sem=sems[1].at[step],
            device_id=level.device(to),
            device_id_type=pl.DeviceIdType.MESH,
        )
        copy.start() if begin else copy.wait()
    if begin:
        return
    mine = level.index * rows
    chunk = tile
    while rows % (chunk * 2) == 0 and chunk < 128:
        chunk *= 2

    def add(i, carry):
        here = pl.ds(pl.multiple_of(i * chunk, tile), chunk)
        total = source[pl.ds(pl.multiple_of(mine + i * chunk, tile), chunk), :].astype(F32)
        for step in range(1, level.count):
            total = total + land[step - 1, here, :].astype(F32)
        out[here, :] = total.astype(out.dtype)
        return carry

    lax.fori_loop(0, rows // chunk, add, 0)


class Gather:
    def __init__(self, levels, piece, result, sems, local):
        self.levels, self.piece, self.result, self.sems = levels, piece, result, sems
        rows, start = result.shape[0], 0
        self.regions = []
        for level in levels:
            rows //= level.count
            start = start + level.index * rows
            self.regions.append((start, rows))
        self.keep = pltpu.make_async_copy(piece, self.region(len(levels) - 1), local)

    def region(self, at):
        start, rows = self.regions[at]
        return self.result.at[pl.ds(pl.multiple_of(start, 8), rows)]

    def move(self, at, begin):
        level, last = self.levels[at], at == len(self.levels) - 1
        mine = self.region(at)
        for step, to in enumerate(level.others(), 1):
            copy = pltpu.make_async_remote_copy(
                src_ref=self.piece if last else mine,
                dst_ref=mine,
                send_sem=self.sems[2 * at].at[step],
                recv_sem=self.sems[2 * at + 1].at[step],
                device_id=level.device(to),
                device_id_type=pl.DeviceIdType.MESH,
            )
            copy.start() if begin else copy.wait()
        if last:
            self.keep.start() if begin else self.keep.wait()


def sems_of(levels):
    return [sem for count in levels for sem in pair_of_sems(count)]


def offsets_row(shape, dim, sign):
    place = iota(shape, dim)
    row = jnp.floor((place.astype(F32) + 0.5) * (1.0 / EXTENT)).astype(I32)
    col = place - row * EXTENT

    def logged(step):
        e = sign * (step - (WS - 1)).astype(F32) * (8.0 / (WS - 1))
        size = jnp.log2(jnp.abs(e) + 1.0) * (1.0 / 3.0)
        return jnp.where(e < 0.0, -size, size)

    return logged(row), logged(col)


def spread_matrix(mirrored):
    token = iota((384, AREA), 1)
    row = div_ws(token)
    lin = row * EXTENT + (token - row * WS)
    if mirrored:
        lin = (WS - 1) * EXTENT + (WS - 1) - lin
    return (iota((384, AREA), 0) == lin).astype(F32)


def prep_kernel(
    capacity, routes, cot, w1, b1, w2, ls, slot_col, slot_row, zbuf, table, scale, flat, u_ref, route_col
):
    slots = zbuf.shape[1]
    experts = zbuf.shape[0]
    route_col[...] = jnp.transpose(
        jnp.broadcast_to(routes[...].astype(F32), (128, TOKENS)), (1, 0)
    )
    before = (iota((AREA, AREA), 1) < iota((AREA, AREA), 0)).astype(BF16)
    carry = jnp.zeros((1, 128), F32)
    for block in range(TOKENS // AREA):
        rows = pl.ds(block * AREA, AREA)
        route = route_col[rows, 0:1]
        onehot = (route == iota((AREA, 128), 1).astype(F32)).astype(F32)
        ahead = dot(before, onehot.astype(BF16), 1, 0) + carry
        position = jnp.sum(ahead * onehot, axis=1, keepdims=True)
        carry = carry + col_sum(onehot)
        slot = route * slots + position
        slot_col[rows, :] = jnp.where(position < capacity, slot, -1.0).astype(I32)
    slot_row[...] = jnp.transpose(
        jnp.broadcast_to(slot_col[...].astype(F32), (TOKENS, 128)), (1, 0)
    )[0:1, :].astype(I32)

    for row in range(SIDE):
        flat[row * SIDE : (row + 1) * SIDE, :] = cot[row].astype(F32)
    low = flat[...].astype(BF16)
    for expert in range(experts):
        pick = (iota((slots, TOKENS), 0) + expert * slots == slot_row[...]).astype(BF16)
        zbuf[expert] = dot(pick, low, 1, 0).astype(BF16)

    scale[...] = jnp.exp(row_of(ls))
    f_row, f_col = offsets_row((UNITS, TABLE), 1, 1.0)
    w1t = jnp.transpose(w1[...], (1, 0))
    b1t = jnp.transpose(row_of(b1), (1, 0))
    hidden, _ = gelu_pair(w1t[:, 0:1] * f_row + w1t[:, 1:2] * f_col + b1t[:, 0:1])
    values = 16.0 * jax.nn.sigmoid(exact_dot(w2[...], hidden, 1, 0))
    spread = spread_matrix(False).astype(BF16)
    for head in range(HEADS):
        line = jnp.broadcast_to(values[head : head + 1, :], (16, TABLE))
        line = pltpu.roll(line, 0, 1, stride=1, stride_axis=0)
        for key_row in range(WS):
            shift = (EXTENT * key_row - (WS - 1) * EXTENT - (WS - 1)) % TABLE
            rolled = pltpu.roll(line, shift, 1)
            u_ref[key_row * WS : (key_row + 1) * WS, :] = rolled[:WS, :384]
        high, low_part = split(u_ref[...])
        table[head] = dot(high, spread, 1, 0) + dot(low_part, spread, 1, 0)


def prep(routes, cotangent, w1, b1, w2, ls, experts, capacity, slots):
    return pl.pallas_call(
        functools.partial(prep_kernel, capacity),
        out_shape=(
            full((TOKENS, 1), I32),
            full((1, TOKENS), I32),
            full((experts, slots, D), BF16),
            full((HEADS, AREA, AREA)),
            full((1, HEADS)),
        ),
        scratch_shapes=[
            pltpu.VMEM((TOKENS, D), F32),
            pltpu.VMEM((AREA, 384), F32),
            pltpu.VMEM((TOKENS, 128), F32),
        ],
        compiler_params=params(),
        name="prep",
    )(routes, cotangent, w1, b1, w2, ls)


def window_labels(window, shift_row, shift_col):
    def labels(shape, dim):
        token = iota(shape, dim)
        row = div_ws(token)
        col = token - row * WS + lax.rem(window, ACROSS) * WS
        row = row + lax.div(window, ACROSS) * WS

        def region(place, shift):
            last = jnp.where(place < SIDE - shift, 1, 2)
            return jnp.where(place < SIDE - WS, 0, last)

        return region(row, shift_row) * 3 + region(col, shift_col)

    return labels((AREA, 1), 0), labels((1, AREA), 1)


def roll_to_windows(read_row, doubled, windows, shift_row, shift_col):
    for row in range(SIDE):
        line = read_row(row)
        doubled[row, :SIDE, :] = line
        doubled[row, SIDE:, :] = line[:WS, :]
    for row in range(SIDE):
        source = row + shift_row
        source = jnp.where(source >= SIDE, source - SIDE, source)
        line = pltpu.roll(doubled[source], SIDE + WS - shift_col, 0)
        for across in range(ACROSS):
            start = ((row // WS) * ACROSS + across) * AREA + (row % WS) * WS
            windows[start : start + WS, :] = line[across * WS : (across + 1) * WS, :]


def roll_to_image(windows, doubled, write_row, shift_row, shift_col):
    for row in range(SIDE):
        for across in range(ACROSS):
            start = ((row // WS) * ACROSS + across) * AREA + (row % WS) * WS
            line = windows[start : start + WS, :]
            doubled[row, across * WS : (across + 1) * WS, :] = line
            if across == ACROSS - 1:
                doubled[row, SIDE:, :] = line
    for row in range(SIDE):
        source = row - shift_row
        source = jnp.where(source < 0, source + SIDE, source)
        write_row(row, pltpu.roll(doubled[source], shift_col, 0)[:SIDE, :])


def attend_kernel(
    cot_slots, shifts, scale, tokens, in_weight, in_bias, table, out_weight, out_bias, gain, offset,
    cot_arrived, normed, n_out, rstd_out, joint, probs, mixture, win_t, inverse,
    doubled, windows, in_weight_t, bias_col, joined, send, recv, local,
):
    window = pl.program_id(0)
    shift_row, shift_col = shifts[0, 0], shifts[0, 1]
    me = lax.axis_index("expert")
    count = cot_slots.shape[0]

    def move(step):
        to = partner(me, step, count)
        return pltpu.make_async_remote_copy(
            src_ref=cot_slots.at[to],
            dst_ref=cot_arrived.at[me],
            send_sem=send.at[step],
            recv_sem=recv.at[step],
            device_id={"expert": to},
            device_id_type=pl.DeviceIdType.MESH,
        )

    keep = pltpu.make_async_copy(cot_slots.at[me], cot_arrived.at[me], local)

    @pl.when(window == 0)
    def _():
        greet([{"expert": partner(me, step, count)} for step in range(1, count)])
        for step in range(1, count):
            move(step).start()
        keep.start()
        roll_to_windows(
            lambda row: tokens[row].astype(F32), doubled, windows, shift_row, shift_col
        )
        in_weight_t[...] = jnp.transpose(in_weight[...], (1, 0))
        bias_col[:, 0:2] = jnp.transpose(in_bias[...], (1, 0))

    mine = windows[pl.ds(pl.multiple_of(window * AREA, 16), AREA), :].astype(BF16)
    win_t[0, :D, :] = jnp.transpose(mine, (1, 0))
    win_t[0, D:, :] = (iota((16, AREA), 0) == 0).astype(BF16)
    label_keys, label_queries = window_labels(window, shift_row, shift_col)
    mask = jnp.where(label_keys == label_queries, 0.0, -100.0)
    joined[...] = dot(in_weight_t[...], mine, 1, 1)

    def unit(rows, bias, place):
        shaped = (joined[rows, :] + bias).reshape(HEADS, HEAD, AREA)
        inner = lax.rsqrt(1.0 + jnp.sum(shaped * shaped, axis=1, keepdims=True))
        for head in range(HEADS):
            inverse[0, place + head : place + head + 1, :] = inner[head]
        return (shaped * inner).reshape(D, AREA).astype(BF16)

    queries = unit(slice(0, D), bias_col[:, 0:1], 0)
    keys = unit(slice(D, 2 * D), 0.0, HEADS)
    values = (joined[2 * D :, :] + bias_col[:, 1:2]).astype(BF16)
    joint[0, :D, :] = queries
    joint[0, D : 2 * D, :] = keys
    joint[0, 2 * D :, :] = values
    key_rows = jnp.transpose(keys, (1, 0))
    blank = jnp.zeros((HEAD, AREA), BF16)

    def scores_of(group):
        lanes = key_rows[:, group * 128 : (group + 1) * 128]
        found = []
        for head in range(4):
            at = group * 128 + head * HEAD
            parts = [blank] * 4
            parts[head] = queries[at : at + HEAD, :]
            found.append(dot(lanes, jnp.concatenate(parts, axis=0), 1, 0))
        return found

    ahead = scores_of(0)
    for group in range(HEADS // 4):
        current = ahead
        if group + 1 < HEADS // 4:
            ahead = scores_of(group + 1)
        lows = []
        for i in range(4):
            head = group * 4 + i
            scores = current[i] * scale[0, head] + (table[head] + mask)
            exponent = jnp.exp(scores - jnp.max(scores, axis=0, keepdims=True))
            low = (exponent * (1.0 / col_sum(exponent))).astype(BF16)
            probs[0, head] = low
            lows.append(low)
        for i in range(4):
            at = (group * 4 + i) * HEAD
            mixture[0, at : at + HEAD, :] = dot(values[at : at + HEAD, :], lows[i], 1, 0).astype(BF16)
    branch = dot(mixture[0], out_weight[...], 0, 0) + row_of(out_bias)
    n, rstd = norm_parts(branch)
    normed[...] = n * gain[0:1, :] + offset[0:1, :]
    n_out[...] = n.astype(BF16)
    rstd_out[...] = rstd

    @pl.when(window == WINDOWS - 1)
    def _():
        for step in range(1, count):
            move(step).wait()
        keep.wait()


def attend(
    cot_slots, shifts, scale, tokens, in_weight, in_bias, table, out_weight, out_bias, gain, offset
):
    per_window = lambda *dims: pl.BlockSpec((1,) + dims, lambda w: (w,) + (0,) * len(dims))
    rows = lambda width: pl.BlockSpec((AREA, width), lambda w: (w, 0))
    return pl.pallas_call(
        attend_kernel,
        grid=(WINDOWS,),
        in_specs=[
            pl.BlockSpec(memory_space=pl.ANY),
            smem(),
            smem(),
            whole((SIDE, SIDE, D)),
            whole((D, 3 * D)),
            whole((2, D)),
            whole((HEADS, AREA, AREA)),
            whole((D, D)),
            whole((D,)),
            whole((3, D)),
            whole((3, D)),
        ],
        out_specs=(
            pl.BlockSpec(memory_space=pl.ANY),
            rows(D),
            rows(D),
            rows(1),
            per_window(3 * D, AREA),
            per_window(HEADS, AREA, AREA),
            per_window(D, AREA),
            per_window(D + 16, AREA),
            per_window(2 * HEADS, AREA),
        ),
        out_shape=(
            full(cot_slots.shape, BF16),
            full((TOKENS, D)),
            full((TOKENS, D), BF16),
            full((TOKENS, 1)),
            full((WINDOWS, 3 * D, AREA), BF16),
            full((WINDOWS, HEADS, AREA, AREA), BF16),
            full((WINDOWS, D, AREA), BF16),
            full((WINDOWS, D + 16, AREA), BF16),
            full((WINDOWS, 2 * HEADS, AREA)),
        ),
        scratch_shapes=[
            pltpu.VMEM((SIDE, SIDE + WS, D), F32),
            pltpu.VMEM((TOKENS, D), F32),
            pltpu.VMEM((3 * D, D), BF16),
            pltpu.VMEM((D, 128), F32),
            pltpu.VMEM((3 * D, AREA), F32),
            pltpu.SemaphoreType.DMA((cot_slots.shape[0],)),
            pltpu.SemaphoreType.DMA((cot_slots.shape[0],)),
            pltpu.SemaphoreType.DMA(()),
        ],
        compiler_params=params(collective_id=0, has_side_effects=True),
        name="attend",
    )(cot_slots, shifts, scale, tokens, in_weight, in_bias, table, out_weight, out_bias, gain, offset)


def forward_kernel(
    shifts, tokens, normed, up, up_bias, down, down_bias, gain, offset, slot_row,
    first_low, active, slope, n_out, rstd_out, second, buffer,
    doubled, image, second_low,
):
    step = pl.program_id(0)

    @pl.when(step == 0)
    def _():
        def write_row(row, line):
            image[row * SIDE : (row + 1) * SIDE, :] = line + tokens[row].astype(F32)

        roll_to_image(normed, doubled, write_row, shifts[0, 0], shifts[0, 1])

    rows = pl.ds(pl.multiple_of(step * ROWS, 16), ROWS)
    first = image[rows, :]
    low = first.astype(BF16)
    first_low[...] = low
    up_row = row_of(up_bias)
    branch = jnp.broadcast_to(row_of(down_bias), (ROWS, D))
    for at in range(0, FF, CHUNK):
        hidden = dot(low, up[:, at : at + CHUNK], 1, 0) + up_row[:, at : at + CHUNK]
        activated, derivative = gelu_pair(hidden)
        activated = activated.astype(BF16)
        active[:, at : at + CHUNK] = activated
        slope[:, at : at + CHUNK] = derivative.astype(BF16)
        branch += dot(activated, down[at : at + CHUNK, :], 1, 0)
    n, rstd = norm_parts(branch)
    n_out[...] = n.astype(BF16)
    rstd_out[...] = rstd
    result = first + n * gain[1:2, :] + offset[1:2, :]
    second[...] = result
    second_low[rows, :] = result.astype(BF16)

    @pl.when(step == TOKENS // ROWS - 1)
    def _():
        slots = buffer.shape[1]
        for expert in range(buffer.shape[0]):
            pick = (iota((slots, TOKENS), 0) + expert * slots == slot_row[...]).astype(BF16)
            buffer[expert] = dot(pick, second_low[...], 1, 0).astype(BF16)


def forward(
    shifts, tokens, normed, up, up_bias, down, down_bias, gain, offset, slot_row, experts, slots
):
    rows = lambda width: pl.BlockSpec((ROWS, width), lambda i: (i, 0))
    return pl.pallas_call(
        forward_kernel,
        grid=(TOKENS // ROWS,),
        in_specs=[
            smem(),
            whole((SIDE, SIDE, D)),
            whole((TOKENS, D)),
            whole((D, FF)),
            whole((FF,)),
            whole((FF, D)),
            whole((D,)),
            whole((3, D)),
            whole((3, D)),
            whole((1, TOKENS)),
        ],
        out_specs=(
            rows(D),
            rows(FF),
            rows(FF),
            rows(D),
            rows(1),
            rows(D),
            whole((experts, slots, D)),
        ),
        out_shape=(
            full((TOKENS, D), BF16),
            full((TOKENS, FF), BF16),
            full((TOKENS, FF), BF16),
            full((TOKENS, D), BF16),
            full((TOKENS, 1)),
            full((TOKENS, D)),
            full((experts, slots, D), BF16),
        ),
        scratch_shapes=[
            pltpu.VMEM((SIDE, SIDE + WS, D), F32),
            pltpu.VMEM((TOKENS, D), F32),
            pltpu.VMEM((TOKENS, D), BF16),
        ],
        compiler_params=params(),
        name="forward",
    )(shifts, tokens, normed, up, up_bias, down, down_bias, gain, offset, slot_row)


def expert_kernel(
    buffer, cot, router, up, up_bias, down, down_bias, gain,
    out, grad_in, half,
    arrived, outs, grads, active, slope, up_grad, down_grad_t, up_bias_grad, down_bias_grad,
    packed, land, send, recv, *sum_sems,
):
    core = core_level()
    me = lax.axis_index("expert")
    count, slots, _ = buffer.shape
    others = range(1, count)

    def move(kind, step, source, target, to):
        return pltpu.make_async_remote_copy(
            src_ref=source,
            dst_ref=target,
            send_sem=send.at[kind, step],
            recv_sem=recv.at[kind, step],
            device_id={"expert": to},
            device_id_type=pl.DeviceIdType.MESH,
        )

    greet([{"expert": partner(me, step, count)} for step in others] + core.devices())
    for step in others:
        to = partner(me, step, count)
        move(0, step, buffer.at[to], arrived.at[step], to).start()
    arrived[0] = buffer[me]
    for ref in (up_grad, up_bias_grad, down_grad_t, down_bias_grad):
        ref[...] = jnp.zeros_like(ref)
    router_high, router_low = split(router[...])

    def work(step, carry):
        if count == 4:
            owner = lax.rem(lax.div(me, 2) + lax.div(step, 2), 2) * 2
            owner = owner + lax.rem(lax.rem(me, 2) + lax.rem(step, 2), 2)
        else:
            side = 1
            while side * side < count:
                side *= 2
            if side * side == count:
                owner = lax.rem(lax.div(me, side) + side - lax.div(step, side), side) * side
                owner = owner + lax.rem(lax.rem(me, side) + side - lax.rem(step, side), side)
            else:
                owner = lax.rem(me + count - step, count)

        @pl.when(step > 0)
        def _():
            move(0, step, buffer.at[owner], arrived.at[step], owner).wait_recv()

        features = arrived[step]
        logits = dot(features, router_high, 1, 1) + dot(features, router_low, 1, 1)
        chances = jnp.exp(logits - jnp.max(logits, axis=1, keepdims=True))
        own = jnp.where(iota(chances.shape, 1) == me, chances, 0.0)
        gate = jnp.sum(own, axis=1, keepdims=True) / jnp.sum(chances, axis=1, keepdims=True)

        output = jnp.zeros((slots, D), F32)
        for at in range(0, FF, CHUNK):
            hidden = dot(features, up[:, at : at + CHUNK], 1, 0) + up_bias[:, at : at + CHUNK]
            activated, derivative = gelu_pair(hidden)
            activated = activated.astype(BF16)
            active[:, at : at + CHUNK] = activated
            slope[:, at : at + CHUNK] = derivative
            output += dot(activated, down[at : at + CHUNK, :], 1, 0)
        output = (output + down_bias[...]).astype(BF16)
        outs[step] = output

        @pl.when(step > 0)
        def _():
            move(1, step, outs.at[step], out.at[me], owner).start()

        n, rstd = norm_parts(gate * output.astype(F32))
        grad_output = gate * norm_back(gain[2:3, :] * cot[owner].astype(F32), n, rstd)
        grad_low = grad_output.astype(BF16)
        down_bias_grad[...] += col_sum(grad_low.astype(F32))
        grad_low_t = jnp.transpose(grad_low, (1, 0))
        features_t = jnp.transpose(features, (1, 0))
        grad_features = jnp.zeros((slots, D), F32)
        for at in range(0, FF, CHUNK):
            part = slice(at, at + CHUNK)
            grad_hidden = dot(grad_low, down[part, :], 1, 1) * slope[:, part]
            grad_hidden_low = grad_hidden.astype(BF16)
            up_bias_grad[:, part] += col_sum(grad_hidden)
            down_grad_t[:, part] += dot(grad_low_t, active[:, part], 1, 0)
            up_grad[:, part] += dot(features_t, grad_hidden_low, 1, 0)
            grad_features += dot(grad_hidden_low, up[:, part], 1, 1)
        grads[step] = grad_features.astype(BF16)

        @pl.when(step > 0)
        def _():
            move(2, step, grads.at[step], grad_in.at[me], owner).start()

        return carry

    lax.fori_loop(0, count, work, 0)
    out[me] = outs[0]
    grad_in[me] = grads[0]
    pack_pair(packed, up_grad, down_grad_t)
    packed[2 * FF :, :] = jnp.zeros_like(packed[2 * FF :, :])
    tail = jnp.concatenate(
        [up_bias_grad[:, at : at + D] for at in range(0, FF, D)]
        + [down_bias_grad[...], jnp.zeros((11, D), F32)],
        axis=0,
    )
    packed[2 * FF : 2 * FF + 16, :] = tail.astype(BF16)
    scatter(core, packed, land, half, sum_sems, True)
    for step in others:
        to = partner(me, step, count)
        move(0, step, buffer.at[to], arrived.at[step], to).wait_send()
        for kind, source, target in ((1, outs, out), (2, grads, grad_in)):
            move(kind, step, source.at[step], target.at[me], to).wait()
    scatter(core, packed, land, half, sum_sems, False)


def pack_pair(packed, up_grad, down_grad_t):
    for block in range(FF // D):
        part = slice(block * D, (block + 1) * D)
        packed[part, :] = up_grad[:, part].astype(BF16)
        packed[FF + block * D : FF + (block + 1) * D, :] = jnp.transpose(
            down_grad_t[:, part].astype(BF16), (1, 0)
        )


def run_experts(buffer, cot, router, up, up_bias, down, down_bias, gain, packed_rows):
    count, slots, _ = buffer.shape
    blocks = (count, slots, D)
    return pl.pallas_call(
        expert_kernel,
        out_shape=(full(blocks, BF16), full(blocks, BF16), full((packed_rows // 2, D), BF16)),
        scratch_shapes=[
            pltpu.VMEM(blocks, BF16),
            pltpu.VMEM(blocks, BF16),
            pltpu.VMEM(blocks, BF16),
            pltpu.VMEM((slots, FF), BF16),
            pltpu.VMEM((slots, FF), F32),
            pltpu.VMEM((D, FF), F32),
            pltpu.VMEM((D, FF), F32),
            pltpu.VMEM((1, FF), F32),
            pltpu.VMEM((1, D), F32),
            pltpu.VMEM((packed_rows, D), BF16),
            pltpu.VMEM((1, packed_rows // 2, D), BF16),
            pltpu.SemaphoreType.DMA((3, count)),
            pltpu.SemaphoreType.DMA((3, count)),
            *pair_of_sems(2),
        ],
        compiler_params=params(collective_id=1, has_side_effects=True),
        name="experts",
    )(buffer, cot, router, up, up_bias, down, down_bias, gain)


def backward_kernel(
    second, cot, slot_col, outputs, grads, router, first_low, active, slope, n_in, rstd_in,
    up, down, gain, offset, half,
    result, grad_first, packed, up_bias_grad, down_bias_grad, router_grad,
    gain_grad, offset_grad, piece,
    flat, up_grad, down_grad_t, *sum_refs,
):
    step = pl.program_id(0)
    depth = depth_level()

    if depth.count > 1:
        land, *sum_sems = sum_refs

        @pl.when(step == 0)
        def _():
            greet(depth.devices())
            scatter(depth, half, land, piece, sum_sems, True)

    @pl.when(step == 0)
    def _():
        for ref in (
            up_grad, up_bias_grad, down_grad_t, down_bias_grad, router_grad, gain_grad, offset_grad
        ):
            ref[...] = jnp.zeros_like(ref)

    lines = ROWS // SIDE
    for line in range(lines):
        flat[line * SIDE : (line + 1) * SIDE, :] = cot[line].astype(F32)
    z = flat[...]
    x = second[...]
    slots_all = outputs.shape[0]
    pick = (slot_col[...] == iota((ROWS, slots_all), 1)).astype(BF16)
    picked = dot(pick, outputs[...], 1, 0)
    dispatched = dot(pick, grads[...], 1, 0)

    logits = exact_dot(x, router[...], 1, 1)
    chances = jnp.exp(logits - jnp.max(logits, axis=1, keepdims=True))
    chances = chances / jnp.sum(chances, axis=1, keepdims=True)
    slots = slots_all // chances.shape[1]
    within = slot_col[...] - iota(chances.shape, 1) * slots
    onehot = ((within >= 0) & (within < slots)).astype(F32)
    gate = jnp.sum(chances * onehot, axis=1, keepdims=True)
    n, rstd = norm_parts(gate * picked)
    final = x + n * gain[2:3, :] + offset[2:3, :]
    gain_grad[2:3, :] += col_sum(z * n)
    offset_grad[2:3, :] += col_sum(z)
    grad_moe = norm_back(gain[2:3, :] * z, n, rstd)
    grad_gate = jnp.sum(grad_moe * picked, axis=1, keepdims=True)
    grad_logits = grad_gate * gate * (onehot - chances)
    grad_logits_low = grad_logits.astype(BF16)
    router_grad[...] += dot(grad_logits_low, x.astype(BF16), 0, 0)
    grad_second = z + dispatched + dot(grad_logits_low, router[...].astype(BF16), 1, 0)

    n = n_in[...].astype(F32)
    gain_grad[1:2, :] += col_sum(grad_second * n)
    offset_grad[1:2, :] += col_sum(grad_second)
    grad_branch = norm_back(gain[1:2, :] * grad_second, n, rstd_in[...])
    grad_low = grad_branch.astype(BF16)
    down_bias_grad[...] += col_sum(grad_branch)
    grad_low_t = jnp.transpose(grad_low, (1, 0))
    first_t = jnp.transpose(first_low[...], (1, 0))
    total = jnp.zeros((ROWS, D), F32)
    for at in range(0, FF, CHUNK):
        part = slice(at, at + CHUNK)
        grad_hidden = dot(grad_low, down[part, :], 1, 1) * slope[:, part].astype(F32)
        grad_hidden_low = grad_hidden.astype(BF16)
        up_bias_grad[:, part] += col_sum(grad_hidden)
        down_grad_t[:, part] += dot(grad_low_t, active[:, part], 1, 0)
        up_grad[:, part] += dot(first_t, grad_hidden_low, 1, 0)
        total += dot(grad_hidden_low, up[:, part], 1, 1)
    grad_first[...] = total + grad_second
    flat[...] = final
    for line in range(lines):
        result[line] = flat[line * SIDE : (line + 1) * SIDE, :].astype(BF16)

    @pl.when(step == TOKENS // ROWS - 1)
    def _():
        pack_pair(packed, up_grad, down_grad_t)
        if packed.shape[0] > 2 * FF:
            packed[2 * FF :, :] = jnp.zeros_like(packed[2 * FF :, :])
        if depth.count > 1:
            scatter(depth, half, land, piece, sum_sems, False)
        else:
            piece[...] = half[...]


def backward(
    second, cot, slot_col, outputs, grads, router, first_low, active, slope, n, rstd,
    up, down, gain, offset, half, packed_rows,
):
    depth = lax.axis_size("dp") // 2
    piece = (half.shape[0] // depth, D)
    rows = lambda width: pl.BlockSpec((ROWS, width), lambda i: (i, 0))
    lines = pl.BlockSpec((ROWS // SIDE, SIDE, D), lambda i: (i, 0, 0))
    slots_all = outputs.shape[0]
    return pl.pallas_call(
        backward_kernel,
        grid=(TOKENS // ROWS,),
        in_specs=[
            rows(D),
            lines,
            rows(1),
            whole((slots_all, D)),
            whole((slots_all, D)),
            whole(router.shape),
            rows(D),
            rows(FF),
            rows(FF),
            rows(D),
            rows(1),
            whole((D, FF)),
            whole((FF, D)),
            whole((3, D)),
            whole((3, D)),
            whole(half.shape),
        ],
        out_specs=(
            lines,
            rows(D),
            whole((packed_rows, D)),
            whole((1, FF)),
            whole((1, D)),
            whole(router.shape),
            whole((3, D)),
            whole((3, D)),
            whole(piece),
        ),
        out_shape=(
            full((SIDE, SIDE, D), BF16),
            full((TOKENS, D)),
            full((packed_rows, D), BF16),
            full((1, FF)),
            full((1, D)),
            full(router.shape),
            full((3, D)),
            full((3, D)),
            full(piece, BF16),
        ),
        scratch_shapes=[
            pltpu.VMEM((ROWS, D), F32),
            pltpu.VMEM((D, FF), F32),
            pltpu.VMEM((D, FF), F32),
        ]
        + ([pltpu.VMEM((depth - 1,) + piece, BF16), *pair_of_sems(depth)] if depth > 1 else []),
        compiler_params=params(collective_id=2, has_side_effects=True) if depth > 1 else params(),
        name="backward",
    )(
        second, cot, slot_col, outputs, grads, router, first_low, active, slope, n, rstd,
        up, down, gain, offset, half,
    )


def attend_back_kernel(
    shifts, scale, grad_first, n_in, rstd_in, joint, probs, mixture, win_t, inverse,
    in_weight, out_weight, gain, own_piece, dense,
    own_sum, tokens_grad, packed, in_bias_grad, out_bias_grad, gain_grad, offset_grad, scale_grad,
    table_grad, dense_piece,
    doubled, windows, joint_grad, grads_f32, in_grad, out_grad, *sum_refs,
):
    window = pl.program_id(0)
    shift_row, shift_col = shifts[0, 0], shifts[0, 1]
    core, plane, depth = core_level(), plane_level(), depth_level()
    deep = depth.count > 1
    half, share, core_land, plane_land, *sum_refs = sum_refs
    if deep:
        depth_land, *sum_refs = sum_refs
    local, *sum_refs = sum_refs
    core_sems, plane_sems, depth_sems, sum_refs = (
        sum_refs[0:2], sum_refs[2:4], sum_refs[4:6], sum_refs[6:]
    )
    own = Gather([core, depth] if deep else [core], own_piece, own_sum, sum_refs, local)

    @pl.when(window == 0)
    def _():
        greet(core.devices() + plane.devices() + (depth.devices() if deep else []))
        own.move(len(own.levels) - 1, True)
        scatter(core, dense, core_land, half, core_sems, True)

    @pl.when(window == 1)
    def _():
        scatter(core, dense, core_land, half, core_sems, False)
        scatter(plane, half, plane_land, share, plane_sems, True)

    if deep:

        @pl.when(window == 6)
        def _():
            scatter(plane, half, plane_land, share, plane_sems, False)
            scatter(depth, share, depth_land, dense_piece, depth_sems, True)

        @pl.when(window == 8)
        def _():
            own.move(1, False)
            own.move(0, True)

    @pl.when(window == 0)
    def _():
        for ref in (
            in_grad, out_grad, out_bias_grad, gain_grad, offset_grad, scale_grad, table_grad
        ):
            ref[...] = jnp.zeros_like(ref)
        roll_to_windows(
            lambda row: grad_first[row * SIDE : (row + 1) * SIDE, :],
            doubled, windows, shift_row, shift_col,
        )

    mine = pl.ds(pl.multiple_of(window * AREA, 16), AREA)
    z = windows[mine, :]
    n = n_in[...].astype(F32)
    gain_grad[...] += col_sum(z * n)
    offset_grad[...] += col_sum(z)
    grad_branch = norm_back(gain[0:1, :] * z, n, rstd_in[...])
    grad_low = grad_branch.astype(BF16)
    out_bias_grad[...] += col_sum(grad_branch)
    out_grad[...] += dot(mixture[0], grad_low, 1, 0)
    grad_mixture = dot(out_weight[...], grad_low, 1, 1).astype(BF16)
    value_rows = jnp.transpose(joint[0, 2 * D :, :], (1, 0))
    blank = jnp.zeros((HEAD, AREA), BF16)

    def probs_grads(group):
        lanes = value_rows[:, group * 128 : (group + 1) * 128]
        found = []
        for head in range(4):
            at = group * 128 + head * HEAD
            parts = [blank] * 4
            parts[head] = grad_mixture[at : at + HEAD, :]
            found.append(dot(lanes, jnp.concatenate(parts, axis=0), 1, 0))
        return found

    ahead = probs_grads(0)
    for group in range(HEADS // 4):
        current = ahead
        if group + 1 < HEADS // 4:
            ahead = probs_grads(group + 1)
        raws = []
        for i in range(4):
            head = group * 4 + i
            weight = probs[0, head].astype(F32)
            weighted = weight * current[i]
            grad_scores = weighted - weight * (col_sum(weighted) / col_sum(weight))
            table_grad[head] += grad_scores
            raws.append((grad_scores * scale[0, head]).astype(BF16))
        for i in range(4):
            at = (group * 4 + i) * HEAD
            grads_f32[at : at + HEAD, :] = dot(joint[0, D + at : D + at + HEAD, :], raws[i], 1, 0)
            grads_f32[D + at : D + at + HEAD, :] = dot(joint[0, at : at + HEAD, :], raws[i], 1, 1)
            joint_grad[2 * D + at : 2 * D + at + HEAD, :] = dot(
                grad_mixture[at : at + HEAD, :], probs[0, group * 4 + i], 1, 1
            ).astype(BF16)

    def unit_back(rows, place):
        shaped = grads_f32[rows, :].reshape(HEADS, HEAD, AREA)
        unit = joint[0, rows, :].astype(F32).reshape(HEADS, HEAD, AREA)
        inner = jnp.sum(unit * shaped, axis=1, keepdims=True)
        shaped = shaped - unit * inner
        for head in range(HEADS):
            at = rows.start + head * HEAD
            joint_grad[at : at + HEAD, :] = (
                shaped[head] * inverse[0, place + head : place + head + 1, :]
            ).astype(BF16)
        return inner

    inner = unit_back(slice(0, D), 0)
    for head in range(HEADS):
        scale_grad[head : head + 1, :] += inner[head]
    unit_back(slice(D, 2 * D), HEADS)
    in_grad[...] += dot(win_t[0], joint_grad[...], 1, 1)
    windows[mine, :] = dot(joint_grad[...], in_weight[...], 0, 1)

    @pl.when(window == WINDOWS - 1)
    def _():
        def write_row(row, line):
            tokens_grad[row] = line + grad_first[row * SIDE : (row + 1) * SIDE, :]

        roll_to_image(windows, doubled, write_row, shift_row, shift_col)
        for block in range(3):
            packed[block * D : (block + 1) * D, :] = in_grad[
                :D, block * D : (block + 1) * D
            ].astype(BF16)
        packed[3 * D : 4 * D, :] = out_grad[...].astype(BF16)
        if packed.shape[0] > 4 * D:
            packed[4 * D :, :] = jnp.zeros_like(packed[4 * D :, :])
        in_bias_grad[...] = in_grad[D : D + 1, :]
        if deep:
            scatter(depth, share, depth_land, dense_piece, depth_sems, False)
        else:
            scatter(plane, half, plane_land, share, plane_sems, False)
            dense_piece[...] = share[...]
        own.move(0, False)


def attend_back(
    shifts, scale, grad_first, n, rstd, joint, probs, mixture, win_t, inverse,
    in_weight, out_weight, gain, own_piece, dense, packed_rows,
):
    group = lax.axis_size("expert")
    depth = lax.axis_size("dp") // 2
    half = dense.shape[0] // 2
    share = half // group
    piece = share // depth
    own_rows = own_piece.shape[0] * 2 * depth
    per_window = lambda *dims: pl.BlockSpec((1,) + dims, lambda w: (w,) + (0,) * len(dims))
    rows = lambda width: pl.BlockSpec((AREA, width), lambda w: (w, 0))
    return pl.pallas_call(
        attend_back_kernel,
        grid=(WINDOWS,),
        in_specs=[
            smem(),
            smem(),
            whole((TOKENS, D)),
            rows(D),
            rows(1),
            per_window(3 * D, AREA),
            per_window(HEADS, AREA, AREA),
            per_window(D, AREA),
            per_window(D + 16, AREA),
            per_window(2 * HEADS, AREA),
            whole((D, 3 * D)),
            whole((D, D)),
            whole((3, D)),
            whole(own_piece.shape),
            whole(dense.shape),
        ],
        out_specs=(
            pl.BlockSpec(memory_space=pl.ANY),
            whole((SIDE, SIDE, D)),
            whole((packed_rows, D)),
            whole((1, 3 * D)),
            whole((1, D)),
            whole((1, D)),
            whole((1, D)),
            whole((HEADS, AREA)),
            whole((HEADS, AREA, AREA)),
            whole((piece, D)),
        ),
        out_shape=(
            full((own_rows, D), BF16),
            full((SIDE, SIDE, D)),
            full((packed_rows, D), BF16),
            full((1, 3 * D)),
            full((1, D)),
            full((1, D)),
            full((1, D)),
            full((HEADS, AREA)),
            full((HEADS, AREA, AREA)),
            full((piece, D), BF16),
        ),
        scratch_shapes=[
            pltpu.VMEM((SIDE, SIDE + WS, D), F32),
            pltpu.VMEM((TOKENS, D), F32),
            pltpu.VMEM((3 * D, AREA), BF16),
            pltpu.VMEM((2 * D, AREA), F32),
            pltpu.VMEM((D + 16, 3 * D), F32),
            pltpu.VMEM((D, D), F32),
            pltpu.VMEM((half, D), BF16),
            pltpu.VMEM((share, D), BF16),
            pltpu.VMEM((1, half, D), BF16),
            pltpu.VMEM((group - 1, share, D), BF16),
        ]
        + ([pltpu.VMEM((depth - 1, piece, D), BF16)] if depth > 1 else [])
        + [
            pltpu.SemaphoreType.DMA(()),
            *pair_of_sems(2),
            *pair_of_sems(group),
            *pair_of_sems(depth),
            *sems_of([2, depth] if depth > 1 else [2]),
        ],
        compiler_params=params(collective_id=3, has_side_effects=True),
        name="attend_back",
    )(
        shifts, scale, grad_first, n, rstd, joint, probs, mixture, win_t, inverse,
        in_weight, out_weight, gain, own_piece, dense,
    )


SMALL = (
    ("in_bias", 1, 3 * D),
    ("out_bias", 1, D),
    ("up_bias", 1, FF),
    ("down_bias", 1, D),
    ("gain_first", 1, D),
    ("gain_rest", 2, D),
    ("offset_first", 1, D),
    ("offset_rest", 2, D),
    ("table_one", 3, UNITS),
    ("table_two", HEADS, UNITS),
    ("scale", 1, 128),
    ("router", 0, D),
)


def small_places(experts):
    places, at = {}, 0
    for name, rows, width in SMALL:
        rows = rows or experts
        places[name] = (at, rows, width)
        at += rows * (width // 128)
    return places, at


def put_small(ref, places, name, value):
    at, rows, width = places[name]
    for lane in range(0, width, 128):
        ref[at : at + rows, :] = value[:, lane : lane + 128]
        at += rows


def get_small(ref, places, name):
    at, rows, width = places[name]
    return jnp.concatenate(
        [ref[at + i * rows : at + (i + 1) * rows, :] for i in range(width // 128)], axis=1
    )


def values_back(table_grad, values_grad):
    spread = spread_matrix(True).astype(BF16)
    for head in range(HEADS):
        high, low = split(table_grad[head])
        flat = dot(high, spread, 1, 1) + dot(low, spread, 1, 1)
        flat = jnp.concatenate([flat, jnp.zeros((AREA, TABLE - 384), F32)], axis=1)
        total = jnp.zeros((16, TABLE), F32)
        for key_row in range(WS):
            line = flat[key_row * WS : (key_row + 1) * WS, :]
            line = jnp.concatenate([line, jnp.zeros((16 - WS, TABLE), F32)], axis=0)
            total += pltpu.roll(line, EXTENT * key_row, 1)
        total = pltpu.roll(total, 0, 1, stride=1, stride_axis=0)
        values_grad[head : head + 1, :] = col_sum(total)


def net_back(values_grad, w1, b1, w2):
    f_row, f_col = offsets_row((UNITS, TABLE), 1, -1.0)
    w1t = jnp.transpose(w1[...], (1, 0))
    b1t = jnp.transpose(row_of(b1), (1, 0))
    hidden, slope = gelu_pair(w1t[:, 0:1] * f_row + w1t[:, 1:2] * f_col + b1t[:, 0:1])
    chance = jax.nn.sigmoid(exact_dot(w2[...], hidden, 1, 0))
    grad_pre = values_grad[:HEADS, :] * (16.0 * chance * (1.0 - chance))
    grad_hidden = exact_dot(w2[...], grad_pre, 0, 0) * slope
    f_row, f_col = offsets_row((8, TABLE), 1, -1.0)
    kind = iota((8, TABLE), 0)
    factors = jnp.where(kind == 0, f_row, jnp.where(kind == 1, f_col, 1.0))
    return exact_dot(factors, grad_hidden, 1, 1)[:3, :], exact_dot(grad_pre, hidden, 1, 1)


class Whole:
    def __init__(self, levels, refs, source, result):
        count = len(levels)
        lands, outs, refs = refs[:count], refs[count : 2 * count], refs[2 * count :]
        scatter_sems, gather_sems, local = refs[: 2 * count], refs[2 * count : 4 * count], refs[-1]
        sources = [source] + list(outs[:-1])
        gather = Gather(levels, outs[-1], result, gather_sems, local)
        self.moves = [
            functools.partial(
                scatter, levels[i], sources[i], lands[i], outs[i], scatter_sems[2 * i : 2 * i + 2]
            )
            for i in range(count)
        ] + [functools.partial(gather.move, i) for i in reversed(range(count))]
        self.at = 0

    @staticmethod
    def scratch(rows, width, dtype, counts):
        lands, outs = [], []
        for count in counts:
            rows //= count
            lands.append(pltpu.VMEM((count - 1, rows, width), dtype))
            outs.append(pltpu.VMEM((rows, width), dtype))
        return lands + outs + sems_of(counts) * 2 + [pltpu.SemaphoreType.DMA(())]

    def advance(self):
        if self.at > len(self.moves):
            return
        if self.at:
            self.moves[self.at - 1](False)
        if self.at < len(self.moves):
            self.moves[self.at](True)
        self.at += 1


def finish_kernel(
    places, per_sum,
    dense_piece, last, table_grad, scale_rows, w1, b1, w2, in_bias, out_bias, up_bias, down_bias,
    gain_first, gain_rest, offset_first, offset_rest, router,
    dense_sum, last_sum, small_sum,
    values_grad, small, *refs,
):
    core, plane, depth = core_level(), plane_level(), depth_level()
    levels = [core, plane] + ([depth] if depth.count > 1 else [])
    greet([device for level in levels for device in level.devices()])
    last_total = Whole(levels, refs[:per_sum], last, last_sum)
    small_total = Whole(levels, refs[per_sum : 2 * per_sum], small, small_sum)
    *dense_sems, local = refs[2 * per_sum :]
    dense = Gather(levels, dense_piece, dense_sum, dense_sems, local)
    dense.move(len(levels) - 1, True)
    last_total.advance()
    values_back(table_grad, values_grad)
    last_total.advance()
    dense.move(len(levels) - 1, False)
    dense.move(len(levels) - 2, True)
    table_one, table_two = net_back(values_grad, w1, b1, w2)
    small[...] = jnp.zeros_like(small)
    put_small(small, places, "table_one", table_one)
    put_small(small, places, "table_two", table_two)
    scales = exact_dot(jnp.ones((8, AREA), F32), scale_rows[...], 1, 1)[0:1, :]
    put_small(
        small, places, "scale", jnp.concatenate([scales, jnp.zeros((1, 128 - HEADS), F32)], axis=1)
    )
    put_small(small, places, "in_bias", in_bias[...])
    put_small(small, places, "out_bias", out_bias[...])
    put_small(small, places, "up_bias", up_bias[...])
    put_small(small, places, "down_bias", down_bias[...])
    put_small(small, places, "gain_first", gain_first[...])
    put_small(small, places, "gain_rest", gain_rest[1:, :])
    put_small(small, places, "offset_first", offset_first[...])
    put_small(small, places, "offset_rest", offset_rest[1:, :])
    put_small(small, places, "router", router[...])
    small_total.advance()
    last_total.advance()
    small_total.advance()
    if len(levels) > 2:
        dense.move(1, False)
        dense.move(0, True)
    for _ in range(2 * len(levels) - 1):
        last_total.advance()
        small_total.advance()
    dense.move(0, False)


def finish(small_rows, experts, dense_rows, dense_piece, last, *args):
    places, _ = small_places(experts)
    group, depth = lax.axis_size("expert"), lax.axis_size("dp") // 2
    counts = [2, group] + ([depth] if depth > 1 else [])
    last_scratch = Whole.scratch(last.shape[0], D, BF16, counts)
    small_scratch = Whole.scratch(small_rows, 128, F32, counts)
    anywhere = pl.BlockSpec(memory_space=pl.ANY)
    vmem = pl.BlockSpec(memory_space=pltpu.VMEM)
    return pl.pallas_call(
        functools.partial(finish_kernel, places, len(last_scratch)),
        in_specs=[vmem] * (2 + len(args)),
        out_specs=(anywhere,) * 3,
        out_shape=(
            full((dense_rows, D), BF16),
            full(last.shape, BF16),
            full((small_rows, 128)),
        ),
        scratch_shapes=[
            pltpu.VMEM((16, TABLE), F32),
            pltpu.VMEM((small_rows, 128), F32),
            *last_scratch,
            *small_scratch,
            *sems_of(counts),
            pltpu.SemaphoreType.DMA(()),
        ],
        compiler_params=params(collective_id=4, has_side_effects=True),
        name="finish",
    )(dense_piece, last, *args)


def unpack_kernel(
    places, own, dense, last, small,
    in_grad, in_bias, scale, table_first, table_first_bias, table_second, out_grad, out_bias,
    up_grad, up_bias, down_grad, down_bias, router, own_up, own_up_bias, own_down, own_down_bias,
    gain, offset,
):
    for block in range(3):
        part = slice(block * D, (block + 1) * D)
        in_grad[:, part] = last[part, :].astype(F32)
    out_grad[...] = last[3 * D : 4 * D, :].astype(F32)
    for source, up, down in ((dense, up_grad, down_grad), (own, own_up, own_down)):
        for block in range(FF // D):
            part = slice(block * D, (block + 1) * D)
            up[:, part] = source[part, :].astype(F32)
            down[part, :] = source[FF + block * D : FF + (block + 1) * D, :].astype(F32)
    tail = own[2 * FF : 2 * FF + 16, :].astype(F32)
    for block in range(FF // D):
        own_up_bias[:, block * D : (block + 1) * D] = tail[block : block + 1, :]
    own_down_bias[...] = tail[FF // D : FF // D + 1, :]
    get = functools.partial(get_small, small, places)
    row = get("in_bias")
    in_bias[0:1, :] = row[:, :D]
    in_bias[1:2, :] = row[:, 2 * D :]
    scale[...] = get("scale")[:, :HEADS].reshape(HEADS)
    one = get("table_one")
    table_first[...] = one[0:2, :]
    table_first_bias[...] = one[2:3, :].reshape(UNITS)
    table_second[...] = get("table_two")
    out_bias[...] = get("out_bias").reshape(D)
    up_bias[...] = get("up_bias").reshape(FF)
    down_bias[...] = get("down_bias").reshape(D)
    router[...] = get("router")
    gain[0:1, :] = get("gain_first")
    gain[1:3, :] = get("gain_rest")
    offset[0:1, :] = get("offset_first")
    offset[1:3, :] = get("offset_rest")


def unpack(own, dense, last, small, experts):
    places, _ = small_places(experts)
    return pl.pallas_call(
        functools.partial(unpack_kernel, places),
        out_shape=(
            full((D, 3 * D)),
            full((2, D)),
            full((HEADS,)),
            full((2, UNITS)),
            full((UNITS,)),
            full((HEADS, UNITS)),
            full((D, D)),
            full((D,)),
            full((D, FF)),
            full((FF,)),
            full((FF, D)),
            full((D,)),
            full((experts, D)),
            full((D, FF)),
            full((1, FF)),
            full((FF, D)),
            full((1, D)),
            full((3, D)),
            full((3, D)),
        ),
        compiler_params=params(),
        name="unpack",
    )(own, dense, last, small)


def per_device(
    tokens, shifts, routes, cotangent, in_weight, in_bias, logit_scale,
    bias_net_first_weight, bias_net_first_bias, bias_net_second_weight,
    out_weight, out_bias, up_weight, up_bias, down_weight, down_bias, router_weight,
    expert_up, expert_up_bias, expert_down, expert_down_bias, norm_gain, norm_bias,
):
    experts = router_weight.shape[1]
    dp = lax.axis_size("dp")
    group = lax.axis_size("expert")
    capacity = (5 * TOKENS + 4 * experts - 1) // (4 * experts)
    slots = -(-capacity // 16) * 16
    own_counts, both_counts = [2, dp // 2], [2, group, dp // 2]
    own_rows = padded_rows(2 * FF + 16, own_counts, 16)
    dense_rows = padded_rows(2 * FF, both_counts, 16)
    last_rows = padded_rows(4 * D, both_counts, 16)
    small_rows = padded_rows(small_places(experts)[1], both_counts, 8)

    picture = tokens.reshape(SIDE, SIDE, D)
    cot = cotangent.reshape(SIDE, SIDE, D)
    router_t = router_weight.T
    second_t = bias_net_second_weight.T

    slot_col, slot_row, cot_slots, table, scale = prep(
        routes.reshape(1, TOKENS), cot, bias_net_first_weight, bias_net_first_bias, second_t,
        logit_scale, experts, capacity, slots,
    )
    cot_arrived, normed, n_zero, rstd_zero, joint, probs, mixture, win_t, inverse = attend(
        cot_slots, shifts, scale, picture, in_weight, in_bias, table,
        out_weight, out_bias, norm_gain, norm_bias,
    )
    first_low, active, slope, n_one, rstd_one, second, buffer = forward(
        shifts, picture, normed, up_weight, up_bias, down_weight,
        down_bias, norm_gain, norm_bias, slot_row, experts, slots,
    )
    returned, grad_returned, own_half = run_experts(
        buffer, cot_arrived, router_t, expert_up[0], expert_up_bias, expert_down[0],
        expert_down_bias, norm_gain, own_rows,
    )
    (
        result, grad_first, dense_packed, up_bias_grad, down_bias_grad, router_grad,
        gain_grad, offset_grad, own_piece,
    ) = backward(
        second, cot, slot_col, returned.reshape(-1, D), grad_returned.reshape(-1, D),
        router_t, first_low, active, slope, n_one, rstd_one, up_weight, down_weight,
        norm_gain, norm_bias, own_half, dense_rows,
    )
    (
        own_sum, tokens_grad, last_packed, in_bias_grad, out_bias_grad, gain_zero, offset_zero,
        scale_rows, table_grad, dense_piece,
    ) = attend_back(
        shifts, scale, grad_first, n_zero, rstd_zero, joint, probs, mixture, win_t, inverse,
        in_weight, out_weight, norm_gain, own_piece, dense_packed, last_rows,
    )
    dense_sum, last_sum, small_sum = finish(
        small_rows, experts, dense_rows, dense_piece, last_packed, table_grad, scale_rows,
        bias_net_first_weight, bias_net_first_bias, second_t, in_bias_grad, out_bias_grad,
        up_bias_grad, down_bias_grad, gain_zero, gain_grad, offset_zero, offset_grad, router_grad,
    )
    (
        in_weight_grad, in_bias_grad, scale_grad, table_one, table_bias, table_two, out_grad,
        out_bias_grad, up_grad, up_bias_grad, down_grad, down_bias_grad, router_grad,
        own_up, own_up_bias, own_down, own_down_bias, gain_grad, offset_grad,
    ) = unpack(own_sum, dense_sum, last_sum, small_sum, experts)
    return (
        result.reshape(tokens.shape),
        tokens_grad.reshape(tokens.shape),
        in_weight_grad,
        in_bias_grad,
        scale_grad,
        table_one,
        table_bias,
        table_two.T,
        out_grad,
        out_bias_grad,
        up_grad,
        up_bias_grad,
        down_grad,
        down_bias_grad,
        router_grad.T,
        own_up[None],
        own_up_bias,
        own_down[None],
        own_down_bias,
        gain_grad,
        offset_grad,
    )


def solution(mesh):
    split_all = P(("dp", "expert"))
    placed = (split_all,) * 4 + (P(),) * 13 + (P("expert"),) * 4 + (P(),) * 2
    return jax.shard_map(
        per_device,
        mesh=mesh,
        in_specs=placed,
        out_specs=(split_all,) * 2 + (P(),) * 13 + (P("expert"),) * 4 + (P(),) * 2,
        check_vma=False,
    )
```

```python
import functools

import jax
import jax.numpy as jnp
from jax import lax
from jax.experimental import pallas as pl
from jax.experimental.pallas import tpu as pltpu
from jax.sharding import PartitionSpec as P

D = 384
HEADS = 12
HEAD = D // HEADS
WS = 12
SIDE = 36
AREA = WS * WS
ACROSS = SIDE // WS
WINDOWS = ACROSS * ACROSS
TOKENS = SIDE * SIDE
FF = 1536
EXTENT = 2 * WS - 1
UNITS = 512
GROUPS = 3
TABLE = 640
ROWS = 432
CHUNK = 256
F32 = jnp.float32
BF16 = jnp.bfloat16
I32 = jnp.int32
VMEM_LIMIT = 63 * 1024 * 1024


def dot(left, right, left_dim, right_dim):
    return lax.dot_general(
        left, right, (((left_dim,), (right_dim,)), ((), ())), preferred_element_type=F32
    )


def exact_dot(left, right, left_dim, right_dim):
    return lax.dot_general(
        left,
        right,
        (((left_dim,), (right_dim,)), ((), ())),
        preferred_element_type=F32,
        precision=lax.Precision.HIGHEST,
    )


def split(values):
    high = values.astype(BF16)
    return high, (values - high.astype(F32)).astype(BF16)


def iota(shape, dim):
    return lax.broadcasted_iota(I32, shape, dim)


def gelu_pair(values):
    size = jnp.abs(values)
    t = 1.0 / (1.0 + 0.2316419 * size)
    bell = jnp.exp(-0.5 * values * values) * 0.3989422804014327
    series = t * (
        0.319381530
        + t * (-0.356563782 + t * (1.781477937 + t * (-1.821255978 + t * 1.330274429)))
    )
    tail = series * bell
    phi = jnp.where(values >= 0.0, 1.0 - tail, tail)
    return values * phi, phi + values * bell


def norm_parts(values):
    centered = values - jnp.mean(values, axis=-1, keepdims=True)
    rstd = lax.rsqrt(jnp.mean(centered * centered, axis=-1, keepdims=True) + 1e-05)
    return centered * rstd, rstd


def norm_back(grad_n, n, rstd):
    return rstd * (
        grad_n
        - jnp.mean(grad_n, axis=-1, keepdims=True)
        - n * jnp.mean(grad_n * n, axis=-1, keepdims=True)
    )


def row_of(ref):
    return ref[...].reshape(1, ref.shape[0])


def col_sum(values):
    return jnp.sum(values, axis=0, keepdims=True)


def div_ws(values):
    return (values * 171) >> 11


def full(shape, dtype=F32):
    return jax.ShapeDtypeStruct(shape, dtype)


def whole(shape):
    return pl.BlockSpec(shape, lambda *_: (0,) * len(shape))


def smem():
    return pl.BlockSpec(memory_space=pltpu.SMEM)


def params(**more):
    return pltpu.CompilerParams(vmem_limit_bytes=VMEM_LIMIT, **more)


def partner(me, step, count):
    side = 1
    while side * side < count:
        side *= 2
    if side * side != count:
        return lax.rem(me + step, count)
    row = lax.rem(lax.div(me, side) + step // side, side)
    col = lax.rem(lax.rem(me, side) + step % side, side)
    return row * side + col


def opposite(step, count):
    side = 1
    while side * side < count:
        side *= 2
    if side * side != count:
        return (count - step) % count
    return ((side - step // side) % side) * side + (side - step % side) % side


def greet(devices):
    barrier = pltpu.get_barrier_semaphore()
    for device in devices:
        pl.semaphore_signal(barrier, inc=1, device_id=device, device_id_type=pl.DeviceIdType.MESH)
    pl.semaphore_wait(barrier, len(devices))


class Level:
    def __init__(self, count, index, device):
        self.count, self.index, self.device = count, index, device

    def others(self):
        return [lax.rem(self.index + step, self.count) for step in range(1, self.count)]

    def devices(self):
        return [self.device(to) for to in self.others()]


def core_level():
    place = lax.div(lax.axis_index("dp"), 2)
    return Level(2, lax.rem(lax.axis_index("dp"), 2), lambda j: {"dp": place * 2 + j})


def plane_level():
    return Level(lax.axis_size("expert"), lax.axis_index("expert"), lambda j: {"expert": j})


def depth_level():
    core = lax.rem(lax.axis_index("dp"), 2)
    place = lax.div(lax.axis_index("dp"), 2)
    return Level(lax.axis_size("dp") // 2, place, lambda j: {"dp": j * 2 + core})


def padded_rows(rows, counts, tile):
    unit = tile
    for count in counts:
        unit *= count
    return -(-rows // unit) * unit


def pair_of_sems():
    return [pltpu.SemaphoreType.DMA(()), pltpu.SemaphoreType.DMA(())]


def wait_all(sent, received, sems, level):
    copy = pltpu.make_async_remote_copy(
        src_ref=sent,
        dst_ref=received,
        send_sem=sems[0],
        recv_sem=sems[1],
        device_id=level.device(level.others()[0]),
        device_id_type=pl.DeviceIdType.MESH,
    )
    copy.wait()


def scatter(level, source, land, out, sems, begin):
    rows = source.shape[0] // level.count
    tile = 16 if source.dtype == BF16 else 8
    if begin:
        for step, to in enumerate(level.others(), 1):
            pltpu.make_async_remote_copy(
                src_ref=source.at[pl.ds(pl.multiple_of(to * rows, tile), rows)],
                dst_ref=land.at[pl.ds((step - 1) * rows, rows)],
                send_sem=sems[0],
                recv_sem=sems[1],
                device_id=level.device(to),
                device_id_type=pl.DeviceIdType.MESH,
            ).start()
        return
    wait_all(source.at[pl.ds(0, land.shape[0])], land, sems, level)
    mine = level.index * rows
    chunk = tile
    while rows % (chunk * 2) == 0 and chunk < 128:
        chunk *= 2

    def add(i, carry):
        here = pl.ds(pl.multiple_of(i * chunk, tile), chunk)
        total = source[pl.ds(pl.multiple_of(mine + i * chunk, tile), chunk), :].astype(F32)
        for step in range(1, level.count):
            total = total + land[
                pl.ds(pl.multiple_of((step - 1) * rows + i * chunk, tile), chunk), :
            ].astype(F32)
        out[here, :] = total.astype(out.dtype)
        return carry

    lax.fori_loop(0, rows // chunk, add, 0)


class Gather:
    def __init__(self, levels, piece, result, sems, local):
        self.levels, self.piece, self.result, self.sems = levels, piece, result, sems
        rows, start = result.shape[0], 0
        self.regions = []
        for level in levels:
            rows //= level.count
            start = start + level.index * rows
            self.regions.append((start, rows))
        self.keep = pltpu.make_async_copy(piece, self.region(len(levels) - 1), local)

    def region(self, at):
        start, rows = self.regions[at]
        return self.result.at[pl.ds(pl.multiple_of(start, 8), rows)]

    def move(self, at, begin):
        level, last = self.levels[at], at == len(self.levels) - 1
        mine = self.region(at)
        sems = self.sems[2 * at : 2 * at + 2]
        if begin:
            for to in level.others():
                pltpu.make_async_remote_copy(
                    src_ref=self.piece if last else mine,
                    dst_ref=mine,
                    send_sem=sems[0],
                    recv_sem=sems[1],
                    device_id=level.device(to),
                    device_id_type=pl.DeviceIdType.MESH,
                ).start()
        else:
            some = self.result.at[pl.ds(0, (level.count - 1) * self.regions[at][1])]
            wait_all(some, some, sems, level)
        if last:
            self.keep.start() if begin else self.keep.wait()


def sems_of(levels):
    return [sem for _ in levels for sem in pair_of_sems()]


def offsets_row(shape, dim, sign):
    place = iota(shape, dim)
    row = jnp.floor((place.astype(F32) + 0.5) * (1.0 / EXTENT)).astype(I32)
    col = place - row * EXTENT

    def logged(step):
        e = sign * (step - (WS - 1)).astype(F32) * (8.0 / (WS - 1))
        size = jnp.log2(jnp.abs(e) + 1.0) * (1.0 / 3.0)
        return jnp.where(e < 0.0, -size, size)

    return logged(row), logged(col)


def spread_matrix(mirrored):
    token = iota((384, AREA), 1)
    row = div_ws(token)
    lin = row * EXTENT + (token - row * WS)
    if mirrored:
        lin = (WS - 1) * EXTENT + (WS - 1) - lin
    return (iota((384, AREA), 0) == lin).astype(F32)


def prep_kernel(
    capacity, routes, cot, w1, b1, w2, ls, slot_col, slot_row, zbuf, table, scale, flat, u_ref, route_col
):
    slots = zbuf.shape[1]
    experts = zbuf.shape[0]
    route_col[...] = jnp.transpose(
        jnp.broadcast_to(routes[...].astype(F32), (128, TOKENS)), (1, 0)
    )
    before = (iota((AREA, AREA), 1) < iota((AREA, AREA), 0)).astype(BF16)
    carry = jnp.zeros((1, 128), F32)
    for block in range(TOKENS // AREA):
        rows = pl.ds(block * AREA, AREA)
        route = route_col[rows, 0:1]
        onehot = (route == iota((AREA, 128), 1).astype(F32)).astype(F32)
        ahead = dot(before, onehot.astype(BF16), 1, 0) + carry
        position = jnp.sum(ahead * onehot, axis=1, keepdims=True)
        carry = carry + col_sum(onehot)
        slot = route * slots + position
        slot_col[rows, :] = jnp.where(position < capacity, slot, -1.0).astype(I32)
    slot_row[...] = jnp.transpose(
        jnp.broadcast_to(slot_col[...].astype(F32), (TOKENS, 128)), (1, 0)
    )[0:1, :].astype(I32)

    for row in range(SIDE):
        flat[row * SIDE : (row + 1) * SIDE, :] = cot[row].astype(F32)
    low = flat[...].astype(BF16)
    for expert in range(experts):
        pick = (iota((slots, TOKENS), 0) + expert * slots == slot_row[...]).astype(BF16)
        zbuf[expert] = dot(pick, low, 1, 0).astype(BF16)

    scale[...] = jnp.exp(row_of(ls))
    f_row, f_col = (found[0:1, :] for found in offsets_row((8, TABLE), 1, 1.0))
    w1t = jnp.transpose(w1[...], (1, 0))
    b1t = jnp.transpose(row_of(b1), (1, 0))
    hidden, _ = gelu_pair(w1t[:, 0:1] * f_row + w1t[:, 1:2] * f_col + b1t[:, 0:1])
    values = 16.0 * jax.nn.sigmoid(exact_dot(w2[...], hidden, 1, 0))
    spread = spread_matrix(False).astype(BF16)
    for head in range(HEADS):
        line = jnp.broadcast_to(values[head : head + 1, :], (16, TABLE))
        line = pltpu.roll(line, 0, 1, stride=1, stride_axis=0)
        for key_row in range(WS):
            shift = (EXTENT * key_row - (WS - 1) * EXTENT - (WS - 1)) % TABLE
            rolled = pltpu.roll(line, shift, 1)
            u_ref[key_row * WS : (key_row + 1) * WS, :] = rolled[:WS, :384]
        high, low_part = split(u_ref[...])
        table[head] = dot(high, spread, 1, 0) + dot(low_part, spread, 1, 0)


def prep(routes, cotangent, w1, b1, w2, ls, experts, capacity, slots):
    return pl.pallas_call(
        functools.partial(prep_kernel, capacity),
        out_shape=(
            full((TOKENS, 1), I32),
            full((1, TOKENS), I32),
            full((experts, slots, D), BF16),
            full((HEADS, AREA, AREA)),
            full((1, HEADS)),
        ),
        scratch_shapes=[
            pltpu.VMEM((TOKENS, D), F32),
            pltpu.VMEM((AREA, 384), F32),
            pltpu.VMEM((TOKENS, 128), F32),
        ],
        compiler_params=params(),
        name="prep",
    )(routes, cotangent, w1, b1, w2, ls)


def window_labels(window, shift_row, shift_col):
    def labels(shape, dim):
        token = iota(shape, dim)
        row = div_ws(token)
        col = token - row * WS + lax.rem(window, ACROSS) * WS
        row = row + lax.div(window, ACROSS) * WS

        def region(place, shift):
            last = jnp.where(place < SIDE - shift, 1, 2)
            return jnp.where(place < SIDE - WS, 0, last)

        return region(row, shift_row) * 3 + region(col, shift_col)

    return labels((AREA, 1), 0), labels((1, AREA), 1)


def roll_to_windows(read_row, doubled, windows, shift_row, shift_col):
    for row in range(SIDE):
        line = read_row(row)
        doubled[row, :SIDE, :] = line
        doubled[row, SIDE:, :] = line[:WS, :]
    for row in range(SIDE):
        source = row + shift_row
        source = jnp.where(source >= SIDE, source - SIDE, source)
        line = pltpu.roll(doubled[source], SIDE + WS - shift_col, 0)
        for across in range(ACROSS):
            start = ((row // WS) * ACROSS + across) * AREA + (row % WS) * WS
            windows[start : start + WS, :] = line[across * WS : (across + 1) * WS, :]


def roll_to_image(windows, doubled, write_row, shift_row, shift_col):
    for row in range(SIDE):
        for across in range(ACROSS):
            start = ((row // WS) * ACROSS + across) * AREA + (row % WS) * WS
            line = windows[start : start + WS, :]
            doubled[row, across * WS : (across + 1) * WS, :] = line
            if across == ACROSS - 1:
                doubled[row, SIDE:, :] = line
    for row in range(SIDE):
        source = row - shift_row
        source = jnp.where(source < 0, source + SIDE, source)
        write_row(row, pltpu.roll(doubled[source], shift_col, 0)[:SIDE, :])


def attend_kernel(
    cot_slots, shifts, scale, tokens, in_weight, in_bias, table, out_weight, out_bias, gain, offset,
    cot_arrived, normed, n_out, rstd_out, joint, probs, mixture, win_t, inverse,
    doubled, windows, in_weight_t, bias_col, joined, send, recv, local,
):
    window = pl.program_id(0)
    shift_row, shift_col = shifts[0, 0], shifts[0, 1]
    me = lax.axis_index("expert")
    count = cot_slots.shape[0]

    def move(step):
        to = partner(me, step, count)
        return pltpu.make_async_remote_copy(
            src_ref=cot_slots.at[to],
            dst_ref=cot_arrived.at[me],
            send_sem=send.at[step],
            recv_sem=recv.at[step],
            device_id={"expert": to},
            device_id_type=pl.DeviceIdType.MESH,
        )

    keep = pltpu.make_async_copy(cot_slots.at[me], cot_arrived.at[me], local)

    @pl.when(window == 0)
    def _():
        greet([{"expert": partner(me, step, count)} for step in range(1, count)])
        for step in range(1, count):
            move(step).start()
        keep.start()
        roll_to_windows(
            lambda row: tokens[row].astype(F32), doubled, windows, shift_row, shift_col
        )
        in_weight_t[...] = jnp.transpose(in_weight[...], (1, 0))
        bias_col[:, 0:2] = jnp.transpose(in_bias[...], (1, 0))

    mine = windows[pl.ds(pl.multiple_of(window * AREA, 16), AREA), :].astype(BF16)
    win_t[0, :D, :] = jnp.transpose(mine, (1, 0))
    win_t[0, D:, :] = (iota((16, AREA), 0) == 0).astype(BF16)
    label_keys, label_queries = window_labels(window, shift_row, shift_col)
    mask = jnp.where(label_keys == label_queries, 0.0, -100.0)
    joined[...] = dot(in_weight_t[...], mine, 1, 1)

    def unit(rows, bias, place):
        shaped = (joined[rows, :] + bias).reshape(HEADS, HEAD, AREA)
        inner = lax.rsqrt(1.0 + jnp.sum(shaped * shaped, axis=1, keepdims=True))
        for head in range(HEADS):
            at = place + head % 4
            inverse[0, head // 4, at : at + 1, :] = inner[head]
        return (shaped * inner).reshape(D, AREA).astype(BF16)

    queries = unit(slice(0, D), bias_col[:, 0:1], 0)
    keys = unit(slice(D, 2 * D), 0.0, 4)
    values = (joined[2 * D :, :] + bias_col[:, 1:2]).astype(BF16)
    for group in range(GROUPS):
        part = slice(group * 128, (group + 1) * 128)
        joint[0, group, 0:128, :] = queries[part, :]
        joint[0, group, 128:256, :] = keys[part, :]
        joint[0, group, 256:384, :] = values[part, :]
    key_rows = jnp.transpose(keys, (1, 0))
    blank = jnp.zeros((HEAD, AREA), BF16)

    def scores_of(group):
        lanes = key_rows[:, group * 128 : (group + 1) * 128]
        found = []
        for head in range(4):
            at = group * 128 + head * HEAD
            parts = [blank] * 4
            parts[head] = queries[at : at + HEAD, :]
            found.append(dot(lanes, jnp.concatenate(parts, axis=0), 1, 0))
        return found

    ahead = scores_of(0)
    for group in range(GROUPS):
        current = ahead
        if group + 1 < GROUPS:
            ahead = scores_of(group + 1)
        lows = []
        for i in range(4):
            head = group * 4 + i
            scores = current[i] * scale[0, head] + (table[head] + mask)
            exponent = jnp.exp(scores - jnp.max(scores, axis=0, keepdims=True))
            low = (exponent * (1.0 / col_sum(exponent))).astype(BF16)
            probs[0, head] = low
            lows.append(low)
        for i in range(4):
            at = (group * 4 + i) * HEAD
            mixture[0, at : at + HEAD, :] = dot(values[at : at + HEAD, :], lows[i], 1, 0).astype(BF16)
    branch = dot(mixture[0], out_weight[...], 0, 0) + row_of(out_bias)
    n, rstd = norm_parts(branch)
    normed[...] = n * gain[0:1, :] + offset[0:1, :]
    n_out[...] = n.astype(BF16)
    rstd_out[...] = rstd

    @pl.when(window == WINDOWS - 1)
    def _():
        for step in range(1, count):
            move(step).wait()
        keep.wait()


def attend(
    cot_slots, shifts, scale, tokens, in_weight, in_bias, table, out_weight, out_bias, gain, offset
):
    per_window = lambda *dims: pl.BlockSpec((1,) + dims, lambda w: (w,) + (0,) * len(dims))
    rows = lambda width: pl.BlockSpec((AREA, width), lambda w: (w, 0))
    return pl.pallas_call(
        attend_kernel,
        grid=(WINDOWS,),
        in_specs=[
            pl.BlockSpec(memory_space=pl.ANY),
            smem(),
            smem(),
            whole((SIDE, SIDE, D)),
            whole((D, 3 * D)),
            whole((2, D)),
            whole((HEADS, AREA, AREA)),
            whole((D, D)),
            whole((D,)),
            whole((3, D)),
            whole((3, D)),
        ],
        out_specs=(
            pl.BlockSpec(memory_space=pl.ANY),
            rows(D),
            rows(D),
            rows(1),
            per_window(GROUPS, D, AREA),
            per_window(HEADS, AREA, AREA),
            per_window(D, AREA),
            per_window(D + 16, AREA),
            per_window(GROUPS, 8, AREA),
        ),
        out_shape=(
            full(cot_slots.shape, BF16),
            full((TOKENS, D)),
            full((TOKENS, D), BF16),
            full((TOKENS, 1)),
            full((WINDOWS, GROUPS, D, AREA), BF16),
            full((WINDOWS, HEADS, AREA, AREA), BF16),
            full((WINDOWS, D, AREA), BF16),
            full((WINDOWS, D + 16, AREA), BF16),
            full((WINDOWS, GROUPS, 8, AREA)),
        ),
        scratch_shapes=[
            pltpu.VMEM((SIDE, SIDE + WS, D), F32),
            pltpu.VMEM((TOKENS, D), F32),
            pltpu.VMEM((3 * D, D), BF16),
            pltpu.VMEM((D, 128), F32),
            pltpu.VMEM((3 * D, AREA), F32),
            pltpu.SemaphoreType.DMA((cot_slots.shape[0],)),
            pltpu.SemaphoreType.DMA((cot_slots.shape[0],)),
            pltpu.SemaphoreType.DMA(()),
        ],
        compiler_params=params(collective_id=0, has_side_effects=True),
        name="attend",
    )(cot_slots, shifts, scale, tokens, in_weight, in_bias, table, out_weight, out_bias, gain, offset)


def forward_kernel(
    shifts, tokens, normed, up, up_bias, down, down_bias, gain, offset, slot_row,
    first_low, active, slope, n_out, rstd_out, second, buffer,
    doubled, image, second_low,
):
    step = pl.program_id(0)

    @pl.when(step == 0)
    def _():
        def write_row(row, line):
            image[row * SIDE : (row + 1) * SIDE, :] = line + tokens[row].astype(F32)

        roll_to_image(normed, doubled, write_row, shifts[0, 0], shifts[0, 1])

    rows = pl.ds(pl.multiple_of(step * ROWS, 16), ROWS)
    first = image[rows, :]
    low = first.astype(BF16)
    first_low[...] = low
    up_row = row_of(up_bias)
    branch = jnp.broadcast_to(row_of(down_bias), (ROWS, D))
    for at in range(0, FF, CHUNK):
        hidden = dot(low, up[:, at : at + CHUNK], 1, 0) + up_row[:, at : at + CHUNK]
        activated, derivative = gelu_pair(hidden)
        activated = activated.astype(BF16)
        active[:, at : at + CHUNK] = activated
        slope[:, at : at + CHUNK] = derivative.astype(BF16)
        branch += dot(activated, down[at : at + CHUNK, :], 1, 0)
    n, rstd = norm_parts(branch)
    n_out[...] = n.astype(BF16)
    rstd_out[...] = rstd
    result = first + n * gain[1:2, :] + offset[1:2, :]
    second[...] = result
    second_low[rows, :] = result.astype(BF16)

    @pl.when(step == TOKENS // ROWS - 1)
    def _():
        slots = buffer.shape[1]
        for expert in range(buffer.shape[0]):
            pick = (iota((slots, TOKENS), 0) + expert * slots == slot_row[...]).astype(BF16)
            buffer[expert] = dot(pick, second_low[...], 1, 0).astype(BF16)


def forward(
    shifts, tokens, normed, up, up_bias, down, down_bias, gain, offset, slot_row, experts, slots
):
    rows = lambda width: pl.BlockSpec((ROWS, width), lambda i: (i, 0))
    return pl.pallas_call(
        forward_kernel,
        grid=(TOKENS // ROWS,),
        in_specs=[
            smem(),
            whole((SIDE, SIDE, D)),
            whole((TOKENS, D)),
            whole((D, FF)),
            whole((FF,)),
            whole((FF, D)),
            whole((D,)),
            whole((3, D)),
            whole((3, D)),
            whole((1, TOKENS)),
        ],
        out_specs=(
            rows(D),
            rows(FF),
            rows(FF),
            rows(D),
            rows(1),
            rows(D),
            whole((experts, slots, D)),
        ),
        out_shape=(
            full((TOKENS, D), BF16),
            full((TOKENS, FF), BF16),
            full((TOKENS, FF), BF16),
            full((TOKENS, D), BF16),
            full((TOKENS, 1)),
            full((TOKENS, D)),
            full((experts, slots, D), BF16),
        ),
        scratch_shapes=[
            pltpu.VMEM((SIDE, SIDE + WS, D), F32),
            pltpu.VMEM((TOKENS, D), F32),
            pltpu.VMEM((TOKENS, D), BF16),
        ],
        compiler_params=params(),
        name="forward",
    )(shifts, tokens, normed, up, up_bias, down, down_bias, gain, offset, slot_row)


def expert_kernel(
    buffer, cot, router, up, up_bias, down, down_bias, gain,
    out, grad_in, half,
    arrived, outs, grads, active, slope, up_grad, down_grad_t, up_bias_grad, down_bias_grad,
    packed, land, send, recv, *sum_sems,
):
    core = core_level()
    me = lax.axis_index("expert")
    count, slots, _ = buffer.shape
    others = range(1, count)

    def move(kind, step, source, target, to):
        return pltpu.make_async_remote_copy(
            src_ref=source,
            dst_ref=target,
            send_sem=send.at[kind, step],
            recv_sem=recv.at[kind, step],
            device_id={"expert": to},
            device_id_type=pl.DeviceIdType.MESH,
        )

    greet([{"expert": partner(me, step, count)} for step in others] + core.devices())
    for step in others:
        to = partner(me, step, count)
        move(0, step, buffer.at[to], arrived.at[step], to).start()
    arrived[0] = buffer[me]
    for ref in (up_grad, up_bias_grad, down_grad_t, down_bias_grad):
        ref[...] = jnp.zeros_like(ref)
    router_high, router_low = split(router[...])

    def work(step, carry):
        if count == 4:
            owner = lax.rem(lax.div(me, 2) + lax.div(step, 2), 2) * 2
            owner = owner + lax.rem(lax.rem(me, 2) + lax.rem(step, 2), 2)
        else:
            side = 1
            while side * side < count:
                side *= 2
            if side * side == count:
                owner = lax.rem(lax.div(me, side) + side - lax.div(step, side), side) * side
                owner = owner + lax.rem(lax.rem(me, side) + side - lax.rem(step, side), side)
            else:
                owner = lax.rem(me + count - step, count)

        @pl.when(step > 0)
        def _():
            move(0, step, buffer.at[owner], arrived.at[step], owner).wait_recv()

        features = arrived[step]
        logits = dot(features, router_high, 1, 1) + dot(features, router_low, 1, 1)
        chances = jnp.exp(logits - jnp.max(logits, axis=1, keepdims=True))
        own = jnp.where(iota(chances.shape, 1) == me, chances, 0.0)
        gate = jnp.sum(own, axis=1, keepdims=True) / jnp.sum(chances, axis=1, keepdims=True)

        output = jnp.zeros((slots, D), F32)
        for at in range(0, FF, CHUNK):
            hidden = dot(features, up[:, at : at + CHUNK], 1, 0) + up_bias[:, at : at + CHUNK]
            activated, derivative = gelu_pair(hidden)
            activated = activated.astype(BF16)
            active[:, at : at + CHUNK] = activated
            slope[:, at : at + CHUNK] = derivative
            output += dot(activated, down[at : at + CHUNK, :], 1, 0)
        output = (output + down_bias[...]).astype(BF16)
        outs[step] = output

        @pl.when(step > 0)
        def _():
            move(1, step, outs.at[step], out.at[me], owner).start()

        n, rstd = norm_parts(gate * output.astype(F32))
        grad_output = gate * norm_back(gain[2:3, :] * cot[owner].astype(F32), n, rstd)
        grad_low = grad_output.astype(BF16)
        down_bias_grad[...] += col_sum(grad_low.astype(F32))
        grad_low_t = jnp.transpose(grad_low, (1, 0))
        features_t = jnp.transpose(features, (1, 0))
        grad_features = jnp.zeros((slots, D), F32)
        for at in range(0, FF, CHUNK):
            part = slice(at, at + CHUNK)
            grad_hidden = dot(grad_low, down[part, :], 1, 1) * slope[:, part]
            grad_hidden_low = grad_hidden.astype(BF16)
            up_bias_grad[:, part] += col_sum(grad_hidden)
            down_grad_t[:, part] += dot(grad_low_t, active[:, part], 1, 0)
            up_grad[:, part] += dot(features_t, grad_hidden_low, 1, 0)
            grad_features += dot(grad_hidden_low, up[:, part], 1, 1)
        grads[step] = grad_features.astype(BF16)

        @pl.when(step > 0)
        def _():
            move(2, step, grads.at[step], grad_in.at[me], owner).start()

        return carry

    lax.fori_loop(0, count, work, 0)
    out[me] = outs[0]
    grad_in[me] = grads[0]
    pack_pair(packed, up_grad, down_grad_t)
    packed[2 * FF :, :] = jnp.zeros_like(packed[2 * FF :, :])
    tail = jnp.concatenate(
        [up_bias_grad[:, at : at + D] for at in range(0, FF, D)]
        + [down_bias_grad[...], jnp.zeros((11, D), F32)],
        axis=0,
    )
    packed[2 * FF : 2 * FF + 16, :] = tail.astype(BF16)
    scatter(core, packed, land, half, sum_sems, True)
    for step in others:
        to = partner(me, step, count)
        move(0, step, buffer.at[to], arrived.at[step], to).wait_send()
        for kind, source, target in ((1, outs, out), (2, grads, grad_in)):
            move(kind, step, source.at[step], target.at[me], to).wait()
    scatter(core, packed, land, half, sum_sems, False)


def pack_pair(packed, up_grad, down_grad_t):
    for block in range(FF // D):
        part = slice(block * D, (block + 1) * D)
        packed[part, :] = up_grad[:, part].astype(BF16)
        packed[FF + block * D : FF + (block + 1) * D, :] = jnp.transpose(
            down_grad_t[:, part].astype(BF16), (1, 0)
        )


def run_experts(buffer, cot, router, up, up_bias, down, down_bias, gain, packed_rows):
    count, slots, _ = buffer.shape
    blocks = (count, slots, D)
    return pl.pallas_call(
        expert_kernel,
        out_shape=(full(blocks, BF16), full(blocks, BF16), full((packed_rows // 2, D), BF16)),
        scratch_shapes=[
            pltpu.VMEM(blocks, BF16),
            pltpu.VMEM(blocks, BF16),
            pltpu.VMEM(blocks, BF16),
            pltpu.VMEM((slots, FF), BF16),
            pltpu.VMEM((slots, FF), F32),
            pltpu.VMEM((D, FF), F32),
            pltpu.VMEM((D, FF), F32),
            pltpu.VMEM((1, FF), F32),
            pltpu.VMEM((1, D), F32),
            pltpu.VMEM((packed_rows, D), BF16),
            pltpu.VMEM((packed_rows // 2, D), BF16),
            pltpu.SemaphoreType.DMA((3, count)),
            pltpu.SemaphoreType.DMA((3, count)),
            *pair_of_sems(),
        ],
        compiler_params=params(collective_id=1, has_side_effects=True),
        name="experts",
    )(buffer, cot, router, up, up_bias, down, down_bias, gain)


SMALL = (
    ("in_bias0", 1, D),
    ("in_bias1", 1, D),
    ("in_bias2", 1, D),
    ("out_bias", 1, D),
    ("up_bias", FF // D, D),
    ("down_bias", 1, D),
    ("gain", 3, D),
    ("offset", 3, D),
    ("table_one", 3, UNITS),
    ("table_two", HEADS, UNITS),
    ("scale0", 1, 128),
    ("scale1", 1, 128),
    ("scale2", 1, 128),
    ("router", 0, D),
)


def small_places(experts):
    places, at = {}, 0
    for name, rows, width in SMALL:
        rows = rows or experts
        places[name] = (at, rows, width)
        at += rows * (width // 128)
    return places, at


def put_lanes(ref, at, value):
    rows, width = value.shape
    for lane in range(0, width, 128):
        ref[at : at + rows, :] = value[:, lane : lane + 128]
        at += rows


def get_lanes(ref, at, rows, width):
    return jnp.concatenate(
        [ref[at + i * rows : at + (i + 1) * rows, :] for i in range(width // 128)], axis=1
    )


def put_small(ref, places, name, value):
    put_lanes(ref, places[name][0], value)


def get_small(ref, places, name):
    return get_lanes(ref, *places[name])


def values_back(table_grad, values_grad, heads):
    spread = spread_matrix(True).astype(BF16)
    for head in heads:
        high, low = split(table_grad[head % 4])
        flat = dot(high, spread, 1, 1) + dot(low, spread, 1, 1)
        flat = jnp.concatenate([flat, jnp.zeros((AREA, TABLE - 384), F32)], axis=1)
        total = jnp.zeros((16, TABLE), F32)
        for key_row in range(WS):
            line = flat[key_row * WS : (key_row + 1) * WS, :]
            line = jnp.concatenate([line, jnp.zeros((16 - WS, TABLE), F32)], axis=0)
            total += pltpu.roll(line, EXTENT * key_row, 1)
        total = pltpu.roll(total, 0, 1, stride=1, stride_axis=0)
        values_grad[head : head + 1, :] = col_sum(total)


def net_again(w1, b1, w2):
    f_row, f_col = (found[0:1, :] for found in offsets_row((8, TABLE), 1, -1.0))
    w1t = jnp.transpose(w1[...], (1, 0))
    b1t = jnp.transpose(row_of(b1), (1, 0))
    hidden, slope = gelu_pair(w1t[:, 0:1] * f_row + w1t[:, 1:2] * f_col + b1t[:, 0:1])
    chance = jax.nn.sigmoid(exact_dot(w2[...], hidden, 1, 0))
    return hidden, slope, 16.0 * chance * (1.0 - chance)


def net_back(values_grad, hidden, slope, chance_slope, w2):
    grad_pre = values_grad[:HEADS, :] * chance_slope[:HEADS, :]
    grad_hidden = exact_dot(w2[...], grad_pre, 0, 0) * slope[...].astype(F32)
    f_row, f_col = offsets_row((8, TABLE), 1, -1.0)
    kind = iota((8, TABLE), 0)
    factors = jnp.where(kind == 0, f_row, jnp.where(kind == 1, f_col, 1.0))
    return exact_dot(factors, grad_hidden, 1, 1)[:3, :], exact_dot(grad_pre, hidden[...].astype(F32), 1, 1)


class Sum:
    def __init__(self, levels, refs, source, result, scattered=0):
        count, fresh = len(levels), len(levels) - scattered
        lands, outs, refs = refs[:fresh], refs[fresh : 2 * fresh], refs[2 * fresh :]
        scatter_sems, gather_sems, local = refs[: 2 * fresh], refs[2 * fresh : -1], refs[-1]
        sources = [source] + list(outs)
        gather = Gather(levels, sources[-1], result, gather_sems, local)
        self.moves = [
            functools.partial(
                scatter, levels[scattered + i], sources[i], lands[i], outs[i],
                scatter_sems[2 * i : 2 * i + 2],
            )
            for i in range(fresh)
        ] + [functools.partial(gather.move, i) for i in reversed(range(count))]

    @staticmethod
    def scratch(rows, dtype, width, counts, scattered=0):
        lands, outs = [], []
        for count in counts[scattered:]:
            rows //= count
            lands.append(pltpu.VMEM(((count - 1) * rows, width), dtype))
            outs.append(pltpu.VMEM((rows, width), dtype))
        return (
            lands + outs + sems_of(counts[scattered:]) + sems_of(counts) + [pltpu.SemaphoreType.DMA(())]
        )

    def do(self, k):
        if 0 < k <= len(self.moves):
            self.moves[k - 1](False)
        if k < len(self.moves):
            self.moves[k](True)


class Line:
    def __init__(self, core, line, refs, source, result):
        self.core, self.line, self.source, self.result = core, line, source, result
        count = line.count
        self.share = source.shape[0] // count
        self.half = source.shape[0]
        self.core_sems, self.local, refs = refs[0:2], refs[2], refs[3:]
        self.held = source
        self.moves = []
        if count > 1:
            self.held, self.land, self.scatter_sems, self.gather_sems = (
                refs[0], refs[1], refs[2:4], refs[4:6]
            )
            self.moves += [functools.partial(self.scatter, t) for t in range(1, count)]
            self.moves += [functools.partial(self.gather, t) for t in range(1, count)]
        self.moves.append(self.swap)

    @staticmethod
    def scratch(rows, count):
        more = []
        if count > 1:
            more = [
                pltpu.VMEM((rows, D), BF16),
                pltpu.VMEM((2, count - 1, rows // count, D), BF16),
            ] + [pltpu.SemaphoreType.DMA((2, count - 1))] * 4
        return pair_of_sems() + [pltpu.SemaphoreType.DMA(())] + more

    def start(self):
        if self.line.count > 1:
            fetch = pltpu.make_async_copy(self.source, self.held, self.local)
            fetch.start()
            fetch.wait()

    def rows_of(self, ref, share, base=0):
        start = pl.multiple_of(base + share * self.share, 16)
        return ref.at[pl.ds(start, self.share)]

    def base(self):
        return self.core.index * self.half

    def copy(self, source, target, sems, way, t, to):
        return pltpu.make_async_remote_copy(
            src_ref=source,
            dst_ref=target,
            send_sem=sems[0].at[way, t - 1],
            recv_sem=sems[1].at[way, t - 1],
            device_id=self.line.device(to),
            device_id_type=pl.DeviceIdType.MESH,
        )

    def scatter(self, t, begin):
        count, index = self.line.count, self.line.index
        for way in range(2):
            place = (count - 1 - index) if way else index
            shares = lambda j: (count - 1 - j) if way else j
            to = index - 1 if way else index + 1
            sent = self.copy(
                self.rows_of(self.held, shares(count + place - t)),
                self.land.at[way, t - 1], self.scatter_sems, way, t, to,
            )

            @pl.when((place + 1 <= t) & (place < count - 1))
            def _():
                sent.start() if begin else sent.wait_send()

            if not begin:

                @pl.when((place <= t) & (place >= 1))
                def _():
                    share = shares(count + place - 1 - t)
                    self.copy(
                        self.rows_of(self.held, share), self.land.at[way, t - 1],
                        self.scatter_sems, way, t, to,
                    ).wait_recv()
                    mine = self.rows_of(self.held, share)
                    mine[...] = (
                        mine[...].astype(F32) + self.land[way, t - 1].astype(F32)
                    ).astype(BF16)

    def gather(self, t, begin):
        count, index = self.line.count, self.line.index
        own = self.rows_of(self.held, index)
        keep = pltpu.make_async_copy(own, self.rows_of(self.result, index, self.base()), self.local)
        for way in range(2):
            to = index - 1 if way else index + 1
            origin = index + (t - 1) if way else index - (t - 1)
            there = self.rows_of(self.result, origin, self.base())
            sent = self.copy(own if t == 1 else there, there, self.gather_sems, way, t, to)
            sends = (
                (index > 0) & (origin <= count - 1) if way else (index < count - 1) & (origin >= 0)
            )

            @pl.when(sends)
            def _():
                sent.start() if begin else sent.wait_send()

            if not begin:
                origin = index + t if way else index - t

                @pl.when(origin <= count - 1 if way else origin >= 0)
                def _():
                    there = self.rows_of(self.result, origin, self.base())
                    self.copy(there, there, self.gather_sems, way, t, to).wait_recv()

        if t == 1:
            keep.start() if begin else keep.wait()

    def swap(self, begin):
        mine = self.result.at[pl.ds(pl.multiple_of(self.base(), 16), self.half)]
        alone = self.line.count == 1
        copy = pltpu.make_async_remote_copy(
            src_ref=self.source if alone else mine,
            dst_ref=mine,
            send_sem=self.core_sems[0],
            recv_sem=self.core_sems[1],
            device_id=self.core.devices()[0],
            device_id_type=pl.DeviceIdType.MESH,
        )
        copy.start() if begin else copy.wait()
        if alone:
            keep = pltpu.make_async_copy(self.source, mine, self.local)
            keep.start() if begin else keep.wait()

    def do(self, k):
        if 0 < k <= len(self.moves):
            self.moves[k - 1](False)
        if k < len(self.moves):
            self.moves[k](True)


PART_A = TOKENS // ROWS
PART_B = FF // D
PART_C = GROUPS * ACROSS
TRIPLE = WINDOWS // ACROSS
STARTS = {
    0: [("own", 0)],
    2: [("own", 1)],
    4: [("own", 2)],
    8: [("first", 3)],
    9: [("first", 4), ("rest", 2)],
    10: [("rest", 3)],
    11: [("rest", 4), ("own", 3)],
    12: [("first", 5)],
    13: [("first", 6), ("own", 4)],
    14: [("rest", 5), ("early", 1)],
    15: [("rest", 6), ("early", 2), ("own", 5)],
}
ENDS = {4: [("first", 0)], 5: [("first", 1)], 6: [("rest", 0)], 12: [("early", 0)]}
MIDDLE = [("rest", 1)], [("first", 2)]
SUMS = ("own", "first", "rest", "early", "late", "small")


def head_places(early, late):
    return (early, 0), (early, 4 * D), (late, 0)


def backward_kernel(
    places, sizes,
    shifts, scale, second, cot, slot_col, n_one, rstd_one, outputs, grads, router,
    first_low, active, slope, up, down, gain, offset, half,
    n_zero, rstd_zero, joint, probs, mixture, win_t, inverse, in_q, in_k, in_v, out_weight,
    w1, b1, w2,
    result, tokens_grad, own_sum, first_sum, rest_sum, early_sum, late_sum, small_sum,
    flat, grad_low_all, grad_low_t, first_t, grad_hidden_all, total, dense,
    doubled, windows, grad_mix, joint_grad, grads_f32, in_grad, out_grad, early, late,
    table_grad, values_grad, hidden_net, slope_net, chance_net,
    small, up_bias_grad, down_bias_grad, router_grad, gain_grad, offset_grad, out_bias_grad,
    in_bias_grad, scale_grad,
    *refs,
):
    step = pl.program_id(0)
    shift_row, shift_col = shifts[0, 0], shifts[0, 1]
    core, plane, depth = core_level(), plane_level(), depth_level()
    deep = [depth] if depth.count > 1 else []
    levels = [core, plane] + deep
    sums = {}
    dense_half = dense.shape[0] // 2
    first = dense.at[pl.ds(0, dense_half)]
    rest = dense.at[pl.ds(dense_half, dense_half)]
    sources = (half, first, rest, early, late, small)
    results = (own_sum, first_sum, rest_sum, early_sum, late_sum, small_sum)
    for name, source, target, size in zip(SUMS, sources, results, sizes):
        mine, refs = refs[:size], refs[size:]
        if name == "own":
            sums[name] = Line(core, depth, mine, source, target)
        else:
            sums[name] = Sum(levels, mine, source, target)

    def at(place, action):
        pl.when(step == place)(action)

    def moves(plan):
        for place, work in plan.items():

            def action(work=work):
                for name, k in work:
                    sums[name].do(k)

            at(place, action)

    @functools.partial(at, 0)
    def _():
        greet([device for level in levels for device in level.devices()])
        for ref in (
            router_grad, gain_grad, offset_grad, down_bias_grad, out_bias_grad, out_grad,
            scale_grad, small,
        ):
            ref[...] = jnp.zeros_like(ref)
        for ref, used in ((first, 12 * D), (rest, 12 * D), (early, 8 * D), (late, 4 * D)):
            if ref.shape[0] > used:
                ref[used:, :] = jnp.zeros_like(ref[used:, :])
        sums["own"].start()

    moves(STARTS)

    @pl.when(step < PART_A)
    def _():
        lines = ROWS // SIDE
        for line in range(lines):
            flat[line * SIDE : (line + 1) * SIDE, :] = cot[line].astype(F32)
        z = flat[...]
        x = second[...]
        slots_all = outputs.shape[0]
        pick = (slot_col[...] == iota((ROWS, slots_all), 1)).astype(BF16)
        picked = dot(pick, outputs[...], 1, 0)
        dispatched = dot(pick, grads[...], 1, 0)

        logits = exact_dot(x, router[...], 1, 1)
        chances = jnp.exp(logits - jnp.max(logits, axis=1, keepdims=True))
        chances = chances / jnp.sum(chances, axis=1, keepdims=True)
        slots = slots_all // chances.shape[1]
        within = slot_col[...] - iota(chances.shape, 1) * slots
        onehot = ((within >= 0) & (within < slots)).astype(F32)
        gate = jnp.sum(chances * onehot, axis=1, keepdims=True)
        n, rstd = norm_parts(gate * picked)
        final = x + n * gain[2:3, :] + offset[2:3, :]
        gain_grad[2:3, :] += col_sum(z * n)
        offset_grad[2:3, :] += col_sum(z)
        grad_moe = norm_back(gain[2:3, :] * z, n, rstd)
        grad_gate = jnp.sum(grad_moe * picked, axis=1, keepdims=True)
        grad_logits = grad_gate * gate * (onehot - chances)
        grad_logits_low = grad_logits.astype(BF16)
        router_grad[...] += dot(grad_logits_low, x.astype(BF16), 0, 0)
        grad_second = z + dispatched + dot(grad_logits_low, router[...].astype(BF16), 1, 0)

        n = n_one[...].astype(F32)
        gain_grad[1:2, :] += col_sum(grad_second * n)
        offset_grad[1:2, :] += col_sum(grad_second)
        grad_branch = norm_back(gain[1:2, :] * grad_second, n, rstd_one[...])
        rows = pl.ds(pl.multiple_of(step * ROWS, 16), ROWS)
        grad_low_all[rows, :] = grad_branch.astype(BF16)
        down_bias_grad[...] += col_sum(grad_branch)
        total[rows, :] = grad_second
        flat[...] = final
        for line in range(lines):
            result[line] = flat[line * SIDE : (line + 1) * SIDE, :].astype(BF16)

    @functools.partial(at, PART_A)
    def _():
        grad_low_t[...] = jnp.transpose(grad_low_all[...], (1, 0))
        first_t[...] = jnp.transpose(first_low[...], (1, 0))

    @pl.when((step >= PART_A) & (step < PART_A + PART_B))
    def _():
        bias_row = jnp.zeros((1, D), F32)
        for tile in range(TOKENS // ROWS):
            rows = slice(tile * ROWS, (tile + 1) * ROWS)
            grad_hidden = dot(grad_low_all[rows, :], down[...], 1, 1) * slope[rows, :].astype(F32)
            bias_row += col_sum(grad_hidden)
            grad_hidden_low = grad_hidden.astype(BF16)
            grad_hidden_all[rows, :] = grad_hidden_low
            total[rows, :] += dot(grad_hidden_low, up[...], 1, 1)
        up_bias_grad[pl.ds(step - PART_A, 1), :] = bias_row
        up_part = dot(first_t[...], grad_hidden_all[...], 1, 0).astype(BF16)
        down_part = jnp.transpose(
            dot(grad_low_t[...], active[...], 1, 0).astype(BF16), (1, 0)
        )
        for block in range(PART_B):

            def place(block=block):
                start = (block // 2) * dense_half + (block % 2) * 6 * D
                put_lanes(dense, start, up_part)
                put_lanes(dense, start + 3 * D, down_part)

            at(PART_A + block, place)

    @functools.partial(at, PART_A + PART_B)
    def _():
        hidden, net_slope, chance = net_again(w1, b1, w2)
        hidden_net[...] = hidden.astype(BF16)
        slope_net[...] = net_slope.astype(BF16)
        chance_net[:HEADS, :] = chance
        for name, k in MIDDLE[0]:
            sums[name].do(k)
        roll_to_windows(
            lambda row: total[row * SIDE : (row + 1) * SIDE, :],
            doubled, windows, shift_row, shift_col,
        )

        for name, k in MIDDLE[1]:
            sums[name].do(k)

        def one(window, carry):
            mine = pl.ds(pl.multiple_of(window * AREA, 16), AREA)
            z = windows[mine, :]
            n = n_zero[mine, :].astype(F32)
            gain_grad[0:1, :] += col_sum(z * n)
            offset_grad[0:1, :] += col_sum(z)
            grad_branch = norm_back(gain[0:1, :] * z, n, rstd_zero[mine, :])
            grad_low = grad_branch.astype(BF16)
            out_bias_grad[...] += col_sum(grad_branch)
            out_grad[...] += dot(mixture[window], grad_low, 1, 0)
            grad_mix[window] = dot(out_weight[...], grad_low, 1, 1).astype(BF16)
            return carry

        lax.fori_loop(0, WINDOWS, one, 0)
        for group, (into, start) in enumerate(head_places(early, late)):
            put_lanes(into, start + 3 * D, out_grad[group * 128 : (group + 1) * 128, :].astype(BF16))

    @pl.when(step >= PART_A + PART_B)
    def _():
        place = step - (PART_A + PART_B)
        group = lax.div(place, ACROSS)
        third = lax.rem(place, ACROSS)
        blank = jnp.zeros((HEAD, AREA), BF16)
        features = pl.ds(pl.multiple_of(group * 128, 128), 128)
        in_part = jnp.concatenate([in_q[...], in_k[...], in_v[...]], axis=1)

        @pl.when(third == 0)
        def _():
            in_grad[...] = jnp.zeros_like(in_grad)
            table_grad[...] = jnp.zeros_like(table_grad)

        def probs_grads(i):
            lanes = jnp.transpose(joint[i, 0, 256:384, :], (1, 0))
            coming = grad_mix[third * TRIPLE + i, features, :]
            found = []
            for head in range(4):
                parts = [blank] * 4
                parts[head] = coming[head * HEAD : (head + 1) * HEAD, :]
                found.append(dot(lanes, jnp.concatenate(parts, axis=0), 1, 0))
            return found, coming

        ahead = probs_grads(0)
        for i in range(TRIPLE):
            current, coming = ahead
            if i + 1 < TRIPLE:
                ahead = probs_grads(i + 1)
            raws = []
            for head in range(4):
                weight = probs[i, head].astype(F32)
                weighted = weight * current[head]
                grad_scores = weighted - weight * (col_sum(weighted) / col_sum(weight))
                table_grad[head] += grad_scores
                raws.append((grad_scores * scale[0, group * 4 + head]).astype(BF16))
            for head in range(4):
                own = slice(head * HEAD, (head + 1) * HEAD)
                keys = slice(128 + head * HEAD, 128 + (head + 1) * HEAD)
                grads_f32[own, :] = dot(joint[i, 0, keys, :], raws[head], 1, 0)
                grads_f32[keys, :] = dot(joint[i, 0, own, :], raws[head], 1, 1)
                joint_grad[256 + head * HEAD : 256 + (head + 1) * HEAD, :] = dot(
                    coming[own, :], probs[i, head], 1, 1
                ).astype(BF16)
            shaped = grads_f32[...].reshape(8, HEAD, AREA)
            unit = joint[i, 0, :256, :].astype(F32).reshape(8, HEAD, AREA)
            inner = jnp.sum(unit * shaped, axis=1, keepdims=True)
            shaped = shaped - unit * inner
            for part in range(8):
                joint_grad[part * HEAD : (part + 1) * HEAD, :] = (
                    shaped[part] * inverse[i, 0, part : part + 1, :]
                ).astype(BF16)
                if part < 4:
                    scale_grad[group, part : part + 1, :] += inner[part]
            joint_rows = jnp.transpose(joint_grad[...], (1, 0))
            in_grad[...] += dot(win_t[i], joint_rows, 1, 0)
            grad_window = dot(joint_rows, in_part, 1, 1)
            mine = pl.ds(pl.multiple_of((third * TRIPLE + i) * AREA, 16), AREA)
            kept = jnp.where(group == 0, 0.0, 1.0)
            windows[mine, :] = windows[mine, :] * kept + grad_window

    for group, (into, start) in enumerate(head_places(early, late)):

        def group_end(group=group, into=into, start=start):
            put_lanes(into, start, in_grad[:D, :].astype(BF16))
            in_bias_grad[group : group + 1, :] = in_grad[D : D + 1, :]

        at(PART_A + PART_B + (group + 1) * ACROSS - 1, group_end)
    moves(ENDS)
    for group in range(GROUPS - 1):
        heads = range(group * 4, group * 4 + 4)
        at(
            PART_A + PART_B + (group + 1) * ACROSS - 1,
            functools.partial(values_back, table_grad, values_grad, heads),
        )

    @functools.partial(at, PART_A + PART_B + PART_C - 1)
    def _():
        sums["late"].do(0)
        values_back(table_grad, values_grad, range(8, HEADS))
        sums["late"].do(1)
        table_one, table_two = net_back(values_grad, hidden_net, slope_net, chance_net, w2)
        put = functools.partial(put_small, small, places)
        put("table_one", table_one)
        put("table_two", table_two)
        for group in range(GROUPS):
            row = exact_dot(jnp.ones((8, AREA), F32), scale_grad[group], 1, 1)[0:1, :]
            put("scale%d" % group, jnp.concatenate([row, jnp.zeros((1, 120), F32)], axis=1))
            put("in_bias%d" % group, in_bias_grad[group : group + 1, :])
        put("out_bias", out_bias_grad[...])
        put("up_bias", up_bias_grad[...])
        put("down_bias", down_bias_grad[...])
        put("gain", gain_grad[...])
        put("offset", offset_grad[...])
        put("router", router_grad[...])
        sums["early"].do(3)
        sums["small"].do(0)
        sums["late"].do(2)
        sums["early"].do(4)
        sums["small"].do(1)

        def write_row(row, line):
            line = line + total[row * SIDE : (row + 1) * SIDE, :]
            for lane in range(D // 128):
                tokens_grad[pl.ds(row * SIDE * (D // 128) + lane, SIDE, stride=D // 128), :] = line[
                    :, lane * 128 : (lane + 1) * 128
                ]

        roll_to_image(windows, doubled, write_row, shift_row, shift_col)
        for k in range(2, 7):
            sums["small"].do(k)
            sums["late"].do(k + 1)
            if k < 4:
                sums["early"].do(k + 3)
            if k == 3:
                sums["own"].do(6)
        for k in range(7, len(sums["own"].moves) + 1):
            sums["own"].do(k)


def backward(
    small_rows, experts, shifts, scale, second, cot, slot_col, n_one, rstd_one, outputs, grads,
    router, first_low, active, slope, up, down, gain, offset, half,
    n_zero, rstd_zero, joint, probs, mixture, win_t, inverse, in_weight, out_weight, w1, b1, w2,
):
    places, _ = small_places(experts)
    group, depth = lax.axis_size("expert"), lax.axis_size("dp") // 2
    counts = [2, group] + ([depth] if depth > 1 else [])
    dense_rows = padded_rows(12 * D, counts, 16)
    early_rows = padded_rows(8 * D, counts, 16)
    last_rows = padded_rows(4 * D, counts, 16)
    sum_scratch = [Line.scratch(half.shape[0], depth)]
    for rows_of in (dense_rows, dense_rows, early_rows, last_rows):
        sum_scratch += [Sum.scratch(rows_of, BF16, 128, counts)]
    sum_scratch += [Sum.scratch(small_rows, F32, 128, counts)]

    part_a = lambda i: jnp.minimum(i, PART_A - 1)
    part_b = lambda i: jnp.clip(i - PART_A, 0, PART_B - 1)
    part_c = lambda i: jnp.maximum(i - PART_A - PART_B, 0)
    third = lambda i: lax.rem(part_c(i), ACROSS)
    heads = lambda i: lax.div(part_c(i), ACROSS)
    rows = lambda width: pl.BlockSpec((ROWS, width), lambda i: (part_a(i), 0))
    lines = pl.BlockSpec((ROWS // SIDE, SIDE, D), lambda i: (part_a(i), 0, 0))
    hidden = pl.BlockSpec((TOKENS, D), lambda i: (0, part_b(i)))
    in_third = lambda j: pl.BlockSpec((D, 128), lambda i: (0, j * GROUPS + heads(i)))
    anywhere = pl.BlockSpec(memory_space=pl.ANY)
    once = lambda shape: pl.BlockSpec(
        shape, lambda *_: (0,) * len(shape), pipeline_mode=pl.Buffered(1)
    )
    return pl.pallas_call(
        functools.partial(backward_kernel, places, [len(part) for part in sum_scratch]),
        grid=(PART_A + PART_B + PART_C,),
        in_specs=[
            smem(),
            smem(),
            rows(D),
            lines,
            rows(1),
            rows(D),
            rows(1),
            once(outputs.shape),
            once(grads.shape),
            once(router.shape),
            once((TOKENS, D)),
            hidden,
            hidden,
            pl.BlockSpec((D, D), lambda i: (0, part_b(i))),
            pl.BlockSpec((D, D), lambda i: (part_b(i), 0)),
            once((3, D)),
            once((3, D)),
            anywhere,
            once((TOKENS, D)),
            once((TOKENS, 1)),
            pl.BlockSpec((TRIPLE, 1, D, AREA), lambda i: (third(i), heads(i), 0, 0)),
            pl.BlockSpec((TRIPLE, 4, AREA, AREA), lambda i: (third(i), heads(i), 0, 0)),
            once((WINDOWS, D, AREA)),
            pl.BlockSpec((TRIPLE, D + 16, AREA), lambda i: (third(i), 0, 0)),
            pl.BlockSpec((TRIPLE, 1, 8, AREA), lambda i: (third(i), heads(i), 0, 0)),
            in_third(0),
            in_third(1),
            in_third(2),
            once((D, D)),
            once(w1.shape),
            once(b1.shape),
            once(w2.shape),
        ],
        out_specs=(lines, whole((TOKENS * D // 128, 128))) + (anywhere,) * 6,
        out_shape=(
            full((SIDE, SIDE, D), BF16),
            full((TOKENS * D // 128, 128)),
            full((2 * half.shape[0], D), BF16),
            full((dense_rows, 128), BF16),
            full((dense_rows, 128), BF16),
            full((early_rows, 128), BF16),
            full((last_rows, 128), BF16),
            full((small_rows, 128)),
        ),
        scratch_shapes=[
            pltpu.VMEM((ROWS, D), F32),
            pltpu.VMEM((TOKENS, D), BF16),
            pltpu.VMEM((D, TOKENS), BF16),
            pltpu.VMEM((D, TOKENS), BF16),
            pltpu.VMEM((TOKENS, D), BF16),
            pltpu.VMEM((TOKENS, D), F32),
            pltpu.VMEM((2 * dense_rows, 128), BF16),
            pltpu.VMEM((SIDE, SIDE + WS, D), F32),
            pltpu.VMEM((TOKENS, D), F32),
            pltpu.VMEM((WINDOWS, D, AREA), BF16),
            pltpu.VMEM((D, AREA), BF16),
            pltpu.VMEM((256, AREA), F32),
            pltpu.VMEM((D + 16, D), F32),
            pltpu.VMEM((D, D), F32),
            pltpu.VMEM((early_rows, 128), BF16),
            pltpu.VMEM((last_rows, 128), BF16),
            pltpu.VMEM((4, AREA, AREA), F32),
            pltpu.VMEM((16, TABLE), F32),
            pltpu.VMEM((UNITS, TABLE), BF16),
            pltpu.VMEM((UNITS, TABLE), BF16),
            pltpu.VMEM((16, TABLE), F32),
            pltpu.VMEM((small_rows, 128), F32),
            pltpu.VMEM((PART_B, D), F32),
            pltpu.VMEM((1, D), F32),
            pltpu.VMEM(router.shape, F32),
            pltpu.VMEM((3, D), F32),
            pltpu.VMEM((3, D), F32),
            pltpu.VMEM((1, D), F32),
            pltpu.VMEM((GROUPS, D), F32),
            pltpu.VMEM((GROUPS, 8, AREA), F32),
        ]
        + [ref for part in sum_scratch for ref in part],
        compiler_params=params(collective_id=2, has_side_effects=True),
        name="backward",
    )(
        shifts, scale, second, cot, slot_col, n_one, rstd_one, outputs, grads, router,
        first_low, active, slope, up, down, gain, offset, half,
        n_zero, rstd_zero, joint, probs, mixture, win_t, inverse,
        in_weight, in_weight, in_weight, out_weight, w1, b1, w2,
    )


def unpack_kernel(
    places, own, first, rest, early, late, small,
    in_grad, in_bias, scale, table_first, table_first_bias, table_second, out_grad, out_bias,
    up_grad, up_bias, down_grad, down_bias, router, own_up, own_up_bias, own_down, own_down_bias,
    gain, offset,
):
    get = functools.partial(get_small, small, places)
    scales = []
    for group, (source, start) in enumerate(head_places(early, late)):
        row = get("in_bias%d" % group)
        for third in range(3):
            lanes = slice(third * D + group * 128, third * D + (group + 1) * 128)
            at = start + third * D
            in_grad[:, lanes] = source[at : at + D, :].astype(F32)
        part = get_lanes(source, start + 3 * D, 128, D)
        out_grad[group * 128 : (group + 1) * 128, :] = part.astype(F32)
        in_bias[0:1, group * 128 : (group + 1) * 128] = row[:, 0:128]
        in_bias[1:2, group * 128 : (group + 1) * 128] = row[:, 256:384]
        scales.append(get("scale%d" % group)[:, :4])
    scale[...] = jnp.concatenate(scales, axis=1).reshape(HEADS)
    for block in range(FF // D):
        part = slice(block * D, (block + 1) * D)
        dense, start = (first, rest)[block // 2], (block % 2) * 6 * D
        up_grad[:, part] = get_lanes(dense, start, D, D).astype(F32)
        down_grad[part, :] = get_lanes(dense, start + 3 * D, D, D).astype(F32)
        own_up[:, part] = own[part, :].astype(F32)
        own_down[part, :] = own[FF + block * D : FF + (block + 1) * D, :].astype(F32)
    tail = own[2 * FF : 2 * FF + 16, :].astype(F32)
    up_rows = get("up_bias")
    for block in range(FF // D):
        own_up_bias[:, block * D : (block + 1) * D] = tail[block : block + 1, :]
    own_down_bias[...] = tail[FF // D : FF // D + 1, :]
    up_bias[...] = jnp.concatenate(
        [up_rows[block : block + 1, :] for block in range(FF // D)], axis=1
    ).reshape(FF)
    one = get("table_one")
    table_first[...] = one[0:2, :]
    table_first_bias[...] = one[2:3, :].reshape(UNITS)
    table_second[...] = get("table_two")
    out_bias[...] = get("out_bias").reshape(D)
    down_bias[...] = get("down_bias").reshape(D)
    router[...] = get("router")
    gain[...] = get("gain")
    offset[...] = get("offset")


def unpack(parts, experts):
    places, _ = small_places(experts)
    return pl.pallas_call(
        functools.partial(unpack_kernel, places),
        out_shape=(
            full((D, 3 * D)),
            full((2, D)),
            full((HEADS,)),
            full((2, UNITS)),
            full((UNITS,)),
            full((HEADS, UNITS)),
            full((D, D)),
            full((D,)),
            full((D, FF)),
            full((FF,)),
            full((FF, D)),
            full((D,)),
            full((experts, D)),
            full((D, FF)),
            full((1, FF)),
            full((FF, D)),
            full((1, D)),
            full((3, D)),
            full((3, D)),
        ),
        compiler_params=params(),
        name="unpack",
    )(*parts)


def per_device(
    tokens, shifts, routes, cotangent, in_weight, in_bias, logit_scale,
    bias_net_first_weight, bias_net_first_bias, bias_net_second_weight,
    out_weight, out_bias, up_weight, up_bias, down_weight, down_bias, router_weight,
    expert_up, expert_up_bias, expert_down, expert_down_bias, norm_gain, norm_bias,
):
    experts = router_weight.shape[1]
    dp = lax.axis_size("dp")
    group = lax.axis_size("expert")
    capacity = (5 * TOKENS + 4 * experts - 1) // (4 * experts)
    slots = -(-capacity // 16) * 16
    own_rows = padded_rows(2 * FF + 16, [2, dp // 2], 16)
    small_rows = padded_rows(small_places(experts)[1], [2, group, dp // 2], 8)

    picture = tokens.reshape(SIDE, SIDE, D)
    cot = cotangent.reshape(SIDE, SIDE, D)
    router_t = router_weight.T
    second_t = bias_net_second_weight.T

    slot_col, slot_row, cot_slots, table, scale = prep(
        routes.reshape(1, TOKENS), cot, bias_net_first_weight, bias_net_first_bias, second_t,
        logit_scale, experts, capacity, slots,
    )
    cot_arrived, normed, n_zero, rstd_zero, joint, probs, mixture, win_t, inverse = attend(
        cot_slots, shifts, scale, picture, in_weight, in_bias, table,
        out_weight, out_bias, norm_gain, norm_bias,
    )
    first_low, active, slope, n_one, rstd_one, second, buffer = forward(
        shifts, picture, normed, up_weight, up_bias, down_weight,
        down_bias, norm_gain, norm_bias, slot_row, experts, slots,
    )
    returned, grad_returned, own_half = run_experts(
        buffer, cot_arrived, router_t, expert_up[0], expert_up_bias, expert_down[0],
        expert_down_bias, norm_gain, own_rows,
    )
    result, tokens_grad, *parts = backward(
        small_rows, experts, shifts, scale, second, cot, slot_col, n_one, rstd_one,
        returned.reshape(-1, D), grad_returned.reshape(-1, D), router_t, first_low, active, slope,
        up_weight, down_weight, norm_gain, norm_bias, own_half,
        n_zero, rstd_zero, joint, probs, mixture, win_t, inverse, in_weight, out_weight,
        bias_net_first_weight, bias_net_first_bias, second_t,
    )
    (
        in_weight_grad, in_bias_grad, scale_grad, table_one, table_bias, table_two, out_grad,
        out_bias_grad, up_grad, up_bias_grad, down_grad, down_bias_grad, router_grad,
        own_up, own_up_bias, own_down, own_down_bias, gain_grad, offset_grad,
    ) = unpack(parts, experts)
    return (
        result.reshape(tokens.shape),
        tokens_grad.reshape(tokens.shape),
        in_weight_grad,
        in_bias_grad,
        scale_grad,
        table_one,
        table_bias,
        table_two.T,
        out_grad,
        out_bias_grad,
        up_grad,
        up_bias_grad,
        down_grad,
        down_bias_grad,
        router_grad.T,
        own_up[None],
        own_up_bias,
        own_down[None],
        own_down_bias,
        gain_grad,
        offset_grad,
    )


def solution(mesh):
    split_all = P(("dp", "expert"))
    placed = (split_all,) * 4 + (P(),) * 13 + (P("expert"),) * 4 + (P(),) * 2
    return jax.shard_map(
        per_device,
        mesh=mesh,
        in_specs=placed,
        out_specs=(split_all,) * 2 + (P(),) * 13 + (P("expert"),) * 4 + (P(),) * 2,
        check_vma=False,
    )
```

```python
import functools

import jax
import jax.numpy as jnp
from jax import lax
from jax.experimental import pallas as pl
from jax.experimental.pallas import tpu as pltpu
from jax.sharding import PartitionSpec as P

D = 384
HEADS = 12
HEAD = D // HEADS
WS = 12
SIDE = 36
AREA = WS * WS
ACROSS = SIDE // WS
WINDOWS = ACROSS * ACROSS
TOKENS = SIDE * SIDE
FF = 1536
EXTENT = 2 * WS - 1
UNITS = 512
GROUPS = 3
TABLE = 640
ROWS = 432
CHUNK = 256
F32 = jnp.float32
BF16 = jnp.bfloat16
I32 = jnp.int32
VMEM_LIMIT = 63 * 1024 * 1024


def dot(left, right, left_dim, right_dim):
    return lax.dot_general(
        left, right, (((left_dim,), (right_dim,)), ((), ())), preferred_element_type=F32
    )


def exact_dot(left, right, left_dim, right_dim):
    return lax.dot_general(
        left,
        right,
        (((left_dim,), (right_dim,)), ((), ())),
        preferred_element_type=F32,
        precision=lax.Precision.HIGHEST,
    )


def split(values):
    high = values.astype(BF16)
    return high, (values - high.astype(F32)).astype(BF16)


def iota(shape, dim):
    return lax.broadcasted_iota(I32, shape, dim)


def gelu_pair(values):
    size = jnp.abs(values)
    t = 1.0 / (1.0 + 0.2316419 * size)
    bell = jnp.exp(-0.5 * values * values) * 0.3989422804014327
    series = t * (
        0.319381530
        + t * (-0.356563782 + t * (1.781477937 + t * (-1.821255978 + t * 1.330274429)))
    )
    tail = series * bell
    phi = jnp.where(values >= 0.0, 1.0 - tail, tail)
    return values * phi, phi + values * bell


def norm_parts(values):
    centered = values - jnp.mean(values, axis=-1, keepdims=True)
    rstd = lax.rsqrt(jnp.mean(centered * centered, axis=-1, keepdims=True) + 1e-05)
    return centered * rstd, rstd


def norm_back(grad_n, n, rstd):
    return rstd * (
        grad_n
        - jnp.mean(grad_n, axis=-1, keepdims=True)
        - n * jnp.mean(grad_n * n, axis=-1, keepdims=True)
    )


def row_of(ref):
    return ref[...].reshape(1, ref.shape[0])


def col_sum(values):
    return jnp.sum(values, axis=0, keepdims=True)


def div_ws(values):
    return (values * 171) >> 11


def full(shape, dtype=F32):
    return jax.ShapeDtypeStruct(shape, dtype)


def whole(shape):
    return pl.BlockSpec(shape, lambda *_: (0,) * len(shape))


def smem():
    return pl.BlockSpec(memory_space=pltpu.SMEM)


def params(**more):
    return pltpu.CompilerParams(vmem_limit_bytes=VMEM_LIMIT, **more)


def partner(me, step, count):
    side = 1
    while side * side < count:
        side *= 2
    if side * side != count:
        return lax.rem(me + step, count)
    row = lax.rem(lax.div(me, side) + step // side, side)
    col = lax.rem(lax.rem(me, side) + step % side, side)
    return row * side + col


def opposite(step, count):
    side = 1
    while side * side < count:
        side *= 2
    if side * side != count:
        return (count - step) % count
    return ((side - step // side) % side) * side + (side - step % side) % side


def greet(devices):
    barrier = pltpu.get_barrier_semaphore()
    for device in devices:
        pl.semaphore_signal(barrier, inc=1, device_id=device, device_id_type=pl.DeviceIdType.MESH)
    pl.semaphore_wait(barrier, len(devices))


class Level:
    def __init__(self, count, index, device):
        self.count, self.index, self.device = count, index, device

    def others(self):
        return [lax.rem(self.index + step, self.count) for step in range(1, self.count)]

    def devices(self):
        return [self.device(to) for to in self.others()]


def core_level():
    place = lax.div(lax.axis_index("dp"), 2)
    return Level(2, lax.rem(lax.axis_index("dp"), 2), lambda j: {"dp": place * 2 + j})


def plane_level():
    return Level(lax.axis_size("expert"), lax.axis_index("expert"), lambda j: {"expert": j})


def depth_level():
    core = lax.rem(lax.axis_index("dp"), 2)
    place = lax.div(lax.axis_index("dp"), 2)
    return Level(lax.axis_size("dp") // 2, place, lambda j: {"dp": j * 2 + core})


def padded_rows(rows, counts, tile):
    unit = tile
    for count in counts:
        unit *= count
    return -(-rows // unit) * unit


def pair_of_sems():
    return [pltpu.SemaphoreType.DMA(()), pltpu.SemaphoreType.DMA(())]


def wait_all(sent, received, sems, level):
    copy = pltpu.make_async_remote_copy(
        src_ref=sent,
        dst_ref=received,
        send_sem=sems[0],
        recv_sem=sems[1],
        device_id=level.device(level.others()[0]),
        device_id_type=pl.DeviceIdType.MESH,
    )
    copy.wait()


def scatter(level, source, land, out, sems, begin):
    rows = source.shape[0] // level.count
    tile = 16 if source.dtype == BF16 else 8
    if begin:
        for step, to in enumerate(level.others(), 1):
            pltpu.make_async_remote_copy(
                src_ref=source.at[pl.ds(pl.multiple_of(to * rows, tile), rows)],
                dst_ref=land.at[pl.ds((step - 1) * rows, rows)],
                send_sem=sems[0],
                recv_sem=sems[1],
                device_id=level.device(to),
                device_id_type=pl.DeviceIdType.MESH,
            ).start()
        return
    wait_all(source.at[pl.ds(0, land.shape[0])], land, sems, level)
    mine = level.index * rows
    chunk = tile
    while rows % (chunk * 2) == 0 and chunk < 128:
        chunk *= 2

    def add(i, carry):
        here = pl.ds(pl.multiple_of(i * chunk, tile), chunk)
        total = source[pl.ds(pl.multiple_of(mine + i * chunk, tile), chunk), :].astype(F32)
        for step in range(1, level.count):
            total = total + land[
                pl.ds(pl.multiple_of((step - 1) * rows + i * chunk, tile), chunk), :
            ].astype(F32)
        out[here, :] = total.astype(out.dtype)
        return carry

    lax.fori_loop(0, rows // chunk, add, 0)


class Gather:
    def __init__(self, levels, piece, result, sems, local):
        self.levels, self.piece, self.result, self.sems = levels, piece, result, sems
        rows, start = result.shape[0], 0
        self.regions = []
        for level in levels:
            rows //= level.count
            start = start + level.index * rows
            self.regions.append((start, rows))
        self.keep = pltpu.make_async_copy(piece, self.region(len(levels) - 1), local)

    def region(self, at):
        start, rows = self.regions[at]
        return self.result.at[pl.ds(pl.multiple_of(start, 8), rows)]

    def move(self, at, begin):
        level, last = self.levels[at], at == len(self.levels) - 1
        mine = self.region(at)
        sems = self.sems[2 * at : 2 * at + 2]
        if begin:
            for to in level.others():
                pltpu.make_async_remote_copy(
                    src_ref=self.piece if last else mine,
                    dst_ref=mine,
                    send_sem=sems[0],
                    recv_sem=sems[1],
                    device_id=level.device(to),
                    device_id_type=pl.DeviceIdType.MESH,
                ).start()
        else:
            some = self.result.at[pl.ds(0, (level.count - 1) * self.regions[at][1])]
            wait_all(some, some, sems, level)
        if last:
            self.keep.start() if begin else self.keep.wait()


def sems_of(levels):
    return [sem for _ in levels for sem in pair_of_sems()]


def offsets_row(shape, dim, sign):
    place = iota(shape, dim)
    row = jnp.floor((place.astype(F32) + 0.5) * (1.0 / EXTENT)).astype(I32)
    col = place - row * EXTENT

    def logged(step):
        e = sign * (step - (WS - 1)).astype(F32) * (8.0 / (WS - 1))
        size = jnp.log2(jnp.abs(e) + 1.0) * (1.0 / 3.0)
        return jnp.where(e < 0.0, -size, size)

    return logged(row), logged(col)


def spread_matrix(mirrored):
    token = iota((384, AREA), 1)
    row = div_ws(token)
    lin = row * EXTENT + (token - row * WS)
    if mirrored:
        lin = (WS - 1) * EXTENT + (WS - 1) - lin
    return (iota((384, AREA), 0) == lin).astype(F32)


def prep_kernel(
    capacity, routes, cot, w1, b1, w2, ls, slot_col, slot_row, zbuf, table, scale, flat, u_ref, route_col
):
    slots = zbuf.shape[1]
    experts = zbuf.shape[0]
    route_col[...] = jnp.transpose(
        jnp.broadcast_to(routes[...].astype(F32), (128, TOKENS)), (1, 0)
    )
    before = (iota((AREA, AREA), 1) < iota((AREA, AREA), 0)).astype(BF16)
    carry = jnp.zeros((1, 128), F32)
    for block in range(TOKENS // AREA):
        rows = pl.ds(block * AREA, AREA)
        route = route_col[rows, 0:1]
        onehot = (route == iota((AREA, 128), 1).astype(F32)).astype(F32)
        ahead = dot(before, onehot.astype(BF16), 1, 0) + carry
        position = jnp.sum(ahead * onehot, axis=1, keepdims=True)
        carry = carry + col_sum(onehot)
        slot = route * slots + position
        slot_col[rows, :] = jnp.where(position < capacity, slot, -1.0).astype(I32)
    slot_row[...] = jnp.transpose(
        jnp.broadcast_to(slot_col[...].astype(F32), (TOKENS, 128)), (1, 0)
    )[0:1, :].astype(I32)

    for row in range(SIDE):
        flat[row * SIDE : (row + 1) * SIDE, :] = cot[row].astype(F32)
    low = flat[...].astype(BF16)
    for expert in range(experts):
        pick = (iota((slots, TOKENS), 0) + expert * slots == slot_row[...]).astype(BF16)
        zbuf[expert] = dot(pick, low, 1, 0).astype(BF16)

    scale[...] = jnp.exp(row_of(ls))
    f_row, f_col = (found[0:1, :] for found in offsets_row((8, TABLE), 1, 1.0))
    w1t = jnp.transpose(w1[...], (1, 0))
    b1t = jnp.transpose(row_of(b1), (1, 0))
    hidden, _ = gelu_pair(w1t[:, 0:1] * f_row + w1t[:, 1:2] * f_col + b1t[:, 0:1])
    values = 16.0 * jax.nn.sigmoid(exact_dot(w2[...], hidden, 1, 0))
    spread = spread_matrix(False).astype(BF16)
    for head in range(HEADS):
        line = jnp.broadcast_to(values[head : head + 1, :], (16, TABLE))
        line = pltpu.roll(line, 0, 1, stride=1, stride_axis=0)
        for key_row in range(WS):
            shift = (EXTENT * key_row - (WS - 1) * EXTENT - (WS - 1)) % TABLE
            rolled = pltpu.roll(line, shift, 1)
            u_ref[key_row * WS : (key_row + 1) * WS, :] = rolled[:WS, :384]
        high, low_part = split(u_ref[...])
        table[head] = dot(high, spread, 1, 0) + dot(low_part, spread, 1, 0)


def prep(routes, cotangent, w1, b1, w2, ls, experts, capacity, slots):
    return pl.pallas_call(
        functools.partial(prep_kernel, capacity),
        out_shape=(
            full((TOKENS, 1), I32),
            full((1, TOKENS), I32),
            full((experts, slots, D), BF16),
            full((HEADS, AREA, AREA)),
            full((1, HEADS)),
        ),
        scratch_shapes=[
            pltpu.VMEM((TOKENS, D), F32),
            pltpu.VMEM((AREA, 384), F32),
            pltpu.VMEM((TOKENS, 128), F32),
        ],
        compiler_params=params(),
        name="prep",
    )(routes, cotangent, w1, b1, w2, ls)


def window_labels(window, shift_row, shift_col):
    def labels(shape, dim):
        token = iota(shape, dim)
        row = div_ws(token)
        col = token - row * WS + lax.rem(window, ACROSS) * WS
        row = row + lax.div(window, ACROSS) * WS

        def region(place, shift):
            last = jnp.where(place < SIDE - shift, 1, 2)
            return jnp.where(place < SIDE - WS, 0, last)

        return region(row, shift_row) * 3 + region(col, shift_col)

    return labels((AREA, 1), 0), labels((1, AREA), 1)


def roll_to_windows(read_row, doubled, windows, shift_row, shift_col):
    for row in range(SIDE):
        line = read_row(row)
        doubled[row, :SIDE, :] = line
        doubled[row, SIDE:, :] = line[:WS, :]
    for row in range(SIDE):
        source = row + shift_row
        source = jnp.where(source >= SIDE, source - SIDE, source)
        line = pltpu.roll(doubled[source], SIDE + WS - shift_col, 0)
        for across in range(ACROSS):
            start = ((row // WS) * ACROSS + across) * AREA + (row % WS) * WS
            windows[start : start + WS, :] = line[across * WS : (across + 1) * WS, :]


def roll_to_image(windows, doubled, write_row, shift_row, shift_col):
    for row in range(SIDE):
        for across in range(ACROSS):
            start = ((row // WS) * ACROSS + across) * AREA + (row % WS) * WS
            line = windows[start : start + WS, :]
            doubled[row, across * WS : (across + 1) * WS, :] = line
            if across == ACROSS - 1:
                doubled[row, SIDE:, :] = line
    for row in range(SIDE):
        source = row - shift_row
        source = jnp.where(source < 0, source + SIDE, source)
        write_row(row, pltpu.roll(doubled[source], shift_col, 0)[:SIDE, :])


def attend_kernel(
    cot_slots, shifts, scale, tokens, in_weight, in_bias, table, out_weight, out_bias, gain, offset,
    cot_arrived, normed, n_out, rstd_out, joint, probs, mixture, win_t, inverse,
    doubled, windows, in_weight_t, bias_col, joined, send, recv, local,
):
    window = pl.program_id(0)
    shift_row, shift_col = shifts[0, 0], shifts[0, 1]
    me = lax.axis_index("expert")
    count = cot_slots.shape[0]

    def move(step):
        to = partner(me, step, count)
        return pltpu.make_async_remote_copy(
            src_ref=cot_slots.at[to],
            dst_ref=cot_arrived.at[me],
            send_sem=send.at[step],
            recv_sem=recv.at[step],
            device_id={"expert": to},
            device_id_type=pl.DeviceIdType.MESH,
        )

    keep = pltpu.make_async_copy(cot_slots.at[me], cot_arrived.at[me], local)

    @pl.when(window == 0)
    def _():
        greet([{"expert": partner(me, step, count)} for step in range(1, count)])
        for step in range(1, count):
            move(step).start()
        keep.start()
        roll_to_windows(
            lambda row: tokens[row].astype(F32), doubled, windows, shift_row, shift_col
        )
        in_weight_t[...] = jnp.transpose(in_weight[...], (1, 0))
        bias_col[:, 0:2] = jnp.transpose(in_bias[...], (1, 0))

    mine = windows[pl.ds(pl.multiple_of(window * AREA, 16), AREA), :].astype(BF16)
    win_t[0, :D, :] = jnp.transpose(mine, (1, 0))
    win_t[0, D:, :] = (iota((16, AREA), 0) == 0).astype(BF16)
    label_keys, label_queries = window_labels(window, shift_row, shift_col)
    mask = jnp.where(label_keys == label_queries, 0.0, -100.0)
    joined[...] = dot(in_weight_t[...], mine, 1, 1)

    def unit(rows, bias, place):
        shaped = (joined[rows, :] + bias).reshape(HEADS, HEAD, AREA)
        inner = lax.rsqrt(1.0 + jnp.sum(shaped * shaped, axis=1, keepdims=True))
        for head in range(HEADS):
            at = place + head % 4
            inverse[0, head // 4, at : at + 1, :] = inner[head]
        return (shaped * inner).reshape(D, AREA).astype(BF16)

    queries = unit(slice(0, D), bias_col[:, 0:1], 0)
    keys = unit(slice(D, 2 * D), 0.0, 4)
    values = (joined[2 * D :, :] + bias_col[:, 1:2]).astype(BF16)
    for group in range(GROUPS):
        part = slice(group * 128, (group + 1) * 128)
        joint[0, group, 0:128, :] = queries[part, :]
        joint[0, group, 128:256, :] = keys[part, :]
        joint[0, group, 256:384, :] = values[part, :]
    key_rows = jnp.transpose(keys, (1, 0))
    blank = jnp.zeros((HEAD, AREA), BF16)

    def scores_of(group):
        lanes = key_rows[:, group * 128 : (group + 1) * 128]
        found = []
        for head in range(4):
            at = group * 128 + head * HEAD
            parts = [blank] * 4
            parts[head] = queries[at : at + HEAD, :]
            found.append(dot(lanes, jnp.concatenate(parts, axis=0), 1, 0))
        return found

    ahead = scores_of(0)
    for group in range(GROUPS):
        current = ahead
        if group + 1 < GROUPS:
            ahead = scores_of(group + 1)
        lows = []
        for i in range(4):
            head = group * 4 + i
            scores = current[i] * scale[0, head] + (table[head] + mask)
            exponent = jnp.exp(scores - jnp.max(scores, axis=0, keepdims=True))
            low = (exponent * (1.0 / col_sum(exponent))).astype(BF16)
            probs[0, head] = low
            lows.append(low)
        for i in range(4):
            at = (group * 4 + i) * HEAD
            mixture[0, at : at + HEAD, :] = dot(values[at : at + HEAD, :], lows[i], 1, 0).astype(BF16)
    branch = dot(mixture[0], out_weight[...], 0, 0) + row_of(out_bias)
    n, rstd = norm_parts(branch)
    normed[...] = n * gain[0:1, :] + offset[0:1, :]
    n_out[...] = n.astype(BF16)
    rstd_out[...] = rstd

    @pl.when(window == WINDOWS - 1)
    def _():
        for step in range(1, count):
            move(step).wait()
        keep.wait()


def attend(
    cot_slots, shifts, scale, tokens, in_weight, in_bias, table, out_weight, out_bias, gain, offset
):
    per_window = lambda *dims: pl.BlockSpec((1,) + dims, lambda w: (w,) + (0,) * len(dims))
    rows = lambda width: pl.BlockSpec((AREA, width), lambda w: (w, 0))
    return pl.pallas_call(
        attend_kernel,
        grid=(WINDOWS,),
        in_specs=[
            pl.BlockSpec(memory_space=pl.ANY),
            smem(),
            smem(),
            whole((SIDE, SIDE, D)),
            whole((D, 3 * D)),
            whole((2, D)),
            whole((HEADS, AREA, AREA)),
            whole((D, D)),
            whole((D,)),
            whole((3, D)),
            whole((3, D)),
        ],
        out_specs=(
            pl.BlockSpec(memory_space=pl.ANY),
            rows(D),
            rows(D),
            rows(1),
            per_window(GROUPS, D, AREA),
            per_window(HEADS, AREA, AREA),
            per_window(D, AREA),
            per_window(D + 16, AREA),
            per_window(GROUPS, 8, AREA),
        ),
        out_shape=(
            full(cot_slots.shape, BF16),
            full((TOKENS, D)),
            full((TOKENS, D), BF16),
            full((TOKENS, 1)),
            full((WINDOWS, GROUPS, D, AREA), BF16),
            full((WINDOWS, HEADS, AREA, AREA), BF16),
            full((WINDOWS, D, AREA), BF16),
            full((WINDOWS, D + 16, AREA), BF16),
            full((WINDOWS, GROUPS, 8, AREA)),
        ),
        scratch_shapes=[
            pltpu.VMEM((SIDE, SIDE + WS, D), F32),
            pltpu.VMEM((TOKENS, D), F32),
            pltpu.VMEM((3 * D, D), BF16),
            pltpu.VMEM((D, 128), F32),
            pltpu.VMEM((3 * D, AREA), F32),
            pltpu.SemaphoreType.DMA((cot_slots.shape[0],)),
            pltpu.SemaphoreType.DMA((cot_slots.shape[0],)),
            pltpu.SemaphoreType.DMA(()),
        ],
        compiler_params=params(collective_id=0, has_side_effects=True),
        name="attend",
    )(cot_slots, shifts, scale, tokens, in_weight, in_bias, table, out_weight, out_bias, gain, offset)


def forward_kernel(
    shifts, tokens, normed, up, up_bias, down, down_bias, gain, offset, slot_row,
    first_low, active, slope, n_out, rstd_out, second, buffer,
    doubled, image, second_low,
):
    step = pl.program_id(0)

    @pl.when(step == 0)
    def _():
        def write_row(row, line):
            image[row * SIDE : (row + 1) * SIDE, :] = line + tokens[row].astype(F32)

        roll_to_image(normed, doubled, write_row, shifts[0, 0], shifts[0, 1])

    rows = pl.ds(pl.multiple_of(step * ROWS, 16), ROWS)
    first = image[rows, :]
    low = first.astype(BF16)
    first_low[...] = low
    up_row = row_of(up_bias)
    branch = jnp.broadcast_to(row_of(down_bias), (ROWS, D))
    for at in range(0, FF, CHUNK):
        hidden = dot(low, up[:, at : at + CHUNK], 1, 0) + up_row[:, at : at + CHUNK]
        activated, derivative = gelu_pair(hidden)
        activated = activated.astype(BF16)
        active[:, at : at + CHUNK] = activated
        slope[:, at : at + CHUNK] = derivative.astype(BF16)
        branch += dot(activated, down[at : at + CHUNK, :], 1, 0)
    n, rstd = norm_parts(branch)
    n_out[...] = n.astype(BF16)
    rstd_out[...] = rstd
    result = first + n * gain[1:2, :] + offset[1:2, :]
    second[...] = result
    second_low[rows, :] = result.astype(BF16)

    @pl.when(step == TOKENS // ROWS - 1)
    def _():
        slots = buffer.shape[1]
        for expert in range(buffer.shape[0]):
            pick = (iota((slots, TOKENS), 0) + expert * slots == slot_row[...]).astype(BF16)
            buffer[expert] = dot(pick, second_low[...], 1, 0).astype(BF16)


def forward(
    shifts, tokens, normed, up, up_bias, down, down_bias, gain, offset, slot_row, experts, slots
):
    rows = lambda width: pl.BlockSpec((ROWS, width), lambda i: (i, 0))
    return pl.pallas_call(
        forward_kernel,
        grid=(TOKENS // ROWS,),
        in_specs=[
            smem(),
            whole((SIDE, SIDE, D)),
            whole((TOKENS, D)),
            whole((D, FF)),
            whole((FF,)),
            whole((FF, D)),
            whole((D,)),
            whole((3, D)),
            whole((3, D)),
            whole((1, TOKENS)),
        ],
        out_specs=(
            rows(D),
            rows(FF),
            rows(FF),
            rows(D),
            rows(1),
            rows(D),
            whole((experts, slots, D)),
        ),
        out_shape=(
            full((TOKENS, D), BF16),
            full((TOKENS, FF), BF16),
            full((TOKENS, FF), BF16),
            full((TOKENS, D), BF16),
            full((TOKENS, 1)),
            full((TOKENS, D)),
            full((experts, slots, D), BF16),
        ),
        scratch_shapes=[
            pltpu.VMEM((SIDE, SIDE + WS, D), F32),
            pltpu.VMEM((TOKENS, D), F32),
            pltpu.VMEM((TOKENS, D), BF16),
        ],
        compiler_params=params(),
        name="forward",
    )(shifts, tokens, normed, up, up_bias, down, down_bias, gain, offset, slot_row)


def expert_kernel(
    buffer, cot, router, up, up_bias, down, down_bias, gain,
    outs, grad_in, half, gain_row,
    arrived, grads, active, slope, up_grad, down_grad_t, up_bias_grad, down_bias_grad,
    packed, land, send, recv, *sum_sems,
):
    core = core_level()
    me = lax.axis_index("expert")
    count, slots, _ = buffer.shape
    others = range(1, count)

    def move(kind, step, source, target, to):
        return pltpu.make_async_remote_copy(
            src_ref=source,
            dst_ref=target,
            send_sem=send.at[kind, step],
            recv_sem=recv.at[kind, step],
            device_id={"expert": to},
            device_id_type=pl.DeviceIdType.MESH,
        )

    greet([{"expert": partner(me, step, count)} for step in others] + core.devices())
    for step in others:
        to = partner(me, step, count)
        move(0, step, buffer.at[to], arrived.at[step], to).start()
    arrived[0] = buffer[me]
    for ref in (up_grad, up_bias_grad, down_grad_t, down_bias_grad, gain_row):
        ref[...] = jnp.zeros_like(ref)
    router_high, router_low = split(router[...])

    def work(step, carry):
        if count == 4:
            owner = lax.rem(lax.div(me, 2) + lax.div(step, 2), 2) * 2
            owner = owner + lax.rem(lax.rem(me, 2) + lax.rem(step, 2), 2)
        else:
            side = 1
            while side * side < count:
                side *= 2
            if side * side == count:
                owner = lax.rem(lax.div(me, side) + side - lax.div(step, side), side) * side
                owner = owner + lax.rem(lax.rem(me, side) + side - lax.rem(step, side), side)
            else:
                owner = lax.rem(me + count - step, count)

        @pl.when(step > 0)
        def _():
            move(0, step, buffer.at[owner], arrived.at[step], owner).wait_recv()

        features = arrived[step]
        logits = dot(features, router_high, 1, 1) + dot(features, router_low, 1, 1)
        chances = jnp.exp(logits - jnp.max(logits, axis=1, keepdims=True))
        own = jnp.where(iota(chances.shape, 1) == me, chances, 0.0)
        gate = jnp.sum(own, axis=1, keepdims=True) / jnp.sum(chances, axis=1, keepdims=True)

        output = jnp.zeros((slots, D), F32)
        for at in range(0, FF, CHUNK):
            hidden = dot(features, up[:, at : at + CHUNK], 1, 0) + up_bias[:, at : at + CHUNK]
            activated, derivative = gelu_pair(hidden)
            activated = activated.astype(BF16)
            active[:, at : at + CHUNK] = activated
            slope[:, at : at + CHUNK] = derivative
            output += dot(activated, down[at : at + CHUNK, :], 1, 0)
        output = (output + down_bias[...]).astype(BF16)
        outs[owner] = output
        output = output.astype(F32)
        n, rstd = norm_parts(gate * output)
        z = cot[owner].astype(F32)
        gain_row[...] += col_sum(z * n)
        grad_moe = norm_back(gain[2:3, :] * z, n, rstd)
        inner = gate * jnp.sum(grad_moe * output, axis=1, keepdims=True)
        inner = jnp.transpose(jnp.broadcast_to(inner, (slots, 128)), (1, 0))[0:1, :]
        lanes = min(slots, D)
        lines = [inner[:, :lanes], jnp.zeros((1, 2 * D - slots), F32)]
        if slots > D:
            lines = [inner[:, :D], inner[:, D:], jnp.zeros((1, 2 * D - slots), F32)]
        inner = jnp.concatenate(lines, axis=1)
        inner = jnp.concatenate([inner[:, :D], inner[:, D:], jnp.zeros((14, D), F32)], axis=0)
        grads[step, slots:, :] = inner.astype(BF16)
        grad_low = (gate * grad_moe).astype(BF16)
        down_bias_grad[...] += col_sum(grad_low.astype(F32))
        grad_low_t = jnp.transpose(grad_low, (1, 0))
        features_t = jnp.transpose(features, (1, 0))
        grad_features = jnp.zeros((slots, D), F32)
        for at in range(0, FF, CHUNK):
            part = slice(at, at + CHUNK)
            grad_hidden = dot(grad_low, down[part, :], 1, 1) * slope[:, part]
            grad_hidden_low = grad_hidden.astype(BF16)
            up_bias_grad[:, part] += col_sum(grad_hidden)
            down_grad_t[:, part] += dot(grad_low_t, active[:, part], 1, 0)
            up_grad[:, part] += dot(features_t, grad_hidden_low, 1, 0)
            grad_features += dot(grad_hidden_low, up[:, part], 1, 1)
        grads[step, :slots, :] = grad_features.astype(BF16)

        @pl.when(step > 0)
        def _():
            move(1, step, grads.at[step], grad_in.at[me], owner).start()

        return carry

    lax.fori_loop(0, count, work, 0)
    grad_in[me] = grads[0]
    pack_pair(packed, up_grad, down_grad_t)
    packed[2 * FF :, :] = jnp.zeros_like(packed[2 * FF :, :])
    tail = jnp.concatenate(
        [up_bias_grad[:, at : at + D] for at in range(0, FF, D)]
        + [down_bias_grad[...], jnp.zeros((11, D), F32)],
        axis=0,
    )
    packed[2 * FF : 2 * FF + 16, :] = tail.astype(BF16)
    scatter(core, packed, land, half, sum_sems, True)
    for step in others:
        to = partner(me, step, count)
        move(0, step, buffer.at[to], arrived.at[step], to).wait_send()
        move(1, step, grads.at[step], grad_in.at[me], to).wait()
    scatter(core, packed, land, half, sum_sems, False)


def pack_pair(packed, up_grad, down_grad_t):
    for block in range(FF // D):
        part = slice(block * D, (block + 1) * D)
        packed[part, :] = up_grad[:, part].astype(BF16)
        packed[FF + block * D : FF + (block + 1) * D, :] = jnp.transpose(
            down_grad_t[:, part].astype(BF16), (1, 0)
        )


def run_experts(buffer, cot, router, up, up_bias, down, down_bias, gain, packed_rows):
    count, slots, _ = buffer.shape
    blocks, wider = (count, slots, D), (count, slots + 16, D)
    return pl.pallas_call(
        expert_kernel,
        out_shape=(
            full(blocks, BF16),
            full(wider, BF16),
            full((packed_rows // 2, D), BF16),
            full((1, D)),
        ),
        scratch_shapes=[
            pltpu.VMEM(blocks, BF16),
            pltpu.VMEM(wider, BF16),
            pltpu.VMEM((slots, FF), BF16),
            pltpu.VMEM((slots, FF), F32),
            pltpu.VMEM((D, FF), F32),
            pltpu.VMEM((D, FF), F32),
            pltpu.VMEM((1, FF), F32),
            pltpu.VMEM((1, D), F32),
            pltpu.VMEM((packed_rows, D), BF16),
            pltpu.VMEM((packed_rows // 2, D), BF16),
            pltpu.SemaphoreType.DMA((2, count)),
            pltpu.SemaphoreType.DMA((2, count)),
            *pair_of_sems(),
        ],
        compiler_params=params(collective_id=1, has_side_effects=True),
        name="experts",
    )(buffer, cot, router, up, up_bias, down, down_bias, gain)


SMALL = (
    ("in_bias0", 1, D),
    ("in_bias1", 1, D),
    ("in_bias2", 1, D),
    ("out_bias", 1, D),
    ("up_bias", FF // D, D),
    ("down_bias", 1, D),
    ("gain", 3, D),
    ("offset", 3, D),
    ("table_one", 3, UNITS),
    ("table_two", HEADS, UNITS),
    ("scale0", 1, 128),
    ("scale1", 1, 128),
    ("scale2", 1, 128),
    ("router", 0, D),
)


def small_places(experts):
    places, at = {}, 0
    for name, rows, width in SMALL:
        rows = rows or experts
        places[name] = (at, rows, width)
        at += rows * (width // 128)
    return places, at


def put_lanes(ref, at, value):
    rows, width = value.shape
    for lane in range(0, width, 128):
        ref[at : at + rows, :] = value[:, lane : lane + 128]
        at += rows


def get_lanes(ref, at, rows, width):
    return jnp.concatenate(
        [ref[at + i * rows : at + (i + 1) * rows, :] for i in range(width // 128)], axis=1
    )


def put_small(ref, places, name, value):
    put_lanes(ref, places[name][0], value)


def get_small(ref, places, name):
    return get_lanes(ref, *places[name])


def values_back(table_grad, values_grad, heads):
    spread = spread_matrix(True).astype(BF16)
    for head in heads:
        high, low = split(table_grad[head % 4])
        flat = dot(high, spread, 1, 1) + dot(low, spread, 1, 1)
        flat = jnp.concatenate([flat, jnp.zeros((AREA, TABLE - 384), F32)], axis=1)
        total = jnp.zeros((16, TABLE), F32)
        for key_row in range(WS):
            line = flat[key_row * WS : (key_row + 1) * WS, :]
            line = jnp.concatenate([line, jnp.zeros((16 - WS, TABLE), F32)], axis=0)
            total += pltpu.roll(line, EXTENT * key_row, 1)
        total = pltpu.roll(total, 0, 1, stride=1, stride_axis=0)
        values_grad[head : head + 1, :] = col_sum(total)


def net_again(w1, b1, w2):
    f_row, f_col = (found[0:1, :] for found in offsets_row((8, TABLE), 1, -1.0))
    w1t = jnp.transpose(w1[...], (1, 0))
    b1t = jnp.transpose(row_of(b1), (1, 0))
    hidden, slope = gelu_pair(w1t[:, 0:1] * f_row + w1t[:, 1:2] * f_col + b1t[:, 0:1])
    chance = jax.nn.sigmoid(exact_dot(w2[...], hidden, 1, 0))
    return hidden, slope, 16.0 * chance * (1.0 - chance)


def net_back(values_grad, hidden, slope, chance_slope, w2):
    grad_pre = values_grad[:HEADS, :] * chance_slope[:HEADS, :]
    grad_hidden = exact_dot(w2[...], grad_pre, 0, 0) * slope[...].astype(F32)
    f_row, f_col = offsets_row((8, TABLE), 1, -1.0)
    kind = iota((8, TABLE), 0)
    factors = jnp.where(kind == 0, f_row, jnp.where(kind == 1, f_col, 1.0))
    return exact_dot(factors, grad_hidden, 1, 1)[:3, :], exact_dot(grad_pre, hidden[...].astype(F32), 1, 1)


class Sum:
    def __init__(self, levels, refs, source, result, scattered=0):
        count, fresh = len(levels), len(levels) - scattered
        lands, outs, refs = refs[:fresh], refs[fresh : 2 * fresh], refs[2 * fresh :]
        scatter_sems, gather_sems, local = refs[: 2 * fresh], refs[2 * fresh : -1], refs[-1]
        sources = [source] + list(outs)
        gather = Gather(levels, sources[-1], result, gather_sems, local)
        self.moves = [
            functools.partial(
                scatter, levels[scattered + i], sources[i], lands[i], outs[i],
                scatter_sems[2 * i : 2 * i + 2],
            )
            for i in range(fresh)
        ] + [functools.partial(gather.move, i) for i in reversed(range(count))]

    @staticmethod
    def scratch(rows, dtype, width, counts, scattered=0):
        lands, outs = [], []
        for count in counts[scattered:]:
            rows //= count
            lands.append(pltpu.VMEM(((count - 1) * rows, width), dtype))
            outs.append(pltpu.VMEM((rows, width), dtype))
        return (
            lands + outs + sems_of(counts[scattered:]) + sems_of(counts) + [pltpu.SemaphoreType.DMA(())]
        )

    def do(self, k):
        if 0 < k <= len(self.moves):
            self.moves[k - 1](False)
        if k < len(self.moves):
            self.moves[k](True)


class Line:
    def __init__(self, core, line, refs, source, result):
        self.core, self.line, self.source, self.result = core, line, source, result
        count = line.count
        self.share = source.shape[0] // count
        self.half = source.shape[0]
        self.core_sems, self.local, refs = refs[0:2], refs[2], refs[3:]
        self.held = source
        self.moves = []
        if count > 1:
            self.held, self.land, self.scatter_sems, self.gather_sems = (
                refs[0], refs[1], refs[2:4], refs[4:6]
            )
            self.moves += [functools.partial(self.scatter, t) for t in range(1, count)]
            self.moves += [functools.partial(self.gather, t) for t in range(1, count)]
        self.moves.append(self.swap)

    @staticmethod
    def scratch(rows, count):
        more = []
        if count > 1:
            more = [
                pltpu.VMEM((rows, D), BF16),
                pltpu.VMEM((2, count - 1, rows // count, D), BF16),
            ] + [pltpu.SemaphoreType.DMA((2, count - 1))] * 4
        return pair_of_sems() + [pltpu.SemaphoreType.DMA(())] + more

    def start(self):
        if self.line.count > 1:
            fetch = pltpu.make_async_copy(self.source, self.held, self.local)
            fetch.start()
            fetch.wait()

    def rows_of(self, ref, share, base=0):
        start = pl.multiple_of(base + share * self.share, 16)
        return ref.at[pl.ds(start, self.share)]

    def base(self):
        return self.core.index * self.half

    def copy(self, source, target, sems, way, t, to):
        return pltpu.make_async_remote_copy(
            src_ref=source,
            dst_ref=target,
            send_sem=sems[0].at[way, t - 1],
            recv_sem=sems[1].at[way, t - 1],
            device_id=self.line.device(to),
            device_id_type=pl.DeviceIdType.MESH,
        )

    def scatter(self, t, begin):
        count, index = self.line.count, self.line.index
        for way in range(2):
            place = (count - 1 - index) if way else index
            shares = lambda j: (count - 1 - j) if way else j
            to = index - 1 if way else index + 1
            sent = self.copy(
                self.rows_of(self.held, shares(count + place - t)),
                self.land.at[way, t - 1], self.scatter_sems, way, t, to,
            )

            @pl.when((place + 1 <= t) & (place < count - 1))
            def _():
                sent.start() if begin else sent.wait_send()

            if not begin:

                @pl.when((place <= t) & (place >= 1))
                def _():
                    share = shares(count + place - 1 - t)
                    self.copy(
                        self.rows_of(self.held, share), self.land.at[way, t - 1],
                        self.scatter_sems, way, t, to,
                    ).wait_recv()
                    mine = self.rows_of(self.held, share)
                    mine[...] = (
                        mine[...].astype(F32) + self.land[way, t - 1].astype(F32)
                    ).astype(BF16)

    def gather(self, t, begin):
        count, index = self.line.count, self.line.index
        own = self.rows_of(self.held, index)
        keep = pltpu.make_async_copy(own, self.rows_of(self.result, index, self.base()), self.local)
        for way in range(2):
            to = index - 1 if way else index + 1
            origin = index + (t - 1) if way else index - (t - 1)
            there = self.rows_of(self.result, origin, self.base())
            sent = self.copy(own if t == 1 else there, there, self.gather_sems, way, t, to)
            sends = (
                (index > 0) & (origin <= count - 1) if way else (index < count - 1) & (origin >= 0)
            )

            @pl.when(sends)
            def _():
                sent.start() if begin else sent.wait_send()

            if not begin:
                origin = index + t if way else index - t

                @pl.when(origin <= count - 1 if way else origin >= 0)
                def _():
                    there = self.rows_of(self.result, origin, self.base())
                    self.copy(there, there, self.gather_sems, way, t, to).wait_recv()

        if t == 1:
            keep.start() if begin else keep.wait()

    def swap(self, begin):
        mine = self.result.at[pl.ds(pl.multiple_of(self.base(), 16), self.half)]
        alone = self.line.count == 1
        copy = pltpu.make_async_remote_copy(
            src_ref=self.source if alone else mine,
            dst_ref=mine,
            send_sem=self.core_sems[0],
            recv_sem=self.core_sems[1],
            device_id=self.core.devices()[0],
            device_id_type=pl.DeviceIdType.MESH,
        )
        copy.start() if begin else copy.wait()
        if alone:
            keep = pltpu.make_async_copy(self.source, mine, self.local)
            keep.start() if begin else keep.wait()

    def do(self, k):
        if 0 < k <= len(self.moves):
            self.moves[k - 1](False)
        if k < len(self.moves):
            self.moves[k](True)


PART_A = TOKENS // ROWS
PART_B = FF // D
PART_C = GROUPS * ACROSS
TRIPLE = WINDOWS // ACROSS
RESULT = PART_B + PART_C
STARTS = {
    0: [("own", 0)],
    2: [("own", 1)],
    4: [("own", 2)],
    8: [("first", 3)],
    9: [("first", 4), ("rest", 2)],
    10: [("rest", 3)],
    11: [("rest", 4), ("own", 3)],
    12: [("first", 5)],
    13: [("first", 6), ("own", 4)],
    14: [("rest", 5), ("early", 1)],
    15: [("rest", 6), ("early", 2), ("own", 5)],
}
ENDS = {4: [("first", 0)], 5: [("first", 1)], 6: [("rest", 0)], 12: [("early", 0)]}
MIDDLE = [("rest", 1)], [("first", 2)]
SUMS = ("own", "first", "rest", "early", "late", "small")


def head_places(early, late):
    return (early, 0), (early, 4 * D), (late, 0)


def backward_kernel(
    places, sizes,
    shifts, scale, second, cot, slot_col, n_one, rstd_one, outputs, grads, router,
    first_low, active, slope, up, down, gain, offset, half, gain_row,
    n_zero, rstd_zero, joint, probs, mixture, win_t, inverse, in_q, in_k, in_v, out_weight,
    w1, b1, w2,
    result, tokens_grad, own_sum, first_sum, rest_sum, early_sum, late_sum, small_sum,
    flat, grad_low_all, grad_low_t, first_t, grad_hidden_all, total, dense,
    doubled, windows, grad_mix, joint_grad, grads_f32, in_grad, out_grad, early, late,
    table_grad, values_grad, hidden_net, slope_net, chance_net,
    small, up_bias_grad, down_bias_grad, router_grad, gain_grad, offset_grad, out_bias_grad,
    in_bias_grad, scale_grad, out_arrived, out_send, out_recv, out_local,
    *refs,
):
    step = pl.program_id(0)
    shift_row, shift_col = shifts[0, 0], shifts[0, 1]
    core, plane, depth = core_level(), plane_level(), depth_level()
    deep = [depth] if depth.count > 1 else []
    levels = [core, plane] + deep
    sums = {}
    dense_half = dense.shape[0] // 2
    first = dense.at[pl.ds(0, dense_half)]
    rest = dense.at[pl.ds(dense_half, dense_half)]
    sources = (half, first, rest, early, late, small)
    results = (own_sum, first_sum, rest_sum, early_sum, late_sum, small_sum)
    for name, source, target, size in zip(SUMS, sources, results, sizes):
        mine, refs = refs[:size], refs[size:]
        if name == "own":
            sums[name] = Line(core, depth, mine, source, target)
        else:
            sums[name] = Sum(levels, mine, source, target)

    def at(place, action):
        pl.when(step == place)(action)

    def send_out(to):
        return pltpu.make_async_remote_copy(
            src_ref=outputs.at[to],
            dst_ref=out_arrived.at[plane.index],
            send_sem=out_send,
            recv_sem=out_recv,
            device_id=plane.device(to),
            device_id_type=pl.DeviceIdType.MESH,
        )

    keep_out = pltpu.make_async_copy(
        outputs.at[plane.index], out_arrived.at[plane.index], out_local
    )

    def moves(plan):
        for place, work in plan.items():

            def action(work=work):
                for name, k in work:
                    sums[name].do(k)

            at(place, action)

    @functools.partial(at, 0)
    def _():
        greet([device for level in levels for device in level.devices()])
        for ref in (
            router_grad, gain_grad, offset_grad, down_bias_grad, out_bias_grad, out_grad,
            scale_grad, small,
        ):
            ref[...] = jnp.zeros_like(ref)
        for ref, used in ((first, 12 * D), (rest, 12 * D), (early, 8 * D), (late, 4 * D)):
            if ref.shape[0] > used:
                ref[used:, :] = jnp.zeros_like(ref[used:, :])
        gain_grad[2:3, :] = gain_row[...]
        sums["own"].start()
        for to in plane.others():
            send_out(to).start()
        keep_out.start()

    moves(STARTS)

    @functools.partial(at, RESULT)
    def _():
        some = out_arrived.at[pl.ds(0, plane.count - 1)]
        wait_all(some, some, (out_send, out_recv), plane)
        keep_out.wait()

    slots = out_arrived.shape[1]

    def pick_of(expert):
        return (slot_col[...] - expert * slots == iota((ROWS, slots), 1)).astype(BF16)

    def chances_of(x):
        logits = exact_dot(x, router[...], 1, 1)
        chances = jnp.exp(logits - jnp.max(logits, axis=1, keepdims=True))
        chances = chances / jnp.sum(chances, axis=1, keepdims=True)
        within = slot_col[...] - iota(chances.shape, 1) * slots
        onehot = ((within >= 0) & (within < slots)).astype(F32)
        return chances, onehot

    def write_result():
        x = second[...]
        chances, onehot = chances_of(x)
        gate = jnp.sum(chances * onehot, axis=1, keepdims=True)
        picked = jnp.zeros((ROWS, D), F32)
        for expert in range(plane.count):
            picked += dot(pick_of(expert), out_arrived[expert], 1, 0)
        n, _ = norm_parts(gate * picked)
        flat[...] = x + n * gain[2:3, :] + offset[2:3, :]
        for line in range(ROWS // SIDE):
            result[line] = flat[line * SIDE : (line + 1) * SIDE, :].astype(BF16)

    for place in range(RESULT, RESULT + PART_A - 1):
        at(place, write_result)

    @pl.when(step < PART_A)
    def _():
        lines = ROWS // SIDE
        for line in range(lines):
            flat[line * SIDE : (line + 1) * SIDE, :] = cot[line].astype(F32)
        z = flat[...]
        x = second[...]
        dispatched = jnp.zeros((ROWS, D), F32)
        inner = jnp.zeros((ROWS, 16), F32)
        for expert in range(plane.count):
            pick = pick_of(expert)
            dispatched += dot(pick, grads[expert, :slots, :], 1, 0)
            row = grads[expert, slots : slots + 1, : min(slots, D)]
            if slots > D:
                row = jnp.concatenate(
                    [row, grads[expert, slots + 1 : slots + 2, : slots - D]], axis=1
                )
            inner += dot(pick, jnp.broadcast_to(row, (16, slots)), 1, 1)
        chances, onehot = chances_of(x)
        offset_grad[2:3, :] += col_sum(z)
        grad_logits = inner[:, 0:1] * (onehot - chances)
        grad_logits_low = grad_logits.astype(BF16)
        router_grad[...] += dot(grad_logits_low, x.astype(BF16), 0, 0)
        grad_second = z + dispatched + dot(grad_logits_low, router[...].astype(BF16), 1, 0)

        n = n_one[...].astype(F32)
        gain_grad[1:2, :] += col_sum(grad_second * n)
        offset_grad[1:2, :] += col_sum(grad_second)
        grad_branch = norm_back(gain[1:2, :] * grad_second, n, rstd_one[...])
        rows = pl.ds(pl.multiple_of(step * ROWS, 16), ROWS)
        grad_low_all[rows, :] = grad_branch.astype(BF16)
        down_bias_grad[...] += col_sum(grad_branch)
        total[rows, :] = grad_second

    @functools.partial(at, PART_A)
    def _():
        grad_low_t[...] = jnp.transpose(grad_low_all[...], (1, 0))
        first_t[...] = jnp.transpose(first_low[...], (1, 0))

    @pl.when((step >= PART_A) & (step < PART_A + PART_B))
    def _():
        bias_row = jnp.zeros((1, D), F32)
        for tile in range(TOKENS // ROWS):
            rows = slice(tile * ROWS, (tile + 1) * ROWS)
            grad_hidden = dot(grad_low_all[rows, :], down[...], 1, 1) * slope[rows, :].astype(F32)
            bias_row += col_sum(grad_hidden)
            grad_hidden_low = grad_hidden.astype(BF16)
            grad_hidden_all[rows, :] = grad_hidden_low
            total[rows, :] += dot(grad_hidden_low, up[...], 1, 1)
        up_bias_grad[pl.ds(step - PART_A, 1), :] = bias_row
        up_part = dot(first_t[...], grad_hidden_all[...], 1, 0).astype(BF16)
        down_part = jnp.transpose(
            dot(grad_low_t[...], active[...], 1, 0).astype(BF16), (1, 0)
        )
        for block in range(PART_B):

            def place(block=block):
                start = (block // 2) * dense_half + (block % 2) * 6 * D
                put_lanes(dense, start, up_part)
                put_lanes(dense, start + 3 * D, down_part)

            at(PART_A + block, place)

    @functools.partial(at, PART_A + PART_B)
    def _():
        hidden, net_slope, chance = net_again(w1, b1, w2)
        hidden_net[...] = hidden.astype(BF16)
        slope_net[...] = net_slope.astype(BF16)
        chance_net[:HEADS, :] = chance
        for name, k in MIDDLE[0]:
            sums[name].do(k)
        roll_to_windows(
            lambda row: total[row * SIDE : (row + 1) * SIDE, :],
            doubled, windows, shift_row, shift_col,
        )

        for name, k in MIDDLE[1]:
            sums[name].do(k)

        def one(window, carry):
            mine = pl.ds(pl.multiple_of(window * AREA, 16), AREA)
            z = windows[mine, :]
            n = n_zero[mine, :].astype(F32)
            gain_grad[0:1, :] += col_sum(z * n)
            offset_grad[0:1, :] += col_sum(z)
            grad_branch = norm_back(gain[0:1, :] * z, n, rstd_zero[mine, :])
            grad_low = grad_branch.astype(BF16)
            out_bias_grad[...] += col_sum(grad_branch)
            out_grad[...] += dot(mixture[window], grad_low, 1, 0)
            grad_mix[window] = dot(out_weight[...], grad_low, 1, 1).astype(BF16)
            return carry

        lax.fori_loop(0, WINDOWS, one, 0)
        for group, (into, start) in enumerate(head_places(early, late)):
            put_lanes(into, start + 3 * D, out_grad[group * 128 : (group + 1) * 128, :].astype(BF16))

    @pl.when(step >= PART_A + PART_B)
    def _():
        place = step - (PART_A + PART_B)
        group = lax.div(place, ACROSS)
        third = lax.rem(place, ACROSS)
        blank = jnp.zeros((HEAD, AREA), BF16)
        features = pl.ds(pl.multiple_of(group * 128, 128), 128)
        in_part = jnp.concatenate([in_q[...], in_k[...], in_v[...]], axis=1)

        @pl.when(third == 0)
        def _():
            in_grad[...] = jnp.zeros_like(in_grad)
            table_grad[...] = jnp.zeros_like(table_grad)

        def probs_grads(i):
            lanes = jnp.transpose(joint[i, 0, 256:384, :], (1, 0))
            coming = grad_mix[third * TRIPLE + i, features, :]
            found = []
            for head in range(4):
                parts = [blank] * 4
                parts[head] = coming[head * HEAD : (head + 1) * HEAD, :]
                found.append(dot(lanes, jnp.concatenate(parts, axis=0), 1, 0))
            return found, coming

        ahead = probs_grads(0)
        for i in range(TRIPLE):
            current, coming = ahead
            if i + 1 < TRIPLE:
                ahead = probs_grads(i + 1)
            raws = []
            for head in range(4):
                weight = probs[i, head].astype(F32)
                weighted = weight * current[head]
                grad_scores = weighted - weight * (col_sum(weighted) / col_sum(weight))
                table_grad[head] += grad_scores
                raws.append((grad_scores * scale[0, group * 4 + head]).astype(BF16))
            for head in range(4):
                own = slice(head * HEAD, (head + 1) * HEAD)
                keys = slice(128 + head * HEAD, 128 + (head + 1) * HEAD)
                grads_f32[own, :] = dot(joint[i, 0, keys, :], raws[head], 1, 0)
                grads_f32[keys, :] = dot(joint[i, 0, own, :], raws[head], 1, 1)
                joint_grad[256 + head * HEAD : 256 + (head + 1) * HEAD, :] = dot(
                    coming[own, :], probs[i, head], 1, 1
                ).astype(BF16)
            shaped = grads_f32[...].reshape(8, HEAD, AREA)
            unit = joint[i, 0, :256, :].astype(F32).reshape(8, HEAD, AREA)
            inner = jnp.sum(unit * shaped, axis=1, keepdims=True)
            shaped = shaped - unit * inner
            for part in range(8):
                joint_grad[part * HEAD : (part + 1) * HEAD, :] = (
                    shaped[part] * inverse[i, 0, part : part + 1, :]
                ).astype(BF16)
                if part < 4:
                    scale_grad[group, part : part + 1, :] += inner[part]
            joint_rows = jnp.transpose(joint_grad[...], (1, 0))
            in_grad[...] += dot(win_t[i], joint_rows, 1, 0)
            grad_window = dot(joint_rows, in_part, 1, 1)
            mine = pl.ds(pl.multiple_of((third * TRIPLE + i) * AREA, 16), AREA)
            kept = jnp.where(group == 0, 0.0, 1.0)
            windows[mine, :] = windows[mine, :] * kept + grad_window

    for group, (into, start) in enumerate(head_places(early, late)):

        def group_end(group=group, into=into, start=start):
            put_lanes(into, start, in_grad[:D, :].astype(BF16))
            in_bias_grad[group : group + 1, :] = in_grad[D : D + 1, :]

        at(PART_A + PART_B + (group + 1) * ACROSS - 1, group_end)
    moves(ENDS)
    for group in range(GROUPS - 1):
        heads = range(group * 4, group * 4 + 4)
        at(
            PART_A + PART_B + (group + 1) * ACROSS - 1,
            functools.partial(values_back, table_grad, values_grad, heads),
        )

    @functools.partial(at, PART_A + PART_B + PART_C - 1)
    def _():
        sums["late"].do(0)
        values_back(table_grad, values_grad, range(8, HEADS))
        sums["late"].do(1)
        table_one, table_two = net_back(values_grad, hidden_net, slope_net, chance_net, w2)
        put = functools.partial(put_small, small, places)
        put("table_one", table_one)
        put("table_two", table_two)
        for group in range(GROUPS):
            row = exact_dot(jnp.ones((8, AREA), F32), scale_grad[group], 1, 1)[0:1, :]
            put("scale%d" % group, jnp.concatenate([row, jnp.zeros((1, 120), F32)], axis=1))
            put("in_bias%d" % group, in_bias_grad[group : group + 1, :])
        put("out_bias", out_bias_grad[...])
        put("up_bias", up_bias_grad[...])
        put("down_bias", down_bias_grad[...])
        put("gain", gain_grad[...])
        put("offset", offset_grad[...])
        put("router", router_grad[...])
        sums["early"].do(3)
        sums["small"].do(0)
        sums["late"].do(2)
        sums["early"].do(4)
        sums["small"].do(1)

        write_result()

        def write_row(row, line):
            line = line + total[row * SIDE : (row + 1) * SIDE, :]
            for lane in range(D // 128):
                tokens_grad[pl.ds(row * SIDE * (D // 128) + lane, SIDE, stride=D // 128), :] = line[
                    :, lane * 128 : (lane + 1) * 128
                ]

        roll_to_image(windows, doubled, write_row, shift_row, shift_col)
        for k in range(2, 7):
            sums["small"].do(k)
            sums["late"].do(k + 1)
            if k < 4:
                sums["early"].do(k + 3)
            if k == 3:
                sums["own"].do(6)
        for k in range(7, len(sums["own"].moves) + 1):
            sums["own"].do(k)


def backward(
    small_rows, experts, shifts, scale, second, cot, slot_col, n_one, rstd_one, outputs, grads,
    router, first_low, active, slope, up, down, gain, offset, half, gain_row,
    n_zero, rstd_zero, joint, probs, mixture, win_t, inverse, in_weight, out_weight, w1, b1, w2,
):
    places, _ = small_places(experts)
    group, depth = lax.axis_size("expert"), lax.axis_size("dp") // 2
    counts = [2, group] + ([depth] if depth > 1 else [])
    dense_rows = padded_rows(12 * D, counts, 16)
    early_rows = padded_rows(8 * D, counts, 16)
    last_rows = padded_rows(4 * D, counts, 16)
    sum_scratch = [Line.scratch(half.shape[0], depth)]
    for rows_of in (dense_rows, dense_rows, early_rows, last_rows):
        sum_scratch += [Sum.scratch(rows_of, BF16, 128, counts)]
    sum_scratch += [Sum.scratch(small_rows, F32, 128, counts)]

    part_a = lambda i: jnp.minimum(i, PART_A - 1)
    again = lambda i: jnp.maximum(i - RESULT, 0)
    twice = lambda i: jnp.where(i < RESULT, part_a(i), again(i))
    part_b = lambda i: jnp.clip(i - PART_A, 0, PART_B - 1)
    part_c = lambda i: jnp.maximum(i - PART_A - PART_B, 0)
    third = lambda i: lax.rem(part_c(i), ACROSS)
    heads = lambda i: lax.div(part_c(i), ACROSS)
    rows = lambda width: pl.BlockSpec((ROWS, width), lambda i: (part_a(i), 0))
    lines = pl.BlockSpec((ROWS // SIDE, SIDE, D), lambda i: (part_a(i), 0, 0))
    hidden = pl.BlockSpec((TOKENS, D), lambda i: (0, part_b(i)))
    in_third = lambda j: pl.BlockSpec((D, 128), lambda i: (0, j * GROUPS + heads(i)))
    anywhere = pl.BlockSpec(memory_space=pl.ANY)
    once = lambda shape: pl.BlockSpec(
        shape, lambda *_: (0,) * len(shape), pipeline_mode=pl.Buffered(1)
    )
    return pl.pallas_call(
        functools.partial(backward_kernel, places, [len(part) for part in sum_scratch]),
        grid=(PART_A + PART_B + PART_C,),
        in_specs=[
            smem(),
            smem(),
            pl.BlockSpec((ROWS, D), lambda i: (twice(i), 0)),
            lines,
            pl.BlockSpec((ROWS, 1), lambda i: (twice(i), 0)),
            rows(D),
            rows(1),
            anywhere,
            once(grads.shape),
            once(router.shape),
            once((TOKENS, D)),
            hidden,
            hidden,
            pl.BlockSpec((D, D), lambda i: (0, part_b(i))),
            pl.BlockSpec((D, D), lambda i: (part_b(i), 0)),
            once((3, D)),
            once((3, D)),
            anywhere,
            once((1, D)),
            once((TOKENS, D)),
            once((TOKENS, 1)),
            pl.BlockSpec((TRIPLE, 1, D, AREA), lambda i: (third(i), heads(i), 0, 0)),
            pl.BlockSpec((TRIPLE, 4, AREA, AREA), lambda i: (third(i), heads(i), 0, 0)),
            once((WINDOWS, D, AREA)),
            pl.BlockSpec((TRIPLE, D + 16, AREA), lambda i: (third(i), 0, 0)),
            pl.BlockSpec((TRIPLE, 1, 8, AREA), lambda i: (third(i), heads(i), 0, 0)),
            in_third(0),
            in_third(1),
            in_third(2),
            once((D, D)),
            once(w1.shape),
            once(b1.shape),
            once(w2.shape),
        ],
        out_specs=(
            pl.BlockSpec((ROWS // SIDE, SIDE, D), lambda i: (again(i), 0, 0)),
            whole((TOKENS * D // 128, 128)),
        ) + (anywhere,) * 6,
        out_shape=(
            full((SIDE, SIDE, D), BF16),
            full((TOKENS * D // 128, 128)),
            full((2 * half.shape[0], D), BF16),
            full((dense_rows, 128), BF16),
            full((dense_rows, 128), BF16),
            full((early_rows, 128), BF16),
            full((last_rows, 128), BF16),
            full((small_rows, 128)),
        ),
        scratch_shapes=[
            pltpu.VMEM((ROWS, D), F32),
            pltpu.VMEM((TOKENS, D), BF16),
            pltpu.VMEM((D, TOKENS), BF16),
            pltpu.VMEM((D, TOKENS), BF16),
            pltpu.VMEM((TOKENS, D), BF16),
            pltpu.VMEM((TOKENS, D), F32),
            pltpu.VMEM((2 * dense_rows, 128), BF16),
            pltpu.VMEM((SIDE, SIDE + WS, D), F32),
            pltpu.VMEM((TOKENS, D), F32),
            pltpu.VMEM((WINDOWS, D, AREA), BF16),
            pltpu.VMEM((D, AREA), BF16),
            pltpu.VMEM((256, AREA), F32),
            pltpu.VMEM((D + 16, D), F32),
            pltpu.VMEM((D, D), F32),
            pltpu.VMEM((early_rows, 128), BF16),
            pltpu.VMEM((last_rows, 128), BF16),
            pltpu.VMEM((4, AREA, AREA), F32),
            pltpu.VMEM((16, TABLE), F32),
            pltpu.VMEM((UNITS, TABLE), BF16),
            pltpu.VMEM((UNITS, TABLE), BF16),
            pltpu.VMEM((16, TABLE), F32),
            pltpu.VMEM((small_rows, 128), F32),
            pltpu.VMEM((PART_B, D), F32),
            pltpu.VMEM((1, D), F32),
            pltpu.VMEM(router.shape, F32),
            pltpu.VMEM((3, D), F32),
            pltpu.VMEM((3, D), F32),
            pltpu.VMEM((1, D), F32),
            pltpu.VMEM((GROUPS, D), F32),
            pltpu.VMEM((GROUPS, 8, AREA), F32),
            pltpu.VMEM(outputs.shape, BF16),
            pltpu.SemaphoreType.DMA(()),
            pltpu.SemaphoreType.DMA(()),
            pltpu.SemaphoreType.DMA(()),
        ]
        + [ref for part in sum_scratch for ref in part],
        compiler_params=params(collective_id=2, has_side_effects=True),
        name="backward",
    )(
        shifts, scale, second, cot, slot_col, n_one, rstd_one, outputs, grads, router,
        first_low, active, slope, up, down, gain, offset, half, gain_row,
        n_zero, rstd_zero, joint, probs, mixture, win_t, inverse,
        in_weight, in_weight, in_weight, out_weight, w1, b1, w2,
    )


def unpack_kernel(
    places, own, first, rest, early, late, small,
    in_grad, in_bias, scale, table_first, table_first_bias, table_second, out_grad, out_bias,
    up_grad, up_bias, down_grad, down_bias, router, own_up, own_up_bias, own_down, own_down_bias,
    gain, offset,
):
    step = pl.program_id(0)
    for block in range(FF // D):

        def write(block=block):
            dense, start = (first, rest)[block // 2], (block % 2) * 6 * D
            up_grad[...] = get_lanes(dense, start, D, D).astype(F32)
            down_grad[...] = get_lanes(dense, start + 3 * D, D, D).astype(F32)
            own_up[...] = own[block * D : (block + 1) * D, :].astype(F32)
            own_down[...] = own[FF + block * D : FF + (block + 1) * D, :].astype(F32)

        pl.when(step == block)(write)

    @pl.when(step == 0)
    def _():
        unpack_rest(
            places, own, early, late, small, in_grad, in_bias, scale, table_first,
            table_first_bias, table_second, out_grad, out_bias, up_bias, down_bias, router,
            own_up_bias, own_down_bias, gain, offset,
        )


def unpack_rest(
    places, own, early, late, small, in_grad, in_bias, scale, table_first, table_first_bias,
    table_second, out_grad, out_bias, up_bias, down_bias, router, own_up_bias, own_down_bias,
    gain, offset,
):
    get = functools.partial(get_small, small, places)
    scales = []
    for group, (source, start) in enumerate(head_places(early, late)):
        row = get("in_bias%d" % group)
        for third in range(3):
            lanes = slice(third * D + group * 128, third * D + (group + 1) * 128)
            at = start + third * D
            in_grad[:, lanes] = source[at : at + D, :].astype(F32)
        part = get_lanes(source, start + 3 * D, 128, D)
        out_grad[group * 128 : (group + 1) * 128, :] = part.astype(F32)
        in_bias[0:1, group * 128 : (group + 1) * 128] = row[:, 0:128]
        in_bias[1:2, group * 128 : (group + 1) * 128] = row[:, 256:384]
        scales.append(get("scale%d" % group)[:, :4])
    scale[...] = jnp.concatenate(scales, axis=1).reshape(HEADS)
    tail = own[2 * FF : 2 * FF + 16, :].astype(F32)
    up_rows = get("up_bias")
    for block in range(FF // D):
        own_up_bias[:, block * D : (block + 1) * D] = tail[block : block + 1, :]
    own_down_bias[...] = tail[FF // D : FF // D + 1, :]
    up_bias[...] = jnp.concatenate(
        [up_rows[block : block + 1, :] for block in range(FF // D)], axis=1
    ).reshape(FF)
    one = get("table_one")
    table_first[...] = one[0:2, :]
    table_first_bias[...] = one[2:3, :].reshape(UNITS)
    table_second[...] = get("table_two")
    out_bias[...] = get("out_bias").reshape(D)
    down_bias[...] = get("down_bias").reshape(D)
    router[...] = get("router")
    gain[...] = get("gain")
    offset[...] = get("offset")


def unpack(parts, experts):
    places, _ = small_places(experts)
    return pl.pallas_call(
        functools.partial(unpack_kernel, places),
        grid=(FF // D,),
        in_specs=[whole(part.shape) for part in parts],
        out_specs=(
            whole((D, 3 * D)),
            whole((2, D)),
            whole((HEADS,)),
            whole((2, UNITS)),
            whole((UNITS,)),
            whole((HEADS, UNITS)),
            whole((D, D)),
            whole((D,)),
            pl.BlockSpec((D, D), lambda i: (0, i)),
            whole((FF,)),
            pl.BlockSpec((D, D), lambda i: (i, 0)),
            whole((D,)),
            whole((experts, D)),
            pl.BlockSpec((D, D), lambda i: (0, i)),
            whole((1, FF)),
            pl.BlockSpec((D, D), lambda i: (i, 0)),
            whole((1, D)),
            whole((3, D)),
            whole((3, D)),
        ),
        out_shape=(
            full((D, 3 * D)),
            full((2, D)),
            full((HEADS,)),
            full((2, UNITS)),
            full((UNITS,)),
            full((HEADS, UNITS)),
            full((D, D)),
            full((D,)),
            full((D, FF)),
            full((FF,)),
            full((FF, D)),
            full((D,)),
            full((experts, D)),
            full((D, FF)),
            full((1, FF)),
            full((FF, D)),
            full((1, D)),
            full((3, D)),
            full((3, D)),
        ),
        compiler_params=params(),
        name="unpack",
    )(*parts)


def per_device(
    tokens, shifts, routes, cotangent, in_weight, in_bias, logit_scale,
    bias_net_first_weight, bias_net_first_bias, bias_net_second_weight,
    out_weight, out_bias, up_weight, up_bias, down_weight, down_bias, router_weight,
    expert_up, expert_up_bias, expert_down, expert_down_bias, norm_gain, norm_bias,
):
    experts = router_weight.shape[1]
    dp = lax.axis_size("dp")
    group = lax.axis_size("expert")
    capacity = (5 * TOKENS + 4 * experts - 1) // (4 * experts)
    slots = -(-capacity // 16) * 16
    own_rows = padded_rows(2 * FF + 16, [2, dp // 2], 16)
    small_rows = padded_rows(small_places(experts)[1], [2, group, dp // 2], 8)

    picture = tokens.reshape(SIDE, SIDE, D)
    cot = cotangent.reshape(SIDE, SIDE, D)
    router_t = router_weight.T
    second_t = bias_net_second_weight.T

    slot_col, slot_row, cot_slots, table, scale = prep(
        routes.reshape(1, TOKENS), cot, bias_net_first_weight, bias_net_first_bias, second_t,
        logit_scale, experts, capacity, slots,
    )
    cot_arrived, normed, n_zero, rstd_zero, joint, probs, mixture, win_t, inverse = attend(
        cot_slots, shifts, scale, picture, in_weight, in_bias, table,
        out_weight, out_bias, norm_gain, norm_bias,
    )
    first_low, active, slope, n_one, rstd_one, second, buffer = forward(
        shifts, picture, normed, up_weight, up_bias, down_weight,
        down_bias, norm_gain, norm_bias, slot_row, experts, slots,
    )
    outputs, grad_returned, own_half, gain_row = run_experts(
        buffer, cot_arrived, router_t, expert_up[0], expert_up_bias, expert_down[0],
        expert_down_bias, norm_gain, own_rows,
    )
    result, tokens_grad, *parts = backward(
        small_rows, experts, shifts, scale, second, cot, slot_col, n_one, rstd_one,
        outputs, grad_returned, router_t, first_low, active, slope,
        up_weight, down_weight, norm_gain, norm_bias, own_half, gain_row,
        n_zero, rstd_zero, joint, probs, mixture, win_t, inverse, in_weight, out_weight,
        bias_net_first_weight, bias_net_first_bias, second_t,
    )
    (
        in_weight_grad, in_bias_grad, scale_grad, table_one, table_bias, table_two, out_grad,
        out_bias_grad, up_grad, up_bias_grad, down_grad, down_bias_grad, router_grad,
        own_up, own_up_bias, own_down, own_down_bias, gain_grad, offset_grad,
    ) = unpack(parts, experts)
    return (
        result.reshape(tokens.shape),
        tokens_grad.reshape(tokens.shape),
        in_weight_grad,
        in_bias_grad,
        scale_grad,
        table_one,
        table_bias,
        table_two.T,
        out_grad,
        out_bias_grad,
        up_grad,
        up_bias_grad,
        down_grad,
        down_bias_grad,
        router_grad.T,
        own_up[None],
        own_up_bias,
        own_down[None],
        own_down_bias,
        gain_grad,
        offset_grad,
    )


def solution(mesh):
    split_all = P(("dp", "expert"))
    placed = (split_all,) * 4 + (P(),) * 13 + (P("expert"),) * 4 + (P(),) * 2
    return jax.shard_map(
        per_device,
        mesh=mesh,
        in_specs=placed,
        out_specs=(split_all,) * 2 + (P(),) * 13 + (P("expert"),) * 4 + (P(),) * 2,
        check_vma=False,
    )
```

```python
import functools

import jax
import jax.numpy as jnp
from jax import lax
from jax.experimental import pallas as pl
from jax.experimental.pallas import tpu as pltpu
from jax.sharding import PartitionSpec as P

D = 384
HEADS = 12
HEAD = D // HEADS
WS = 12
SIDE = 36
AREA = WS * WS
ACROSS = SIDE // WS
WINDOWS = ACROSS * ACROSS
TOKENS = SIDE * SIDE
FF = 1536
EXTENT = 2 * WS - 1
UNITS = 512
GROUPS = 3
TABLE = 640
ROWS = 432
CHUNK = 256
F32 = jnp.float32
BF16 = jnp.bfloat16
I32 = jnp.int32
VMEM_LIMIT = 63 * 1024 * 1024


def dot(left, right, left_dim, right_dim):
    return lax.dot_general(
        left, right, (((left_dim,), (right_dim,)), ((), ())), preferred_element_type=F32
    )


def exact_dot(left, right, left_dim, right_dim):
    return lax.dot_general(
        left,
        right,
        (((left_dim,), (right_dim,)), ((), ())),
        preferred_element_type=F32,
        precision=lax.Precision.HIGHEST,
    )


def split(values):
    high = values.astype(BF16)
    return high, (values - high.astype(F32)).astype(BF16)


def iota(shape, dim):
    return lax.broadcasted_iota(I32, shape, dim)


def gelu_pair(values):
    size = jnp.abs(values)
    t = 1.0 / (1.0 + 0.2316419 * size)
    bell = jnp.exp(-0.5 * values * values) * 0.3989422804014327
    series = t * (
        0.319381530
        + t * (-0.356563782 + t * (1.781477937 + t * (-1.821255978 + t * 1.330274429)))
    )
    tail = series * bell
    phi = jnp.where(values >= 0.0, 1.0 - tail, tail)
    return values * phi, phi + values * bell


def norm_parts(values):
    centered = values - jnp.mean(values, axis=-1, keepdims=True)
    rstd = lax.rsqrt(jnp.mean(centered * centered, axis=-1, keepdims=True) + 1e-05)
    return centered * rstd, rstd


def norm_back(grad_n, n, rstd):
    return rstd * (
        grad_n
        - jnp.mean(grad_n, axis=-1, keepdims=True)
        - n * jnp.mean(grad_n * n, axis=-1, keepdims=True)
    )


def row_of(ref):
    return ref[...].reshape(1, ref.shape[0])


def col_sum(values):
    return jnp.sum(values, axis=0, keepdims=True)


def div_ws(values):
    return (values * 171) >> 11


def full(shape, dtype=F32):
    return jax.ShapeDtypeStruct(shape, dtype)


def whole(shape):
    return pl.BlockSpec(shape, lambda *_: (0,) * len(shape))


def smem():
    return pl.BlockSpec(memory_space=pltpu.SMEM)


def params(**more):
    return pltpu.CompilerParams(vmem_limit_bytes=VMEM_LIMIT, **more)


def partner(me, step, count):
    side = 1
    while side * side < count:
        side *= 2
    if side * side != count:
        return lax.rem(me + step, count)
    row = lax.rem(lax.div(me, side) + step // side, side)
    col = lax.rem(lax.rem(me, side) + step % side, side)
    return row * side + col


def opposite(step, count):
    side = 1
    while side * side < count:
        side *= 2
    if side * side != count:
        return (count - step) % count
    return ((side - step // side) % side) * side + (side - step % side) % side


def greet(devices):
    barrier = pltpu.get_barrier_semaphore()
    for device in devices:
        pl.semaphore_signal(barrier, inc=1, device_id=device, device_id_type=pl.DeviceIdType.MESH)
    pl.semaphore_wait(barrier, len(devices))


class Level:
    def __init__(self, count, index, device):
        self.count, self.index, self.device = count, index, device

    def others(self):
        return [lax.rem(self.index + step, self.count) for step in range(1, self.count)]

    def devices(self):
        return [self.device(to) for to in self.others()]


def core_level():
    place = lax.div(lax.axis_index("dp"), 2)
    return Level(2, lax.rem(lax.axis_index("dp"), 2), lambda j: {"dp": place * 2 + j})


def plane_level():
    return Level(lax.axis_size("expert"), lax.axis_index("expert"), lambda j: {"expert": j})


def depth_level():
    core = lax.rem(lax.axis_index("dp"), 2)
    place = lax.div(lax.axis_index("dp"), 2)
    return Level(lax.axis_size("dp") // 2, place, lambda j: {"dp": j * 2 + core})


def padded_rows(rows, counts, tile):
    unit = tile
    for count in counts:
        unit *= count
    return -(-rows // unit) * unit


def pair_of_sems():
    return [pltpu.SemaphoreType.DMA(()), pltpu.SemaphoreType.DMA(())]


def wait_all(sent, received, sems, level):
    copy = pltpu.make_async_remote_copy(
        src_ref=sent,
        dst_ref=received,
        send_sem=sems[0],
        recv_sem=sems[1],
        device_id=level.device(level.others()[0]),
        device_id_type=pl.DeviceIdType.MESH,
    )
    copy.wait()


def scatter(level, source, land, out, sems, begin):
    rows = source.shape[0] // level.count
    tile = 16 if source.dtype == BF16 else 8
    if begin:
        for step, to in enumerate(level.others(), 1):
            pltpu.make_async_remote_copy(
                src_ref=source.at[pl.ds(pl.multiple_of(to * rows, tile), rows)],
                dst_ref=land.at[pl.ds((step - 1) * rows, rows)],
                send_sem=sems[0],
                recv_sem=sems[1],
                device_id=level.device(to),
                device_id_type=pl.DeviceIdType.MESH,
            ).start()
        return
    wait_all(source.at[pl.ds(0, land.shape[0])], land, sems, level)
    mine = level.index * rows
    chunk = tile
    while rows % (chunk * 2) == 0 and chunk < 128:
        chunk *= 2

    def add(i, carry):
        here = pl.ds(pl.multiple_of(i * chunk, tile), chunk)
        total = source[pl.ds(pl.multiple_of(mine + i * chunk, tile), chunk), :].astype(F32)
        for step in range(1, level.count):
            total = total + land[
                pl.ds(pl.multiple_of((step - 1) * rows + i * chunk, tile), chunk), :
            ].astype(F32)
        out[here, :] = total.astype(out.dtype)
        return carry

    lax.fori_loop(0, rows // chunk, add, 0)


class Gather:
    def __init__(self, levels, piece, result, sems, local):
        self.levels, self.piece, self.result, self.sems = levels, piece, result, sems
        rows, start = result.shape[0], 0
        self.regions = []
        for level in levels:
            rows //= level.count
            start = start + level.index * rows
            self.regions.append((start, rows))
        self.keep = pltpu.make_async_copy(piece, self.region(len(levels) - 1), local)

    def region(self, at):
        start, rows = self.regions[at]
        return self.result.at[pl.ds(pl.multiple_of(start, 8), rows)]

    def move(self, at, begin):
        level, last = self.levels[at], at == len(self.levels) - 1
        mine = self.region(at)
        sems = self.sems[2 * at : 2 * at + 2]
        if begin:
            for to in level.others():
                pltpu.make_async_remote_copy(
                    src_ref=self.piece if last else mine,
                    dst_ref=mine,
                    send_sem=sems[0],
                    recv_sem=sems[1],
                    device_id=level.device(to),
                    device_id_type=pl.DeviceIdType.MESH,
                ).start()
        else:
            some = self.result.at[pl.ds(0, (level.count - 1) * self.regions[at][1])]
            wait_all(some, some, sems, level)
        if last:
            self.keep.start() if begin else self.keep.wait()


def sems_of(levels):
    return [sem for _ in levels for sem in pair_of_sems()]


def offsets_row(shape, dim, sign):
    place = iota(shape, dim)
    row = jnp.floor((place.astype(F32) + 0.5) * (1.0 / EXTENT)).astype(I32)
    col = place - row * EXTENT

    def logged(step):
        e = sign * (step - (WS - 1)).astype(F32) * (8.0 / (WS - 1))
        size = jnp.log2(jnp.abs(e) + 1.0) * (1.0 / 3.0)
        return jnp.where(e < 0.0, -size, size)

    return logged(row), logged(col)


def spread_matrix(mirrored):
    token = iota((384, AREA), 1)
    row = div_ws(token)
    lin = row * EXTENT + (token - row * WS)
    if mirrored:
        lin = (WS - 1) * EXTENT + (WS - 1) - lin
    return (iota((384, AREA), 0) == lin).astype(F32)


def prep_kernel(
    capacity, routes, cot, w1, b1, w2, ls, slot_col, slot_row, zbuf, table, scale, flat, u_ref, route_col
):
    slots = zbuf.shape[1]
    experts = zbuf.shape[0]
    route_col[...] = jnp.transpose(
        jnp.broadcast_to(routes[...].astype(F32), (128, TOKENS)), (1, 0)
    )
    before = (iota((AREA, AREA), 1) < iota((AREA, AREA), 0)).astype(BF16)
    carry = jnp.zeros((1, 128), F32)
    for block in range(TOKENS // AREA):
        rows = pl.ds(block * AREA, AREA)
        route = route_col[rows, 0:1]
        onehot = (route == iota((AREA, 128), 1).astype(F32)).astype(F32)
        ahead = dot(before, onehot.astype(BF16), 1, 0) + carry
        position = jnp.sum(ahead * onehot, axis=1, keepdims=True)
        carry = carry + col_sum(onehot)
        slot = route * slots + position
        slot_col[rows, :] = jnp.where(position < capacity, slot, -1.0).astype(I32)
    slot_row[...] = jnp.transpose(
        jnp.broadcast_to(slot_col[...].astype(F32), (TOKENS, 128)), (1, 0)
    )[0:1, :].astype(I32)

    for row in range(SIDE):
        flat[row * SIDE : (row + 1) * SIDE, :] = cot[row].astype(F32)
    low = flat[...].astype(BF16)
    for expert in range(experts):
        pick = (iota((slots, TOKENS), 0) + expert * slots == slot_row[...]).astype(BF16)
        zbuf[expert] = dot(pick, low, 1, 0).astype(BF16)

    scale[...] = jnp.exp(row_of(ls))
    f_row, f_col = (found[0:1, :] for found in offsets_row((8, TABLE), 1, 1.0))
    w1t = jnp.transpose(w1[...], (1, 0))
    b1t = jnp.transpose(row_of(b1), (1, 0))
    hidden, _ = gelu_pair(w1t[:, 0:1] * f_row + w1t[:, 1:2] * f_col + b1t[:, 0:1])
    values = 16.0 * jax.nn.sigmoid(exact_dot(w2[...], hidden, 1, 0))
    spread = spread_matrix(False).astype(BF16)
    for head in range(HEADS):
        line = jnp.broadcast_to(values[head : head + 1, :], (16, TABLE))
        line = pltpu.roll(line, 0, 1, stride=1, stride_axis=0)
        for key_row in range(WS):
            shift = (EXTENT * key_row - (WS - 1) * EXTENT - (WS - 1)) % TABLE
            rolled = pltpu.roll(line, shift, 1)
            u_ref[key_row * WS : (key_row + 1) * WS, :] = rolled[:WS, :384]
        high, low_part = split(u_ref[...])
        table[head] = dot(high, spread, 1, 0) + dot(low_part, spread, 1, 0)


def prep(routes, cotangent, w1, b1, w2, ls, experts, capacity, slots):
    return pl.pallas_call(
        functools.partial(prep_kernel, capacity),
        out_shape=(
            full((TOKENS, 1), I32),
            full((1, TOKENS), I32),
            full((experts, slots, D), BF16),
            full((HEADS, AREA, AREA)),
            full((1, HEADS)),
        ),
        scratch_shapes=[
            pltpu.VMEM((TOKENS, D), F32),
            pltpu.VMEM((AREA, 384), F32),
            pltpu.VMEM((TOKENS, 128), F32),
        ],
        compiler_params=params(),
        name="prep",
    )(routes, cotangent, w1, b1, w2, ls)


def window_labels(window, shift_row, shift_col):
    def labels(shape, dim):
        token = iota(shape, dim)
        row = div_ws(token)
        col = token - row * WS + lax.rem(window, ACROSS) * WS
        row = row + lax.div(window, ACROSS) * WS

        def region(place, shift):
            last = jnp.where(place < SIDE - shift, 1, 2)
            return jnp.where(place < SIDE - WS, 0, last)

        return region(row, shift_row) * 3 + region(col, shift_col)

    return labels((AREA, 1), 0), labels((1, AREA), 1)


def roll_to_windows(read_row, doubled, windows, shift_row, shift_col):
    for row in range(SIDE):
        line = read_row(row)
        doubled[row, :SIDE, :] = line
        doubled[row, SIDE:, :] = line[:WS, :]
    for row in range(SIDE):
        source = row + shift_row
        source = jnp.where(source >= SIDE, source - SIDE, source)
        line = pltpu.roll(doubled[source], SIDE + WS - shift_col, 0)
        for across in range(ACROSS):
            start = ((row // WS) * ACROSS + across) * AREA + (row % WS) * WS
            windows[start : start + WS, :] = line[across * WS : (across + 1) * WS, :]


def roll_to_image(windows, doubled, write_row, shift_row, shift_col):
    for row in range(SIDE):
        for across in range(ACROSS):
            start = ((row // WS) * ACROSS + across) * AREA + (row % WS) * WS
            line = windows[start : start + WS, :]
            doubled[row, across * WS : (across + 1) * WS, :] = line
            if across == ACROSS - 1:
                doubled[row, SIDE:, :] = line
    for row in range(SIDE):
        source = row - shift_row
        source = jnp.where(source < 0, source + SIDE, source)
        write_row(row, pltpu.roll(doubled[source], shift_col, 0)[:SIDE, :])


def attend_kernel(
    cot_slots, shifts, scale, tokens, in_weight, in_bias, table, out_weight, out_bias, gain, offset,
    cot_arrived, normed, n_out, rstd_out, joint, probs, mixture, win_t, inverse,
    doubled, windows, in_weight_t, bias_col, joined, send, recv, local,
):
    window = pl.program_id(0)
    shift_row, shift_col = shifts[0, 0], shifts[0, 1]
    me = lax.axis_index("expert")
    count = cot_slots.shape[0]

    def move(step):
        to = partner(me, step, count)
        return pltpu.make_async_remote_copy(
            src_ref=cot_slots.at[to],
            dst_ref=cot_arrived.at[me],
            send_sem=send.at[step],
            recv_sem=recv.at[step],
            device_id={"expert": to},
            device_id_type=pl.DeviceIdType.MESH,
        )

    keep = pltpu.make_async_copy(cot_slots.at[me], cot_arrived.at[me], local)

    @pl.when(window == 0)
    def _():
        greet([{"expert": partner(me, step, count)} for step in range(1, count)])
        for step in range(1, count):
            move(step).start()
        keep.start()
        roll_to_windows(
            lambda row: tokens[row].astype(F32), doubled, windows, shift_row, shift_col
        )
        in_weight_t[...] = jnp.transpose(in_weight[...], (1, 0))
        bias_col[:, 0:2] = jnp.transpose(in_bias[...], (1, 0))

    mine = windows[pl.ds(pl.multiple_of(window * AREA, 16), AREA), :].astype(BF16)
    win_t[0, :D, :] = jnp.transpose(mine, (1, 0))
    win_t[0, D:, :] = (iota((16, AREA), 0) == 0).astype(BF16)
    label_keys, label_queries = window_labels(window, shift_row, shift_col)
    mask = jnp.where(label_keys == label_queries, 0.0, -100.0)
    joined[...] = dot(in_weight_t[...], mine, 1, 1)

    def unit(rows, bias, place):
        shaped = (joined[rows, :] + bias).reshape(HEADS, HEAD, AREA)
        inner = lax.rsqrt(1.0 + jnp.sum(shaped * shaped, axis=1, keepdims=True))
        for head in range(HEADS):
            at = place + head % 4
            inverse[0, head // 4, at : at + 1, :] = inner[head]
        return (shaped * inner).reshape(D, AREA).astype(BF16)

    queries = unit(slice(0, D), bias_col[:, 0:1], 0)
    keys = unit(slice(D, 2 * D), 0.0, 4)
    values = (joined[2 * D :, :] + bias_col[:, 1:2]).astype(BF16)
    for group in range(GROUPS):
        part = slice(group * 128, (group + 1) * 128)
        joint[0, group, 0:128, :] = queries[part, :]
        joint[0, group, 128:256, :] = keys[part, :]
        joint[0, group, 256:384, :] = values[part, :]
    key_rows = jnp.transpose(keys, (1, 0))
    blank = jnp.zeros((HEAD, AREA), BF16)

    def scores_of(group):
        lanes = key_rows[:, group * 128 : (group + 1) * 128]
        found = []
        for head in range(4):
            at = group * 128 + head * HEAD
            parts = [blank] * 4
            parts[head] = queries[at : at + HEAD, :]
            found.append(dot(lanes, jnp.concatenate(parts, axis=0), 1, 0))
        return found

    ahead = scores_of(0)
    for group in range(GROUPS):
        current = ahead
        if group + 1 < GROUPS:
            ahead = scores_of(group + 1)
        lows = []
        for i in range(4):
            head = group * 4 + i
            scores = current[i] * scale[0, head] + (table[head] + mask)
            exponent = jnp.exp(scores - jnp.max(scores, axis=0, keepdims=True))
            low = (exponent * (1.0 / col_sum(exponent))).astype(BF16)
            probs[0, head] = low
            lows.append(low)
        for i in range(4):
            at = (group * 4 + i) * HEAD
            mixture[0, at : at + HEAD, :] = dot(values[at : at + HEAD, :], lows[i], 1, 0).astype(BF16)
    branch = dot(mixture[0], out_weight[...], 0, 0) + row_of(out_bias)
    n, rstd = norm_parts(branch)
    normed[...] = n * gain[0:1, :] + offset[0:1, :]
    n_out[...] = n.astype(BF16)
    rstd_out[...] = rstd

    @pl.when(window == WINDOWS - 1)
    def _():
        for step in range(1, count):
            move(step).wait()
        keep.wait()


def attend(
    cot_slots, shifts, scale, tokens, in_weight, in_bias, table, out_weight, out_bias, gain, offset
):
    per_window = lambda *dims: pl.BlockSpec((1,) + dims, lambda w: (w,) + (0,) * len(dims))
    rows = lambda width: pl.BlockSpec((AREA, width), lambda w: (w, 0))
    return pl.pallas_call(
        attend_kernel,
        grid=(WINDOWS,),
        in_specs=[
            pl.BlockSpec(memory_space=pl.ANY),
            smem(),
            smem(),
            whole((SIDE, SIDE, D)),
            whole((D, 3 * D)),
            whole((2, D)),
            whole((HEADS, AREA, AREA)),
            whole((D, D)),
            whole((D,)),
            whole((3, D)),
            whole((3, D)),
        ],
        out_specs=(
            pl.BlockSpec(memory_space=pl.ANY),
            rows(D),
            rows(D),
            rows(1),
            per_window(GROUPS, D, AREA),
            per_window(HEADS, AREA, AREA),
            per_window(D, AREA),
            per_window(D + 16, AREA),
            per_window(GROUPS, 8, AREA),
        ),
        out_shape=(
            full(cot_slots.shape, BF16),
            full((TOKENS, D)),
            full((TOKENS, D), BF16),
            full((TOKENS, 1)),
            full((WINDOWS, GROUPS, D, AREA), BF16),
            full((WINDOWS, HEADS, AREA, AREA), BF16),
            full((WINDOWS, D, AREA), BF16),
            full((WINDOWS, D + 16, AREA), BF16),
            full((WINDOWS, GROUPS, 8, AREA)),
        ),
        scratch_shapes=[
            pltpu.VMEM((SIDE, SIDE + WS, D), F32),
            pltpu.VMEM((TOKENS, D), F32),
            pltpu.VMEM((3 * D, D), BF16),
            pltpu.VMEM((D, 128), F32),
            pltpu.VMEM((3 * D, AREA), F32),
            pltpu.SemaphoreType.DMA((cot_slots.shape[0],)),
            pltpu.SemaphoreType.DMA((cot_slots.shape[0],)),
            pltpu.SemaphoreType.DMA(()),
        ],
        compiler_params=params(collective_id=0, has_side_effects=True),
        name="attend",
    )(cot_slots, shifts, scale, tokens, in_weight, in_bias, table, out_weight, out_bias, gain, offset)


def forward_kernel(
    shifts, tokens, normed, up, up_bias, down, down_bias, gain, offset, slot_row,
    first_low, active, slope, n_out, rstd_out, second, buffer,
    doubled, image, second_low,
):
    step = pl.program_id(0)

    @pl.when(step == 0)
    def _():
        def write_row(row, line):
            image[row * SIDE : (row + 1) * SIDE, :] = line + tokens[row].astype(F32)

        roll_to_image(normed, doubled, write_row, shifts[0, 0], shifts[0, 1])

    rows = pl.ds(pl.multiple_of(step * ROWS, 16), ROWS)
    first = image[rows, :]
    low = first.astype(BF16)
    first_low[...] = low
    up_row = row_of(up_bias)
    branch = jnp.broadcast_to(row_of(down_bias), (ROWS, D))
    for at in range(0, FF, CHUNK):
        hidden = dot(low, up[:, at : at + CHUNK], 1, 0) + up_row[:, at : at + CHUNK]
        activated, derivative = gelu_pair(hidden)
        activated = activated.astype(BF16)
        active[:, at : at + CHUNK] = activated
        slope[:, at : at + CHUNK] = derivative.astype(BF16)
        branch += dot(activated, down[at : at + CHUNK, :], 1, 0)
    n, rstd = norm_parts(branch)
    n_out[...] = n.astype(BF16)
    rstd_out[...] = rstd
    result = first + n * gain[1:2, :] + offset[1:2, :]
    second[...] = result
    second_low[rows, :] = result.astype(BF16)

    @pl.when(step == TOKENS // ROWS - 1)
    def _():
        slots = buffer.shape[1]
        for expert in range(buffer.shape[0]):
            pick = (iota((slots, TOKENS), 0) + expert * slots == slot_row[...]).astype(BF16)
            buffer[expert] = dot(pick, second_low[...], 1, 0).astype(BF16)


def forward(
    shifts, tokens, normed, up, up_bias, down, down_bias, gain, offset, slot_row, experts, slots
):
    rows = lambda width: pl.BlockSpec((ROWS, width), lambda i: (i, 0))
    return pl.pallas_call(
        forward_kernel,
        grid=(TOKENS // ROWS,),
        in_specs=[
            smem(),
            whole((SIDE, SIDE, D)),
            whole((TOKENS, D)),
            whole((D, FF)),
            whole((FF,)),
            whole((FF, D)),
            whole((D,)),
            whole((3, D)),
            whole((3, D)),
            whole((1, TOKENS)),
        ],
        out_specs=(
            rows(D),
            rows(FF),
            rows(FF),
            rows(D),
            rows(1),
            rows(D),
            whole((experts, slots, D)),
        ),
        out_shape=(
            full((TOKENS, D), BF16),
            full((TOKENS, FF), BF16),
            full((TOKENS, FF), BF16),
            full((TOKENS, D), BF16),
            full((TOKENS, 1)),
            full((TOKENS, D)),
            full((experts, slots, D), BF16),
        ),
        scratch_shapes=[
            pltpu.VMEM((SIDE, SIDE + WS, D), F32),
            pltpu.VMEM((TOKENS, D), F32),
            pltpu.VMEM((TOKENS, D), BF16),
        ],
        compiler_params=params(),
        name="forward",
    )(shifts, tokens, normed, up, up_bias, down, down_bias, gain, offset, slot_row)


def expert_kernel(
    buffer, cot, router, up, up_bias, down, down_bias, gain,
    outs, grad_in, half, gain_row,
    arrived, grads, active, slope, up_grad, down_grad_t, up_bias_grad, down_bias_grad,
    packed, land, send, recv, *sum_sems,
):
    core = core_level()
    me = lax.axis_index("expert")
    count, slots, _ = buffer.shape
    others = range(1, count)

    def move(kind, step, source, target, to):
        return pltpu.make_async_remote_copy(
            src_ref=source,
            dst_ref=target,
            send_sem=send.at[kind, step],
            recv_sem=recv.at[kind, step],
            device_id={"expert": to},
            device_id_type=pl.DeviceIdType.MESH,
        )

    greet([{"expert": partner(me, step, count)} for step in others] + core.devices())
    for step in others:
        to = partner(me, step, count)
        move(0, step, buffer.at[to], arrived.at[step], to).start()
    arrived[0] = buffer[me]
    for ref in (up_grad, up_bias_grad, down_grad_t, down_bias_grad, gain_row):
        ref[...] = jnp.zeros_like(ref)
    router_high, router_low = split(router[...])

    def work(step, carry):
        if count == 4:
            owner = lax.rem(lax.div(me, 2) + lax.div(step, 2), 2) * 2
            owner = owner + lax.rem(lax.rem(me, 2) + lax.rem(step, 2), 2)
        else:
            side = 1
            while side * side < count:
                side *= 2
            if side * side == count:
                owner = lax.rem(lax.div(me, side) + side - lax.div(step, side), side) * side
                owner = owner + lax.rem(lax.rem(me, side) + side - lax.rem(step, side), side)
            else:
                owner = lax.rem(me + count - step, count)

        @pl.when(step > 0)
        def _():
            move(0, step, buffer.at[owner], arrived.at[step], owner).wait_recv()

        features = arrived[step]
        logits = dot(features, router_high, 1, 1) + dot(features, router_low, 1, 1)
        chances = jnp.exp(logits - jnp.max(logits, axis=1, keepdims=True))
        own = jnp.where(iota(chances.shape, 1) == me, chances, 0.0)
        gate = jnp.sum(own, axis=1, keepdims=True) / jnp.sum(chances, axis=1, keepdims=True)

        output = jnp.zeros((slots, D), F32)
        for at in range(0, FF, CHUNK):
            hidden = dot(features, up[:, at : at + CHUNK], 1, 0) + up_bias[:, at : at + CHUNK]
            activated, derivative = gelu_pair(hidden)
            activated = activated.astype(BF16)
            active[:, at : at + CHUNK] = activated
            slope[:, at : at + CHUNK] = derivative
            output += dot(activated, down[at : at + CHUNK, :], 1, 0)
        output = (output + down_bias[...]).astype(BF16)
        outs[owner] = output
        output = output.astype(F32)
        n, rstd = norm_parts(gate * output)
        z = cot[owner].astype(F32)
        gain_row[...] += col_sum(z * n)
        grad_moe = norm_back(gain[2:3, :] * z, n, rstd)
        inner = gate * jnp.sum(grad_moe * output, axis=1, keepdims=True)
        inner = jnp.transpose(jnp.broadcast_to(inner, (slots, 128)), (1, 0))[0:1, :]
        lanes = min(slots, D)
        lines = [inner[:, :lanes], jnp.zeros((1, 2 * D - slots), F32)]
        if slots > D:
            lines = [inner[:, :D], inner[:, D:], jnp.zeros((1, 2 * D - slots), F32)]
        inner = jnp.concatenate(lines, axis=1)
        inner = jnp.concatenate([inner[:, :D], inner[:, D:], jnp.zeros((14, D), F32)], axis=0)
        grads[step, slots:, :] = inner.astype(BF16)
        grad_low = (gate * grad_moe).astype(BF16)
        down_bias_grad[...] += col_sum(grad_low.astype(F32))
        grad_low_t = jnp.transpose(grad_low, (1, 0))
        features_t = jnp.transpose(features, (1, 0))
        grad_features = jnp.zeros((slots, D), F32)
        for at in range(0, FF, CHUNK):
            part = slice(at, at + CHUNK)
            grad_hidden = dot(grad_low, down[part, :], 1, 1) * slope[:, part]
            grad_hidden_low = grad_hidden.astype(BF16)
            up_bias_grad[:, part] += col_sum(grad_hidden)
            down_grad_t[:, part] += dot(grad_low_t, active[:, part], 1, 0)
            up_grad[:, part] += dot(features_t, grad_hidden_low, 1, 0)
            grad_features += dot(grad_hidden_low, up[:, part], 1, 1)
        grads[step, :slots, :] = grad_features.astype(BF16)

        @pl.when(step > 0)
        def _():
            move(1, step, grads.at[step], grad_in.at[me], owner).start()

        return carry

    lax.fori_loop(0, count, work, 0)
    grad_in[me] = grads[0]
    pack_pair(packed, up_grad, down_grad_t)
    packed[2 * FF :, :] = jnp.zeros_like(packed[2 * FF :, :])
    tail = jnp.concatenate(
        [up_bias_grad[:, at : at + D] for at in range(0, FF, D)]
        + [down_bias_grad[...], jnp.zeros((11, D), F32)],
        axis=0,
    )
    packed[2 * FF : 2 * FF + 16, :] = tail.astype(BF16)
    scatter(core, packed, land, half, sum_sems, True)
    for step in others:
        to = partner(me, step, count)
        move(0, step, buffer.at[to], arrived.at[step], to).wait_send()
        move(1, step, grads.at[step], grad_in.at[me], to).wait()
    scatter(core, packed, land, half, sum_sems, False)


def pack_pair(packed, up_grad, down_grad_t):
    for block in range(FF // D):
        part = slice(block * D, (block + 1) * D)
        packed[part, :] = up_grad[:, part].astype(BF16)
        packed[FF + block * D : FF + (block + 1) * D, :] = jnp.transpose(
            down_grad_t[:, part].astype(BF16), (1, 0)
        )


def run_experts(buffer, cot, router, up, up_bias, down, down_bias, gain, packed_rows):
    count, slots, _ = buffer.shape
    blocks, wider = (count, slots, D), (count, slots + 16, D)
    return pl.pallas_call(
        expert_kernel,
        out_shape=(
            full(blocks, BF16),
            full(wider, BF16),
            full((packed_rows // 2, D), BF16),
            full((1, D)),
        ),
        scratch_shapes=[
            pltpu.VMEM(blocks, BF16),
            pltpu.VMEM(wider, BF16),
            pltpu.VMEM((slots, FF), BF16),
            pltpu.VMEM((slots, FF), F32),
            pltpu.VMEM((D, FF), F32),
            pltpu.VMEM((D, FF), F32),
            pltpu.VMEM((1, FF), F32),
            pltpu.VMEM((1, D), F32),
            pltpu.VMEM((packed_rows, D), BF16),
            pltpu.VMEM((packed_rows // 2, D), BF16),
            pltpu.SemaphoreType.DMA((2, count)),
            pltpu.SemaphoreType.DMA((2, count)),
            *pair_of_sems(),
        ],
        compiler_params=params(collective_id=1, has_side_effects=True),
        name="experts",
    )(buffer, cot, router, up, up_bias, down, down_bias, gain)


SMALL = (
    ("in_bias0", 1, D),
    ("in_bias1", 1, D),
    ("in_bias2", 1, D),
    ("out_bias", 1, D),
    ("up_bias", FF // D, D),
    ("down_bias", 1, D),
    ("gain", 3, D),
    ("offset", 3, D),
    ("table_one", 3, UNITS),
    ("table_two", HEADS, UNITS),
    ("scale0", 1, 128),
    ("scale1", 1, 128),
    ("scale2", 1, 128),
    ("router", 0, D),
)


def small_places(experts):
    places, at = {}, 0
    for name, rows, width in SMALL:
        rows = rows or experts
        places[name] = (at, rows, width)
        at += rows * (width // 128)
    return places, at


def put_lanes(ref, at, value):
    rows, width = value.shape
    for lane in range(0, width, 128):
        ref[at : at + rows, :] = value[:, lane : lane + 128]
        at += rows


def get_lanes(ref, at, rows, width):
    return jnp.concatenate(
        [ref[at + i * rows : at + (i + 1) * rows, :] for i in range(width // 128)], axis=1
    )


def put_small(ref, places, name, value):
    put_lanes(ref, places[name][0], value)


def get_small(ref, places, name):
    return get_lanes(ref, *places[name])


def values_back(table_grad, values_grad, heads):
    spread = spread_matrix(True).astype(BF16)
    for head in heads:
        high, low = split(table_grad[head % 4])
        flat = dot(high, spread, 1, 1) + dot(low, spread, 1, 1)
        flat = jnp.concatenate([flat, jnp.zeros((AREA, TABLE - 384), F32)], axis=1)
        total = jnp.zeros((16, TABLE), F32)
        for key_row in range(WS):
            line = flat[key_row * WS : (key_row + 1) * WS, :]
            line = jnp.concatenate([line, jnp.zeros((16 - WS, TABLE), F32)], axis=0)
            total += pltpu.roll(line, EXTENT * key_row, 1)
        total = pltpu.roll(total, 0, 1, stride=1, stride_axis=0)
        values_grad[head : head + 1, :] = col_sum(total)


def net_again(w1, b1, w2):
    f_row, f_col = (found[0:1, :] for found in offsets_row((8, TABLE), 1, -1.0))
    w1t = jnp.transpose(w1[...], (1, 0))
    b1t = jnp.transpose(row_of(b1), (1, 0))
    hidden, slope = gelu_pair(w1t[:, 0:1] * f_row + w1t[:, 1:2] * f_col + b1t[:, 0:1])
    chance = jax.nn.sigmoid(exact_dot(w2[...], hidden, 1, 0))
    return hidden, slope, 16.0 * chance * (1.0 - chance)


def net_back(values_grad, hidden, slope, chance_slope, w2):
    grad_pre = values_grad[:HEADS, :] * chance_slope[:HEADS, :]
    grad_hidden = exact_dot(w2[...], grad_pre, 0, 0) * slope[...].astype(F32)
    f_row, f_col = offsets_row((8, TABLE), 1, -1.0)
    kind = iota((8, TABLE), 0)
    factors = jnp.where(kind == 0, f_row, jnp.where(kind == 1, f_col, 1.0))
    return exact_dot(factors, grad_hidden, 1, 1)[:3, :], exact_dot(grad_pre, hidden[...].astype(F32), 1, 1)


class Sum:
    def __init__(self, levels, refs, source, result, scattered=0):
        count, fresh = len(levels), len(levels) - scattered
        lands, outs, refs = refs[:fresh], refs[fresh : 2 * fresh], refs[2 * fresh :]
        scatter_sems, gather_sems, local = refs[: 2 * fresh], refs[2 * fresh : -1], refs[-1]
        sources = [source] + list(outs)
        gather = Gather(levels, sources[-1], result, gather_sems, local)
        self.moves = [
            functools.partial(
                scatter, levels[scattered + i], sources[i], lands[i], outs[i],
                scatter_sems[2 * i : 2 * i + 2],
            )
            for i in range(fresh)
        ] + [functools.partial(gather.move, i) for i in reversed(range(count))]

    @staticmethod
    def scratch(rows, dtype, width, counts, scattered=0):
        lands, outs = [], []
        for count in counts[scattered:]:
            rows //= count
            lands.append(pltpu.VMEM(((count - 1) * rows, width), dtype))
            outs.append(pltpu.VMEM((rows, width), dtype))
        return (
            lands + outs + sems_of(counts[scattered:]) + sems_of(counts) + [pltpu.SemaphoreType.DMA(())]
        )

    def do(self, k):
        if 0 < k <= len(self.moves):
            self.moves[k - 1](False)
        if k < len(self.moves):
            self.moves[k](True)


class Line:
    def __init__(self, core, line, refs, source, result):
        self.core, self.line, self.source, self.result = core, line, source, result
        count = line.count
        self.share = source.shape[0] // count
        self.half = source.shape[0]
        self.core_sems, self.local, refs = refs[0:2], refs[2], refs[3:]
        self.held = source
        self.moves = []
        if count > 1:
            self.held, self.land, self.scatter_sems, self.gather_sems = (
                refs[0], refs[1], refs[2:4], refs[4:6]
            )
            self.moves += [functools.partial(self.scatter, t) for t in range(1, count)]
            self.moves += [functools.partial(self.gather, t) for t in range(1, count)]
        self.moves.append(self.swap)

    @staticmethod
    def scratch(rows, count):
        more = []
        if count > 1:
            more = [
                pltpu.VMEM((rows, D), BF16),
                pltpu.VMEM((2, count - 1, rows // count, D), BF16),
            ] + [pltpu.SemaphoreType.DMA((2, count - 1))] * 4
        return pair_of_sems() + [pltpu.SemaphoreType.DMA(())] + more

    def start(self):
        if self.line.count > 1:
            fetch = pltpu.make_async_copy(self.source, self.held, self.local)
            fetch.start()
            fetch.wait()

    def rows_of(self, ref, share, base=0):
        start = pl.multiple_of(base + share * self.share, 16)
        return ref.at[pl.ds(start, self.share)]

    def base(self):
        return self.core.index * self.half

    def copy(self, source, target, sems, way, t, to):
        return pltpu.make_async_remote_copy(
            src_ref=source,
            dst_ref=target,
            send_sem=sems[0].at[way, t - 1],
            recv_sem=sems[1].at[way, t - 1],
            device_id=self.line.device(to),
            device_id_type=pl.DeviceIdType.MESH,
        )

    def scatter(self, t, begin):
        count, index = self.line.count, self.line.index
        for way in range(2):
            place = (count - 1 - index) if way else index
            shares = lambda j: (count - 1 - j) if way else j
            to = index - 1 if way else index + 1
            sent = self.copy(
                self.rows_of(self.held, shares(count + place - t)),
                self.land.at[way, t - 1], self.scatter_sems, way, t, to,
            )

            @pl.when((place + 1 <= t) & (place < count - 1))
            def _():
                sent.start() if begin else sent.wait_send()

            if not begin:

                @pl.when((place <= t) & (place >= 1))
                def _():
                    share = shares(count + place - 1 - t)
                    self.copy(
                        self.rows_of(self.held, share), self.land.at[way, t - 1],
                        self.scatter_sems, way, t, to,
                    ).wait_recv()
                    mine = self.rows_of(self.held, share)
                    mine[...] = (
                        mine[...].astype(F32) + self.land[way, t - 1].astype(F32)
                    ).astype(BF16)

    def gather(self, t, begin):
        count, index = self.line.count, self.line.index
        own = self.rows_of(self.held, index)
        keep = pltpu.make_async_copy(own, self.rows_of(self.result, index, self.base()), self.local)
        for way in range(2):
            to = index - 1 if way else index + 1
            origin = index + (t - 1) if way else index - (t - 1)
            there = self.rows_of(self.result, origin, self.base())
            sent = self.copy(own if t == 1 else there, there, self.gather_sems, way, t, to)
            sends = (
                (index > 0) & (origin <= count - 1) if way else (index < count - 1) & (origin >= 0)
            )

            @pl.when(sends)
            def _():
                sent.start() if begin else sent.wait_send()

            if not begin:
                origin = index + t if way else index - t

                @pl.when(origin <= count - 1 if way else origin >= 0)
                def _():
                    there = self.rows_of(self.result, origin, self.base())
                    self.copy(there, there, self.gather_sems, way, t, to).wait_recv()

        if t == 1:
            keep.start() if begin else keep.wait()

    def swap(self, begin):
        mine = self.result.at[pl.ds(pl.multiple_of(self.base(), 16), self.half)]
        alone = self.line.count == 1
        copy = pltpu.make_async_remote_copy(
            src_ref=self.source if alone else mine,
            dst_ref=mine,
            send_sem=self.core_sems[0],
            recv_sem=self.core_sems[1],
            device_id=self.core.devices()[0],
            device_id_type=pl.DeviceIdType.MESH,
        )
        copy.start() if begin else copy.wait()
        if alone:
            keep = pltpu.make_async_copy(self.source, mine, self.local)
            keep.start() if begin else keep.wait()

    def do(self, k):
        if 0 < k <= len(self.moves):
            self.moves[k - 1](False)
        if k < len(self.moves):
            self.moves[k](True)


PART_A = TOKENS // ROWS
PART_B = FF // D
PART_C = GROUPS * ACROSS
TRIPLE = WINDOWS // ACROSS
RESULT = PART_B + PART_C
STARTS = {
    0: [("own", 0)],
    2: [("own", 1)],
    4: [("own", 2)],
    8: [("first", 3)],
    10: [("first", 4), ("rest", 2)],
    11: [("own", 3)],
    12: [("rest", 3)],
    13: [("first", 5), ("own", 4)],
    14: [("early", 1), ("rest", 4)],
    15: [("first", 6), ("own", 5)],
}
ENDS = {4: [("first", 0)], 5: [("first", 1)], 6: [("rest", 0)], 12: [("early", 0)]}
MIDDLE = [], [("rest", 1), ("first", 2)]
SUMS = ("own", "first", "rest", "early", "late", "small")


def head_places(early, late):
    return (early, 0), (early, 4 * D), (late, 0)


def backward_kernel(
    places, sizes,
    shifts, scale, second, cot, slot_col, n_one, rstd_one, outputs, grads, router,
    first_low, active, slope, up, down, gain, offset, half, gain_row,
    n_zero, rstd_zero, joint, probs, mixture, win_t, inverse, in_q, in_k, in_v, out_weight,
    w1, b1, w2,
    result, tokens_grad, own_sum, first_sum, rest_sum, early_sum, late_sum, small_sum,
    flat, grad_low_all, grad_low_t, first_t, grad_hidden_all, total, dense,
    doubled, windows, grad_mix, joint_grad, grads_f32, in_grad, out_grad, early, late,
    table_grad, values_grad, hidden_net, slope_net, chance_net,
    small, up_bias_grad, down_bias_grad, router_grad, gain_grad, offset_grad, out_bias_grad,
    in_bias_grad, scale_grad, out_arrived, out_send, out_recv, out_local,
    *refs,
):
    step = pl.program_id(0)
    shift_row, shift_col = shifts[0, 0], shifts[0, 1]
    core, plane, depth = core_level(), plane_level(), depth_level()
    deep = [depth] if depth.count > 1 else []
    levels = [core, plane] + deep
    sums = {}
    dense_half = dense.shape[0] // 2
    first = dense.at[pl.ds(0, dense_half)]
    rest = dense.at[pl.ds(dense_half, dense_half)]
    sources = (half, first, rest, early, late, small)
    results = (own_sum, first_sum, rest_sum, early_sum, late_sum, small_sum)
    for name, source, target, size in zip(SUMS, sources, results, sizes):
        mine, refs = refs[:size], refs[size:]
        if name == "own":
            sums[name] = Line(core, depth, mine, source, target)
        else:
            sums[name] = Sum(levels, mine, source, target)

    def at(place, action):
        pl.when(step == place)(action)

    def send_out(to):
        return pltpu.make_async_remote_copy(
            src_ref=outputs.at[to],
            dst_ref=out_arrived.at[plane.index],
            send_sem=out_send,
            recv_sem=out_recv,
            device_id=plane.device(to),
            device_id_type=pl.DeviceIdType.MESH,
        )

    keep_out = pltpu.make_async_copy(
        outputs.at[plane.index], out_arrived.at[plane.index], out_local
    )

    def moves(plan):
        for place, work in plan.items():

            def action(work=work):
                for name, k in work:
                    sums[name].do(k)

            at(place, action)

    @functools.partial(at, 0)
    def _():
        greet([device for level in levels for device in level.devices()])
        for ref in (
            router_grad, gain_grad, offset_grad, down_bias_grad, out_bias_grad, out_grad,
            scale_grad, small,
        ):
            ref[...] = jnp.zeros_like(ref)
        for ref, used in ((first, 12 * D), (rest, 12 * D), (early, 8 * D), (late, 4 * D)):
            if ref.shape[0] > used:
                ref[used:, :] = jnp.zeros_like(ref[used:, :])
        gain_grad[2:3, :] = gain_row[...]
        sums["own"].start()
        for to in plane.others():
            send_out(to).start()
        keep_out.start()

    moves(STARTS)

    @functools.partial(at, RESULT)
    def _():
        some = out_arrived.at[pl.ds(0, plane.count - 1)]
        wait_all(some, some, (out_send, out_recv), plane)
        keep_out.wait()

    slots = out_arrived.shape[1]

    def pick_of(expert):
        return (slot_col[...] - expert * slots == iota((ROWS, slots), 1)).astype(BF16)

    def chances_of(x):
        logits = exact_dot(x, router[...], 1, 1)
        chances = jnp.exp(logits - jnp.max(logits, axis=1, keepdims=True))
        chances = chances / jnp.sum(chances, axis=1, keepdims=True)
        within = slot_col[...] - iota(chances.shape, 1) * slots
        onehot = ((within >= 0) & (within < slots)).astype(F32)
        return chances, onehot

    def write_result():
        x = second[...]
        chances, onehot = chances_of(x)
        gate = jnp.sum(chances * onehot, axis=1, keepdims=True)
        picked = jnp.zeros((ROWS, D), F32)
        for expert in range(plane.count):
            picked += dot(pick_of(expert), out_arrived[expert], 1, 0)
        n, _ = norm_parts(gate * picked)
        flat[...] = x + n * gain[2:3, :] + offset[2:3, :]
        for line in range(ROWS // SIDE):
            result[line] = flat[line * SIDE : (line + 1) * SIDE, :].astype(BF16)

    for place in range(RESULT, RESULT + PART_A - 1):
        at(place, write_result)

    @pl.when(step < PART_A)
    def _():
        lines = ROWS // SIDE
        for line in range(lines):
            flat[line * SIDE : (line + 1) * SIDE, :] = cot[line].astype(F32)
        z = flat[...]
        x = second[...]
        dispatched = jnp.zeros((ROWS, D), F32)
        inner = jnp.zeros((ROWS, 16), F32)
        for expert in range(plane.count):
            pick = pick_of(expert)
            dispatched += dot(pick, grads[expert, :slots, :], 1, 0)
            row = grads[expert, slots : slots + 1, : min(slots, D)]
            if slots > D:
                row = jnp.concatenate(
                    [row, grads[expert, slots + 1 : slots + 2, : slots - D]], axis=1
                )
            inner += dot(pick, jnp.broadcast_to(row, (16, slots)), 1, 1)
        chances, onehot = chances_of(x)
        offset_grad[2:3, :] += col_sum(z)
        grad_logits = inner[:, 0:1] * (onehot - chances)
        grad_logits_low = grad_logits.astype(BF16)
        router_grad[...] += dot(grad_logits_low, x.astype(BF16), 0, 0)
        grad_second = z + dispatched + dot(grad_logits_low, router[...].astype(BF16), 1, 0)

        n = n_one[...].astype(F32)
        gain_grad[1:2, :] += col_sum(grad_second * n)
        offset_grad[1:2, :] += col_sum(grad_second)
        grad_branch = norm_back(gain[1:2, :] * grad_second, n, rstd_one[...])
        rows = pl.ds(pl.multiple_of(step * ROWS, 16), ROWS)
        grad_low_all[rows, :] = grad_branch.astype(BF16)
        down_bias_grad[...] += col_sum(grad_branch)
        total[rows, :] = grad_second

    @functools.partial(at, PART_A)
    def _():
        grad_low_t[...] = jnp.transpose(grad_low_all[...], (1, 0))
        first_t[...] = jnp.transpose(first_low[...], (1, 0))

    @pl.when((step >= PART_A) & (step < PART_A + PART_B))
    def _():
        bias_row = jnp.zeros((1, D), F32)
        for tile in range(TOKENS // ROWS):
            rows = slice(tile * ROWS, (tile + 1) * ROWS)
            grad_hidden = dot(grad_low_all[rows, :], down[...], 1, 1) * slope[rows, :].astype(F32)
            bias_row += col_sum(grad_hidden)
            grad_hidden_low = grad_hidden.astype(BF16)
            grad_hidden_all[rows, :] = grad_hidden_low
            total[rows, :] += dot(grad_hidden_low, up[...], 1, 1)
        up_bias_grad[pl.ds(step - PART_A, 1), :] = bias_row
        up_part = dot(first_t[...], grad_hidden_all[...], 1, 0).astype(BF16)
        down_part = jnp.transpose(
            dot(grad_low_t[...], active[...], 1, 0).astype(BF16), (1, 0)
        )
        for block in range(PART_B):

            def place(block=block):
                start = (block // 2) * dense_half + (block % 2) * 6 * D
                put_lanes(dense, start, up_part)
                put_lanes(dense, start + 3 * D, down_part)

            at(PART_A + block, place)

    @functools.partial(at, PART_A + PART_B)
    def _():
        hidden, net_slope, chance = net_again(w1, b1, w2)
        hidden_net[...] = hidden.astype(BF16)
        slope_net[...] = net_slope.astype(BF16)
        chance_net[:HEADS, :] = chance
        for name, k in MIDDLE[0]:
            sums[name].do(k)
        roll_to_windows(
            lambda row: total[row * SIDE : (row + 1) * SIDE, :],
            doubled, windows, shift_row, shift_col,
        )

        for name, k in MIDDLE[1]:
            sums[name].do(k)

        def one(window, carry):
            mine = pl.ds(pl.multiple_of(window * AREA, 16), AREA)
            z = windows[mine, :]
            n = n_zero[mine, :].astype(F32)
            gain_grad[0:1, :] += col_sum(z * n)
            offset_grad[0:1, :] += col_sum(z)
            grad_branch = norm_back(gain[0:1, :] * z, n, rstd_zero[mine, :])
            grad_low = grad_branch.astype(BF16)
            out_bias_grad[...] += col_sum(grad_branch)
            out_grad[...] += dot(mixture[window], grad_low, 1, 0)
            grad_mix[window] = dot(out_weight[...], grad_low, 1, 1).astype(BF16)
            return carry

        lax.fori_loop(0, WINDOWS, one, 0)
        for group, (into, start) in enumerate(head_places(early, late)):
            put_lanes(into, start + 3 * D, out_grad[group * 128 : (group + 1) * 128, :].astype(BF16))

    @pl.when(step >= PART_A + PART_B)
    def _():
        place = step - (PART_A + PART_B)
        group = lax.div(place, ACROSS)
        third = lax.rem(place, ACROSS)
        blank = jnp.zeros((HEAD, AREA), BF16)
        features = pl.ds(pl.multiple_of(group * 128, 128), 128)
        in_part = jnp.concatenate([in_q[...], in_k[...], in_v[...]], axis=1)

        @pl.when(third == 0)
        def _():
            in_grad[...] = jnp.zeros_like(in_grad)
            table_grad[...] = jnp.zeros_like(table_grad)

        def probs_grads(i):
            lanes = jnp.transpose(joint[i, 0, 256:384, :], (1, 0))
            coming = grad_mix[third * TRIPLE + i, features, :]
            found = []
            for head in range(4):
                parts = [blank] * 4
                parts[head] = coming[head * HEAD : (head + 1) * HEAD, :]
                found.append(dot(lanes, jnp.concatenate(parts, axis=0), 1, 0))
            return found, coming

        ahead = probs_grads(0)
        for i in range(TRIPLE):
            current, coming = ahead
            if i + 1 < TRIPLE:
                ahead = probs_grads(i + 1)
            raws = []
            for head in range(4):
                weight = probs[i, head].astype(F32)
                weighted = weight * current[head]
                grad_scores = weighted - weight * (col_sum(weighted) / col_sum(weight))
                table_grad[head] += grad_scores
                raws.append((grad_scores * scale[0, group * 4 + head]).astype(BF16))
            for head in range(4):
                own = slice(head * HEAD, (head + 1) * HEAD)
                keys = slice(128 + head * HEAD, 128 + (head + 1) * HEAD)
                grads_f32[own, :] = dot(joint[i, 0, keys, :], raws[head], 1, 0)
                grads_f32[keys, :] = dot(joint[i, 0, own, :], raws[head], 1, 1)
                joint_grad[256 + head * HEAD : 256 + (head + 1) * HEAD, :] = dot(
                    coming[own, :], probs[i, head], 1, 1
                ).astype(BF16)
            shaped = grads_f32[...].reshape(8, HEAD, AREA)
            unit = joint[i, 0, :256, :].astype(F32).reshape(8, HEAD, AREA)
            inner = jnp.sum(unit * shaped, axis=1, keepdims=True)
            shaped = shaped - unit * inner
            for part in range(8):
                joint_grad[part * HEAD : (part + 1) * HEAD, :] = (
                    shaped[part] * inverse[i, 0, part : part + 1, :]
                ).astype(BF16)
                if part < 4:
                    scale_grad[group, part : part + 1, :] += inner[part]
            joint_rows = jnp.transpose(joint_grad[...], (1, 0))
            in_grad[...] += dot(win_t[i], joint_rows, 1, 0)
            grad_window = dot(joint_rows, in_part, 1, 1)
            mine = pl.ds(pl.multiple_of((third * TRIPLE + i) * AREA, 16), AREA)
            kept = jnp.where(group == 0, 0.0, 1.0)
            windows[mine, :] = windows[mine, :] * kept + grad_window

    for group, (into, start) in enumerate(head_places(early, late)):

        def group_end(group=group, into=into, start=start):
            put_lanes(into, start, in_grad[:D, :].astype(BF16))
            in_bias_grad[group : group + 1, :] = in_grad[D : D + 1, :]

        at(PART_A + PART_B + (group + 1) * ACROSS - 1, group_end)
    moves(ENDS)
    for group in range(GROUPS - 1):
        heads = range(group * 4, group * 4 + 4)
        at(
            PART_A + PART_B + (group + 1) * ACROSS - 1,
            functools.partial(values_back, table_grad, values_grad, heads),
        )

    @functools.partial(at, PART_A + PART_B + PART_C - 1)
    def _():
        sums["late"].do(0)
        values_back(table_grad, values_grad, range(8, HEADS))
        sums["late"].do(1)
        sums["early"].do(2)
        table_one, table_two = net_back(values_grad, hidden_net, slope_net, chance_net, w2)
        put = functools.partial(put_small, small, places)
        put("table_one", table_one)
        put("table_two", table_two)
        for group in range(GROUPS):
            row = exact_dot(jnp.ones((8, AREA), F32), scale_grad[group], 1, 1)[0:1, :]
            put("scale%d" % group, jnp.concatenate([row, jnp.zeros((1, 120), F32)], axis=1))
            put("in_bias%d" % group, in_bias_grad[group : group + 1, :])
        put("out_bias", out_bias_grad[...])
        put("up_bias", up_bias_grad[...])
        put("down_bias", down_bias_grad[...])
        put("gain", gain_grad[...])
        put("offset", offset_grad[...])
        put("router", router_grad[...])
        sums["small"].do(0)
        sums["late"].do(2)
        sums["early"].do(3)
        sums["small"].do(1)

        write_result()

        def write_row(row, line):
            line = line + total[row * SIDE : (row + 1) * SIDE, :]
            for lane in range(D // 128):
                tokens_grad[pl.ds(row * SIDE * (D // 128) + lane, SIDE, stride=D // 128), :] = line[
                    :, lane * 128 : (lane + 1) * 128
                ]

        roll_to_image(windows, doubled, write_row, shift_row, shift_col)
        for k in range(2, 7):
            sums["small"].do(k)
            sums["late"].do(k + 1)
            if k == 2:
                sums["early"].do(4)
            if k == 3:
                sums["own"].do(6)
            if k in (3, 5):
                sums["rest"].do(4 + k // 2)
            if k in (4, 6):
                sums["early"].do(3 + k // 2)
        for k in range(7, len(sums["own"].moves) + 1):
            sums["own"].do(k)


def backward(
    small_rows, experts, shifts, scale, second, cot, slot_col, n_one, rstd_one, outputs, grads,
    router, first_low, active, slope, up, down, gain, offset, half, gain_row,
    n_zero, rstd_zero, joint, probs, mixture, win_t, inverse, in_weight, out_weight, w1, b1, w2,
):
    places, _ = small_places(experts)
    group, depth = lax.axis_size("expert"), lax.axis_size("dp") // 2
    counts = [2, group] + ([depth] if depth > 1 else [])
    dense_rows = padded_rows(12 * D, counts, 16)
    early_rows = padded_rows(8 * D, counts, 16)
    last_rows = padded_rows(4 * D, counts, 16)
    sum_scratch = [Line.scratch(half.shape[0], depth)]
    for rows_of in (dense_rows, dense_rows, early_rows, last_rows):
        sum_scratch += [Sum.scratch(rows_of, BF16, 128, counts)]
    sum_scratch += [Sum.scratch(small_rows, F32, 128, counts)]

    part_a = lambda i: jnp.minimum(i, PART_A - 1)
    again = lambda i: jnp.maximum(i - RESULT, 0)
    twice = lambda i: jnp.where(i < RESULT, part_a(i), again(i))
    part_b = lambda i: jnp.clip(i - PART_A, 0, PART_B - 1)
    part_c = lambda i: jnp.maximum(i - PART_A - PART_B, 0)
    third = lambda i: lax.rem(part_c(i), ACROSS)
    heads = lambda i: lax.div(part_c(i), ACROSS)
    rows = lambda width: pl.BlockSpec((ROWS, width), lambda i: (part_a(i), 0))
    lines = pl.BlockSpec((ROWS // SIDE, SIDE, D), lambda i: (part_a(i), 0, 0))
    hidden = pl.BlockSpec((TOKENS, D), lambda i: (0, part_b(i)))
    in_third = lambda j: pl.BlockSpec((D, 128), lambda i: (0, j * GROUPS + heads(i)))
    anywhere = pl.BlockSpec(memory_space=pl.ANY)
    once = lambda shape: pl.BlockSpec(
        shape, lambda *_: (0,) * len(shape), pipeline_mode=pl.Buffered(1)
    )
    return pl.pallas_call(
        functools.partial(backward_kernel, places, [len(part) for part in sum_scratch]),
        grid=(PART_A + PART_B + PART_C,),
        in_specs=[
            smem(),
            smem(),
            pl.BlockSpec((ROWS, D), lambda i: (twice(i), 0)),
            lines,
            pl.BlockSpec((ROWS, 1), lambda i: (twice(i), 0)),
            rows(D),
            rows(1),
            anywhere,
            once(grads.shape),
            once(router.shape),
            once((TOKENS, D)),
            hidden,
            hidden,
            pl.BlockSpec((D, D), lambda i: (0, part_b(i))),
            pl.BlockSpec((D, D), lambda i: (part_b(i), 0)),
            once((3, D)),
            once((3, D)),
            anywhere,
            once((1, D)),
            once((TOKENS, D)),
            once((TOKENS, 1)),
            pl.BlockSpec((TRIPLE, 1, D, AREA), lambda i: (third(i), heads(i), 0, 0)),
            pl.BlockSpec((TRIPLE, 4, AREA, AREA), lambda i: (third(i), heads(i), 0, 0)),
            once((WINDOWS, D, AREA)),
            pl.BlockSpec((TRIPLE, D + 16, AREA), lambda i: (third(i), 0, 0)),
            pl.BlockSpec((TRIPLE, 1, 8, AREA), lambda i: (third(i), heads(i), 0, 0)),
            in_third(0),
            in_third(1),
            in_third(2),
            once((D, D)),
            once(w1.shape),
            once(b1.shape),
            once(w2.shape),
        ],
        out_specs=(
            pl.BlockSpec((ROWS // SIDE, SIDE, D), lambda i: (again(i), 0, 0)),
            whole((TOKENS * D // 128, 128)),
        ) + (anywhere,) * 6,
        out_shape=(
            full((SIDE, SIDE, D), BF16),
            full((TOKENS * D // 128, 128)),
            full((2 * half.shape[0], D), BF16),
            full((dense_rows, 128), BF16),
            full((dense_rows, 128), BF16),
            full((early_rows, 128), BF16),
            full((last_rows, 128), BF16),
            full((small_rows, 128)),
        ),
        scratch_shapes=[
            pltpu.VMEM((ROWS, D), F32),
            pltpu.VMEM((TOKENS, D), BF16),
            pltpu.VMEM((D, TOKENS), BF16),
            pltpu.VMEM((D, TOKENS), BF16),
            pltpu.VMEM((TOKENS, D), BF16),
            pltpu.VMEM((TOKENS, D), F32),
            pltpu.VMEM((2 * dense_rows, 128), BF16),
            pltpu.VMEM((SIDE, SIDE + WS, D), F32),
            pltpu.VMEM((TOKENS, D), F32),
            pltpu.VMEM((WINDOWS, D, AREA), BF16),
            pltpu.VMEM((D, AREA), BF16),
            pltpu.VMEM((256, AREA), F32),
            pltpu.VMEM((D + 16, D), F32),
            pltpu.VMEM((D, D), F32),
            pltpu.VMEM((early_rows, 128), BF16),
            pltpu.VMEM((last_rows, 128), BF16),
            pltpu.VMEM((4, AREA, AREA), F32),
            pltpu.VMEM((16, TABLE), F32),
            pltpu.VMEM((UNITS, TABLE), BF16),
            pltpu.VMEM((UNITS, TABLE), BF16),
            pltpu.VMEM((16, TABLE), F32),
            pltpu.VMEM((small_rows, 128), F32),
            pltpu.VMEM((PART_B, D), F32),
            pltpu.VMEM((1, D), F32),
            pltpu.VMEM(router.shape, F32),
            pltpu.VMEM((3, D), F32),
            pltpu.VMEM((3, D), F32),
            pltpu.VMEM((1, D), F32),
            pltpu.VMEM((GROUPS, D), F32),
            pltpu.VMEM((GROUPS, 8, AREA), F32),
            pltpu.VMEM(outputs.shape, BF16),
            pltpu.SemaphoreType.DMA(()),
            pltpu.SemaphoreType.DMA(()),
            pltpu.SemaphoreType.DMA(()),
        ]
        + [ref for part in sum_scratch for ref in part],
        compiler_params=params(collective_id=2, has_side_effects=True),
        name="backward",
    )(
        shifts, scale, second, cot, slot_col, n_one, rstd_one, outputs, grads, router,
        first_low, active, slope, up, down, gain, offset, half, gain_row,
        n_zero, rstd_zero, joint, probs, mixture, win_t, inverse,
        in_weight, in_weight, in_weight, out_weight, w1, b1, w2,
    )


def unpack_kernel(
    places, own, first, rest, early, late, small,
    in_grad, in_bias, scale, table_first, table_first_bias, table_second, out_grad, out_bias,
    up_grad, up_bias, down_grad, down_bias, router, own_up, own_up_bias, own_down, own_down_bias,
    gain, offset,
):
    step = pl.program_id(0)
    for block in range(FF // D):

        def write(block=block):
            dense, start = (first, rest)[block // 2], (block % 2) * 6 * D
            up_grad[...] = get_lanes(dense, start, D, D).astype(F32)
            down_grad[...] = get_lanes(dense, start + 3 * D, D, D).astype(F32)
            own_up[...] = own[block * D : (block + 1) * D, :].astype(F32)
            own_down[...] = own[FF + block * D : FF + (block + 1) * D, :].astype(F32)

        pl.when(step == block)(write)

    @pl.when(step == 0)
    def _():
        unpack_rest(
            places, own, early, late, small, in_grad, in_bias, scale, table_first,
            table_first_bias, table_second, out_grad, out_bias, up_bias, down_bias, router,
            own_up_bias, own_down_bias, gain, offset,
        )


def unpack_rest(
    places, own, early, late, small, in_grad, in_bias, scale, table_first, table_first_bias,
    table_second, out_grad, out_bias, up_bias, down_bias, router, own_up_bias, own_down_bias,
    gain, offset,
):
    get = functools.partial(get_small, small, places)
    scales = []
    for group, (source, start) in enumerate(head_places(early, late)):
        row = get("in_bias%d" % group)
        for third in range(3):
            lanes = slice(third * D + group * 128, third * D + (group + 1) * 128)
            at = start + third * D
            in_grad[:, lanes] = source[at : at + D, :].astype(F32)
        part = get_lanes(source, start + 3 * D, 128, D)
        out_grad[group * 128 : (group + 1) * 128, :] = part.astype(F32)
        in_bias[0:1, group * 128 : (group + 1) * 128] = row[:, 0:128]
        in_bias[1:2, group * 128 : (group + 1) * 128] = row[:, 256:384]
        scales.append(get("scale%d" % group)[:, :4])
    scale[...] = jnp.concatenate(scales, axis=1).reshape(HEADS)
    tail = own[2 * FF : 2 * FF + 16, :].astype(F32)
    up_rows = get("up_bias")
    for block in range(FF // D):
        own_up_bias[:, block * D : (block + 1) * D] = tail[block : block + 1, :]
    own_down_bias[...] = tail[FF // D : FF // D + 1, :]
    up_bias[...] = jnp.concatenate(
        [up_rows[block : block + 1, :] for block in range(FF // D)], axis=1
    ).reshape(FF)
    one = get("table_one")
    table_first[...] = one[0:2, :]
    table_first_bias[...] = one[2:3, :].reshape(UNITS)
    table_second[...] = get("table_two")
    out_bias[...] = get("out_bias").reshape(D)
    down_bias[...] = get("down_bias").reshape(D)
    router[...] = get("router")
    gain[...] = get("gain")
    offset[...] = get("offset")


def unpack(parts, experts):
    places, _ = small_places(experts)
    return pl.pallas_call(
        functools.partial(unpack_kernel, places),
        grid=(FF // D,),
        in_specs=[whole(part.shape) for part in parts],
        out_specs=(
            whole((D, 3 * D)),
            whole((2, D)),
            whole((HEADS,)),
            whole((2, UNITS)),
            whole((UNITS,)),
            whole((HEADS, UNITS)),
            whole((D, D)),
            whole((D,)),
            pl.BlockSpec((D, D), lambda i: (0, i)),
            whole((FF,)),
            pl.BlockSpec((D, D), lambda i: (i, 0)),
            whole((D,)),
            whole((experts, D)),
            pl.BlockSpec((D, D), lambda i: (0, i)),
            whole((1, FF)),
            pl.BlockSpec((D, D), lambda i: (i, 0)),
            whole((1, D)),
            whole((3, D)),
            whole((3, D)),
        ),
        out_shape=(
            full((D, 3 * D)),
            full((2, D)),
            full((HEADS,)),
            full((2, UNITS)),
            full((UNITS,)),
            full((HEADS, UNITS)),
            full((D, D)),
            full((D,)),
            full((D, FF)),
            full((FF,)),
            full((FF, D)),
            full((D,)),
            full((experts, D)),
            full((D, FF)),
            full((1, FF)),
            full((FF, D)),
            full((1, D)),
            full((3, D)),
            full((3, D)),
        ),
        compiler_params=params(),
        name="unpack",
    )(*parts)


def per_device(
    tokens, shifts, routes, cotangent, in_weight, in_bias, logit_scale,
    bias_net_first_weight, bias_net_first_bias, bias_net_second_weight,
    out_weight, out_bias, up_weight, up_bias, down_weight, down_bias, router_weight,
    expert_up, expert_up_bias, expert_down, expert_down_bias, norm_gain, norm_bias,
):
    experts = router_weight.shape[1]
    dp = lax.axis_size("dp")
    group = lax.axis_size("expert")
    capacity = (5 * TOKENS + 4 * experts - 1) // (4 * experts)
    slots = -(-capacity // 16) * 16
    own_rows = padded_rows(2 * FF + 16, [2, dp // 2], 16)
    small_rows = padded_rows(small_places(experts)[1], [2, group, dp // 2], 8)

    picture = tokens.reshape(SIDE, SIDE, D)
    cot = cotangent.reshape(SIDE, SIDE, D)
    router_t = router_weight.T
    second_t = bias_net_second_weight.T

    slot_col, slot_row, cot_slots, table, scale = prep(
        routes.reshape(1, TOKENS), cot, bias_net_first_weight, bias_net_first_bias, second_t,
        logit_scale, experts, capacity, slots,
    )
    cot_arrived, normed, n_zero, rstd_zero, joint, probs, mixture, win_t, inverse = attend(
        cot_slots, shifts, scale, picture, in_weight, in_bias, table,
        out_weight, out_bias, norm_gain, norm_bias,
    )
    first_low, active, slope, n_one, rstd_one, second, buffer = forward(
        shifts, picture, normed, up_weight, up_bias, down_weight,
        down_bias, norm_gain, norm_bias, slot_row, experts, slots,
    )
    outputs, grad_returned, own_half, gain_row = run_experts(
        buffer, cot_arrived, router_t, expert_up[0], expert_up_bias, expert_down[0],
        expert_down_bias, norm_gain, own_rows,
    )
    result, tokens_grad, *parts = backward(
        small_rows, experts, shifts, scale, second, cot, slot_col, n_one, rstd_one,
        outputs, grad_returned, router_t, first_low, active, slope,
        up_weight, down_weight, norm_gain, norm_bias, own_half, gain_row,
        n_zero, rstd_zero, joint, probs, mixture, win_t, inverse, in_weight, out_weight,
        bias_net_first_weight, bias_net_first_bias, second_t,
    )
    (
        in_weight_grad, in_bias_grad, scale_grad, table_one, table_bias, table_two, out_grad,
        out_bias_grad, up_grad, up_bias_grad, down_grad, down_bias_grad, router_grad,
        own_up, own_up_bias, own_down, own_down_bias, gain_grad, offset_grad,
    ) = unpack(parts, experts)
    return (
        result.reshape(tokens.shape),
        tokens_grad.reshape(tokens.shape),
        in_weight_grad,
        in_bias_grad,
        scale_grad,
        table_one,
        table_bias,
        table_two.T,
        out_grad,
        out_bias_grad,
        up_grad,
        up_bias_grad,
        down_grad,
        down_bias_grad,
        router_grad.T,
        own_up[None],
        own_up_bias,
        own_down[None],
        own_down_bias,
        gain_grad,
        offset_grad,
    )


def solution(mesh):
    split_all = P(("dp", "expert"))
    placed = (split_all,) * 4 + (P(),) * 13 + (P("expert"),) * 4 + (P(),) * 2
    return jax.shard_map(
        per_device,
        mesh=mesh,
        in_specs=placed,
        out_specs=(split_all,) * 2 + (P(),) * 13 + (P("expert"),) * 4 + (P(),) * 2,
        check_vma=False,
    )
```
